32 devices in a mesh: dp: 4 (over x, core), space: 8 (over z, y).
Axes of the slice: x: 2, y: 2, z: 4, core: 2. Of those that a mesh axis runs over, the one named last changes fastest.
Arguments:
- volume: bfloat16 [4, 64, 32, 2048], P('dp', 'space'), may hold values from -6 to 6
- weight_first: bfloat16 [1728, 128], P('dp'), may hold values from -0.15625 to 0.15625
- weight_second: bfloat16 [3456, 256], P('dp'), may hold values from -0.109375 to 0.109375
- cotangent: bfloat16 [4, 16, 8, 2048], P('dp', 'space'), may hold values from -6 to 6
Outputs:
- activations: bfloat16 [4, 16, 8, 2048], P('dp', 'space')
- input_gradient: bfloat16 [4, 64, 32, 2048], P('dp', 'space')
- first_gradient: float32 [1728, 128], P('dp')
- second_gradient: float32 [3456, 256], P('dp')
The draws below stay inside these ranges and needn't reach their ends.
All inputs are finite; a program needn't handle non-finite values.
Results may differ from the reference program's by a relative error of at most 0.012.
Values may be sent and summed in bfloat16 or wider, within the bound.
No kernel may reach another device: no remote copies, remote signals or barrier semaphores. Data moves between devices by JAX's collectives and lax.ppermute only.
A program may use at most 64 MiB of HBM per device.

```python
import jax
import jax.numpy as jnp
from jax import lax

CIN = 64
CMID = 128
COUT = 256
S = 32
BATCH = 4
NX = 64


def with_spikes(values, stream_key, source, target, shards_of, factor):
    def block_of(axis_at):
        return (jnp.arange(values.shape[axis_at]) // (values.shape[axis_at] // shards_of)).reshape((-1,) + (1,) * (values.ndim - 1 - axis_at))

    first = jax.random.permutation(stream_key, shards_of)[block_of(target)]
    far = (block_of(target) + shards_of // 2) % shards_of
    return jnp.where((block_of(source) == first) | (block_of(source) == far), factor * values, values)


def steps_of(rng, extent, split, least, largest):
    factor_of, own = 1.0, jax.random.fold_in(rng, 6)
    for position, parts in split:
        heights = jnp.exp(jax.random.uniform(jax.random.fold_in(own, position), (parts,), jnp.float32, least / len(split), largest / len(split)))
        factor_of = factor_of * jnp.repeat(heights, extent[position] // parts).reshape([-1 if axis == position else 1 for axis in range(len(extent))])
    return factor_of


def scatter_about(stream_key, extent, spread, bound, shards=(), dtype=jnp.bfloat16):
    drawn = spread * jax.random.normal(stream_key, extent, jnp.float32)
    if shards:
        drawn = drawn * steps_of(stream_key, extent, shards, -0.22, 0.18)
    return jnp.clip(drawn, -bound, bound).astype(dtype)


def noise_with(rng, shape, scale, limit, split, heavy, kind=jnp.bfloat16):
    drawn = scale * jax.random.normal(rng, shape, jnp.float32)
    if split:
        drawn = drawn * steps_of(rng, shape, split, -0.22, 0.18)
    return jnp.clip(with_spikes(drawn, jax.random.fold_in(rng, 3), *heavy), -limit, limit).astype(kind)


def setup_inputs(seed: int = 0) -> dict:
    keys = jax.random.split(jax.random.key(seed), 5)
    volume = scatter_about(keys[0], (BATCH, NX, S, S * CIN), 1.0, 6.0, ((0, 4), (1, 8)))
    weight_first = scatter_about(keys[1], (27 * CIN, CMID), (27 * CIN) ** -0.5, 0.15625, ((0, 4),))
    weight_second = scatter_about(keys[2], (27 * CMID, COUT), (27 * CMID) ** -0.5, 0.109375, ((0, 4),))
    cotangent = noise_with(keys[3], (BATCH, NX // 4, S // 4, (S // 4) * COUT), 1.0, 6.0, ((0, 4), (1, 8)), (1, 3, 8, 2.0))
    return dict(volume=volume, weight_first=weight_first, weight_second=weight_second, cotangent=cotangent)


LEAK_SLOPE = 0.2
LAYOUT = ("NDHWC", "DHWIO", "NDHWC")


def activate(values):
    return LEAK_SLOPE * values + (1.0 - LEAK_SLOPE) * jax.nn.softplus(values)


def activate_slope(values):
    return LEAK_SLOPE + (1.0 - LEAK_SLOPE) * jax.nn.sigmoid(values)


def pad_lower(tensor):
    return jnp.pad(tensor, ((0, 0), (1, 0), (1, 0), (1, 0), (0, 0)))


def convolve(padded, kernel):
    return lax.conv_general_dilated(padded, kernel, (2, 2, 2), ((0, 0), (0, 0), (0, 0)), dimension_numbers=LAYOUT, preferred_element_type=jnp.float32)


def convolve_back(delta, kernel):
    flipped = jnp.transpose(kernel[::-1, ::-1, ::-1], (0, 1, 2, 4, 3))
    return lax.conv_general_dilated(delta, flipped, (1, 1, 1), ((2, 2), (1, 2), (1, 2)), lhs_dilation=(2, 2, 2), dimension_numbers=LAYOUT, preferred_element_type=jnp.float32)


def kernel_gradient(padded, delta):
    samples, out_depth, out_rows, out_columns, features = delta.shape
    channels = padded.shape[-1]
    flat_delta = delta.reshape(-1, features)
    pieces = []
    for offset in range(27):
        depth_tap = offset // 9
        row_tap = offset // 3 % 3
        column_tap = offset % 3
        window = lax.slice(padded, (0, depth_tap, row_tap, column_tap, 0), (samples, depth_tap + 2 * out_depth - 1, row_tap + 2 * out_rows - 1, column_tap + 2 * out_columns - 1, channels), (1, 2, 2, 2, 1))
        pieces.append(jnp.dot(window.reshape(-1, channels).T, flat_delta, preferred_element_type=jnp.float32))
    return jnp.concatenate(pieces, axis=0)


def reference(volume, weight_first, weight_second, cotangent):
    samples = volume.shape[0]
    depth_cells = volume.shape[1]
    side_cells = volume.shape[2]
    kernel_first = weight_first.reshape(3, 3, 3, CIN, CMID)
    kernel_second = weight_second.reshape(3, 3, 3, CMID, COUT)

    def sample_pass(operands):
        sample_volume, sample_cot = operands
        inputs = sample_volume.reshape(1, depth_cells, side_cells, side_cells, CIN)
        padded_input = pad_lower(inputs)
        linear_first = convolve(padded_input, kernel_first)
        hidden = activate(linear_first).astype(jnp.bfloat16)
        padded_hidden = pad_lower(hidden)
        linear_second = convolve(padded_hidden, kernel_second)
        activations = activate(linear_second).astype(jnp.bfloat16)
        incoming = sample_cot.reshape(linear_second.shape).astype(jnp.float32)
        delta_second = (incoming * activate_slope(linear_second)).astype(jnp.bfloat16)
        hidden_delta = convolve_back(delta_second, kernel_second)[:, 1:]
        delta_first = (hidden_delta * activate_slope(linear_first)).astype(jnp.bfloat16)
        input_delta = convolve_back(delta_first, kernel_first)[:, 1:].astype(jnp.bfloat16)
        return (activations.reshape(sample_cot.shape), input_delta.reshape(sample_volume.shape), kernel_gradient(padded_input, delta_first), kernel_gradient(padded_hidden, delta_second))

    activations, input_gradient, tally_first, tally_second = lax.map(sample_pass, (volume, cotangent))
    cells_first = samples * (depth_cells // 2) * (side_cells // 2) * (side_cells // 2)
    cells_second = samples * (depth_cells // 4) * (side_cells // 4) * (side_cells // 4)
    first_gradient = jnp.sum(tally_first, axis=0) * (float(cells_first) ** -0.5)
    second_gradient = jnp.sum(tally_second, axis=0) * (float(cells_second) ** -0.5)
    return activations, input_gradient, first_gradient, second_gradient
```

```python
import functools

import jax
import jax.numpy as jnp
from jax import lax
from jax.experimental import pallas as pl
from jax.experimental.pallas import tpu as pltpu
from jax.sharding import PartitionSpec as P

LEAK_SLOPE = 0.2
F32 = jnp.float32
BF16 = jnp.bfloat16
VMEM_LIMIT = 48 * 1024 * 1024


def activate(values):
    small = jnp.exp(-jnp.abs(values))
    return LEAK_SLOPE * values + (1.0 - LEAK_SLOPE) * (
        jnp.maximum(values, 0.0) + jnp.log(1.0 + small)
    )


def activate_slope(values):
    small = jnp.exp(-jnp.abs(values))
    inverse = 1.0 / (1.0 + small)
    return LEAK_SLOPE + (1.0 - LEAK_SLOPE) * jnp.where(
        values >= 0.0, inverse, small * inverse
    )


def block_row(rows, width):
    return lax.broadcasted_iota(jnp.int32, (rows, width), 0) % 8


def from_before(block):
    moved = pltpu.roll(block, 1, 0)
    return jnp.where(block_row(*block.shape) == 0, 0.0, moved)


def from_after(block):
    moved = pltpu.roll(block, block.shape[0] - 1, 0)
    return jnp.where(block_row(*block.shape) == 7, 0.0, moved)


def call(kernel, out_shape, scratch, *operands, smem=(), flops=0, aliases=None):
    nbytes = sum(a.size * a.dtype.itemsize for a in (*operands, *jax.tree.leaves(out_shape)))
    specs = [pl.BlockSpec(memory_space=pltpu.SMEM)] * len(smem)
    specs += [pl.BlockSpec(memory_space=pltpu.VMEM)] * len(operands)
    return pl.pallas_call(
        kernel,
        out_shape=out_shape,
        in_specs=specs,
        out_specs=jax.tree.map(lambda _: pl.BlockSpec(memory_space=pltpu.VMEM), out_shape),
        scratch_shapes=scratch,
        compiler_params=pltpu.CompilerParams(vmem_limit_bytes=VMEM_LIMIT),
        cost_estimate=pl.CostEstimate(flops=flops, bytes_accessed=nbytes, transcendentals=0),
    )(*smem, *operands)


def sds(shape, dtype):
    return jax.ShapeDtypeStruct(shape, dtype)


def sort_kernel(planes, in_ref, out_ref, wide):
    pairs = wide.shape[0]
    for plane in range(planes):
        for pair in range(pairs):
            wide[pair] = in_ref[plane, :, pair * 128 : (pair + 1) * 128].astype(F32)
        classes = [
            wide[:, pl.ds(r, 8, stride=4), :].reshape(pairs * 8, 128) for r in range(4)
        ]
        before = from_before(classes[3])
        for tap, (even, odd) in enumerate(
            ((before, classes[1]), (classes[0], classes[2]), (classes[1], classes[3]))
        ):
            both = jnp.concatenate(
                [even.reshape(pairs, 1, 8, 128), odd.reshape(pairs, 1, 8, 128)], axis=1
            )
            out_ref[plane, tap] = both.reshape(pairs * 16, 128).astype(BF16)


def sorted_planes(volume):
    planes, rows, width = volume.shape
    pairs = width // 128
    return call(
        functools.partial(sort_kernel, planes),
        sds((planes, 3, pairs * 16, 128), BF16),
        [pltpu.VMEM((pairs, rows, 128), F32)],
        volume,
    )


def put_rows(dst, pieces, offsets):
    rows = pieces[0].shape[0]
    for index, piece in enumerate(pieces):
        dst[pl.ds(pl.multiple_of(offsets[index], 16), rows), :] = piece[...]


def gather_taps(columns, sorted_ref, halo_ref, first, count, base):
    planes = sorted_ref.shape[0]
    rows = sorted_ref.shape[2]
    halo = halo_ref.shape[0]
    for cell in range(count):
        at = base + cell * rows
        for a in range(3):
            plane = 2 * (first + cell) - 1 + a
            for e in range(3):
                source = halo_ref.at[plane + halo, e] if plane < 0 else sorted_ref.at[plane, e]
                left = (a * 3 + e) * 256
                columns[at : at + 16, left : left + 128] = jnp.zeros((16, 128), BF16)
                columns[at + 16 : at + rows, left : left + 128] = source[0 : rows - 16, :]
                columns[at : at + rows, left + 128 : left + 256] = source[...]


def forward_first_kernel(
    offsets, alive, sorted_ref, halo_ref, w0, w1, w2, w3,
    slope_ref, windows_ref, sorted_halo, wide, columns, whole, padded, hidden,
):
    halo = halo_ref.shape[0]
    planes = sorted_ref.shape[0]
    rows = sorted_ref.shape[2]
    cells = planes // 2
    sort_kernel(halo, halo_ref, sorted_halo, wide)
    put_rows(whole, (w0, w1, w2, w3), offsets)
    for tap in range(9):
        padded[tap * 256 : tap * 256 + 64, :] = jnp.zeros((64, 128), BF16)
        padded[tap * 256 + 64 : (tap + 1) * 256, :] = whole[tap * 192 : (tap + 1) * 192, :]
    gather_taps(columns, sorted_ref, sorted_halo, -1, cells + 1, 0)
    linear = jnp.dot(columns[...], padded[...], preferred_element_type=F32)
    slope_ref[...] = activate_slope(linear[rows:])
    hidden[...] = activate(linear).reshape(hidden.shape)
    hidden[0] = hidden[0] * alive[0]
    pairs = rows // 16
    half = pairs // 2
    for out in range(cells // 2):
        for a in range(3):
            plane = 2 * out + a
            for e in range(3):
                for f in range(3):
                    block = hidden[plane, :, 0 if f == 1 else 1, 0 if e == 1 else 1]
                    block = block.reshape(half * 8, 128)
                    if e == 0:
                        block = from_before(block)
                    if f == 0:
                        block = jnp.concatenate(
                            [jnp.zeros((8, 128), F32), block[: half * 8 - 8]], axis=0
                        )
                    left = ((a * 3 + e) * 3 + f) * 128
                    windows_ref[out * half * 8 : (out + 1) * half * 8, left : left + 128] = (
                        block.astype(BF16)
                    )


def forward_first(sorted_volume, halo, shards, offsets, alive):
    planes, _, rows, _ = sorted_volume.shape
    cells = planes // 2
    shard = shards[0].shape[0]
    pairs = rows // 16
    return call(
        forward_first_kernel,
        (sds((cells * rows, 128), F32), sds((cells * rows // 8, 27 * 128), BF16)),
        [
            pltpu.VMEM((halo.shape[0], 3, rows, 128), BF16),
            pltpu.VMEM((pairs, halo.shape[1], 128), F32),
            pltpu.VMEM(((cells + 1) * rows, 9 * 256), BF16),
            pltpu.VMEM((4 * shard, 128), BF16),
            pltpu.VMEM((9 * 256, 128), BF16),
            pltpu.VMEM((cells + 1, pairs // 2, 2, 2, 8, 128), F32),
        ],
        sorted_volume, halo, *shards,
        smem=(offsets, alive),
        flops=2 * (cells + 1) * rows * 9 * 256 * 128,
    )


def forward_second_kernel(
    offsets, windows_ref, cot_ref, w0, w1, w2, w3,
    act_ref, delta_ref, g0, g1, g2, g3, whole, total,
):
    put_rows(whole, (w0, w1, w2, w3), offsets)
    linear = jnp.dot(windows_ref[...], whole[...], preferred_element_type=F32)
    outs, _, width = cot_ref.shape
    features = linear.shape[1]
    count = width // features
    acted = activate(linear)
    slope = activate_slope(linear)
    deltas = []
    for out in range(outs):
        base = out * count * 8
        act_ref[out] = jnp.concatenate(
            [acted[base + q * 8 : base + (q + 1) * 8] for q in range(count)], axis=1
        ).astype(BF16)
        cot = cot_ref[out].astype(F32)
        deltas.append(
            jnp.concatenate(
                [cot[:, q * features : (q + 1) * features] for q in range(count)], axis=0
            )
        )
    delta = (jnp.concatenate(deltas, axis=0) * slope).astype(BF16)
    delta_ref[...] = delta
    total[...] = lax.dot_general(
        windows_ref[...], delta, (((0,), (0,)), ((), ())), preferred_element_type=F32
    ).astype(BF16)
    rows = g0.shape[0]
    for index, piece in enumerate((g0, g1, g2, g3)):
        piece[...] = total[pl.ds(pl.multiple_of(offsets[index], 16), rows), :]


def forward_second(windows, cot, shards, offsets):
    rows, features = shards[0].shape
    piece = sds((rows, features), BF16)
    return call(
        forward_second_kernel,
        (sds(cot.shape, BF16), sds((windows.shape[0], features), BF16), piece, piece, piece, piece),
        [pltpu.VMEM((4 * rows, features), BF16), pltpu.VMEM((4 * rows, features), BF16)],
        windows, cot, *shards,
        smem=(offsets,),
        flops=4 * windows.shape[0] * 4 * rows * features,
    )


def back_second_kernel(offsets, delta_ref, w0, w1, w2, w3, rim_ref, spread_ref, whole, product):
    put_rows(whole, (w0, w1, w2, w3), offsets)
    product[...] = lax.dot_general(
        delta_ref[...], whole[...], (((1,), (1,)), ((), ())), preferred_element_type=F32
    )
    cells, half = spread_ref.shape[0], spread_ref.shape[1]
    size = half * 8

    def term(out, a, e, f):
        left = ((a * 3 + e) * 3 + f) * 128
        block = product[out * size : (out + 1) * size, left : left + 128]
        if f == 0:
            block = jnp.concatenate([block[8:], jnp.zeros((8, 128), F32)], axis=0)
        if e == 0:
            block = from_after(block)
        return block

    for plane in range(-1, cells):
        taps = [
            (out, a) for out in range(cells // 2) for a in range(3) if 2 * out - 1 + a == plane
        ]
        for column in range(2):
            for row in range(2):
                sums = sum(
                    term(out, a, e, f)
                    for out, a in taps
                    for e in ((0, 2) if row else (1,))
                    for f in ((0, 2) if column else (1,))
                ).reshape(half, 8, 128)
                if plane < 0:
                    rim_ref[:, column, row] = sums
                else:
                    spread_ref[plane, :, column, row] = sums


def back_second(delta, shards, offsets, cells):
    rows, features = shards[0].shape
    half = delta.shape[0] // (cells // 2) // 8
    return call(
        back_second_kernel,
        (sds((half, 2, 2, 8, 128), F32), sds((cells, half, 2, 2, 8, 128), F32)),
        [pltpu.VMEM((4 * rows, features), BF16), pltpu.VMEM((delta.shape[0], 4 * rows), F32)],
        delta, *shards,
        smem=(offsets,),
        flops=2 * delta.shape[0] * 4 * rows * features,
    )


def back_first_kernel(
    offsets, spread_ref, rim_ref, slope_ref, sorted_ref, halo_ref,
    delta_ref, g0, g1, g2, g3, sorted_halo, wide, columns, total,
):
    rows = sorted_ref.shape[2]
    cells = sorted_ref.shape[0] // 2
    sort_kernel(1, halo_ref, sorted_halo, wide)
    gather_taps(columns, sorted_ref, sorted_halo, 0, cells, 0)
    last = (cells - 1) * rows
    delta_ref[:last, :] = (spread_ref[:last, :] * slope_ref[:last, :]).astype(BF16)
    delta_ref[last:, :] = (
        (spread_ref[last:, :] + rim_ref[...].astype(F32)) * slope_ref[last:, :]
    ).astype(BF16)
    flipped = jnp.transpose(delta_ref[...].astype(F32)).astype(BF16)
    tally = jnp.dot(flipped, columns[...], preferred_element_type=F32)
    for tap in range(9):
        turned = jnp.transpose(tally[:, tap * 256 : (tap + 1) * 256])
        total[tap * 192 : (tap + 1) * 192, :] = turned[64:].astype(BF16)
    size = g0.shape[0]
    for index, piece in enumerate((g0, g1, g2, g3)):
        piece[...] = total[pl.ds(pl.multiple_of(offsets[index], 16), size), :]


def back_first(spread, rim, slope, sorted_volume, halo, offsets, shard):
    planes, _, rows, _ = sorted_volume.shape
    cells = planes // 2
    piece = sds((shard, 128), BF16)
    return call(
        back_first_kernel,
        (sds((cells * rows, 128), BF16), piece, piece, piece, piece),
        [
            pltpu.VMEM((1, 3, rows, 128), BF16),
            pltpu.VMEM((rows // 16, halo.shape[1], 128), F32),
            pltpu.VMEM((cells * rows, 9 * 256), BF16),
            pltpu.VMEM((4 * shard, 128), BF16),
        ],
        spread, rim, slope, sorted_volume, halo,
        smem=(offsets,),
        flops=2 * cells * rows * 9 * 256 * 128,
    )


def back_input_kernel(
    offsets, delta_ref, w0, w1, w2, w3, rim_ref, last_ref, out_ref, whole, turned, pairs, product, wide
):
    put_rows(whole, (w0, w1, w2, w3), offsets)
    for tap in range(9):
        top = tap * 128
        turned[top : top + 128, 0:128] = whole[tap * 192 + 64 : (tap + 1) * 192, :]
        turned[top : top + 64, 128:256] = jnp.zeros((64, 128), BF16)
        turned[top + 64 : top + 128, 128:256] = whole[tap * 192 : tap * 192 + 64, :]
    planes, side, width = out_ref.shape
    cells = planes // 2
    rows = delta_ref.shape[0] // cells
    groups = rows // 16
    for cell in range(cells):
        at = cell * rows
        pairs[at : at + rows, 0:128] = delta_ref[at : at + rows, :]
        pairs[at : at + rows - 16, 128:256] = delta_ref[at + 16 : at + rows, :]
        pairs[at + rows - 16 : at + rows, 128:256] = jnp.zeros((16, 128), BF16)
    product[...] = lax.dot_general(
        pairs[...], turned[...], (((1,), (1,)), ((), ())), preferred_element_type=F32
    ).reshape(product.shape)

    def part(cell, a, e, parity):
        left = (a * 3 + e) * 128
        return product[cell * groups : (cell + 1) * groups, parity, :, left : left + 128]

    def after(block):
        flat = block.reshape(groups * 8, 128)
        return from_after(flat).reshape(groups, 8, 128)

    for plane in range(-1, planes):
        taps = [(o, a) for o in range(cells) for a in range(3) if 2 * o - 1 + a == plane]
        wide[:, pl.ds(0, 8, stride=4), :] = sum(part(o, a, 1, 0) for o, a in taps)
        wide[:, pl.ds(1, 8, stride=4), :] = sum(
            part(o, a, 2, 0) + part(o, a, 0, 1) for o, a in taps
        )
        wide[:, pl.ds(2, 8, stride=4), :] = sum(part(o, a, 1, 1) for o, a in taps)
        wide[:, pl.ds(3, 8, stride=4), :] = sum(part(o, a, 2, 1) for o, a in taps) + after(
            sum(part(o, a, 0, 0) for o, a in taps)
        )
        for group in range(groups):
            lanes = slice(group * 128, (group + 1) * 128)
            block = wide[group]
            if plane < 0:
                rim_ref[:, lanes] = block.astype(BF16)
            else:
                out_ref[plane, :, lanes] = block.astype(BF16)
            if plane == planes - 1:
                last_ref[:, lanes] = block


def back_input(delta, shards, offsets, shape):
    planes, side, width = shape
    shard = shards[0].shape[0]
    rows = delta.shape[0]
    return call(
        back_input_kernel,
        (sds((side, width), BF16), sds((side, width), F32), sds(shape, BF16)),
        [
            pltpu.VMEM((4 * shard, 128), BF16),
            pltpu.VMEM((9 * 128, 256), BF16),
            pltpu.VMEM((rows, 256), BF16),
            pltpu.VMEM((rows // 16, 2, 8, 9 * 128), F32),
            pltpu.VMEM((width // 128, side, 128), F32),
        ],
        delta, *shards,
        smem=(offsets,),
        flops=2 * rows * 9 * 128 * 256,
    )


def close_kernel(whole_ref, last_ref, rim_ref, out_ref):
    del whole_ref
    out_ref[0] = (last_ref[...] + rim_ref[...].astype(F32)).astype(BF16)


def close_input(whole, last, rim):
    planes, side, width = whole.shape
    flat = pl.BlockSpec((side, width), lambda i: (0, 0))
    return pl.pallas_call(
        close_kernel,
        grid=(1,),
        out_shape=sds(whole.shape, BF16),
        in_specs=[pl.BlockSpec(memory_space=pl.ANY), flat, flat],
        out_specs=pl.BlockSpec((1, side, width), lambda i: (planes - 1, 0, 0)),
        input_output_aliases={0: 0},
        cost_estimate=pl.CostEstimate(
            flops=0, bytes_accessed=side * width * 8, transcendentals=0
        ),
    )(whole, last, rim)


def pack_kernel(order, *refs):
    (s0, s1, s2, f0, f1, f2, *outs, flat) = refs
    rows = s0.shape[0]
    second = s0[...].astype(F32) + s1[...].astype(F32) + s2[...].astype(F32)
    lanes = second.shape[1] // 128
    for lane in range(lanes):
        flat[lane * rows : (lane + 1) * rows, :] = second[:, lane * 128 : (lane + 1) * 128].astype(BF16)
    top = lanes * rows
    small = f0.shape[0]
    first = f0[...].astype(F32) + f1[...].astype(F32) + f2[...].astype(F32)
    flat[top : top + small, :] = first.astype(BF16)
    rest = flat.shape[0] - top - small
    if rest:
        flat[top + small :, :] = jnp.zeros((rest, 128), BF16)
    size = outs[0].shape[0]
    for index, out in enumerate(outs):
        out[...] = flat[pl.ds(pl.multiple_of(order[index] * size, 16), size), :]


def unpack_kernel(scale_first, scale_second, order, *refs):
    *chunks, first_ref, second_ref, flat = refs
    size = chunks[0].shape[0]
    for index, chunk in enumerate(chunks):
        flat[pl.ds(pl.multiple_of(order[index] * size, 16), size), :] = chunk[...]
    rows, features = second_ref.shape
    for lane in range(features // 128):
        second_ref[:, lane * 128 : (lane + 1) * 128] = (
            flat[lane * rows : (lane + 1) * rows, :].astype(F32) * scale_second
        )
    top = rows * (features // 128)
    first_ref[...] = flat[top : top + first_ref.shape[0], :].astype(F32) * scale_first


def total(pieces):
    return sum(piece.astype(F32) for piece in pieces)


def swap(value, axis, bits):
    size = lax.axis_size(axis)
    return lax.ppermute(value, axis, [(i, i ^ bits) for i in range(size)])


def shifted(value, axis, by):
    size = lax.axis_size(axis)
    pairs = [(i, i + by) for i in range(size) if 0 <= i + by < size]
    return lax.ppermute(value, axis, pairs)


def sum_over_space(chunks):
    count = len(chunks)
    if count == 1:
        return chunks
    group = min(8, count)
    partial = []
    for high in range(0, count, group):
        got = [chunks[high]] + [swap(chunks[high + k], "space", k) for k in range(1, group)]
        partial.append(total(got).astype(BF16))
    if count > group:
        partial = sum_over_space_high(partial, group)
    sums = [None] * count
    for high in range(count // group):
        sums[high * group] = partial[high]
        for k in range(1, group):
            sums[high * group + k] = swap(partial[high], "space", k)
    return sums


def sum_over_space_high(chunks, stride):
    count = len(chunks)
    got = [chunks[0]] + [swap(chunks[k], "space", k * stride) for k in range(1, count)]
    mine = total(got).astype(BF16)
    return [mine] + [swap(mine, "space", k * stride) for k in range(1, count)]


def local(volume, weight_first, weight_second, cotangent):
    samples, planes, side, width = volume.shape
    data = lax.axis_index("dp")
    place = lax.axis_index("space")
    spaces = lax.axis_size("space")
    small, big = weight_first.shape[0], weight_second.shape[0]
    partners = jnp.arange(4, dtype=jnp.int32) ^ data
    offsets_first = partners * small
    offsets_second = partners * big
    alive = (place > 0).astype(F32).reshape(1)
    order = jnp.arange(spaces, dtype=jnp.int32) ^ place

    inputs = volume.reshape(planes, side, width)
    halo = shifted(inputs[planes - 3 :], "space", 1)
    first_x = swap(weight_first, "dp", 2)
    first_core = swap(weight_first, "dp", 1)
    second_x = swap(weight_second, "dp", 2)
    second_core = swap(weight_second, "dp", 1)
    first_far = swap(first_x, "dp", 1)
    second_far = swap(second_x, "dp", 1)
    shards_first = (weight_first, first_core, first_x, first_far)
    shards_second = (weight_second, second_core, second_x, second_far)

    sorted_volume = sorted_planes(inputs)
    slope, windows = forward_first(sorted_volume, halo, shards_first, offsets_first, alive)
    cot = cotangent.reshape(cotangent.shape[1:])
    activations, delta_second, *second = forward_second(windows, cot, shards_second, offsets_second)
    second_sum = second[2].astype(F32) + swap(second[3], "dp", 1).astype(F32)
    second_here = swap(second[1], "dp", 1)
    second_there = swap(second_sum.astype(BF16), "dp", 2)

    cells = planes // 2
    rim, spread = back_second(delta_second, shards_second, offsets_second, cells)
    rim = shifted(rim.reshape(-1, 128).astype(BF16), "space", -1)
    delta_first, *first = back_first(
        spread.reshape(-1, 128), rim, slope, sorted_volume, halo[2:], offsets_first, small
    )
    first_sum = first[2].astype(F32) + swap(first[3], "dp", 1).astype(F32)
    first_here = swap(first[1], "dp", 1)
    first_there = swap(first_sum.astype(BF16), "dp", 2)

    last_rim, last, gradient = back_input(delta_first, shards_first, offsets_first, inputs.shape)
    last_rim = shifted(last_rim, "space", -1)
    input_gradient = close_input(gradient, last, last_rim)

    lanes = weight_second.shape[1] // 128
    rows = lanes * big + small
    size = -(-rows // (16 * spaces)) * 16
    chunk = sds((size, 128), BF16)
    chunks = call(
        pack_kernel,
        (chunk,) * spaces,
        [pltpu.VMEM((size * spaces, 128), BF16)],
        second[0], second_here, second_there, first[0], first_here, first_there,
        smem=(order,),
    )
    sums = sum_over_space(list(chunks))
    cells_first = samples * lax.axis_size("dp") * cells * spaces * (side // 2) ** 2
    cells_second = cells_first // 8
    first_gradient, second_gradient = call(
        functools.partial(unpack_kernel, float(cells_first) ** -0.5, float(cells_second) ** -0.5),
        (sds(weight_first.shape, F32), sds(weight_second.shape, F32)),
        [pltpu.VMEM((size * spaces, 128), BF16)],
        *sums,
        smem=(order,),
    )
    return (
        activations.reshape(cotangent.shape),
        input_gradient.reshape(volume.shape),
        first_gradient,
        second_gradient,
    )


def solution(mesh):
    return jax.shard_map(
        local,
        mesh=mesh,
        in_specs=(
            P("dp", "space", None, None),
            P("dp", None),
            P("dp", None),
            P("dp", "space", None, None),
        ),
        out_specs=(
            P("dp", "space", None, None),
            P("dp", "space", None, None),
            P("dp", None),
            P("dp", None),
        ),
        check_vma=False,
    )
```

```python
import functools

import jax
import jax.numpy as jnp
from jax import lax
from jax.experimental import pallas as pl
from jax.experimental.pallas import tpu as pltpu
from jax.sharding import PartitionSpec as P

LEAK_SLOPE = 0.2
F32 = jnp.float32
BF16 = jnp.bfloat16
VMEM_LIMIT = 48 * 1024 * 1024


def activate(values):
    small = jnp.exp(-jnp.abs(values))
    return LEAK_SLOPE * values + (1.0 - LEAK_SLOPE) * (
        jnp.maximum(values, 0.0) + jnp.log(1.0 + small)
    )


def activate_slope(values):
    small = jnp.exp(-jnp.abs(values))
    inverse = 1.0 / (1.0 + small)
    return LEAK_SLOPE + (1.0 - LEAK_SLOPE) * jnp.where(
        values >= 0.0, inverse, small * inverse
    )


def block_row(rows, width):
    return lax.broadcasted_iota(jnp.int32, (rows, width), 0) % 8


def from_before(block):
    moved = pltpu.roll(block, 1, 0)
    return jnp.where(block_row(*block.shape) == 0, 0.0, moved)


def from_after(block):
    moved = pltpu.roll(block, block.shape[0] - 1, 0)
    return jnp.where(block_row(*block.shape) == 7, 0.0, moved)


def call(kernel, out_shape, scratch, *operands, smem=(), micros=1.0):
    nbytes = sum(a.size * a.dtype.itemsize for a in (*operands, *jax.tree.leaves(out_shape)))
    specs = [pl.BlockSpec(memory_space=pltpu.SMEM)] * len(smem)
    specs += [pl.BlockSpec(memory_space=pltpu.VMEM)] * len(operands)
    return pl.pallas_call(
        kernel,
        out_shape=out_shape,
        in_specs=specs,
        out_specs=jax.tree.map(lambda _: pl.BlockSpec(memory_space=pltpu.VMEM), out_shape),
        scratch_shapes=scratch,
        compiler_params=pltpu.CompilerParams(vmem_limit_bytes=VMEM_LIMIT),
        cost_estimate=pl.CostEstimate(
            flops=int(micros * 1.15e9), bytes_accessed=nbytes, transcendentals=0
        ),
    )(*smem, *operands)


def sds(shape, dtype):
    return jax.ShapeDtypeStruct(shape, dtype)


def sort_kernel(planes, in_ref, out_ref, wide):
    pairs = wide.shape[0]
    for plane in range(planes):
        for pair in range(pairs):
            wide[pair] = in_ref[plane, :, pair * 128 : (pair + 1) * 128].astype(F32)
        classes = [
            wide[:, pl.ds(r, 8, stride=4), :].reshape(pairs * 8, 128) for r in range(4)
        ]
        before = from_before(classes[3])
        for tap, (even, odd) in enumerate(
            ((before, classes[1]), (classes[0], classes[2]), (classes[1], classes[3]))
        ):
            both = jnp.concatenate(
                [even.reshape(pairs, 1, 8, 128), odd.reshape(pairs, 1, 8, 128)], axis=1
            )
            out_ref[plane, tap] = both.reshape(pairs * 16, 128).astype(BF16)


def sorted_planes(volume):
    planes, rows, width = volume.shape
    pairs = width // 128
    return call(
        functools.partial(sort_kernel, planes),
        sds((planes, 3, pairs * 16, 128), BF16),
        [pltpu.VMEM((pairs, rows, 128), F32)],
        volume,
    )


def put_rows(dst, pieces, offsets):
    rows = pieces[0].shape[0]
    for index, piece in enumerate(pieces):
        dst[pl.ds(pl.multiple_of(offsets[index], 16), rows), :] = piece[...]


def gather_taps(columns, sorted_ref, halo_ref, first, count, base):
    rows = sorted_ref.shape[2]
    for cell in range(count):
        at = base + cell * rows
        for a in range(3):
            plane = 2 * (first + cell) - 1 + a
            for e in range(3):
                source = halo_ref.at[0, e] if plane < 0 else sorted_ref.at[plane, e]
                left = (a * 3 + e) * 256
                columns[at : at + 16, left : left + 128] = jnp.zeros((16, 128), BF16)
                columns[at + 16 : at + rows, left : left + 128] = source[0 : rows - 16, :]
                columns[at : at + rows, left + 128 : left + 256] = source[...]


def pad_first(whole, padded):
    for tap in range(9):
        padded[tap * 256 : tap * 256 + 64, :] = jnp.zeros((64, 128), BF16)
        padded[tap * 256 + 64 : (tap + 1) * 256, :] = whole[tap * 192 : (tap + 1) * 192, :]


def take_windows(read, dst, out, a, half):
    for e in range(3):
        for f in range(3):
            block = read(0 if f == 1 else 1, 0 if e == 1 else 1)
            if e == 0:
                block = from_before(block)
            if f == 0:
                block = jnp.concatenate(
                    [jnp.zeros((8, 128), F32), block[: half * 8 - 8]], axis=0
                )
            left = ((a * 3 + e) * 3 + f) * 128
            dst[out * half * 8 : (out + 1) * half * 8, left : left + 128] = block.astype(BF16)


def forward_upper_kernel(
    offsets, sorted_ref, w0, w1, w2, w3, slope_ref, hidden_ref, last_ref, columns, whole, padded
):
    cells = sorted_ref.shape[0] // 2
    put_rows(whole, (w0, w1, w2, w3), offsets)
    pad_first(whole, padded)
    gather_taps(columns, sorted_ref, None, 1, cells - 1, 0)
    linear = jnp.dot(columns[...], padded[...], preferred_element_type=F32)
    hidden = activate(linear)
    hidden_ref[...] = hidden.reshape(hidden_ref.shape)
    last_ref[...] = hidden[hidden.shape[0] - last_ref.shape[0] :].astype(BF16)
    slope_ref[...] = activate_slope(linear)


def forward_upper(sorted_volume, shards, offsets):
    planes, _, rows, _ = sorted_volume.shape
    cells = planes // 2
    shard = shards[0].shape[0]
    some = (cells - 1) * rows
    return call(
        forward_upper_kernel,
        (
            sds((some, 128), F32),
            sds((cells - 1, rows // 32, 2, 2, 8, 128), F32),
            sds((rows, 128), BF16),
        ),
        [
            pltpu.VMEM((some, 9 * 256), BF16),
            pltpu.VMEM((4 * shard, 128), BF16),
            pltpu.VMEM((9 * 256, 128), BF16),
        ],
        sorted_volume, *shards,
        smem=(offsets,),
        micros=2.5,
    )


def forward_lower_kernel(
    offsets, sorted_ref, halo_ref, hidden_ref, below_ref, w0, w1, w2, w3,
    slope_ref, windows_ref, sorted_halo, wide, columns, whole, padded, lowest, below,
):
    rows = sorted_ref.shape[2]
    cells = sorted_ref.shape[0] // 2
    half = rows // 32
    sort_kernel(1, halo_ref, sorted_halo, wide)
    put_rows(whole, (w0, w1, w2, w3), offsets)
    pad_first(whole, padded)
    gather_taps(columns, sorted_ref, sorted_halo, 0, 1, 0)
    linear = jnp.dot(columns[...], padded[...], preferred_element_type=F32)
    slope_ref[...] = activate_slope(linear)
    lowest[...] = activate(linear).reshape(lowest.shape)
    below[...] = below_ref[...].astype(F32).reshape(below.shape)
    for out in range(cells // 2):
        for a in range(3):
            plane = 2 * out - 1 + a
            source = (below, lowest)[plane + 1] if plane < 1 else hidden_ref.at[plane - 1]

            def read(column, row):
                return source[:, column, row].reshape(half * 8, 128)

            take_windows(read, windows_ref, out, a, half)


def forward_lower(sorted_volume, halo, hidden, below, shards, offsets):
    planes, _, rows, _ = sorted_volume.shape
    cells = planes // 2
    shard = shards[0].shape[0]
    return call(
        forward_lower_kernel,
        (sds((rows, 128), F32), sds((cells * rows // 8, 27 * 128), BF16)),
        [
            pltpu.VMEM((1, 3, rows, 128), BF16),
            pltpu.VMEM((rows // 16, halo.shape[1], 128), F32),
            pltpu.VMEM((rows, 9 * 256), BF16),
            pltpu.VMEM((4 * shard, 128), BF16),
            pltpu.VMEM((9 * 256, 128), BF16),
            pltpu.VMEM(hidden.shape[1:], F32),
            pltpu.VMEM(hidden.shape[1:], F32),
        ],
        sorted_volume, halo, hidden, below, *shards,
        smem=(offsets,),
        micros=1.5,
    )


def put_pieces(flat, outs, slots, order):
    for index, out in enumerate(outs):
        count, size, _ = out.shape
        for place in range(count):
            row = pl.multiple_of(order[place] * size, 16)
            out[place] = flat[slots[index], pl.ds(row, size), :]


def forward_second_kernel(
    offsets, slots, order, windows_ref, cot_ref, w0, w1, w2, w3,
    act_ref, delta_ref, lowest_ref, g0, g1, g2, g3, whole, flat,
):
    put_rows(whole, (w0, w1, w2, w3), offsets)
    linear = jnp.dot(windows_ref[...], whole[...], preferred_element_type=F32)
    outs, _, width = cot_ref.shape
    features = linear.shape[1]
    count = width // features
    acted = activate(linear)
    slope = activate_slope(linear)
    deltas = []
    for out in range(outs):
        base = out * count * 8
        act_ref[out] = jnp.concatenate(
            [acted[base + q * 8 : base + (q + 1) * 8] for q in range(count)], axis=1
        ).astype(BF16)
        cot = cot_ref[out].astype(F32)
        deltas.append(
            jnp.concatenate(
                [cot[:, q * features : (q + 1) * features] for q in range(count)], axis=0
            )
        )
    delta = (jnp.concatenate(deltas, axis=0) * slope).astype(BF16)
    delta_ref[...] = delta
    lowest_ref[...] = delta[: count * 8]
    total = lax.dot_general(
        windows_ref[...], delta, (((0,), (0,)), ((), ())), preferred_element_type=F32
    ).astype(BF16)
    rows = w0.shape[0]
    lanes = features // 128
    for shard in range(4):
        for lane in range(lanes):
            flat[shard, lane * rows : (lane + 1) * rows, :] = total[
                shard * rows : (shard + 1) * rows, lane * 128 : (lane + 1) * 128
            ]
        rest = flat.shape[1] - lanes * rows
        if rest:
            flat[shard, lanes * rows :, :] = jnp.zeros((rest, 128), BF16)
    put_pieces(flat, (g0, g1, g2, g3), slots, order)


def forward_second(windows, cot, shards, offsets, slots, order, places, size):
    rows, features = shards[0].shape
    piece = sds((places, size, 128), BF16)
    return call(
        forward_second_kernel,
        (
            sds(cot.shape, BF16),
            sds((windows.shape[0], features), BF16),
            sds((windows.shape[0] // cot.shape[0], features), BF16),
            piece, piece, piece, piece,
        ),
        [
            pltpu.VMEM((4 * rows, features), BF16),
            pltpu.VMEM((4, places * size, 128), BF16),
        ],
        windows, cot, *shards,
        smem=(offsets, slots, order),
        micros=3.0,
    )


def back_second_kernel(
    offsets, slots, order, delta_ref, upper_ref, w0, w1, w2, w3,
    slope_low_ref, slope_ref, sorted_ref, halo_ref,
    out_ref, lowest_ref, g0, g1, g2, g3,
    whole, product, above, sorted_halo, wide, columns, flat,
):
    rows = sorted_ref.shape[2]
    cells = sorted_ref.shape[0] // 2
    half = rows // 32
    size = half * 8
    put_rows(whole, (w0, w1, w2, w3), offsets)
    product[...] = lax.dot_general(
        delta_ref[...], whole[...], (((1,), (1,)), ((), ())), preferred_element_type=F32
    )
    above[...] = lax.dot_general(
        upper_ref[...], whole[: 9 * 128, :], (((1,), (1,)), ((), ())), preferred_element_type=F32
    )
    sort_kernel(1, halo_ref, sorted_halo, wide)
    gather_taps(columns, sorted_ref, sorted_halo, 0, cells, 0)

    def term(out, a, e, f):
        left = ((a * 3 + e) * 3 + f) * 128
        if out == cells // 2:
            block = above[:, left : left + 128]
        else:
            block = product[out * size : (out + 1) * size, left : left + 128]
        if f == 0:
            block = jnp.concatenate([block[8:], jnp.zeros((8, 128), F32)], axis=0)
        if e == 0:
            block = from_after(block)
        return block.reshape(half, 8, 128)

    for plane in range(cells):
        taps = [
            (out, a) for out in range(cells // 2 + 1) for a in range(3) if 2 * out - 1 + a == plane
        ]
        sums = [
            sum(
                term(out, a, e, f)
                for out, a in taps
                for e in ((0, 2) if row else (1,))
                for f in ((0, 2) if column else (1,))
            ).reshape(half, 1, 8, 128)
            for column in range(2)
            for row in range(2)
        ]
        spread = jnp.concatenate(sums, axis=1).reshape(rows, 128)
        slope = slope_low_ref[...] if plane == 0 else slope_ref[(plane - 1) * rows : plane * rows, :]
        delta = (spread * slope).astype(BF16)
        out_ref[plane * rows : (plane + 1) * rows, :] = delta
        if plane == 0:
            lowest_ref[...] = delta
    flipped = jnp.transpose(out_ref[...].astype(F32)).astype(BF16)
    tally = jnp.dot(flipped, columns[...], preferred_element_type=F32)
    shard_rows = 9 * 192 // 4
    for tap in range(9):
        turned = jnp.transpose(tally[:, tap * 256 : (tap + 1) * 256])[64:].astype(BF16)
        at = tap * 192
        while at < (tap + 1) * 192:
            shard = at // shard_rows
            to = min((tap + 1) * 192, (shard + 1) * shard_rows)
            flat[shard, at - shard * shard_rows : to - shard * shard_rows, :] = turned[
                at - tap * 192 : to - tap * 192
            ]
            at = to
    rest = flat.shape[1] - shard_rows
    if rest:
        flat[:, shard_rows:, :] = jnp.zeros((4, rest, 128), BF16)
    put_pieces(flat, (g0, g1, g2, g3), slots, order)


def back_second(
    delta, upper, shards, slopes, sorted_volume, halo, offsets, slots, order, places, size
):
    rows, features = shards[0].shape
    planes, _, width, _ = sorted_volume.shape
    cells = planes // 2
    piece = sds((places, size, 128), BF16)
    return call(
        back_second_kernel,
        (sds((cells * width, 128), BF16), sds((width, 128), BF16), piece, piece, piece, piece),
        [
            pltpu.VMEM((4 * rows, features), BF16),
            pltpu.VMEM((delta.shape[0], 4 * rows), F32),
            pltpu.VMEM((upper.shape[0], 9 * 128), F32),
            pltpu.VMEM((1, 3, width, 128), BF16),
            pltpu.VMEM((width // 16, halo.shape[1], 128), F32),
            pltpu.VMEM((cells * width, 9 * 256), BF16),
            pltpu.VMEM((4, places * size, 128), BF16),
        ],
        delta, upper, *shards, *slopes, sorted_volume, halo,
        smem=(offsets, slots, order),
        micros=3.5,
    )


def back_input_kernel(
    offsets, delta_ref, upper_ref, w0, w1, w2, w3, out_ref, whole, turned, pairs, product, wide
):
    put_rows(whole, (w0, w1, w2, w3), offsets)
    for tap in range(9):
        top = tap * 128
        turned[top : top + 128, 0:128] = whole[tap * 192 + 64 : (tap + 1) * 192, :]
        turned[top : top + 64, 128:256] = jnp.zeros((64, 128), BF16)
        turned[top + 64 : top + 128, 128:256] = whole[tap * 192 : tap * 192 + 64, :]
    planes = out_ref.shape[0]
    cells = planes // 2
    rows = upper_ref.shape[0]
    groups = rows // 16
    for cell in range(cells + 1):
        at = cell * rows
        source = upper_ref if cell == cells else delta_ref.at[at : at + rows]
        pairs[at : at + rows, 0:128] = source[...]
        pairs[at : at + rows - 16, 128:256] = source[16:rows, :]
        pairs[at + rows - 16 : at + rows, 128:256] = jnp.zeros((16, 128), BF16)
    product[...] = lax.dot_general(
        pairs[...], turned[...], (((1,), (1,)), ((), ())), preferred_element_type=F32
    ).reshape(product.shape)

    def part(cell, a, e, parity):
        left = (a * 3 + e) * 128
        return product[cell * groups : (cell + 1) * groups, parity, :, left : left + 128]

    def after(block):
        flat = block.reshape(groups * 8, 128)
        return from_after(flat).reshape(groups, 8, 128)

    for plane in range(planes):
        taps = [(o, a) for o in range(cells + 1) for a in range(3) if 2 * o - 1 + a == plane]
        wide[:, pl.ds(0, 8, stride=4), :] = sum(part(o, a, 1, 0) for o, a in taps)
        wide[:, pl.ds(1, 8, stride=4), :] = sum(
            part(o, a, 2, 0) + part(o, a, 0, 1) for o, a in taps
        )
        wide[:, pl.ds(2, 8, stride=4), :] = sum(part(o, a, 1, 1) for o, a in taps)
        wide[:, pl.ds(3, 8, stride=4), :] = sum(part(o, a, 2, 1) for o, a in taps) + after(
            sum(part(o, a, 0, 0) for o, a in taps)
        )
        for group in range(groups):
            lanes = slice(group * 128, (group + 1) * 128)
            out_ref[plane, :, lanes] = wide[group].astype(BF16)


def back_input(delta, upper, shards, offsets, shape):
    planes, side, width = shape
    shard = shards[0].shape[0]
    rows = delta.shape[0] + upper.shape[0]
    return call(
        back_input_kernel,
        sds(shape, BF16),
        [
            pltpu.VMEM((4 * shard, 128), BF16),
            pltpu.VMEM((9 * 128, 256), BF16),
            pltpu.VMEM((rows, 256), BF16),
            pltpu.VMEM((rows // 16, 2, 8, 9 * 128), F32),
            pltpu.VMEM((width // 128, side, 128), F32),
        ],
        delta, upper, *shards,
        smem=(offsets,),
        micros=3.0,
    )


def unpack_kernel(scale_first, scale_second, order, *refs):
    *chunks, first_ref, second_ref, flat_first, flat_second = refs
    high = len(chunks)
    places = 2 * high
    small = flat_first.shape[0] // places
    big = flat_second.shape[0] // (2 * places)
    for index, chunk in enumerate(chunks):
        for low in range(2):
            place = order[low * high + index]
            for part in range(2):
                row = pl.multiple_of((part * places + place) * big, 16)
                flat_second[pl.ds(row, big), :] = chunk[low, part * big : (part + 1) * big, :]
            row = pl.multiple_of(place * small, 16)
            flat_first[pl.ds(row, small), :] = chunk[low, 2 * big :, :]
    rows, features = second_ref.shape
    for lane in range(features // 128):
        second_ref[:, lane * 128 : (lane + 1) * 128] = (
            flat_second[lane * rows : (lane + 1) * rows, :].astype(F32) * scale_second
        )
    first_ref[...] = flat_first[: first_ref.shape[0], :].astype(F32) * scale_first


def added(*pieces):
    return sum(piece.astype(F32) for piece in pieces).astype(BF16)


def swap(value, axis, bits):
    size = lax.axis_size(axis)
    return lax.ppermute(value, axis, [(i, i ^ bits) for i in range(size)])


def shifted(value, axis, by):
    size = lax.axis_size(axis)
    pairs = [(i, i + by) for i in range(size) if 0 <= i + by < size]
    return lax.ppermute(value, axis, pairs)


def local(volume, weight_first, weight_second, cotangent):
    samples, planes, side, width = volume.shape
    data = lax.axis_index("dp")
    place = lax.axis_index("space")
    spaces = lax.axis_size("space")
    high = spaces // 2
    small, big = weight_first.shape[0], weight_second.shape[0]
    slots = jnp.arange(4, dtype=jnp.int32) ^ data
    offsets_first = slots * small
    offsets_second = slots * big
    steps = jnp.arange(spaces, dtype=jnp.int32)
    order = place ^ (2 * (steps % high) + steps // high)
    order_second = jnp.concatenate([order, spaces + order])
    lanes = weight_second.shape[1] // 128
    size_first = -(-small // (16 * spaces)) * 16
    size_second = -(-lanes * big // (32 * spaces)) * 16

    inputs = volume.reshape(planes, side, width)
    first_x = swap(weight_first, "dp", 2)
    first_core = swap(weight_first, "dp", 1)
    second_x = swap(weight_second, "dp", 2)
    second_core = swap(weight_second, "dp", 1)
    halo = shifted(inputs[planes - 1 :], "space", 1)
    first_far = swap(first_x, "dp", 1)
    shards_first = (weight_first, first_core, first_x, first_far)

    sorted_volume = sorted_planes(inputs)
    slope, hidden, last_hidden = forward_upper(sorted_volume, shards_first, offsets_first)
    hidden_halo = shifted(last_hidden, "space", 1)
    second_x, hidden = lax.optimization_barrier((second_x, hidden))
    slope_low, windows = forward_lower(
        sorted_volume, halo, hidden, hidden_halo, shards_first, offsets_first
    )
    second_far = swap(second_x, "dp", 1)
    shards_second = (weight_second, second_core, second_x, second_far)
    cot = cotangent.reshape(cotangent.shape[1:])
    activations, delta_second, lowest_second, *second = forward_second(
        windows, cot, shards_second, offsets_second, slots, order_second,
        2 * spaces, size_second,
    )
    far = swap(second[3], "dp", 1).reshape(2, 2, high, size_second, 128)
    near = swap(second[1], "dp", 1).reshape(2, 2, high, size_second, 128)
    own = second[0].reshape(2, 2, high, size_second, 128)
    there = second[2].reshape(2, 2, high, size_second, 128)
    upper_second = shifted(lowest_second, "space", -1)
    send_a = added(there[0], far[0])
    send_b = jnp.stack([added(own[1, 1], near[1, 1]), added(there[1, 1], far[1, 1])])
    got_a = swap(send_a, "dp", 2)
    got_b = swap(send_b, "space", 1)
    upper_second, _, _ = lax.optimization_barrier((upper_second, send_a, send_b))

    delta_first, lowest_first, *first = back_second(
        delta_second, upper_second, shards_second, (slope_low, slope), sorted_volume, halo,
        offsets_second, slots, order, spaces, size_first,
    )
    upper_first = shifted(lowest_first, "space", -1)
    far_first = swap(first[3], "dp", 1).reshape(2, high, size_first, 128)
    near_first = swap(first[1], "dp", 1).reshape(2, high, size_first, 128)
    own_first = first[0].reshape(2, high, size_first, 128)
    there_first = first[2].reshape(2, high, size_first, 128)

    send_y = jnp.concatenate(
        [added(own[0, 1], near[0, 1], got_a[1]), added(own_first[1], near_first[1])], axis=1
    )
    send_x = jnp.concatenate(
        [added(there[1, 0], far[1, 0], got_b[1]), added(there_first[0], far_first[0])], axis=1
    )
    got_y = swap(send_y, "space", 1)
    got_x = swap(send_x, "dp", 2)
    pairs = []
    for d in range(4):
        for s in range(spaces):
            pairs.append((d * spaces + s, (d ^ 2) * spaces + (s ^ 1)))
    got_xy = lax.ppermute(added(there_first[1], far_first[1]), ("dp", "space"), pairs)
    held = jnp.concatenate(
        [
            added(own[0, 0], near[0, 0], got_a[0], got_y[:, :size_second]),
            added(own[1, 0], near[1, 0], got_b[0], got_x[:, :size_second]),
            added(
                own_first[0], near_first[0], got_y[:, size_second:], got_x[:, size_second:], got_xy
            ),
        ],
        axis=1,
    )
    held, upper_first = lax.optimization_barrier((held, upper_first))
    mine = added(held[0], *(swap(held[k], "space", 2 * k) for k in range(1, high)))
    both = jnp.stack([mine, swap(mine, "space", 1)])
    chunks = [both] + [swap(both, "space", 2 * k) for k in range(1, high)]

    gradient = back_input(delta_first, upper_first, shards_first, offsets_first, inputs.shape)

    cells_first = samples * lax.axis_size("dp") * (planes // 2) * spaces * (side // 2) ** 2
    cells_second = cells_first // 8
    first_gradient, second_gradient = call(
        functools.partial(unpack_kernel, float(cells_first) ** -0.5, float(cells_second) ** -0.5),
        (sds(weight_first.shape, F32), sds(weight_second.shape, F32)),
        [
            pltpu.VMEM((spaces * size_first, 128), BF16),
            pltpu.VMEM((2 * spaces * size_second, 128), BF16),
        ],
        *chunks,
        smem=(order,),
    )
    return (
        activations.reshape(cotangent.shape),
        gradient.reshape(volume.shape),
        first_gradient,
        second_gradient,
    )


def solution(mesh):
    return jax.shard_map(
        local,
        mesh=mesh,
        in_specs=(
            P("dp", "space", None, None),
            P("dp", None),
            P("dp", None),
            P("dp", "space", None, None),
        ),
        out_specs=(
            P("dp", "space", None, None),
            P("dp", "space", None, None),
            P("dp", None),
            P("dp", None),
        ),
        check_vma=False,
    )
```

```python
import functools

import jax
import jax.numpy as jnp
from jax import lax
from jax.experimental import pallas as pl
from jax.experimental.pallas import tpu as pltpu
from jax.sharding import PartitionSpec as P

LEAK_SLOPE = 0.2
F32 = jnp.float32
BF16 = jnp.bfloat16
VMEM_LIMIT = 48 * 1024 * 1024


def activate(values):
    small = jnp.exp(-jnp.abs(values))
    return LEAK_SLOPE * values + (1.0 - LEAK_SLOPE) * (
        jnp.maximum(values, 0.0) + jnp.log(1.0 + small)
    )


def activate_slope(values):
    small = jnp.exp(-jnp.abs(values))
    inverse = 1.0 / (1.0 + small)
    return LEAK_SLOPE + (1.0 - LEAK_SLOPE) * jnp.where(
        values >= 0.0, inverse, small * inverse
    )


def block_row(rows, width):
    return lax.broadcasted_iota(jnp.int32, (rows, width), 0) % 8


def from_before(block):
    moved = pltpu.roll(block, 1, 0)
    return jnp.where(block_row(*block.shape) == 0, 0.0, moved)


def from_after(block):
    moved = pltpu.roll(block, block.shape[0] - 1, 0)
    return jnp.where(block_row(*block.shape) == 7, 0.0, moved)


def call(kernel, out_shape, scratch, *operands, smem=(), micros=1.0):
    nbytes = sum(a.size * a.dtype.itemsize for a in (*operands, *jax.tree.leaves(out_shape)))
    specs = [pl.BlockSpec(memory_space=pltpu.SMEM)] * len(smem)
    specs += [pl.BlockSpec(memory_space=pltpu.VMEM)] * len(operands)
    return pl.pallas_call(
        kernel,
        out_shape=out_shape,
        in_specs=specs,
        out_specs=jax.tree.map(lambda _: pl.BlockSpec(memory_space=pltpu.VMEM), out_shape),
        scratch_shapes=scratch,
        compiler_params=pltpu.CompilerParams(vmem_limit_bytes=VMEM_LIMIT),
        cost_estimate=pl.CostEstimate(
            flops=int(micros * 1.15e9), bytes_accessed=nbytes, transcendentals=0
        ),
    )(*smem, *operands)


def sds(shape, dtype):
    return jax.ShapeDtypeStruct(shape, dtype)


def sort_kernel(planes, in_ref, out_ref, wide):
    pairs = wide.shape[0]
    for plane in range(planes):
        for pair in range(pairs):
            wide[pair] = in_ref[plane, :, pair * 128 : (pair + 1) * 128].astype(F32)
        classes = [
            wide[:, pl.ds(r, 8, stride=4), :].reshape(pairs * 8, 128) for r in range(4)
        ]
        before = from_before(classes[3])
        for tap, (even, odd) in enumerate(
            ((before, classes[1]), (classes[0], classes[2]), (classes[1], classes[3]))
        ):
            both = jnp.concatenate(
                [even.reshape(pairs, 1, 8, 128), odd.reshape(pairs, 1, 8, 128)], axis=1
            )
            out_ref[plane, tap] = both.reshape(pairs * 16, 128).astype(BF16)


def sorted_planes(volume):
    planes, rows, width = volume.shape
    pairs = width // 128
    return call(
        functools.partial(sort_kernel, planes),
        sds((planes, 3, pairs * 16, 128), BF16),
        [pltpu.VMEM((pairs, rows, 128), F32)],
        volume,
    )


def put_rows(dst, pieces, offsets):
    rows = pieces[0].shape[0]
    for index, piece in enumerate(pieces):
        dst[pl.ds(pl.multiple_of(offsets[index], 16), rows), :] = piece[...]


def gather_taps(columns, sorted_ref, halo_ref, first, count, base):
    rows = sorted_ref.shape[2]
    for cell in range(count):
        at = base + cell * rows
        for a in range(3):
            plane = 2 * (first + cell) - 1 + a
            for e in range(3):
                source = (
                    halo_ref.at[halo_ref.shape[0] + plane, e] if plane < 0 else sorted_ref.at[plane, e]
                )
                left = (a * 3 + e) * 256
                columns[at : at + 16, left : left + 128] = jnp.zeros((16, 128), BF16)
                columns[at + 16 : at + rows, left : left + 128] = source[0 : rows - 16, :]
                columns[at : at + rows, left + 128 : left + 256] = source[...]


def pad_first(whole, padded):
    for tap in range(9):
        padded[tap * 256 : tap * 256 + 64, :] = jnp.zeros((64, 128), BF16)
        padded[tap * 256 + 64 : (tap + 1) * 256, :] = whole[tap * 192 : (tap + 1) * 192, :]


def take_windows(read, dst, out, a, half):
    for e in range(3):
        for f in range(3):
            block = read(0 if f == 1 else 1, 0 if e == 1 else 1)
            if e == 0:
                block = from_before(block)
            if f == 0:
                block = jnp.concatenate(
                    [jnp.zeros((8, 128), F32), block[: half * 8 - 8]], axis=0
                )
            left = ((a * 3 + e) * 3 + f) * 128
            dst[out * half * 8 : (out + 1) * half * 8, left : left + 128] = block.astype(BF16)


def forward_upper_kernel(
    offsets, sorted_ref, w0, w1, w2, w3, slope_ref, hidden_ref, columns, whole, padded
):
    cells = sorted_ref.shape[0] // 2
    put_rows(whole, (w0, w1, w2, w3), offsets)
    pad_first(whole, padded)
    gather_taps(columns, sorted_ref, None, 1, cells - 1, 0)
    linear = jnp.dot(columns[...], padded[...], preferred_element_type=F32)
    hidden = activate(linear)
    hidden_ref[...] = hidden.reshape(hidden_ref.shape)
    slope_ref[...] = activate_slope(linear)


def forward_upper(sorted_volume, shards, offsets):
    planes, _, rows, _ = sorted_volume.shape
    cells = planes // 2
    shard = shards[0].shape[0]
    some = (cells - 1) * rows
    return call(
        forward_upper_kernel,
        (
            sds((some, 128), F32),
            sds((cells - 1, rows // 32, 2, 2, 8, 128), F32),
        ),
        [
            pltpu.VMEM((some, 9 * 256), BF16),
            pltpu.VMEM((4 * shard, 128), BF16),
            pltpu.VMEM((9 * 256, 128), BF16),
        ],
        sorted_volume, *shards,
        smem=(offsets,),
        micros=2.5,
    )


def forward_lower_kernel(
    offsets, alive, sorted_ref, halo_ref, hidden_ref, w0, w1, w2, w3,
    slope_ref, windows_ref, sorted_halo, wide, columns, whole, padded, lowest,
):
    rows = sorted_ref.shape[2]
    cells = sorted_ref.shape[0] // 2
    half = rows // 32
    sort_kernel(halo_ref.shape[0], halo_ref, sorted_halo, wide)
    put_rows(whole, (w0, w1, w2, w3), offsets)
    pad_first(whole, padded)
    gather_taps(columns, sorted_ref, sorted_halo, -1, 2, 0)
    linear = jnp.dot(columns[...], padded[...], preferred_element_type=F32)
    slope_ref[...] = activate_slope(linear)
    lowest[...] = activate(linear).reshape(lowest.shape)
    lowest[0] = lowest[0] * alive[0]
    for out in range(cells // 2):
        for a in range(3):
            plane = 2 * out - 1 + a
            source = lowest.at[plane + 1] if plane < 1 else hidden_ref.at[plane - 1]

            def read(column, row):
                return source[:, column, row].reshape(half * 8, 128)

            take_windows(read, windows_ref, out, a, half)


def forward_lower(sorted_volume, halo, hidden, shards, offsets, alive):
    planes, _, rows, _ = sorted_volume.shape
    cells = planes // 2
    shard = shards[0].shape[0]
    return call(
        forward_lower_kernel,
        (
            sds((2 * rows, 128), F32),
            sds((cells * rows // 8, 27 * 128), BF16),
            sds((halo.shape[0], 3, rows, 128), BF16),
        ),
        [
            pltpu.VMEM((rows // 16, halo.shape[1], 128), F32),
            pltpu.VMEM((2 * rows, 9 * 256), BF16),
            pltpu.VMEM((4 * shard, 128), BF16),
            pltpu.VMEM((9 * 256, 128), BF16),
            pltpu.VMEM((2, *hidden.shape[1:]), F32),
        ],
        sorted_volume, halo, hidden, *shards,
        smem=(offsets, alive),
        micros=2.0,
    )


def put_pieces(flat, outs, slots, order):
    for index, out in enumerate(outs):
        count, size, _ = out.shape
        for place in range(count):
            row = pl.multiple_of(order[place] * size, 16)
            out[place] = flat[slots[index], pl.ds(row, size), :]


def forward_second_kernel(
    offsets, slots, order, windows_ref, cot_ref, w0, w1, w2, w3,
    act_ref, delta_ref, g0, g1, g2, g3, whole, flat,
):
    put_rows(whole, (w0, w1, w2, w3), offsets)
    linear = jnp.dot(windows_ref[...], whole[...], preferred_element_type=F32)
    outs, _, width = cot_ref.shape
    features = linear.shape[1]
    count = width // features
    acted = activate(linear)
    slope = activate_slope(linear)
    deltas = []
    for out in range(outs):
        base = out * count * 8
        act_ref[out] = jnp.concatenate(
            [acted[base + q * 8 : base + (q + 1) * 8] for q in range(count)], axis=1
        ).astype(BF16)
        cot = cot_ref[out].astype(F32)
        deltas.append(
            jnp.concatenate(
                [cot[:, q * features : (q + 1) * features] for q in range(count)], axis=0
            )
        )
    delta = (jnp.concatenate(deltas, axis=0) * slope).astype(BF16)
    delta_ref[...] = delta
    total = lax.dot_general(
        windows_ref[...], delta, (((0,), (0,)), ((), ())), preferred_element_type=F32
    ).astype(BF16)
    rows = w0.shape[0]
    lanes = features // 128
    for shard in range(4):
        for lane in range(lanes):
            flat[shard, lane * rows : (lane + 1) * rows, :] = total[
                shard * rows : (shard + 1) * rows, lane * 128 : (lane + 1) * 128
            ]
        rest = flat.shape[1] - lanes * rows
        if rest:
            flat[shard, lanes * rows :, :] = jnp.zeros((rest, 128), BF16)
    put_pieces(flat, (g0, g1, g2, g3), slots, order)


def forward_second(windows, cot, shards, offsets, slots, order, places, size):
    rows, features = shards[0].shape
    piece = sds((places, size, 128), BF16)
    return call(
        forward_second_kernel,
        (
            sds(cot.shape, BF16),
            sds((windows.shape[0], features), BF16),
            piece, piece, piece, piece,
        ),
        [
            pltpu.VMEM((4 * rows, features), BF16),
            pltpu.VMEM((4, places * size, 128), BF16),
        ],
        windows, cot, *shards,
        smem=(offsets, slots, order),
        micros=3.0,
    )


def back_second_kernel(
    offsets, slots, order, delta_ref, w0, w1, w2, w3,
    slope_low_ref, slope_ref, sorted_ref, halo_ref,
    low_ref, last_ref, down_ref, g0, g1, g2, g3,
    whole, product, columns, deltas, flat,
):
    rows = sorted_ref.shape[2]
    cells = sorted_ref.shape[0] // 2
    half = rows // 32
    size = half * 8
    put_rows(whole, (w0, w1, w2, w3), offsets)
    product[...] = lax.dot_general(
        delta_ref[...], whole[...], (((1,), (1,)), ((), ())), preferred_element_type=F32
    )
    gather_taps(columns, sorted_ref, halo_ref, -1, cells + 1, 0)

    def term(out, a, e, f):
        left = ((a * 3 + e) * 3 + f) * 128
        block = product[out * size : (out + 1) * size, left : left + 128]
        if f == 0:
            block = jnp.concatenate([block[8:], jnp.zeros((8, 128), F32)], axis=0)
        if e == 0:
            block = from_after(block)
        return block.reshape(half, 8, 128)

    for plane in range(-1, cells):
        taps = [
            (out, a) for out in range(cells // 2) for a in range(3) if 2 * out - 1 + a == plane
        ]
        sums = [
            sum(
                term(out, a, e, f)
                for out, a in taps
                for e in ((0, 2) if row else (1,))
                for f in ((0, 2) if column else (1,))
            ).reshape(half, 1, 8, 128)
            for column in range(2)
            for row in range(2)
        ]
        spread = jnp.concatenate(sums, axis=1).reshape(rows, 128)
        if plane < 1:
            slope = slope_low_ref[(plane + 1) * rows : (plane + 2) * rows, :]
        else:
            slope = slope_ref[(plane - 1) * rows : plane * rows, :]
        delta = (spread * slope).astype(BF16)
        deltas[(plane + 1) * rows : (plane + 2) * rows, :] = delta
        if plane < 0:
            down_ref[:rows, :] = spread.astype(BF16)
        if plane == 0:
            down_ref[rows:, :] = delta
        if plane == cells - 1:
            last_ref[...] = spread
        elif plane >= 0:
            low_ref[plane * rows : (plane + 1) * rows, :] = delta
    flipped = jnp.transpose(deltas[...].astype(F32)).astype(BF16)
    tally = jnp.dot(flipped, columns[...], preferred_element_type=F32)
    shard_rows = 9 * 192 // 4
    for tap in range(9):
        turned = jnp.transpose(tally[:, tap * 256 : (tap + 1) * 256])[64:].astype(BF16)
        at = tap * 192
        while at < (tap + 1) * 192:
            shard = at // shard_rows
            to = min((tap + 1) * 192, (shard + 1) * shard_rows)
            flat[shard, at - shard * shard_rows : to - shard * shard_rows, :] = turned[
                at - tap * 192 : to - tap * 192
            ]
            at = to
    rest = flat.shape[1] - shard_rows
    if rest:
        flat[:, shard_rows:, :] = jnp.zeros((4, rest, 128), BF16)
    put_pieces(flat, (g0, g1, g2, g3), slots, order)


def back_second(delta, shards, slopes, sorted_volume, halo, offsets, slots, order, places, size):
    rows, features = shards[0].shape
    planes, _, width, _ = sorted_volume.shape
    cells = planes // 2
    piece = sds((places, size, 128), BF16)
    return call(
        back_second_kernel,
        (
            sds(((cells - 1) * width, 128), BF16),
            sds((width, 128), F32),
            sds((2 * width, 128), BF16),
            piece, piece, piece, piece,
        ),
        [
            pltpu.VMEM((4 * rows, features), BF16),
            pltpu.VMEM((delta.shape[0], 4 * rows), F32),
            pltpu.VMEM(((cells + 1) * width, 9 * 256), BF16),
            pltpu.VMEM(((cells + 1) * width, 128), BF16),
            pltpu.VMEM((4, places * size, 128), BF16),
        ],
        delta, *shards, *slopes, sorted_volume, halo,
        smem=(offsets, slots, order),
        micros=3.5,
    )


def back_input_kernel(
    offsets, low_ref, last_ref, slope_ref, upper_ref, w0, w1, w2, w3,
    out_ref, whole, turned, pairs, product, wide, last,
):
    put_rows(whole, (w0, w1, w2, w3), offsets)
    for tap in range(9):
        top = tap * 128
        turned[top : top + 128, 0:128] = whole[tap * 192 + 64 : (tap + 1) * 192, :]
        turned[top : top + 64, 128:256] = jnp.zeros((64, 128), BF16)
        turned[top + 64 : top + 128, 128:256] = whole[tap * 192 : tap * 192 + 64, :]
    planes = out_ref.shape[0]
    cells = planes // 2
    rows = last_ref.shape[0]
    groups = rows // 16
    last[...] = (
        (last_ref[...] + upper_ref[:rows, :].astype(F32)) * slope_ref[(cells - 2) * rows :, :]
    ).astype(BF16)
    for cell in range(cells + 1):
        at = cell * rows
        if cell < cells - 1:
            source = low_ref.at[at : at + rows]
        else:
            source = last if cell == cells - 1 else upper_ref.at[rows : 2 * rows]
        pairs[at : at + rows, 0:128] = source[...]
        pairs[at : at + rows - 16, 128:256] = source[16:rows, :]
        pairs[at + rows - 16 : at + rows, 128:256] = jnp.zeros((16, 128), BF16)
    product[...] = lax.dot_general(
        pairs[...], turned[...], (((1,), (1,)), ((), ())), preferred_element_type=F32
    ).reshape(product.shape)

    def part(cell, a, e, parity):
        left = (a * 3 + e) * 128
        return product[cell * groups : (cell + 1) * groups, parity, :, left : left + 128]

    def after(block):
        flat = block.reshape(groups * 8, 128)
        return from_after(flat).reshape(groups, 8, 128)

    for plane in range(planes):
        taps = [(o, a) for o in range(cells + 1) for a in range(3) if 2 * o - 1 + a == plane]
        wide[:, pl.ds(0, 8, stride=4), :] = sum(part(o, a, 1, 0) for o, a in taps)
        wide[:, pl.ds(1, 8, stride=4), :] = sum(
            part(o, a, 2, 0) + part(o, a, 0, 1) for o, a in taps
        )
        wide[:, pl.ds(2, 8, stride=4), :] = sum(part(o, a, 1, 1) for o, a in taps)
        wide[:, pl.ds(3, 8, stride=4), :] = sum(part(o, a, 2, 1) for o, a in taps) + after(
            sum(part(o, a, 0, 0) for o, a in taps)
        )
        for group in range(groups):
            lanes = slice(group * 128, (group + 1) * 128)
            out_ref[plane, :, lanes] = wide[group].astype(BF16)


def back_input(low, last, slope, upper, shards, offsets, shape):
    planes, side, width = shape
    shard = shards[0].shape[0]
    rows = low.shape[0] + upper.shape[0]
    return call(
        back_input_kernel,
        sds(shape, BF16),
        [
            pltpu.VMEM((4 * shard, 128), BF16),
            pltpu.VMEM((9 * 128, 256), BF16),
            pltpu.VMEM((rows, 256), BF16),
            pltpu.VMEM((rows // 16, 2, 8, 9 * 128), F32),
            pltpu.VMEM((width // 128, side, 128), F32),
            pltpu.VMEM(last.shape, BF16),
        ],
        low, last, slope, upper, *shards,
        smem=(offsets,),
        micros=3.0,
    )


def unpack_kernel(scale_first, scale_second, order, *refs):
    *chunks, first_ref, second_ref, flat_first, flat_second = refs
    high = len(chunks)
    small = flat_first.shape[0] // (4 * high)
    big = flat_second.shape[0] // (4 * high)
    for index, chunk in enumerate(chunks):
        for low in range(2):
            for part in range(2):
                place = order[(part * 2 + low) * high + index]
                row = pl.multiple_of(place * big, 16)
                flat_second[pl.ds(row, big), :] = chunk[low, part, :big, :]
                row = pl.multiple_of(place * small, 16)
                flat_first[pl.ds(row, small), :] = chunk[low, part, big:, :]
    rows, features = second_ref.shape
    for lane in range(features // 128):
        second_ref[:, lane * 128 : (lane + 1) * 128] = (
            flat_second[lane * rows : (lane + 1) * rows, :].astype(F32) * scale_second
        )
    first_ref[...] = flat_first[: first_ref.shape[0], :].astype(F32) * scale_first


def wide_sum(*pieces):
    return sum(piece.astype(F32) for piece in pieces)


def added(*pieces):
    return wide_sum(*pieces).astype(BF16)


def swap(value, axis, bits):
    size = lax.axis_size(axis)
    return lax.ppermute(value, axis, [(i, i ^ bits) for i in range(size)])


def shifted(value, axis, by):
    size = lax.axis_size(axis)
    pairs = [(i, i + by) for i in range(size) if 0 <= i + by < size]
    return lax.ppermute(value, axis, pairs)


def local(volume, weight_first, weight_second, cotangent):
    samples, planes, side, width = volume.shape
    data = lax.axis_index("dp")
    place = lax.axis_index("space")
    spaces = lax.axis_size("space")
    high = spaces // 2
    small, big = weight_first.shape[0], weight_second.shape[0]
    slots = jnp.arange(4, dtype=jnp.int32) ^ data
    offsets_first = slots * small
    offsets_second = slots * big
    alive = (place > 0).astype(F32).reshape(1)
    steps = jnp.arange(spaces, dtype=jnp.int32)
    order = place ^ (2 * (steps % high) + steps // high)
    order = jnp.concatenate([order, spaces + order])
    lanes = weight_second.shape[1] // 128
    size_first = -(-small // (32 * spaces)) * 16
    size_second = -(-lanes * big // (32 * spaces)) * 16

    inputs = volume.reshape(planes, side, width)
    first_x = swap(weight_first, "dp", 2)
    first_core = swap(weight_first, "dp", 1)
    second_x = swap(weight_second, "dp", 2)
    second_core = swap(weight_second, "dp", 1)
    halo = shifted(inputs[planes - 3 :], "space", 1)
    first_far = swap(first_x, "dp", 1)
    shards_first = (weight_first, first_core, first_x, first_far)

    sorted_volume = sorted_planes(inputs)
    slope, hidden = forward_upper(sorted_volume, shards_first, offsets_first)
    second_x, hidden = lax.optimization_barrier((second_x, hidden))
    second_far = swap(second_x, "dp", 1)
    shards_second = (weight_second, second_core, second_x, second_far)
    slope_low, windows, sorted_halo = forward_lower(
        sorted_volume, halo, hidden, shards_first, offsets_first, alive
    )
    cot = cotangent.reshape(cotangent.shape[1:])
    activations, delta_second, *second = forward_second(
        windows, cot, shards_second, offsets_second, slots, order, 2 * spaces, size_second,
    )
    low, last, down, *first = back_second(
        delta_second, shards_second, (slope_low, slope), sorted_volume, sorted_halo,
        offsets_second, slots, order, 2 * spaces, size_first,
    )
    upper = shifted(down, "space", -1)
    def pieces(value):
        return value.reshape(2, 2, high, -1, 128)

    def joined(at, *terms):
        return jnp.concatenate(
            [
                wide_sum(*(second[at] for second, _ in terms)),
                wide_sum(*(first[at] for _, first in terms)),
            ],
            axis=-2,
        )

    second_far, second_near = swap(second[3], "dp", 1), swap(second[1], "dp", 1)
    first, second_far, second_near = lax.optimization_barrier((first, second_far, second_near))
    far = pieces(second_far), pieces(swap(first[3], "dp", 1))
    near = pieces(second_near), pieces(swap(first[1], "dp", 1))
    own = pieces(second[0]), pieces(first[0])
    there = pieces(second[2]), pieces(first[2])
    got_a = swap(joined(0, there, far).astype(BF16), "dp", 2)
    got_b = swap(
        jnp.stack([joined((1, 1), own, near), joined((1, 1), there, far)]).astype(BF16), "space", 1
    )
    send_y = added(joined((0, 1), own, near), got_a[1])
    send_x = added(joined((1, 0), there, far), got_b[1])
    got_y = swap(send_y, "space", 1)
    got_x = swap(send_x, "dp", 2)
    held = jnp.stack(
        [
            added(joined((0, 0), own, near), got_a[0], got_y),
            added(joined((1, 0), own, near), got_b[0], got_x),
        ],
        axis=1,
    )
    held, upper = lax.optimization_barrier((held, upper))
    mine = added(held[0], *(swap(held[k], "space", 2 * k) for k in range(1, high)))
    both = jnp.stack([mine, swap(mine, "space", 1)])
    chunks = [both] + [swap(both, "space", 2 * k) for k in range(1, high)]

    gradient = back_input(low, last, slope, upper, shards_first, offsets_first, inputs.shape)

    cells_first = samples * lax.axis_size("dp") * (planes // 2) * spaces * (side // 2) ** 2
    cells_second = cells_first // 8
    first_gradient, second_gradient = call(
        functools.partial(unpack_kernel, float(cells_first) ** -0.5, float(cells_second) ** -0.5),
        (sds(weight_first.shape, F32), sds(weight_second.shape, F32)),
        [
            pltpu.VMEM((2 * spaces * size_first, 128), BF16),
            pltpu.VMEM((2 * spaces * size_second, 128), BF16),
        ],
        *chunks,
        smem=(order,),
    )
    return (
        activations.reshape(cotangent.shape),
        gradient.reshape(volume.shape),
        first_gradient,
        second_gradient,
    )


def solution(mesh):
    return jax.shard_map(
        local,
        mesh=mesh,
        in_specs=(
            P("dp", "space", None, None),
            P("dp", None),
            P("dp", None),
            P("dp", "space", None, None),
        ),
        out_specs=(
            P("dp", "space", None, None),
            P("dp", "space", None, None),
            P("dp", None),
            P("dp", None),
        ),
        check_vma=False,
    )
```

```python
import functools

import jax
import jax.numpy as jnp
from jax import lax
from jax.experimental import pallas as pl
from jax.experimental.pallas import tpu as pltpu
from jax.sharding import PartitionSpec as P

LEAK_SLOPE = 0.2
F32 = jnp.float32
BF16 = jnp.bfloat16
VMEM_LIMIT = 24 * 1024 * 1024


def activate(values):
    small = jnp.exp(-jnp.abs(values))
    return LEAK_SLOPE * values + (1.0 - LEAK_SLOPE) * (
        jnp.maximum(values, 0.0) + jnp.log(1.0 + small)
    )


def activate_slope(values):
    small = jnp.exp(-jnp.abs(values))
    inverse = 1.0 / (1.0 + small)
    return LEAK_SLOPE + (1.0 - LEAK_SLOPE) * jnp.where(
        values >= 0.0, inverse, small * inverse
    )


def block_row(rows, width):
    return lax.broadcasted_iota(jnp.int32, (rows, width), 0) % 8


def from_before(block):
    moved = pltpu.roll(block, 1, 0)
    return jnp.where(block_row(*block.shape) == 0, 0.0, moved)


def from_after(block):
    moved = pltpu.roll(block, block.shape[0] - 1, 0)
    return jnp.where(block_row(*block.shape) == 7, 0.0, moved)


def call(kernel, out_shape, scratch, *operands, smem=(), micros=1.0):
    nbytes = sum(a.size * a.dtype.itemsize for a in (*operands, *jax.tree.leaves(out_shape)))
    specs = [pl.BlockSpec(memory_space=pltpu.SMEM)] * len(smem)
    specs += [pl.BlockSpec(memory_space=pltpu.VMEM)] * len(operands)
    return pl.pallas_call(
        kernel,
        out_shape=out_shape,
        in_specs=specs,
        out_specs=jax.tree.map(lambda _: pl.BlockSpec(memory_space=pltpu.VMEM), out_shape),
        scratch_shapes=scratch,
        compiler_params=pltpu.CompilerParams(vmem_limit_bytes=VMEM_LIMIT),
        cost_estimate=pl.CostEstimate(
            flops=int(micros * 1.15e9), bytes_accessed=nbytes, transcendentals=0
        ),
    )(*smem, *operands)


def sds(shape, dtype):
    return jax.ShapeDtypeStruct(shape, dtype)


def sort_kernel(planes, in_ref, out_ref, wide):
    pairs = wide.shape[0]
    for plane in range(planes):
        for pair in range(pairs):
            wide[pair] = in_ref[plane, :, pair * 128 : (pair + 1) * 128].astype(F32)
        classes = [
            wide[:, pl.ds(r, 8, stride=4), :].reshape(pairs * 8, 128) for r in range(4)
        ]
        before = from_before(classes[3])
        for tap, (even, odd) in enumerate(
            ((before, classes[1]), (classes[0], classes[2]), (classes[1], classes[3]))
        ):
            both = jnp.concatenate(
                [even.reshape(pairs, 1, 8, 128), odd.reshape(pairs, 1, 8, 128)], axis=1
            )
            out_ref[plane, tap] = both.reshape(pairs * 16, 128).astype(BF16)


def sorted_planes(volume):
    planes, rows, width = volume.shape
    pairs = width // 128
    return call(
        functools.partial(sort_kernel, planes),
        sds((planes, 3, pairs * 16, 128), BF16),
        [pltpu.VMEM((pairs, rows, 128), F32)],
        volume,
    )


def put_rows(dst, pieces, offsets):
    rows = pieces[0].shape[0]
    for index, piece in enumerate(pieces):
        dst[pl.ds(pl.multiple_of(offsets[index], 16), rows), :] = piece[...]


def put_tap(columns, at, left, source):
    rows = source.shape[0]
    columns[at : at + 16, left : left + 128] = jnp.zeros((16, 128), BF16)
    columns[at + 16 : at + rows, left : left + 128] = source[0 : rows - 16, :]
    columns[at : at + rows, left + 128 : left + 256] = source[...]


def gather_taps(columns, sorted_ref, halo_ref, first, count):
    rows = sorted_ref.shape[2]
    for cell in range(count):
        for a in range(3):
            plane = 2 * (first + cell) - 1 + a
            for e in range(3):
                source = (
                    halo_ref.at[halo_ref.shape[0] + plane, e] if plane < 0 else sorted_ref.at[plane, e]
                )
                put_tap(columns, cell * rows, (a * 3 + e) * 256, source)


def pad_first(whole, padded):
    for tap in range(9):
        padded[tap * 256 : tap * 256 + 64, :] = jnp.zeros((64, 128), BF16)
        padded[tap * 256 + 64 : (tap + 1) * 256, :] = whole[tap * 192 : (tap + 1) * 192, :]


def take_windows(read, dst, out, a, half):
    for e in range(3):
        for f in range(3):
            block = read(0 if f == 1 else 1, 0 if e == 1 else 1)
            if e == 0:
                block = from_before(block)
            if f == 0:
                block = jnp.concatenate(
                    [jnp.zeros((8, 128), F32), block[: half * 8 - 8]], axis=0
                )
            left = ((a * 3 + e) * 3 + f) * 128
            dst[out * half * 8 : (out + 1) * half * 8, left : left + 128] = block.astype(BF16)


def forward_upper_kernel(
    offsets, sorted_ref, w0, w1, w2, w3,
    slope_ref, hidden_ref, partial_ref, padded_ref, columns, some, whole,
):
    cells = sorted_ref.shape[0] // 2
    put_rows(whole, (w0, w1, w2, w3), offsets)
    pad_first(whole, padded_ref)
    gather_taps(columns, sorted_ref, None, 1, cells - 1)
    linear = jnp.dot(columns[...], padded_ref[...], preferred_element_type=F32)
    hidden_ref[...] = activate(linear).reshape(hidden_ref.shape)
    slope_ref[...] = activate_slope(linear)
    for a in range(1, 3):
        for e in range(3):
            put_tap(some, 0, ((a - 1) * 3 + e) * 256, sorted_ref.at[a - 1, e])
    partial_ref[...] = jnp.dot(some[...], padded_ref[3 * 256 :, :], preferred_element_type=F32)


def forward_upper(sorted_volume, shards, offsets):
    planes, _, rows, _ = sorted_volume.shape
    cells = planes // 2
    shard = shards[0].shape[0]
    some = (cells - 1) * rows
    return call(
        forward_upper_kernel,
        (
            sds((some, 128), F32),
            sds((cells - 1, rows // 32, 2, 2, 8, 128), F32),
            sds((rows, 128), F32),
            sds((9 * 256, 128), BF16),
        ),
        [
            pltpu.VMEM((some, 9 * 256), BF16),
            pltpu.VMEM((rows, 6 * 256), BF16),
            pltpu.VMEM((4 * shard, 128), BF16),
        ],
        sorted_volume, *shards,
        smem=(offsets,),
        micros=2.5,
    )


def forward_lower_kernel(
    alive, halo_ref, hidden_ref, partial_ref, padded_ref,
    slope_ref, windows_ref, sorted_ref, wide, columns, some, lowest,
):
    rows = partial_ref.shape[0]
    cells = hidden_ref.shape[0] + 1
    half = rows // 32
    sort_kernel(halo_ref.shape[0], halo_ref, sorted_ref, wide)
    for e in range(3):
        for a in range(3):
            put_tap(columns, 0, (a * 3 + e) * 256, sorted_ref.at[a, e])
        put_tap(some, 0, e * 256, sorted_ref.at[2, e])
    below = jnp.dot(columns[...], padded_ref[...], preferred_element_type=F32)
    here = partial_ref[...] + jnp.dot(
        some[...], padded_ref[: 3 * 256, :], preferred_element_type=F32
    )
    slope_ref[:rows, :] = activate_slope(below)
    slope_ref[rows:, :] = activate_slope(here)
    lowest[0] = (activate(below) * alive[0]).reshape(lowest.shape[1:])
    lowest[1] = activate(here).reshape(lowest.shape[1:])
    for out in range(cells // 2):
        for a in range(3):
            plane = 2 * out - 1 + a
            source = lowest.at[plane + 1] if plane < 1 else hidden_ref.at[plane - 1]

            def read(column, row):
                return source[:, column, row].reshape(half * 8, 128)

            take_windows(read, windows_ref, out, a, half)


def forward_lower(halo, hidden, partial, padded, alive):
    rows = partial.shape[0]
    cells = hidden.shape[0] + 1
    return call(
        forward_lower_kernel,
        (
            sds((2 * rows, 128), F32),
            sds((cells * rows // 8, 27 * 128), BF16),
            sds((halo.shape[0], 3, rows, 128), BF16),
        ),
        [
            pltpu.VMEM((rows // 16, halo.shape[1], 128), F32),
            pltpu.VMEM((rows, 9 * 256), BF16),
            pltpu.VMEM((rows, 3 * 256), BF16),
            pltpu.VMEM((2, *hidden.shape[1:]), F32),
        ],
        halo, hidden, partial, padded,
        smem=(alive,),
        micros=1.5,
    )


def put_pieces(flat, outs, slots, order):
    for index, out in enumerate(outs):
        count, size, _ = out.shape
        for place in range(count):
            row = pl.multiple_of(order[place] * size, 16)
            out[place] = flat[slots[index], pl.ds(row, size), :]


def forward_second_kernel(
    offsets, slots, order, windows_ref, cot_ref, w0, w1, w2, w3,
    act_ref, delta_ref, g0, g1, g2, g3, whole, flat,
):
    put_rows(whole, (w0, w1, w2, w3), offsets)
    linear = jnp.dot(windows_ref[...], whole[...], preferred_element_type=F32)
    outs, _, width = cot_ref.shape
    features = linear.shape[1]
    count = width // features
    acted = activate(linear)
    slope = activate_slope(linear)
    deltas = []
    for out in range(outs):
        base = out * count * 8
        act_ref[out] = jnp.concatenate(
            [acted[base + q * 8 : base + (q + 1) * 8] for q in range(count)], axis=1
        ).astype(BF16)
        cot = cot_ref[out].astype(F32)
        deltas.append(
            jnp.concatenate(
                [cot[:, q * features : (q + 1) * features] for q in range(count)], axis=0
            )
        )
    delta = (jnp.concatenate(deltas, axis=0) * slope).astype(BF16)
    delta_ref[...] = delta
    total = lax.dot_general(
        windows_ref[...], delta, (((0,), (0,)), ((), ())), preferred_element_type=F32
    ).astype(BF16)
    rows = w0.shape[0]
    lanes = features // 128
    for shard in range(4):
        for lane in range(lanes):
            flat[shard, lane * rows : (lane + 1) * rows, :] = total[
                shard * rows : (shard + 1) * rows, lane * 128 : (lane + 1) * 128
            ]
        rest = flat.shape[1] - lanes * rows
        if rest:
            flat[shard, lanes * rows :, :] = jnp.zeros((rest, 128), BF16)
    put_pieces(flat, (g0, g1, g2, g3), slots, order)


def forward_second(windows, cot, shards, offsets, slots, order, places, size):
    rows, features = shards[0].shape
    piece = sds((places, size, 128), BF16)
    return call(
        forward_second_kernel,
        (
            sds(cot.shape, BF16),
            sds((windows.shape[0], features), BF16),
            piece, piece, piece, piece,
        ),
        [
            pltpu.VMEM((4 * rows, features), BF16),
            pltpu.VMEM((4, places * size, 128), BF16),
        ],
        windows, cot, *shards,
        smem=(offsets, slots, order),
        micros=3.0,
    )


def back_second_kernel(
    offsets, slots, order, delta_ref, w0, w1, w2, w3,
    slope_low_ref, slope_ref, sorted_ref, halo_ref,
    low_ref, last_ref, down_ref, g0, g1, g2, g3,
    whole, product, columns, deltas, flat,
):
    rows = sorted_ref.shape[2]
    cells = sorted_ref.shape[0] // 2
    half = rows // 32
    size = half * 8
    put_rows(whole, (w0, w1, w2, w3), offsets)
    product[...] = lax.dot_general(
        delta_ref[...], whole[...], (((1,), (1,)), ((), ())), preferred_element_type=F32
    )
    gather_taps(columns, sorted_ref, halo_ref, -1, cells + 1)

    def term(out, a, e, f):
        left = ((a * 3 + e) * 3 + f) * 128
        block = product[out * size : (out + 1) * size, left : left + 128]
        if f == 0:
            block = jnp.concatenate([block[8:], jnp.zeros((8, 128), F32)], axis=0)
        if e == 0:
            block = from_after(block)
        return block.reshape(half, 8, 128)

    for plane in range(-1, cells):
        taps = [
            (out, a) for out in range(cells // 2) for a in range(3) if 2 * out - 1 + a == plane
        ]
        sums = [
            sum(
                term(out, a, e, f)
                for out, a in taps
                for e in ((0, 2) if row else (1,))
                for f in ((0, 2) if column else (1,))
            ).reshape(half, 1, 8, 128)
            for column in range(2)
            for row in range(2)
        ]
        spread = jnp.concatenate(sums, axis=1).reshape(rows, 128)
        if plane < 1:
            slope = slope_low_ref[(plane + 1) * rows : (plane + 2) * rows, :]
        else:
            slope = slope_ref[(plane - 1) * rows : plane * rows, :]
        delta = (spread * slope).astype(BF16)
        deltas[(plane + 1) * rows : (plane + 2) * rows, :] = delta
        if plane < 0:
            down_ref[:rows, :] = spread.astype(BF16)
        if plane == 0:
            down_ref[rows:, :] = delta
        if plane == cells - 1:
            last_ref[...] = spread
        elif plane >= 0:
            low_ref[plane * rows : (plane + 1) * rows, :] = delta
    flipped = jnp.transpose(deltas[...].astype(F32)).astype(BF16)
    tally = jnp.dot(flipped, columns[...], preferred_element_type=F32)
    shard_rows = 9 * 192 // 4
    for tap in range(9):
        turned = jnp.transpose(tally[:, tap * 256 : (tap + 1) * 256])[64:].astype(BF16)
        at = tap * 192
        while at < (tap + 1) * 192:
            shard = at // shard_rows
            to = min((tap + 1) * 192, (shard + 1) * shard_rows)
            flat[shard, at - shard * shard_rows : to - shard * shard_rows, :] = turned[
                at - tap * 192 : to - tap * 192
            ]
            at = to
    rest = flat.shape[1] - shard_rows
    if rest:
        flat[:, shard_rows:, :] = jnp.zeros((4, rest, 128), BF16)
    put_pieces(flat, (g0, g1, g2, g3), slots, order)


def back_second(delta, shards, slopes, sorted_volume, halo, offsets, slots, order, places, size):
    rows, features = shards[0].shape
    planes, _, width, _ = sorted_volume.shape
    cells = planes // 2
    piece = sds((places, size, 128), BF16)
    return call(
        back_second_kernel,
        (
            sds(((cells - 1) * width, 128), BF16),
            sds((width, 128), F32),
            sds((2 * width, 128), BF16),
            piece, piece, piece, piece,
        ),
        [
            pltpu.VMEM((4 * rows, features), BF16),
            pltpu.VMEM((delta.shape[0], 4 * rows), F32),
            pltpu.VMEM(((cells + 1) * width, 9 * 256), BF16),
            pltpu.VMEM(((cells + 1) * width, 128), BF16),
            pltpu.VMEM((4, places * size, 128), BF16),
        ],
        delta, *shards, *slopes, sorted_volume, halo,
        smem=(offsets, slots, order),
        micros=3.5,
    )


def back_input_kernel(
    offsets, low_ref, last_ref, slope_ref, upper_ref, w0, w1, w2, w3,
    out_ref, whole, turned, pairs, product, wide, last,
):
    put_rows(whole, (w0, w1, w2, w3), offsets)
    for tap in range(9):
        top = tap * 128
        turned[top : top + 128, 0:128] = whole[tap * 192 + 64 : (tap + 1) * 192, :]
        turned[top : top + 64, 128:256] = jnp.zeros((64, 128), BF16)
        turned[top + 64 : top + 128, 128:256] = whole[tap * 192 : tap * 192 + 64, :]
    planes = out_ref.shape[0]
    cells = planes // 2
    rows = last_ref.shape[0]
    groups = rows // 16
    last[...] = (
        (last_ref[...] + upper_ref[:rows, :].astype(F32)) * slope_ref[(cells - 2) * rows :, :]
    ).astype(BF16)
    for cell in range(cells + 1):
        at = cell * rows
        if cell < cells - 1:
            source = low_ref.at[at : at + rows]
        else:
            source = last if cell == cells - 1 else upper_ref.at[rows : 2 * rows]
        pairs[at : at + rows, 0:128] = source[...]
        pairs[at : at + rows - 16, 128:256] = source[16:rows, :]
        pairs[at + rows - 16 : at + rows, 128:256] = jnp.zeros((16, 128), BF16)
    product[...] = lax.dot_general(
        pairs[...], turned[...], (((1,), (1,)), ((), ())), preferred_element_type=F32
    ).reshape(product.shape)

    def part(cell, a, e, parity):
        left = (a * 3 + e) * 128
        return product[cell * groups : (cell + 1) * groups, parity, :, left : left + 128]

    def after(block):
        flat = block.reshape(groups * 8, 128)
        return from_after(flat).reshape(groups, 8, 128)

    for plane in range(planes):
        taps = [(o, a) for o in range(cells + 1) for a in range(3) if 2 * o - 1 + a == plane]
        wide[:, pl.ds(0, 8, stride=4), :] = sum(part(o, a, 1, 0) for o, a in taps)
        wide[:, pl.ds(1, 8, stride=4), :] = sum(
            part(o, a, 2, 0) + part(o, a, 0, 1) for o, a in taps
        )
        wide[:, pl.ds(2, 8, stride=4), :] = sum(part(o, a, 1, 1) for o, a in taps)
        wide[:, pl.ds(3, 8, stride=4), :] = sum(part(o, a, 2, 1) for o, a in taps) + after(
            sum(part(o, a, 0, 0) for o, a in taps)
        )
        for group in range(groups):
            lanes = slice(group * 128, (group + 1) * 128)
            out_ref[plane, :, lanes] = wide[group].astype(BF16)


def back_input(low, last, slope, upper, shards, offsets, shape):
    planes, side, width = shape
    shard = shards[0].shape[0]
    rows = low.shape[0] + upper.shape[0]
    return call(
        back_input_kernel,
        sds(shape, BF16),
        [
            pltpu.VMEM((4 * shard, 128), BF16),
            pltpu.VMEM((9 * 128, 256), BF16),
            pltpu.VMEM((rows, 256), BF16),
            pltpu.VMEM((rows // 16, 2, 8, 9 * 128), F32),
            pltpu.VMEM((width // 128, side, 128), F32),
            pltpu.VMEM(last.shape, BF16),
        ],
        low, last, slope, upper, *shards,
        smem=(offsets,),
        micros=3.0,
    )


def unpack_kernel(scale_first, scale_second, order, *refs):
    *chunks, other, first_ref, second_ref, flat_first, flat_second = refs
    high = len(chunks)
    small = flat_first.shape[0] // (2 * high)
    big = flat_second.shape[0] // (2 * high)
    for low in range(2):
        for index in range(high):
            chunk = other.at[index] if low else chunks[index]
            place = order[low * high + index]
            flat_second[pl.ds(pl.multiple_of(place * big, 16), big), :] = chunk[:big, :]
            flat_first[pl.ds(pl.multiple_of(place * small, 16), small), :] = chunk[big:, :]
    rows, features = second_ref.shape
    for lane in range(features // 128):
        second_ref[:, lane * 128 : (lane + 1) * 128] = (
            flat_second[lane * rows : (lane + 1) * rows, :].astype(F32) * scale_second
        )
    first_ref[...] = flat_first[: first_ref.shape[0], :].astype(F32) * scale_first


def wide_sum(*pieces):
    return sum(piece.astype(F32) for piece in pieces)


def added(*pieces):
    return wide_sum(*pieces).astype(BF16)


def swap(value, axis, bits):
    size = lax.axis_size(axis)
    return lax.ppermute(value, axis, [(i, i ^ bits) for i in range(size)])


def shifted(value, axis, by):
    size = lax.axis_size(axis)
    pairs = [(i, i + by) for i in range(size) if 0 <= i + by < size]
    return lax.ppermute(value, axis, pairs)


def local(volume, weight_first, weight_second, cotangent):
    samples, planes, side, width = volume.shape
    data = lax.axis_index("dp")
    place = lax.axis_index("space")
    spaces = lax.axis_size("space")
    high = spaces // 2
    small, big = weight_first.shape[0], weight_second.shape[0]
    slots = jnp.arange(4, dtype=jnp.int32) ^ data
    offsets_first = slots * small
    offsets_second = slots * big
    alive = (place > 0).astype(F32).reshape(1)
    steps = jnp.arange(spaces, dtype=jnp.int32)
    order = place ^ (2 * (steps % high) + steps // high)
    lanes = weight_second.shape[1] // 128
    size_first = -(-small // (16 * spaces)) * 16
    size_second = -(-lanes * big // (16 * spaces)) * 16

    inputs = volume.reshape(planes, side, width)
    first_x = swap(weight_first, "dp", 2)
    first_core = swap(weight_first, "dp", 1)
    second_x = swap(weight_second, "dp", 2)
    second_core = swap(weight_second, "dp", 1)
    halo = shifted(inputs[planes - 3 :], "space", 1)
    first_far = swap(first_x, "dp", 1)
    shards_first = (weight_first, first_core, first_x, first_far)

    sorted_volume = sorted_planes(inputs)
    slope, hidden, partial, padded = forward_upper(sorted_volume, shards_first, offsets_first)
    second_x, hidden = lax.optimization_barrier((second_x, hidden))
    second_far = swap(second_x, "dp", 1)
    shards_second = (weight_second, second_core, second_x, second_far)
    slope_low, windows, sorted_halo = forward_lower(halo, hidden, partial, padded, alive)
    cot = cotangent.reshape(cotangent.shape[1:])
    activations, delta_second, *second = forward_second(
        windows, cot, shards_second, offsets_second, slots, order, spaces, size_second,
    )
    low, last, down, *first = back_second(
        delta_second, shards_second, (slope_low, slope), sorted_volume, sorted_halo,
        offsets_second, slots, order, spaces, size_first,
    )
    upper = shifted(down, "space", -1)
    def pieces(value):
        return value.reshape(2, high, -1, 128)

    def joined(at, *terms):
        return jnp.concatenate(
            [
                wide_sum(*(second[at] for second, _ in terms)),
                wide_sum(*(first[at] for _, first in terms)),
            ],
            axis=-2,
        )

    second_far, second_near = swap(second[3], "dp", 1), swap(second[1], "dp", 1)
    first, second_far, second_near = lax.optimization_barrier((first, second_far, second_near))
    far = pieces(second_far), pieces(swap(first[3], "dp", 1))
    near = pieces(second_near), pieces(swap(first[1], "dp", 1))
    own = pieces(second[0]), pieces(first[0])
    there = pieces(second[2]), pieces(first[2])
    both = [
        (d * spaces + s, (d ^ 2) * spaces + (s ^ 1)) for d in range(4) for s in range(spaces)
    ]
    got_xy = lax.ppermute(joined(1, there, far).astype(BF16), ("dp", "space"), both)
    got_x = swap(joined(0, there, far).astype(BF16), "dp", 2)
    got_y = swap(joined(1, own, near).astype(BF16), "space", 1)
    held = added(joined(0, own, near), got_x, got_y, got_xy)
    held, upper = lax.optimization_barrier((held, upper))
    mine = added(held[0], *(swap(held[k], "space", 2 * k) for k in range(1, high)))
    chunks = [mine] + [swap(mine, "space", 2 * k) for k in range(1, high)]
    chunks.append(swap(jnp.stack(chunks), "space", 1))

    gradient = back_input(low, last, slope, upper, shards_first, offsets_first, inputs.shape)

    cells_first = samples * lax.axis_size("dp") * (planes // 2) * spaces * (side // 2) ** 2
    cells_second = cells_first // 8
    first_gradient, second_gradient = call(
        functools.partial(unpack_kernel, float(cells_first) ** -0.5, float(cells_second) ** -0.5),
        (sds(weight_first.shape, F32), sds(weight_second.shape, F32)),
        [
            pltpu.VMEM((spaces * size_first, 128), BF16),
            pltpu.VMEM((spaces * size_second, 128), BF16),
        ],
        *chunks,
        smem=(order,),
    )
    return (
        activations.reshape(cotangent.shape),
        gradient.reshape(volume.shape),
        first_gradient,
        second_gradient,
    )


def solution(mesh):
    return jax.shard_map(
        local,
        mesh=mesh,
        in_specs=(
            P("dp", "space", None, None),
            P("dp", None),
            P("dp", None),
            P("dp", "space", None, None),
        ),
        out_specs=(
            P("dp", "space", None, None),
            P("dp", "space", None, None),
            P("dp", None),
            P("dp", None),
        ),
        check_vma=False,
    )
```

```python
import functools

import jax
import jax.numpy as jnp
from jax import lax
from jax.experimental import pallas as pl
from jax.experimental.pallas import tpu as pltpu
from jax.sharding import PartitionSpec as P

LEAK_SLOPE = 0.2
F32 = jnp.float32
BF16 = jnp.bfloat16
VMEM_LIMIT = 24 * 1024 * 1024


def activate(values):
    small = jnp.exp(-jnp.abs(values))
    return LEAK_SLOPE * values + (1.0 - LEAK_SLOPE) * (
        jnp.maximum(values, 0.0) + jnp.log(1.0 + small)
    )


def activate_slope(values):
    small = jnp.exp(-jnp.abs(values))
    inverse = 1.0 / (1.0 + small)
    return LEAK_SLOPE + (1.0 - LEAK_SLOPE) * jnp.where(
        values >= 0.0, inverse, small * inverse
    )


def block_row(rows, width):
    return lax.broadcasted_iota(jnp.int32, (rows, width), 0) % 8


def from_before(block):
    moved = pltpu.roll(block, 1, 0)
    return jnp.where(block_row(*block.shape) == 0, 0.0, moved)


def from_after(block):
    moved = pltpu.roll(block, block.shape[0] - 1, 0)
    return jnp.where(block_row(*block.shape) == 7, 0.0, moved)


def call(kernel, out_shape, scratch, *operands, smem=(), micros=1.0):
    nbytes = sum(a.size * a.dtype.itemsize for a in (*operands, *jax.tree.leaves(out_shape)))
    specs = [pl.BlockSpec(memory_space=pltpu.SMEM)] * len(smem)
    specs += [pl.BlockSpec(memory_space=pltpu.VMEM)] * len(operands)
    return pl.pallas_call(
        kernel,
        out_shape=out_shape,
        in_specs=specs,
        out_specs=jax.tree.map(lambda _: pl.BlockSpec(memory_space=pltpu.VMEM), out_shape),
        scratch_shapes=scratch,
        compiler_params=pltpu.CompilerParams(vmem_limit_bytes=VMEM_LIMIT),
        cost_estimate=pl.CostEstimate(
            flops=int(micros * 1.15e9), bytes_accessed=nbytes, transcendentals=0
        ),
    )(*smem, *operands)


def sds(shape, dtype):
    return jax.ShapeDtypeStruct(shape, dtype)


def sort_kernel(planes, in_ref, out_ref, wide):
    pairs = wide.shape[0]
    for plane in range(planes):
        for pair in range(pairs):
            wide[pair] = in_ref[plane, :, pair * 128 : (pair + 1) * 128].astype(F32)
        classes = [
            wide[:, pl.ds(r, 8, stride=4), :].reshape(pairs * 8, 128) for r in range(4)
        ]
        before = from_before(classes[3])
        for tap, (even, odd) in enumerate(
            ((before, classes[1]), (classes[0], classes[2]), (classes[1], classes[3]))
        ):
            both = jnp.concatenate(
                [even.reshape(pairs, 1, 8, 128), odd.reshape(pairs, 1, 8, 128)], axis=1
            )
            out_ref[plane, tap] = both.reshape(pairs * 16, 128).astype(BF16)


def sorted_planes(volume):
    planes, rows, width = volume.shape
    pairs = width // 128
    return call(
        functools.partial(sort_kernel, planes),
        sds((planes, 3, pairs * 16, 128), BF16),
        [pltpu.VMEM((pairs, rows, 128), F32)],
        volume,
    )


def put_rows(dst, pieces, offsets):
    rows = pieces[0].shape[0]
    for index, piece in enumerate(pieces):
        dst[pl.ds(pl.multiple_of(offsets[index], 16), rows), :] = piece[...]


def put_tap(columns, at, left, source):
    rows = source.shape[0]
    columns[at : at + 16, left : left + 128] = jnp.zeros((16, 128), BF16)
    columns[at + 16 : at + rows, left : left + 128] = source[0 : rows - 16, :]
    columns[at : at + rows, left + 128 : left + 256] = source[...]


def gather_taps(columns, sorted_ref, halo_ref, first, count):
    rows = sorted_ref.shape[2]
    for cell in range(count):
        for a in range(3):
            plane = 2 * (first + cell) - 1 + a
            for e in range(3):
                source = (
                    halo_ref.at[halo_ref.shape[0] + plane, e] if plane < 0 else sorted_ref.at[plane, e]
                )
                put_tap(columns, cell * rows, (a * 3 + e) * 256, source)


def pad_first(whole, padded):
    for tap in range(9):
        padded[tap * 256 : tap * 256 + 64, :] = jnp.zeros((64, 128), BF16)
        padded[tap * 256 + 64 : (tap + 1) * 256, :] = whole[tap * 192 : (tap + 1) * 192, :]


def take_windows(read, dst, out, a, half):
    for e in range(3):
        for f in range(3):
            block = read(0 if f == 1 else 1, 0 if e == 1 else 1)
            if e == 0:
                block = from_before(block)
            if f == 0:
                block = jnp.concatenate(
                    [jnp.zeros((8, 128), F32), block[: half * 8 - 8]], axis=0
                )
            left = ((a * 3 + e) * 3 + f) * 128
            dst[out * half * 8 : (out + 1) * half * 8, left : left + 128] = block.astype(BF16)


def forward_upper_kernel(
    offsets, sorted_ref, w0, w1, w2, w3,
    slope_ref, hidden_ref, partial_ref, padded_ref, columns, some, whole,
):
    cells = sorted_ref.shape[0] // 2
    put_rows(whole, (w0, w1, w2, w3), offsets)
    pad_first(whole, padded_ref)
    gather_taps(columns, sorted_ref, None, 1, cells - 1)
    linear = jnp.dot(columns[...], padded_ref[...], preferred_element_type=F32)
    hidden_ref[...] = activate(linear).reshape(hidden_ref.shape)
    slope_ref[...] = activate_slope(linear)
    for a in range(1, 3):
        for e in range(3):
            put_tap(some, 0, ((a - 1) * 3 + e) * 256, sorted_ref.at[a - 1, e])
    partial_ref[...] = jnp.dot(some[...], padded_ref[3 * 256 :, :], preferred_element_type=F32)


def forward_upper(sorted_volume, shards, offsets):
    planes, _, rows, _ = sorted_volume.shape
    cells = planes // 2
    shard = shards[0].shape[0]
    some = (cells - 1) * rows
    return call(
        forward_upper_kernel,
        (
            sds((some, 128), F32),
            sds((cells - 1, rows // 32, 2, 2, 8, 128), F32),
            sds((rows, 128), F32),
            sds((9 * 256, 128), BF16),
        ),
        [
            pltpu.VMEM((some, 9 * 256), BF16),
            pltpu.VMEM((rows, 6 * 256), BF16),
            pltpu.VMEM((4 * shard, 128), BF16),
        ],
        sorted_volume, *shards,
        smem=(offsets,),
        micros=2.5,
    )


def forward_lower_kernel(
    alive, side, halo_ref, hidden_ref, partial_ref, padded_ref,
    slope_ref, windows_ref, sorted_ref, here_ref, there_ref, wide, columns, some, lowest, planes,
):
    rows = partial_ref.shape[0]
    cells = hidden_ref.shape[0] + 1
    half = rows // 32
    sort_kernel(halo_ref.shape[0], halo_ref, sorted_ref, wide)
    for e in range(3):
        for a in range(3):
            put_tap(columns, 0, (a * 3 + e) * 256, sorted_ref.at[a, e])
        put_tap(some, 0, e * 256, sorted_ref.at[2, e])
    below = jnp.dot(columns[...], padded_ref[...], preferred_element_type=F32)
    here = partial_ref[...] + jnp.dot(
        some[...], padded_ref[: 3 * 256, :], preferred_element_type=F32
    )
    slope_ref[:rows, :] = activate_slope(below)
    slope_ref[rows:, :] = activate_slope(here)
    lowest[0] = (activate(below) * alive[0]).reshape(lowest.shape[1:])
    lowest[1] = activate(here).reshape(lowest.shape[1:])
    for plane in range(cells + 1):
        source = lowest.at[plane] if plane < 2 else hidden_ref.at[plane - 2]
        planes[plane] = source[...].reshape(rows, 128).astype(BF16)
    here_ref[...] = planes[pl.ds(side[0], cells)]
    there_ref[...] = planes[pl.ds(1 - side[0], cells)]
    for out in range(cells // 2):
        for a in range(3):
            plane = 2 * out - 1 + a
            source = lowest.at[plane + 1] if plane < 1 else hidden_ref.at[plane - 1]

            def read(column, row):
                return source[:, column, row].reshape(half * 8, 128)

            take_windows(read, windows_ref, out, a, half)


def forward_lower(halo, hidden, partial, padded, alive, side):
    rows = partial.shape[0]
    cells = hidden.shape[0] + 1
    return call(
        forward_lower_kernel,
        (
            sds((2 * rows, 128), F32),
            sds((cells * rows // 8, 27 * 128), BF16),
            sds((halo.shape[0], 3, rows, 128), BF16),
            sds((cells, rows, 128), BF16),
            sds((cells, rows, 128), BF16),
        ),
        [
            pltpu.VMEM((rows // 16, halo.shape[1], 128), F32),
            pltpu.VMEM((rows, 9 * 256), BF16),
            pltpu.VMEM((rows, 3 * 256), BF16),
            pltpu.VMEM((2, *hidden.shape[1:]), F32),
            pltpu.VMEM((cells + 1, rows, 128), BF16),
        ],
        halo, hidden, partial, padded,
        smem=(alive, side),
        micros=1.5,
    )


def put_pieces(flat, outs, slots, order):
    for index, out in enumerate(outs):
        count, size, _ = out.shape
        for place in range(count):
            row = pl.multiple_of(order[place] * size, 16)
            out[place] = flat[slots[index], pl.ds(row, size), :]


def forward_second_kernel(
    offsets, windows_ref, cot_ref, w0, w1, w2, w3, act_ref, delta_ref, whole
):
    put_rows(whole, (w0, w1, w2, w3), offsets)
    linear = jnp.dot(windows_ref[...], whole[...], preferred_element_type=F32)
    outs, _, width = cot_ref.shape
    features = linear.shape[1]
    count = width // features
    acted = activate(linear)
    slope = activate_slope(linear)
    deltas = []
    for out in range(outs):
        base = out * count * 8
        act_ref[out] = jnp.concatenate(
            [acted[base + q * 8 : base + (q + 1) * 8] for q in range(count)], axis=1
        ).astype(BF16)
        cot = cot_ref[out].astype(F32)
        deltas.append(
            jnp.concatenate(
                [cot[:, q * features : (q + 1) * features] for q in range(count)], axis=0
            )
        )
    delta_ref[...] = (jnp.concatenate(deltas, axis=0) * slope).astype(BF16)


def forward_second(windows, cot, shards, offsets):
    rows, features = shards[0].shape
    return call(
        forward_second_kernel,
        (sds(cot.shape, BF16), sds((windows.shape[0], features), BF16)),
        [pltpu.VMEM((4 * rows, features), BF16)],
        windows, cot, *shards,
        smem=(offsets,),
        micros=1.5,
    )


def second_rows_kernel(
    data, table, order, h0, h1, h2, h3, d0, d1, d2, d3,
    out_ref, wide, windows, deltas, product, flat,
):
    cells, rows, _ = h0.shape
    half = rows // 32
    outs = cells // 2
    size = half * 8
    for sample, (hidden, delta) in enumerate(((h0, d0), (h1, d1), (h2, d2), (h3, d3))):
        wide[sample * cells : (sample + 1) * cells] = (
            hidden[...].astype(F32).reshape(cells, half, 2, 2, 8, 128)
        )
        deltas[sample * outs * size : (sample + 1) * outs * size, :] = delta[...]
    for tap in range(windows.shape[1] // 128):
        e, f = table[data[0], 8 + tap], table[data[0], 16 + tap]
        row = jnp.where(e == 1, 0, 1)
        column = jnp.where(f == 1, 0, 1)
        for sample in range(4):
            for out in range(outs):
                plane = sample * cells + 2 * out + table[data[0], tap]
                block = wide[plane, :, column, row].reshape(size, 128)
                block = jnp.where(e == 0, from_before(block), block)
                later = jnp.concatenate([jnp.zeros((8, 128), F32), block[: size - 8]], axis=0)
                block = jnp.where(f == 0, later, block)
                at = (sample * outs + out) * size
                windows[at : at + size, tap * 128 : (tap + 1) * 128] = block.astype(BF16)
    product[...] = lax.dot_general(
        windows[...], deltas[...], (((0,), (0,)), ((), ())), preferred_element_type=F32
    ).astype(BF16)
    lanes = product.shape[1] // 128
    count, piece, _ = out_ref.shape
    shard = 27 * 128 // 4
    for lane in range(lanes):
        flat[lane * shard : (lane + 1) * shard, :] = product[
            pl.ds(pl.multiple_of(table[data[0], 24], 16), shard), lane * 128 : (lane + 1) * 128
        ]
    rest = flat.shape[0] - lanes * shard
    if rest:
        flat[lanes * shard :, :] = jnp.zeros((rest, 128), BF16)
    for place in range(count):
        out_ref[place] = flat[pl.ds(pl.multiple_of(order[place] * piece, 16), piece), :]


def second_rows(hiddens, deltas, data, order, places, size):
    cells, rows, _ = hiddens[0].shape
    cellrows, features = deltas[0].shape
    taps = 8
    table = []
    for shard in range(4):
        start = shard * 27 // 4
        at = [min(start + tap, 26) for tap in range(taps)]
        table.append(
            [tap // 9 - shard // 2 for tap in at]
            + [tap // 3 % 3 for tap in at]
            + [tap % 3 for tap in at]
            + [shard * (27 * 128 // 4) - start * 128]
        )
    return call(
        second_rows_kernel,
        sds((places, size, 128), BF16),
        [
            pltpu.VMEM((4 * cells, rows // 32, 2, 2, 8, 128), F32),
            pltpu.VMEM((4 * cellrows, taps * 128), BF16),
            pltpu.VMEM((4 * cellrows, features), BF16),
            pltpu.VMEM((taps * 128, features), BF16),
            pltpu.VMEM((places * size, 128), BF16),
        ],
        *hiddens, *deltas,
        smem=(data.reshape(1), jnp.array(table, jnp.int32), order),
        micros=2.0,
    )


def back_second_kernel(
    offsets, slots, order, delta_ref, w0, w1, w2, w3,
    slope_low_ref, slope_ref, sorted_ref, halo_ref,
    low_ref, last_ref, down_ref, g0, g1, g2, g3,
    whole, product, columns, deltas, flat,
):
    rows = sorted_ref.shape[2]
    cells = sorted_ref.shape[0] // 2
    half = rows // 32
    size = half * 8
    put_rows(whole, (w0, w1, w2, w3), offsets)
    product[...] = lax.dot_general(
        delta_ref[...], whole[...], (((1,), (1,)), ((), ())), preferred_element_type=F32
    )
    gather_taps(columns, sorted_ref, halo_ref, -1, cells + 1)

    def term(out, a, e, f):
        left = ((a * 3 + e) * 3 + f) * 128
        block = product[out * size : (out + 1) * size, left : left + 128]
        if f == 0:
            block = jnp.concatenate([block[8:], jnp.zeros((8, 128), F32)], axis=0)
        if e == 0:
            block = from_after(block)
        return block.reshape(half, 8, 128)

    for plane in range(-1, cells):
        taps = [
            (out, a) for out in range(cells // 2) for a in range(3) if 2 * out - 1 + a == plane
        ]
        sums = [
            sum(
                term(out, a, e, f)
                for out, a in taps
                for e in ((0, 2) if row else (1,))
                for f in ((0, 2) if column else (1,))
            ).reshape(half, 1, 8, 128)
            for column in range(2)
            for row in range(2)
        ]
        spread = jnp.concatenate(sums, axis=1).reshape(rows, 128)
        if plane < 1:
            slope = slope_low_ref[(plane + 1) * rows : (plane + 2) * rows, :]
        else:
            slope = slope_ref[(plane - 1) * rows : plane * rows, :]
        delta = (spread * slope).astype(BF16)
        deltas[(plane + 1) * rows : (plane + 2) * rows, :] = delta
        if plane < 0:
            down_ref[:rows, :] = spread.astype(BF16)
        if plane == 0:
            down_ref[rows:, :] = delta
        if plane == cells - 1:
            last_ref[...] = spread
        elif plane >= 0:
            low_ref[plane * rows : (plane + 1) * rows, :] = delta
    flipped = jnp.transpose(deltas[...].astype(F32)).astype(BF16)
    tally = jnp.dot(flipped, columns[...], preferred_element_type=F32)
    shard_rows = 9 * 192 // 4
    for tap in range(9):
        turned = jnp.transpose(tally[:, tap * 256 : (tap + 1) * 256])[64:].astype(BF16)
        at = tap * 192
        while at < (tap + 1) * 192:
            shard = at // shard_rows
            to = min((tap + 1) * 192, (shard + 1) * shard_rows)
            flat[shard, at - shard * shard_rows : to - shard * shard_rows, :] = turned[
                at - tap * 192 : to - tap * 192
            ]
            at = to
    rest = flat.shape[1] - shard_rows
    if rest:
        flat[:, shard_rows:, :] = jnp.zeros((4, rest, 128), BF16)
    put_pieces(flat, (g0, g1, g2, g3), slots, order)


def back_second(delta, shards, slopes, sorted_volume, halo, offsets, slots, order, places, size):
    rows, features = shards[0].shape
    planes, _, width, _ = sorted_volume.shape
    cells = planes // 2
    piece = sds((places, size, 128), BF16)
    return call(
        back_second_kernel,
        (
            sds(((cells - 1) * width, 128), BF16),
            sds((width, 128), F32),
            sds((2 * width, 128), BF16),
            piece, piece, piece, piece,
        ),
        [
            pltpu.VMEM((4 * rows, features), BF16),
            pltpu.VMEM((delta.shape[0], 4 * rows), F32),
            pltpu.VMEM(((cells + 1) * width, 9 * 256), BF16),
            pltpu.VMEM(((cells + 1) * width, 128), BF16),
            pltpu.VMEM((4, places * size, 128), BF16),
        ],
        delta, *shards, *slopes, sorted_volume, halo,
        smem=(offsets, slots, order),
        micros=3.5,
    )


def back_input_kernel(
    offsets, low_ref, last_ref, slope_ref, upper_ref, w0, w1, w2, w3,
    out_ref, whole, turned, pairs, product, wide, last,
):
    put_rows(whole, (w0, w1, w2, w3), offsets)
    for tap in range(9):
        top = tap * 128
        turned[top : top + 128, 0:128] = whole[tap * 192 + 64 : (tap + 1) * 192, :]
        turned[top : top + 64, 128:256] = jnp.zeros((64, 128), BF16)
        turned[top + 64 : top + 128, 128:256] = whole[tap * 192 : tap * 192 + 64, :]
    planes = out_ref.shape[0]
    cells = planes // 2
    rows = last_ref.shape[0]
    groups = rows // 16
    last[...] = (
        (last_ref[...] + upper_ref[:rows, :].astype(F32)) * slope_ref[(cells - 2) * rows :, :]
    ).astype(BF16)
    for cell in range(cells + 1):
        at = cell * rows
        if cell < cells - 1:
            source = low_ref.at[at : at + rows]
        else:
            source = last if cell == cells - 1 else upper_ref.at[rows : 2 * rows]
        pairs[at : at + rows, 0:128] = source[...]
        pairs[at : at + rows - 16, 128:256] = source[16:rows, :]
        pairs[at + rows - 16 : at + rows, 128:256] = jnp.zeros((16, 128), BF16)
    product[...] = lax.dot_general(
        pairs[...], turned[...], (((1,), (1,)), ((), ())), preferred_element_type=F32
    ).reshape(product.shape)

    def part(cell, a, e, parity):
        left = (a * 3 + e) * 128
        return product[cell * groups : (cell + 1) * groups, parity, :, left : left + 128]

    def after(block):
        flat = block.reshape(groups * 8, 128)
        return from_after(flat).reshape(groups, 8, 128)

    for plane in range(planes):
        taps = [(o, a) for o in range(cells + 1) for a in range(3) if 2 * o - 1 + a == plane]
        wide[:, pl.ds(0, 8, stride=4), :] = sum(part(o, a, 1, 0) for o, a in taps)
        wide[:, pl.ds(1, 8, stride=4), :] = sum(
            part(o, a, 2, 0) + part(o, a, 0, 1) for o, a in taps
        )
        wide[:, pl.ds(2, 8, stride=4), :] = sum(part(o, a, 1, 1) for o, a in taps)
        wide[:, pl.ds(3, 8, stride=4), :] = sum(part(o, a, 2, 1) for o, a in taps) + after(
            sum(part(o, a, 0, 0) for o, a in taps)
        )
        for group in range(groups):
            lanes = slice(group * 128, (group + 1) * 128)
            out_ref[plane, :, lanes] = wide[group].astype(BF16)


def back_input(low, last, slope, upper, shards, offsets, shape):
    planes, side, width = shape
    shard = shards[0].shape[0]
    rows = low.shape[0] + upper.shape[0]
    return call(
        back_input_kernel,
        sds(shape, BF16),
        [
            pltpu.VMEM((4 * shard, 128), BF16),
            pltpu.VMEM((9 * 128, 256), BF16),
            pltpu.VMEM((rows, 256), BF16),
            pltpu.VMEM((rows // 16, 2, 8, 9 * 128), F32),
            pltpu.VMEM((width // 128, side, 128), F32),
            pltpu.VMEM(last.shape, BF16),
        ],
        low, last, slope, upper, *shards,
        smem=(offsets,),
        micros=3.0,
    )


def unpack_kernel(scale_first, scale_second, order, *refs):
    *chunks, other, first_ref, second_ref, flat_first, flat_second = refs
    high = len(chunks)
    small = flat_first.shape[0] // (2 * high)
    big = flat_second.shape[0] // (2 * high)
    for low in range(2):
        for index in range(high):
            chunk = other.at[index] if low else chunks[index]
            place = order[low * high + index]
            flat_second[pl.ds(pl.multiple_of(place * big, 16), big), :] = chunk[:big, :]
            flat_first[pl.ds(pl.multiple_of(place * small, 16), small), :] = chunk[big:, :]
    rows, features = second_ref.shape
    for lane in range(features // 128):
        second_ref[:, lane * 128 : (lane + 1) * 128] = (
            flat_second[lane * rows : (lane + 1) * rows, :].astype(F32) * scale_second
        )
    first_ref[...] = flat_first[: first_ref.shape[0], :].astype(F32) * scale_first


def wide_sum(*pieces):
    return sum(piece.astype(F32) for piece in pieces)


def added(*pieces):
    return wide_sum(*pieces).astype(BF16)


def swap(value, axis, bits):
    size = lax.axis_size(axis)
    return lax.ppermute(value, axis, [(i, i ^ bits) for i in range(size)])


def shifted(value, axis, by):
    size = lax.axis_size(axis)
    pairs = [(i, i + by) for i in range(size) if 0 <= i + by < size]
    return lax.ppermute(value, axis, pairs)


def local(volume, weight_first, weight_second, cotangent):
    samples, planes, side, width = volume.shape
    data = lax.axis_index("dp")
    place = lax.axis_index("space")
    spaces = lax.axis_size("space")
    high = spaces // 2
    small, big = weight_first.shape[0], weight_second.shape[0]
    slots = jnp.arange(4, dtype=jnp.int32) ^ data
    offsets_first = slots * small
    offsets_second = slots * big
    alive = (place > 0).astype(F32).reshape(1)
    x_side = lax.shift_right_logical(data, 1)
    steps = jnp.arange(spaces, dtype=jnp.int32)
    order = place ^ (2 * (steps % high) + steps // high)
    lanes = weight_second.shape[1] // 128
    size_first = -(-small // (16 * spaces)) * 16
    size_second = -(-lanes * big // (16 * spaces)) * 16

    inputs = volume.reshape(planes, side, width)
    first_x = swap(weight_first, "dp", 2)
    first_core = swap(weight_first, "dp", 1)
    second_x = swap(weight_second, "dp", 2)
    second_core = swap(weight_second, "dp", 1)
    halo = shifted(inputs[planes - 3 :], "space", 1)
    first_far = swap(first_x, "dp", 1)
    shards_first = (weight_first, first_core, first_x, first_far)

    sorted_volume = sorted_planes(inputs)
    slope, hidden, partial, padded = forward_upper(sorted_volume, shards_first, offsets_first)
    second_x, hidden = lax.optimization_barrier((second_x, hidden))
    second_far = swap(second_x, "dp", 1)
    shards_second = (weight_second, second_core, second_x, second_far)
    slope_low, windows, sorted_halo, hidden_here, hidden_there = forward_lower(
        halo, hidden, partial, padded, alive, x_side.reshape(1)
    )
    cot = cotangent.reshape(cotangent.shape[1:])
    activations, delta_second = forward_second(windows, cot, shards_second, offsets_second)
    hidden_x = swap(hidden_there, "dp", 2)
    delta_x = swap(delta_second, "dp", 2)
    hidden_core = swap(hidden_here, "dp", 1)
    delta_core = swap(delta_second, "dp", 1)
    low, last, down, *first = back_second(
        delta_second, shards_second, (slope_low, slope), sorted_volume, sorted_halo,
        offsets_second, slots, order, spaces, size_first,
    )
    first, delta_x, hidden_x, delta_core, hidden_core = lax.optimization_barrier(
        (first, delta_x, hidden_x, delta_core, hidden_core)
    )
    hiddens = (hidden_here, hidden_core, hidden_x, swap(hidden_x, "dp", 1))
    deltas = (delta_second, delta_core, delta_x, swap(delta_x, "dp", 1))
    second = second_rows(hiddens, deltas, data, order, spaces, size_second)
    upper = shifted(down, "space", -1)
    def pieces(value):
        return value.reshape(2, high, -1, 128)

    second = pieces(second)
    far, near = pieces(swap(first[3], "dp", 1)), pieces(swap(first[1], "dp", 1))
    own, there = pieces(first[0]), pieces(first[2])
    both = [
        (d * spaces + s, (d ^ 2) * spaces + (s ^ 1)) for d in range(4) for s in range(spaces)
    ]
    got_xy = lax.ppermute(added(there[1], far[1]), ("dp", "space"), both)
    got_x = swap(added(there[0], far[0]), "dp", 2)
    got_y = swap(jnp.concatenate([second[1], added(own[1], near[1])], axis=1), "space", 1)
    held = jnp.concatenate(
        [
            added(second[0], got_y[:, :size_second]),
            added(own[0], near[0], got_x, got_xy, got_y[:, size_second:]),
        ],
        axis=1,
    )
    held, upper = lax.optimization_barrier((held, upper))
    mine = added(held[0], *(swap(held[k], "space", 2 * k) for k in range(1, high)))
    chunks = [mine] + [swap(mine, "space", 2 * k) for k in range(1, high)]
    chunks.append(swap(jnp.stack(chunks), "space", 1))

    gradient = back_input(low, last, slope, upper, shards_first, offsets_first, inputs.shape)

    cells_first = samples * lax.axis_size("dp") * (planes // 2) * spaces * (side // 2) ** 2
    cells_second = cells_first // 8
    first_gradient, second_gradient = call(
        functools.partial(unpack_kernel, float(cells_first) ** -0.5, float(cells_second) ** -0.5),
        (sds(weight_first.shape, F32), sds(weight_second.shape, F32)),
        [
            pltpu.VMEM((spaces * size_first, 128), BF16),
            pltpu.VMEM((spaces * size_second, 128), BF16),
        ],
        *chunks,
        smem=(order,),
    )
    return (
        activations.reshape(cotangent.shape),
        gradient.reshape(volume.shape),
        first_gradient,
        second_gradient,
    )


def solution(mesh):
    return jax.shard_map(
        local,
        mesh=mesh,
        in_specs=(
            P("dp", "space", None, None),
            P("dp", None),
            P("dp", None),
            P("dp", "space", None, None),
        ),
        out_specs=(
            P("dp", "space", None, None),
            P("dp", "space", None, None),
            P("dp", None),
            P("dp", None),
        ),
        check_vma=False,
    )
```

```python
import functools

import jax
import jax.numpy as jnp
from jax import lax
from jax.experimental import pallas as pl
from jax.experimental.pallas import tpu as pltpu
from jax.sharding import PartitionSpec as P

LEAK_SLOPE = 0.2
F32 = jnp.float32
BF16 = jnp.bfloat16
VMEM_LIMIT = 24 * 1024 * 1024


def activate(values):
    small = jnp.exp(-jnp.abs(values))
    return LEAK_SLOPE * values + (1.0 - LEAK_SLOPE) * (
        jnp.maximum(values, 0.0) + jnp.log(1.0 + small)
    )


def activate_slope(values):
    small = jnp.exp(-jnp.abs(values))
    inverse = 1.0 / (1.0 + small)
    return LEAK_SLOPE + (1.0 - LEAK_SLOPE) * jnp.where(
        values >= 0.0, inverse, small * inverse
    )


def block_row(rows, width):
    return lax.broadcasted_iota(jnp.int32, (rows, width), 0) % 8


def from_before(block):
    moved = pltpu.roll(block, 1, 0)
    return jnp.where(block_row(*block.shape) == 0, 0.0, moved)


def from_after(block):
    moved = pltpu.roll(block, block.shape[0] - 1, 0)
    return jnp.where(block_row(*block.shape) == 7, 0.0, moved)


def call(kernel, out_shape, scratch, *operands, smem=(), micros=1.0):
    nbytes = sum(a.size * a.dtype.itemsize for a in (*operands, *jax.tree.leaves(out_shape)))
    specs = [pl.BlockSpec(memory_space=pltpu.SMEM)] * len(smem)
    specs += [pl.BlockSpec(memory_space=pltpu.VMEM)] * len(operands)
    return pl.pallas_call(
        kernel,
        out_shape=out_shape,
        in_specs=specs,
        out_specs=jax.tree.map(lambda _: pl.BlockSpec(memory_space=pltpu.VMEM), out_shape),
        scratch_shapes=scratch,
        compiler_params=pltpu.CompilerParams(vmem_limit_bytes=VMEM_LIMIT),
        cost_estimate=pl.CostEstimate(
            flops=int(micros * 1.15e9), bytes_accessed=nbytes, transcendentals=0
        ),
    )(*smem, *operands)


def sds(shape, dtype):
    return jax.ShapeDtypeStruct(shape, dtype)


def sort_kernel(planes, in_ref, out_ref, wide):
    pairs = wide.shape[0]
    for plane in range(planes):
        for pair in range(pairs):
            wide[pair] = in_ref[plane, :, pair * 128 : (pair + 1) * 128].astype(F32)
        classes = [
            wide[:, pl.ds(r, 8, stride=4), :].reshape(pairs * 8, 128) for r in range(4)
        ]
        before = from_before(classes[3])
        for tap, (even, odd) in enumerate(
            ((before, classes[1]), (classes[0], classes[2]), (classes[1], classes[3]))
        ):
            both = jnp.concatenate(
                [even.reshape(pairs, 1, 8, 128), odd.reshape(pairs, 1, 8, 128)], axis=1
            )
            out_ref[plane, tap] = both.reshape(pairs * 16, 128).astype(BF16)


def last_planes_kernel(volume_ref, out_ref, sem):
    count = out_ref.shape[0]
    copy = pltpu.make_async_copy(
        volume_ref.at[pl.ds(volume_ref.shape[0] - count, count)], out_ref, sem
    )
    copy.start()
    copy.wait()


def last_planes(volume, count):
    shape = (count, *volume.shape[1:])
    return pl.pallas_call(
        last_planes_kernel,
        out_shape=sds(shape, BF16),
        in_specs=[pl.BlockSpec(memory_space=pltpu.HBM)],
        out_specs=pl.BlockSpec(memory_space=pltpu.HBM),
        scratch_shapes=[pltpu.SemaphoreType.DMA],
        cost_estimate=pl.CostEstimate(
            flops=0, bytes_accessed=4 * shape[0] * shape[1] * shape[2], transcendentals=0
        ),
    )(volume)


def sorted_planes(volume):
    planes, rows, width = volume.shape
    pairs = width // 128
    return call(
        functools.partial(sort_kernel, planes),
        sds((planes, 3, pairs * 16, 128), BF16),
        [pltpu.VMEM((pairs, rows, 128), F32)],
        volume,
    )


def put_rows(dst, pieces, offsets):
    rows = pieces[0].shape[0]
    for index, piece in enumerate(pieces):
        dst[pl.ds(pl.multiple_of(offsets[index], 16), rows), :] = piece[...]


def put_tap(columns, at, left, source):
    rows = source.shape[0]
    columns[at : at + 16, left : left + 128] = jnp.zeros((16, 128), BF16)
    columns[at + 16 : at + rows, left : left + 128] = source[0 : rows - 16, :]
    columns[at : at + rows, left + 128 : left + 256] = source[...]


def gather_taps(columns, sorted_ref, halo_ref, first, count):
    rows = sorted_ref.shape[2]
    for cell in range(count):
        for a in range(3):
            plane = 2 * (first + cell) - 1 + a
            for e in range(3):
                source = (
                    halo_ref.at[halo_ref.shape[0] + plane, e] if plane < 0 else sorted_ref.at[plane, e]
                )
                put_tap(columns, cell * rows, (a * 3 + e) * 256, source)


def pad_first(whole, padded):
    for tap in range(9):
        padded[tap * 256 : tap * 256 + 64, :] = jnp.zeros((64, 128), BF16)
        padded[tap * 256 + 64 : (tap + 1) * 256, :] = whole[tap * 192 : (tap + 1) * 192, :]


def take_windows(read, dst, out, a, half):
    for e in range(3):
        for f in range(3):
            block = read(0 if f == 1 else 1, 0 if e == 1 else 1)
            if e == 0:
                block = from_before(block)
            if f == 0:
                block = jnp.concatenate(
                    [jnp.zeros((8, 128), F32), block[: half * 8 - 8]], axis=0
                )
            left = ((a * 3 + e) * 3 + f) * 128
            dst[out * half * 8 : (out + 1) * half * 8, left : left + 128] = block.astype(BF16)


def forward_upper_kernel(
    offsets, sorted_ref, w0, w1, w2, w3,
    slope_ref, hidden_ref, middle_ref, partial_ref, padded_ref, columns, some, whole,
):
    cells = sorted_ref.shape[0] // 2
    put_rows(whole, (w0, w1, w2, w3), offsets)
    pad_first(whole, padded_ref)
    gather_taps(columns, sorted_ref, None, 1, cells - 1)
    linear = jnp.dot(columns[...], padded_ref[...], preferred_element_type=F32)
    hidden = activate(linear)
    hidden_ref[...] = hidden.reshape(hidden_ref.shape)
    count = middle_ref.shape[0] * middle_ref.shape[1]
    middle_ref[...] = hidden[:count].reshape(middle_ref.shape).astype(BF16)
    slope_ref[...] = activate_slope(linear)
    for a in range(1, 3):
        for e in range(3):
            put_tap(some, 0, ((a - 1) * 3 + e) * 256, sorted_ref.at[a - 1, e])
    partial_ref[...] = jnp.dot(some[...], padded_ref[3 * 256 :, :], preferred_element_type=F32)


def forward_upper(sorted_volume, shards, offsets):
    planes, _, rows, _ = sorted_volume.shape
    cells = planes // 2
    shard = shards[0].shape[0]
    some = (cells - 1) * rows
    return call(
        forward_upper_kernel,
        (
            sds((some, 128), F32),
            sds((cells - 1, rows // 32, 2, 2, 8, 128), F32),
            sds((cells - 2, rows, 128), BF16),
            sds((rows, 128), F32),
            sds((9 * 256, 128), BF16),
        ),
        [
            pltpu.VMEM((some, 9 * 256), BF16),
            pltpu.VMEM((rows, 6 * 256), BF16),
            pltpu.VMEM((4 * shard, 128), BF16),
        ],
        sorted_volume, *shards,
        smem=(offsets,),
        micros=2.5,
    )


def forward_lower_kernel(
    alive, side, halo_ref, hidden_ref, partial_ref, padded_ref,
    slope_ref, windows_ref, sorted_ref, here_ref, there_ref, wide, columns, some, lowest, planes,
):
    rows = partial_ref.shape[0]
    cells = hidden_ref.shape[0] + 1
    half = rows // 32
    sort_kernel(halo_ref.shape[0], halo_ref, sorted_ref, wide)
    for e in range(3):
        for a in range(3):
            put_tap(columns, 0, (a * 3 + e) * 256, sorted_ref.at[a, e])
        put_tap(some, 0, e * 256, sorted_ref.at[2, e])
    below = jnp.dot(columns[...], padded_ref[...], preferred_element_type=F32)
    here = partial_ref[...] + jnp.dot(
        some[...], padded_ref[: 3 * 256, :], preferred_element_type=F32
    )
    slope_ref[:rows, :] = activate_slope(below)
    slope_ref[rows:, :] = activate_slope(here)
    lowest[0] = (activate(below) * alive[0]).reshape(lowest.shape[1:])
    lowest[1] = activate(here).reshape(lowest.shape[1:])
    planes[0] = lowest[0].reshape(rows, 128).astype(BF16)
    planes[1] = lowest[1].reshape(rows, 128).astype(BF16)
    planes[2] = planes[1]
    planes[3] = hidden_ref[cells - 2].reshape(rows, 128).astype(BF16)
    here_ref[...] = planes[pl.ds(2 * side[0], 2)]
    there_ref[...] = planes[pl.ds(2 - 2 * side[0], 2)]
    for out in range(cells // 2):
        for a in range(3):
            plane = 2 * out - 1 + a
            source = lowest.at[plane + 1] if plane < 1 else hidden_ref.at[plane - 1]

            def read(column, row):
                return source[:, column, row].reshape(half * 8, 128)

            take_windows(read, windows_ref, out, a, half)


def forward_lower(halo, hidden, partial, padded, alive, side):
    rows = partial.shape[0]
    cells = hidden.shape[0] + 1
    return call(
        forward_lower_kernel,
        (
            sds((2 * rows, 128), F32),
            sds((cells * rows // 8, 27 * 128), BF16),
            sds((halo.shape[0], 3, rows, 128), BF16),
            sds((2, rows, 128), BF16),
            sds((2, rows, 128), BF16),
        ),
        [
            pltpu.VMEM((rows // 16, halo.shape[1], 128), F32),
            pltpu.VMEM((rows, 9 * 256), BF16),
            pltpu.VMEM((rows, 3 * 256), BF16),
            pltpu.VMEM((2, *hidden.shape[1:]), F32),
            pltpu.VMEM((4, rows, 128), BF16),
        ],
        halo, hidden, partial, padded,
        smem=(alive, side),
        micros=1.5,
    )


def put_pieces(flat, outs, slots, order):
    for index, out in enumerate(outs):
        count, size, _ = out.shape
        for place in range(count):
            row = pl.multiple_of(order[place] * size, 16)
            out[place] = flat[slots[index], pl.ds(row, size), :]


def forward_second_kernel(
    offsets, windows_ref, cot_ref, w0, w1, w2, w3, act_ref, delta_ref, whole
):
    put_rows(whole, (w0, w1, w2, w3), offsets)
    linear = jnp.dot(windows_ref[...], whole[...], preferred_element_type=F32)
    outs, _, width = cot_ref.shape
    features = linear.shape[1]
    count = width // features
    acted = activate(linear)
    slope = activate_slope(linear)
    deltas = []
    for out in range(outs):
        base = out * count * 8
        act_ref[out] = jnp.concatenate(
            [acted[base + q * 8 : base + (q + 1) * 8] for q in range(count)], axis=1
        ).astype(BF16)
        cot = cot_ref[out].astype(F32)
        deltas.append(
            jnp.concatenate(
                [cot[:, q * features : (q + 1) * features] for q in range(count)], axis=0
            )
        )
    delta_ref[...] = (jnp.concatenate(deltas, axis=0) * slope).astype(BF16)


def forward_second(windows, cot, shards, offsets):
    rows, features = shards[0].shape
    return call(
        forward_second_kernel,
        (sds(cot.shape, BF16), sds((windows.shape[0], features), BF16)),
        [pltpu.VMEM((4 * rows, features), BF16)],
        windows, cot, *shards,
        smem=(offsets,),
        micros=1.5,
    )


def second_rows_kernel(
    data, table, order, e0, e1, e2, e3, m0, m1, m2, m3, d0, d1, d2, d3,
    out_ref, wide, windows, deltas, product, flat,
):
    edges, rows, _ = e0.shape
    cells = edges + m0.shape[0]
    half = rows // 32
    outs = cells // 2
    size = half * 8
    taps = windows.shape[1] // 128
    samples = ((e0, m0, d0), (e1, m1, d1), (e2, m2, d2), (e3, m3, d3))
    for sample, (edge, middle, delta) in enumerate(samples):
        at = sample * cells
        wide[at : at + edges] = edge[...].astype(F32).reshape(edges, half, 2, 2, 8, 128)
        wide[at + edges : at + cells] = (
            middle[...].astype(F32).reshape(cells - edges, half, 2, 2, 8, 128)
        )
        deltas[sample * outs * size : (sample + 1) * outs * size, :] = delta[...]
    for tap in range(taps):
        e, f = table[data[0], tap], table[data[0], taps + tap]
        row = jnp.where(e == 1, 0, 1)
        column = jnp.where(f == 1, 0, 1)
        for sample in range(4):
            for out in range(outs):
                plane = sample * cells + table[data[0], (2 + out) * taps + tap]
                block = wide[plane, :, column, row].reshape(size, 128)
                block = jnp.where(e == 0, from_before(block), block)
                later = jnp.concatenate([jnp.zeros((8, 128), F32), block[: size - 8]], axis=0)
                block = jnp.where(f == 0, later, block)
                at = (sample * outs + out) * size
                windows[at : at + size, tap * 128 : (tap + 1) * 128] = block.astype(BF16)
    product[...] = lax.dot_general(
        windows[...], deltas[...], (((0,), (0,)), ((), ())), preferred_element_type=F32
    ).astype(BF16)
    lanes = product.shape[1] // 128
    count, piece, _ = out_ref.shape
    shard = 27 * 128 // 4
    for lane in range(lanes):
        flat[lane * shard : (lane + 1) * shard, :] = product[
            pl.ds(pl.multiple_of(table[data[0], (2 + outs) * taps], 16), shard), lane * 128 : (lane + 1) * 128
        ]
    rest = flat.shape[0] - lanes * shard
    if rest:
        flat[lanes * shard :, :] = jnp.zeros((rest, 128), BF16)
    for place in range(count):
        out_ref[place] = flat[pl.ds(pl.multiple_of(order[place] * piece, 16), piece), :]


def second_rows(edges, middles, deltas, data, order, places, size):
    _, rows, _ = edges[0].shape
    cells = edges[0].shape[0] + middles[0].shape[0]
    cellrows, features = deltas[0].shape
    taps = 8
    table = []
    for shard in range(4):
        start = shard * 27 // 4
        at = [min(start + tap, 26) for tap in range(taps)]
        held = (-1, 0, *range(1, cells - 1)) if shard < 2 else (0, cells - 1, *range(1, cells - 1))
        table.append(
            [tap // 3 % 3 for tap in at]
            + [tap % 3 for tap in at]
            + [held.index(2 * out - 1 + tap // 9) for out in range(cells // 2) for tap in at]
            + [shard * (27 * 128 // 4) - start * 128]
        )
    return call(
        second_rows_kernel,
        sds((places, size, 128), BF16),
        [
            pltpu.VMEM((4 * cells, rows // 32, 2, 2, 8, 128), F32),
            pltpu.VMEM((4 * cellrows, taps * 128), BF16),
            pltpu.VMEM((4 * cellrows, features), BF16),
            pltpu.VMEM((taps * 128, features), BF16),
            pltpu.VMEM((places * size, 128), BF16),
        ],
        *edges, *middles, *deltas,
        smem=(data.reshape(1), jnp.array(table, jnp.int32), order),
        micros=2.0,
    )


def back_second_kernel(
    offsets, slots, order, delta_ref, w0, w1, w2, w3,
    slope_low_ref, slope_ref, sorted_ref, halo_ref,
    low_ref, last_ref, down_ref, g0, g1, g2, g3,
    whole, product, columns, deltas, flat,
):
    rows = sorted_ref.shape[2]
    cells = sorted_ref.shape[0] // 2
    half = rows // 32
    size = half * 8
    put_rows(whole, (w0, w1, w2, w3), offsets)
    product[...] = lax.dot_general(
        delta_ref[...], whole[...], (((1,), (1,)), ((), ())), preferred_element_type=F32
    )
    gather_taps(columns, sorted_ref, halo_ref, -1, cells + 1)

    def term(out, a, e, f):
        left = ((a * 3 + e) * 3 + f) * 128
        block = product[out * size : (out + 1) * size, left : left + 128]
        if f == 0:
            block = jnp.concatenate([block[8:], jnp.zeros((8, 128), F32)], axis=0)
        if e == 0:
            block = from_after(block)
        return block.reshape(half, 8, 128)

    for plane in range(-1, cells):
        taps = [
            (out, a) for out in range(cells // 2) for a in range(3) if 2 * out - 1 + a == plane
        ]
        sums = [
            sum(
                term(out, a, e, f)
                for out, a in taps
                for e in ((0, 2) if row else (1,))
                for f in ((0, 2) if column else (1,))
            ).reshape(half, 1, 8, 128)
            for column in range(2)
            for row in range(2)
        ]
        spread = jnp.concatenate(sums, axis=1).reshape(rows, 128)
        if plane < 1:
            slope = slope_low_ref[(plane + 1) * rows : (plane + 2) * rows, :]
        else:
            slope = slope_ref[(plane - 1) * rows : plane * rows, :]
        delta = (spread * slope).astype(BF16)
        deltas[(plane + 1) * rows : (plane + 2) * rows, :] = delta
        if plane < 0:
            down_ref[:rows, :] = spread.astype(BF16)
        if plane == 0:
            down_ref[rows:, :] = delta
        if plane == cells - 1:
            last_ref[...] = spread
        elif plane >= 0:
            low_ref[plane * rows : (plane + 1) * rows, :] = delta
    flipped = jnp.transpose(deltas[...].astype(F32)).astype(BF16)
    tally = jnp.dot(flipped, columns[...], preferred_element_type=F32)
    shard_rows = 9 * 192 // 4
    for tap in range(9):
        turned = jnp.transpose(tally[:, tap * 256 : (tap + 1) * 256])[64:].astype(BF16)
        at = tap * 192
        while at < (tap + 1) * 192:
            shard = at // shard_rows
            to = min((tap + 1) * 192, (shard + 1) * shard_rows)
            flat[shard, at - shard * shard_rows : to - shard * shard_rows, :] = turned[
                at - tap * 192 : to - tap * 192
            ]
            at = to
    rest = flat.shape[1] - shard_rows
    if rest:
        flat[:, shard_rows:, :] = jnp.zeros((4, rest, 128), BF16)
    put_pieces(flat, (g0, g1, g2, g3), slots, order)


def back_second(delta, shards, slopes, sorted_volume, halo, offsets, slots, order, places, size):
    rows, features = shards[0].shape
    planes, _, width, _ = sorted_volume.shape
    cells = planes // 2
    piece = sds((places, size, 128), BF16)
    return call(
        back_second_kernel,
        (
            sds(((cells - 1) * width, 128), BF16),
            sds((width, 128), F32),
            sds((2 * width, 128), BF16),
            piece, piece, piece, piece,
        ),
        [
            pltpu.VMEM((4 * rows, features), BF16),
            pltpu.VMEM((delta.shape[0], 4 * rows), F32),
            pltpu.VMEM(((cells + 1) * width, 9 * 256), BF16),
            pltpu.VMEM(((cells + 1) * width, 128), BF16),
            pltpu.VMEM((4, places * size, 128), BF16),
        ],
        delta, *shards, *slopes, sorted_volume, halo,
        smem=(offsets, slots, order),
        micros=3.5,
    )


def back_input_kernel(
    offsets, low_ref, last_ref, slope_ref, upper_ref, w0, w1, w2, w3,
    out_ref, whole, turned, pairs, product, wide, last,
):
    put_rows(whole, (w0, w1, w2, w3), offsets)
    for tap in range(9):
        top = tap * 128
        turned[top : top + 128, 0:128] = whole[tap * 192 + 64 : (tap + 1) * 192, :]
        turned[top : top + 64, 128:256] = jnp.zeros((64, 128), BF16)
        turned[top + 64 : top + 128, 128:256] = whole[tap * 192 : tap * 192 + 64, :]
    planes = out_ref.shape[0]
    cells = planes // 2
    rows = last_ref.shape[0]
    groups = rows // 16
    last[...] = (
        (last_ref[...] + upper_ref[:rows, :].astype(F32)) * slope_ref[(cells - 2) * rows :, :]
    ).astype(BF16)
    for cell in range(cells + 1):
        at = cell * rows
        if cell < cells - 1:
            source = low_ref.at[at : at + rows]
        else:
            source = last if cell == cells - 1 else upper_ref.at[rows : 2 * rows]
        pairs[at : at + rows, 0:128] = source[...]
        pairs[at : at + rows - 16, 128:256] = source[16:rows, :]
        pairs[at + rows - 16 : at + rows, 128:256] = jnp.zeros((16, 128), BF16)
    product[...] = lax.dot_general(
        pairs[...], turned[...], (((1,), (1,)), ((), ())), preferred_element_type=F32
    ).reshape(product.shape)

    def part(cell, a, e, parity):
        left = (a * 3 + e) * 128
        return product[cell * groups : (cell + 1) * groups, parity, :, left : left + 128]

    def after(block):
        flat = block.reshape(groups * 8, 128)
        return from_after(flat).reshape(groups, 8, 128)

    for plane in range(planes):
        taps = [(o, a) for o in range(cells + 1) for a in range(3) if 2 * o - 1 + a == plane]
        wide[:, pl.ds(0, 8, stride=4), :] = sum(part(o, a, 1, 0) for o, a in taps)
        wide[:, pl.ds(1, 8, stride=4), :] = sum(
            part(o, a, 2, 0) + part(o, a, 0, 1) for o, a in taps
        )
        wide[:, pl.ds(2, 8, stride=4), :] = sum(part(o, a, 1, 1) for o, a in taps)
        wide[:, pl.ds(3, 8, stride=4), :] = sum(part(o, a, 2, 1) for o, a in taps) + after(
            sum(part(o, a, 0, 0) for o, a in taps)
        )
        for group in range(groups):
            lanes = slice(group * 128, (group + 1) * 128)
            out_ref[plane, :, lanes] = wide[group].astype(BF16)


def back_input(low, last, slope, upper, shards, offsets, shape):
    planes, side, width = shape
    shard = shards[0].shape[0]
    rows = low.shape[0] + upper.shape[0]
    return call(
        back_input_kernel,
        sds(shape, BF16),
        [
            pltpu.VMEM((4 * shard, 128), BF16),
            pltpu.VMEM((9 * 128, 256), BF16),
            pltpu.VMEM((rows, 256), BF16),
            pltpu.VMEM((rows // 16, 2, 8, 9 * 128), F32),
            pltpu.VMEM((width // 128, side, 128), F32),
            pltpu.VMEM(last.shape, BF16),
        ],
        low, last, slope, upper, *shards,
        smem=(offsets,),
        micros=3.0,
    )


def unpack_kernel(scale_first, scale_second, order, *refs):
    *chunks, other, first_ref, second_ref, flat_first, flat_second = refs
    high = len(chunks)
    small = flat_first.shape[0] // (2 * high)
    big = flat_second.shape[0] // (2 * high)
    for low in range(2):
        for index in range(high):
            chunk = other.at[index] if low else chunks[index]
            place = order[low * high + index]
            flat_second[pl.ds(pl.multiple_of(place * big, 16), big), :] = chunk[:big, :]
            flat_first[pl.ds(pl.multiple_of(place * small, 16), small), :] = chunk[big:, :]
    rows, features = second_ref.shape
    for lane in range(features // 128):
        second_ref[:, lane * 128 : (lane + 1) * 128] = (
            flat_second[lane * rows : (lane + 1) * rows, :].astype(F32) * scale_second
        )
    first_ref[...] = flat_first[: first_ref.shape[0], :].astype(F32) * scale_first


def wide_sum(*pieces):
    return sum(piece.astype(F32) for piece in pieces)


def added(*pieces):
    return wide_sum(*pieces).astype(BF16)


def swap(value, axis, bits):
    size = lax.axis_size(axis)
    return lax.ppermute(value, axis, [(i, i ^ bits) for i in range(size)])


def shifted(value, axis, by):
    size = lax.axis_size(axis)
    pairs = [(i, i + by) for i in range(size) if 0 <= i + by < size]
    return lax.ppermute(value, axis, pairs)


def local(volume, weight_first, weight_second, cotangent):
    samples, planes, side, width = volume.shape
    data = lax.axis_index("dp")
    place = lax.axis_index("space")
    spaces = lax.axis_size("space")
    high = spaces // 2
    small, big = weight_first.shape[0], weight_second.shape[0]
    slots = jnp.arange(4, dtype=jnp.int32) ^ data
    offsets_first = slots * small
    offsets_second = slots * big
    alive = (place > 0).astype(F32).reshape(1)
    x_side = lax.shift_right_logical(data, 1)
    steps = jnp.arange(spaces, dtype=jnp.int32)
    order = place ^ (2 * (steps % high) + steps // high)
    lanes = weight_second.shape[1] // 128
    size_first = -(-small // (16 * spaces)) * 16
    size_second = -(-lanes * big // (16 * spaces)) * 16

    inputs = volume.reshape(planes, side, width)
    uppermost = last_planes(inputs, 3)
    weight_first, uppermost = lax.optimization_barrier((weight_first, uppermost))
    first_x = swap(weight_first, "dp", 2)
    first_core = swap(weight_first, "dp", 1)
    second_x = swap(weight_second, "dp", 2)
    second_core = swap(weight_second, "dp", 1)
    halo = shifted(uppermost, "space", 1)
    first_far = swap(first_x, "dp", 1)
    shards_first = (weight_first, first_core, first_x, first_far)

    sorted_volume = sorted_planes(inputs)
    slope, hidden, middle, partial, padded = forward_upper(
        sorted_volume, shards_first, offsets_first
    )
    middle_x, middle_core = swap(middle, "dp", 2), swap(middle, "dp", 1)
    second_x, hidden = lax.optimization_barrier((second_x, hidden))
    second_far = swap(second_x, "dp", 1)
    shards_second = (weight_second, second_core, second_x, second_far)
    slope_low, windows, sorted_halo, edge, edge_there = forward_lower(
        halo, hidden, partial, padded, alive, x_side.reshape(1)
    )
    cot = cotangent.reshape(cotangent.shape[1:])
    activations, delta_second = forward_second(windows, cot, shards_second, offsets_second)
    edge_x, edge_core = swap(edge_there, "dp", 2), swap(edge, "dp", 1)
    delta_x, delta_core = swap(delta_second, "dp", 2), swap(delta_second, "dp", 1)
    low, last, down, *first = back_second(
        delta_second, shards_second, (slope_low, slope), sorted_volume, sorted_halo,
        offsets_second, slots, order, spaces, size_first,
    )
    first, down, delta_x, edge_x, delta_core, edge_core, middle_x, middle_core = (
        lax.optimization_barrier(
            (first, down, delta_x, edge_x, delta_core, edge_core, middle_x, middle_core)
        )
    )
    second = second_rows(
        (edge, edge_core, edge_x, swap(edge_x, "dp", 1)),
        (middle, middle_core, middle_x, swap(middle_x, "dp", 1)),
        (delta_second, delta_core, delta_x, swap(delta_x, "dp", 1)),
        data, order, spaces, size_second,
    )
    upper = shifted(down, "space", -1)

    def pieces(value):
        return value.reshape(2, high, -1, 128)

    far, near = pieces(swap(first[3], "dp", 1)), pieces(swap(first[1], "dp", 1))
    own, there = pieces(first[0]), pieces(first[2])
    got_x = swap(added(there, far), "dp", 2)
    second = pieces(second)
    got_y = swap(
        jnp.concatenate([second[1], added(own[1], near[1], got_x[1])], axis=1), "space", 1
    )
    held = jnp.concatenate(
        [
            added(second[0], got_y[:, :size_second]),
            added(own[0], near[0], got_x[0], got_y[:, size_second:]),
        ],
        axis=1,
    )
    mine = added(held[0], *(swap(held[k], "space", 2 * k) for k in range(1, high)))
    chunks = [mine] + [swap(mine, "space", 2 * k) for k in range(1, high)]
    chunks.append(swap(jnp.stack(chunks), "space", 1))

    gradient = back_input(low, last, slope, upper, shards_first, offsets_first, inputs.shape)

    cells_first = samples * lax.axis_size("dp") * (planes // 2) * spaces * (side // 2) ** 2
    cells_second = cells_first // 8
    first_gradient, second_gradient = call(
        functools.partial(unpack_kernel, float(cells_first) ** -0.5, float(cells_second) ** -0.5),
        (sds(weight_first.shape, F32), sds(weight_second.shape, F32)),
        [
            pltpu.VMEM((spaces * size_first, 128), BF16),
            pltpu.VMEM((spaces * size_second, 128), BF16),
        ],
        *chunks,
        smem=(order,),
    )
    return (
        activations.reshape(cotangent.shape),
        gradient.reshape(volume.shape),
        first_gradient,
        second_gradient,
    )


def solution(mesh):
    return jax.shard_map(
        local,
        mesh=mesh,
        in_specs=(
            P("dp", "space", None, None),
            P("dp", None),
            P("dp", None),
            P("dp", "space", None, None),
        ),
        out_specs=(
            P("dp", "space", None, None),
            P("dp", "space", None, None),
            P("dp", None),
            P("dp", None),
        ),
        check_vma=False,
    )
```

```python
import functools

import jax
import jax.numpy as jnp
from jax import lax
from jax.experimental import pallas as pl
from jax.experimental.pallas import tpu as pltpu
from jax.sharding import PartitionSpec as P

LEAK_SLOPE = 0.2
F32 = jnp.float32
BF16 = jnp.bfloat16
VMEM_LIMIT = 24 * 1024 * 1024


def activate(values):
    small = jnp.exp(-jnp.abs(values))
    return LEAK_SLOPE * values + (1.0 - LEAK_SLOPE) * (
        jnp.maximum(values, 0.0) + jnp.log(1.0 + small)
    )


def activate_slope(values):
    small = jnp.exp(-jnp.abs(values))
    inverse = 1.0 / (1.0 + small)
    return LEAK_SLOPE + (1.0 - LEAK_SLOPE) * jnp.where(
        values >= 0.0, inverse, small * inverse
    )


def block_row(rows, width):
    return lax.broadcasted_iota(jnp.int32, (rows, width), 0) % 8


def from_before(block):
    moved = pltpu.roll(block, 1, 0)
    return jnp.where(block_row(*block.shape) == 0, 0.0, moved)


def from_after(block):
    moved = pltpu.roll(block, block.shape[0] - 1, 0)
    return jnp.where(block_row(*block.shape) == 7, 0.0, moved)


def call(kernel, out_shape, scratch, *operands, smem=(), micros=1.0):
    nbytes = sum(a.size * a.dtype.itemsize for a in (*operands, *jax.tree.leaves(out_shape)))
    specs = [pl.BlockSpec(memory_space=pltpu.SMEM)] * len(smem)
    specs += [pl.BlockSpec(memory_space=pltpu.VMEM)] * len(operands)
    return pl.pallas_call(
        kernel,
        out_shape=out_shape,
        in_specs=specs,
        out_specs=jax.tree.map(lambda _: pl.BlockSpec(memory_space=pltpu.VMEM), out_shape),
        scratch_shapes=scratch,
        compiler_params=pltpu.CompilerParams(vmem_limit_bytes=VMEM_LIMIT),
        cost_estimate=pl.CostEstimate(
            flops=int(micros * 1.15e9), bytes_accessed=nbytes, transcendentals=0
        ),
    )(*smem, *operands)


def sds(shape, dtype):
    return jax.ShapeDtypeStruct(shape, dtype)


def sort_kernel(planes, in_ref, out_ref, wide):
    pairs = wide.shape[0]
    for plane in range(planes):
        for pair in range(pairs):
            wide[pair] = in_ref[plane, :, pair * 128 : (pair + 1) * 128].astype(F32)
        classes = [
            wide[:, pl.ds(r, 8, stride=4), :].reshape(pairs * 8, 128) for r in range(4)
        ]
        before = from_before(classes[3])
        for tap, (even, odd) in enumerate(
            ((before, classes[1]), (classes[0], classes[2]), (classes[1], classes[3]))
        ):
            both = jnp.concatenate(
                [even.reshape(pairs, 1, 8, 128), odd.reshape(pairs, 1, 8, 128)], axis=1
            )
            out_ref[plane, tap] = both.reshape(pairs * 16, 128).astype(BF16)


def last_planes_kernel(volume_ref, out_ref, sem):
    count = out_ref.shape[0]
    copy = pltpu.make_async_copy(
        volume_ref.at[pl.ds(volume_ref.shape[0] - count, count)], out_ref, sem
    )
    copy.start()
    copy.wait()


def last_planes(volume, count):
    shape = (count, *volume.shape[1:])
    return pl.pallas_call(
        last_planes_kernel,
        out_shape=sds(shape, BF16),
        in_specs=[pl.BlockSpec(memory_space=pltpu.HBM)],
        out_specs=pl.BlockSpec(memory_space=pltpu.VMEM),
        scratch_shapes=[pltpu.SemaphoreType.DMA],
        cost_estimate=pl.CostEstimate(
            flops=0, bytes_accessed=4 * shape[0] * shape[1] * shape[2], transcendentals=0
        ),
    )(volume)


def sorted_planes(volume):
    planes, rows, width = volume.shape
    pairs = width // 128
    return call(
        functools.partial(sort_kernel, planes),
        sds((planes, 3, pairs * 16, 128), BF16),
        [pltpu.VMEM((pairs, rows, 128), F32)],
        volume,
    )


def put_rows(dst, pieces, offsets):
    rows = pieces[0].shape[0]
    for index, piece in enumerate(pieces):
        dst[pl.ds(pl.multiple_of(offsets[index], 16), rows), :] = piece[...]


def put_tap(columns, at, left, source):
    rows = source.shape[0]
    columns[at : at + 16, left : left + 128] = jnp.zeros((16, 128), BF16)
    columns[at + 16 : at + rows, left : left + 128] = source[0 : rows - 16, :]
    columns[at : at + rows, left + 128 : left + 256] = source[...]


def gather_taps(columns, sorted_ref, halo_ref, first, count):
    rows = sorted_ref.shape[2]
    for cell in range(count):
        for a in range(3):
            plane = 2 * (first + cell) - 1 + a
            for e in range(3):
                source = (
                    halo_ref.at[halo_ref.shape[0] + plane, e] if plane < 0 else sorted_ref.at[plane, e]
                )
                put_tap(columns, cell * rows, (a * 3 + e) * 256, source)


def pad_first(whole, padded):
    for tap in range(9):
        padded[tap * 256 : tap * 256 + 64, :] = jnp.zeros((64, 128), BF16)
        padded[tap * 256 + 64 : (tap + 1) * 256, :] = whole[tap * 192 : (tap + 1) * 192, :]


def take_windows(read, dst, out, a, half):
    for e in range(3):
        for f in range(3):
            block = read(0 if f == 1 else 1, 0 if e == 1 else 1)
            if e == 0:
                block = from_before(block)
            if f == 0:
                block = jnp.concatenate(
                    [jnp.zeros((8, 128), F32), block[: half * 8 - 8]], axis=0
                )
            left = ((a * 3 + e) * 3 + f) * 128
            dst[out * half * 8 : (out + 1) * half * 8, left : left + 128] = block.astype(BF16)


def forward_upper_kernel(
    offsets, sorted_ref, w0, w1, w2, w3,
    slope_ref, hidden_ref, middle_ref, partial_ref, padded_ref, columns, some, whole,
):
    cells = sorted_ref.shape[0] // 2
    put_rows(whole, (w0, w1, w2, w3), offsets)
    pad_first(whole, padded_ref)
    gather_taps(columns, sorted_ref, None, 1, cells - 1)
    linear = jnp.dot(columns[...], padded_ref[...], preferred_element_type=F32)
    hidden = activate(linear)
    hidden_ref[...] = hidden.reshape(hidden_ref.shape)
    count = middle_ref.shape[0] * middle_ref.shape[1]
    middle_ref[...] = hidden[:count].reshape(middle_ref.shape).astype(BF16)
    slope_ref[...] = activate_slope(linear)
    for a in range(1, 3):
        for e in range(3):
            put_tap(some, 0, ((a - 1) * 3 + e) * 256, sorted_ref.at[a - 1, e])
    partial_ref[...] = jnp.dot(some[...], padded_ref[3 * 256 :, :], preferred_element_type=F32)


def forward_upper(sorted_volume, shards, offsets):
    planes, _, rows, _ = sorted_volume.shape
    cells = planes // 2
    shard = shards[0].shape[0]
    some = (cells - 1) * rows
    return call(
        forward_upper_kernel,
        (
            sds((some, 128), F32),
            sds((cells - 1, rows // 32, 2, 2, 8, 128), F32),
            sds((cells - 2, rows, 128), BF16),
            sds((rows, 128), F32),
            sds((9 * 256, 128), BF16),
        ),
        [
            pltpu.VMEM((some, 9 * 256), BF16),
            pltpu.VMEM((rows, 6 * 256), BF16),
            pltpu.VMEM((4 * shard, 128), BF16),
        ],
        sorted_volume, *shards,
        smem=(offsets,),
        micros=2.5,
    )


def forward_lower_kernel(
    alive, side, halo_ref, hidden_ref, partial_ref, padded_ref,
    slope_ref, windows_ref, sorted_ref, here_ref, there_ref, wide, columns, some, lowest, planes,
):
    rows = partial_ref.shape[0]
    cells = hidden_ref.shape[0] + 1
    half = rows // 32
    sort_kernel(halo_ref.shape[0], halo_ref, sorted_ref, wide)
    for e in range(3):
        for a in range(3):
            put_tap(columns, 0, (a * 3 + e) * 256, sorted_ref.at[a, e])
        put_tap(some, 0, e * 256, sorted_ref.at[2, e])
    below = jnp.dot(columns[...], padded_ref[...], preferred_element_type=F32)
    here = partial_ref[...] + jnp.dot(
        some[...], padded_ref[: 3 * 256, :], preferred_element_type=F32
    )
    slope_ref[:rows, :] = activate_slope(below)
    slope_ref[rows:, :] = activate_slope(here)
    lowest[0] = (activate(below) * alive[0]).reshape(lowest.shape[1:])
    lowest[1] = activate(here).reshape(lowest.shape[1:])
    planes[0] = lowest[0].reshape(rows, 128).astype(BF16)
    planes[1] = lowest[1].reshape(rows, 128).astype(BF16)
    planes[2] = planes[1]
    planes[3] = hidden_ref[cells - 2].reshape(rows, 128).astype(BF16)
    here_ref[...] = planes[pl.ds(2 * side[0], 2)]
    there_ref[...] = planes[pl.ds(2 - 2 * side[0], 2)]
    for out in range(cells // 2):
        for a in range(3):
            plane = 2 * out - 1 + a
            source = lowest.at[plane + 1] if plane < 1 else hidden_ref.at[plane - 1]

            def read(column, row):
                return source[:, column, row].reshape(half * 8, 128)

            take_windows(read, windows_ref, out, a, half)


def forward_lower(halo, hidden, partial, padded, alive, side):
    rows = partial.shape[0]
    cells = hidden.shape[0] + 1
    return call(
        forward_lower_kernel,
        (
            sds((2 * rows, 128), F32),
            sds((cells * rows // 8, 27 * 128), BF16),
            sds((halo.shape[0], 3, rows, 128), BF16),
            sds((2, rows, 128), BF16),
            sds((2, rows, 128), BF16),
        ),
        [
            pltpu.VMEM((rows // 16, halo.shape[1], 128), F32),
            pltpu.VMEM((rows, 9 * 256), BF16),
            pltpu.VMEM((rows, 3 * 256), BF16),
            pltpu.VMEM((2, *hidden.shape[1:]), F32),
            pltpu.VMEM((4, rows, 128), BF16),
        ],
        halo, hidden, partial, padded,
        smem=(alive, side),
        micros=1.5,
    )


def put_pieces(flat, outs, slots, order):
    for index, out in enumerate(outs):
        count, size, _ = out.shape
        for place in range(count):
            row = pl.multiple_of(order[place] * size, 16)
            out[place] = flat[slots[index], pl.ds(row, size), :]


def forward_second_kernel(
    offsets, windows_ref, cot_ref, w0, w1, w2, w3, act_ref, delta_ref, whole
):
    put_rows(whole, (w0, w1, w2, w3), offsets)
    linear = jnp.dot(windows_ref[...], whole[...], preferred_element_type=F32)
    outs, _, width = cot_ref.shape
    features = linear.shape[1]
    count = width // features
    acted = activate(linear)
    slope = activate_slope(linear)
    deltas = []
    for out in range(outs):
        base = out * count * 8
        act_ref[out] = jnp.concatenate(
            [acted[base + q * 8 : base + (q + 1) * 8] for q in range(count)], axis=1
        ).astype(BF16)
        cot = cot_ref[out].astype(F32)
        deltas.append(
            jnp.concatenate(
                [cot[:, q * features : (q + 1) * features] for q in range(count)], axis=0
            )
        )
    delta_ref[...] = (jnp.concatenate(deltas, axis=0) * slope).astype(BF16)


def forward_second(windows, cot, shards, offsets):
    rows, features = shards[0].shape
    return call(
        forward_second_kernel,
        (sds(cot.shape, BF16), sds((windows.shape[0], features), BF16)),
        [pltpu.VMEM((4 * rows, features), BF16)],
        windows, cot, *shards,
        smem=(offsets,),
        micros=1.5,
    )


def second_rows_kernel(
    data, table, order, e0, e1, e2, e3, m0, m1, m2, m3, d0, d1, d2, d3,
    out_ref, wide, windows, deltas, product, flat,
):
    edges, rows, _ = e0.shape
    cells = edges + m0.shape[0]
    half = rows // 32
    outs = cells // 2
    size = half * 8
    taps = windows.shape[1] // 128
    samples = ((e0, m0, d0), (e1, m1, d1), (e2, m2, d2), (e3, m3, d3))
    for sample, (edge, middle, delta) in enumerate(samples):
        at = sample * cells
        wide[at : at + edges] = edge[...].astype(F32).reshape(edges, half, 2, 2, 8, 128)
        wide[at + edges : at + cells] = (
            middle[...].astype(F32).reshape(cells - edges, half, 2, 2, 8, 128)
        )
        deltas[sample * outs * size : (sample + 1) * outs * size, :] = delta[...]
    for tap in range(taps):
        e, f = table[data[0], tap], table[data[0], taps + tap]
        row = jnp.where(e == 1, 0, 1)
        column = jnp.where(f == 1, 0, 1)
        for sample in range(4):
            for out in range(outs):
                plane = sample * cells + table[data[0], (2 + out) * taps + tap]
                block = wide[plane, :, column, row].reshape(size, 128)
                block = jnp.where(e == 0, from_before(block), block)
                later = jnp.concatenate([jnp.zeros((8, 128), F32), block[: size - 8]], axis=0)
                block = jnp.where(f == 0, later, block)
                at = (sample * outs + out) * size
                windows[at : at + size, tap * 128 : (tap + 1) * 128] = block.astype(BF16)
    product[...] = lax.dot_general(
        windows[...], deltas[...], (((0,), (0,)), ((), ())), preferred_element_type=F32
    ).astype(BF16)
    lanes = product.shape[1] // 128
    count, piece, _ = out_ref.shape
    shard = 27 * 128 // 4
    for lane in range(lanes):
        flat[lane * shard : (lane + 1) * shard, :] = product[
            pl.ds(pl.multiple_of(table[data[0], (2 + outs) * taps], 16), shard), lane * 128 : (lane + 1) * 128
        ]
    rest = flat.shape[0] - lanes * shard
    if rest:
        flat[lanes * shard :, :] = jnp.zeros((rest, 128), BF16)
    for place in range(count):
        out_ref[place] = flat[pl.ds(pl.multiple_of(order[place] * piece, 16), piece), :]


def second_rows(edges, middles, deltas, data, order, places, size):
    _, rows, _ = edges[0].shape
    cells = edges[0].shape[0] + middles[0].shape[0]
    cellrows, features = deltas[0].shape
    taps = 8
    table = []
    for shard in range(4):
        start = shard * 27 // 4
        at = [min(start + tap, 26) for tap in range(taps)]
        held = (-1, 0, *range(1, cells - 1)) if shard < 2 else (0, cells - 1, *range(1, cells - 1))
        table.append(
            [tap // 3 % 3 for tap in at]
            + [tap % 3 for tap in at]
            + [held.index(2 * out - 1 + tap // 9) for out in range(cells // 2) for tap in at]
            + [shard * (27 * 128 // 4) - start * 128]
        )
    return call(
        second_rows_kernel,
        sds((places, size, 128), BF16),
        [
            pltpu.VMEM((4 * cells, rows // 32, 2, 2, 8, 128), F32),
            pltpu.VMEM((4 * cellrows, taps * 128), BF16),
            pltpu.VMEM((4 * cellrows, features), BF16),
            pltpu.VMEM((taps * 128, features), BF16),
            pltpu.VMEM((places * size, 128), BF16),
        ],
        *edges, *middles, *deltas,
        smem=(data.reshape(1), jnp.array(table, jnp.int32), order),
        micros=2.0,
    )


def back_second_kernel(
    offsets, slots, order, delta_ref, w0, w1, w2, w3,
    slope_low_ref, slope_ref, sorted_ref, halo_ref,
    low_ref, last_ref, down_ref, g0, g1, g2, g3,
    whole, product, columns, deltas, flat,
):
    rows = sorted_ref.shape[2]
    cells = sorted_ref.shape[0] // 2
    half = rows // 32
    size = half * 8
    put_rows(whole, (w0, w1, w2, w3), offsets)
    product[...] = lax.dot_general(
        delta_ref[...], whole[...], (((1,), (1,)), ((), ())), preferred_element_type=F32
    )
    gather_taps(columns, sorted_ref, halo_ref, -1, cells + 1)

    def term(out, a, e, f):
        left = ((a * 3 + e) * 3 + f) * 128
        block = product[out * size : (out + 1) * size, left : left + 128]
        if f == 0:
            block = jnp.concatenate([block[8:], jnp.zeros((8, 128), F32)], axis=0)
        if e == 0:
            block = from_after(block)
        return block.reshape(half, 8, 128)

    for plane in range(-1, cells):
        taps = [
            (out, a) for out in range(cells // 2) for a in range(3) if 2 * out - 1 + a == plane
        ]
        sums = [
            sum(
                term(out, a, e, f)
                for out, a in taps
                for e in ((0, 2) if row else (1,))
                for f in ((0, 2) if column else (1,))
            ).reshape(half, 1, 8, 128)
            for column in range(2)
            for row in range(2)
        ]
        spread = jnp.concatenate(sums, axis=1).reshape(rows, 128)
        if plane < 1:
            slope = slope_low_ref[(plane + 1) * rows : (plane + 2) * rows, :]
        else:
            slope = slope_ref[(plane - 1) * rows : plane * rows, :]
        delta = (spread * slope).astype(BF16)
        deltas[(plane + 1) * rows : (plane + 2) * rows, :] = delta
        if plane < 0:
            down_ref[:rows, :] = spread.astype(BF16)
        if plane == 0:
            down_ref[rows:, :] = delta
        if plane == cells - 1:
            last_ref[...] = spread
        elif plane >= 0:
            low_ref[plane * rows : (plane + 1) * rows, :] = delta
    flipped = jnp.transpose(deltas[...].astype(F32)).astype(BF16)
    tally = jnp.dot(flipped, columns[...], preferred_element_type=F32)
    shard_rows = 9 * 192 // 4
    for tap in range(9):
        turned = jnp.transpose(tally[:, tap * 256 : (tap + 1) * 256])[64:].astype(BF16)
        at = tap * 192
        while at < (tap + 1) * 192:
            shard = at // shard_rows
            to = min((tap + 1) * 192, (shard + 1) * shard_rows)
            flat[shard, at - shard * shard_rows : to - shard * shard_rows, :] = turned[
                at - tap * 192 : to - tap * 192
            ]
            at = to
    rest = flat.shape[1] - shard_rows
    if rest:
        flat[:, shard_rows:, :] = jnp.zeros((4, rest, 128), BF16)
    put_pieces(flat, (g0, g1, g2, g3), slots, order)


def back_second(delta, shards, slopes, sorted_volume, halo, offsets, slots, order, places, size):
    rows, features = shards[0].shape
    planes, _, width, _ = sorted_volume.shape
    cells = planes // 2
    piece = sds((places, size, 128), BF16)
    return call(
        back_second_kernel,
        (
            sds(((cells - 1) * width, 128), BF16),
            sds((width, 128), F32),
            sds((2 * width, 128), BF16),
            piece, piece, piece, piece,
        ),
        [
            pltpu.VMEM((4 * rows, features), BF16),
            pltpu.VMEM((delta.shape[0], 4 * rows), F32),
            pltpu.VMEM(((cells + 1) * width, 9 * 256), BF16),
            pltpu.VMEM(((cells + 1) * width, 128), BF16),
            pltpu.VMEM((4, places * size, 128), BF16),
        ],
        delta, *shards, *slopes, sorted_volume, halo,
        smem=(offsets, slots, order),
        micros=3.5,
    )


def back_input_kernel(
    offsets, low_ref, last_ref, slope_ref, upper_ref, w0, w1, w2, w3,
    out_ref, whole, turned, pairs, product, wide, last,
):
    put_rows(whole, (w0, w1, w2, w3), offsets)
    for tap in range(9):
        top = tap * 128
        turned[top : top + 128, 0:128] = whole[tap * 192 + 64 : (tap + 1) * 192, :]
        turned[top : top + 64, 128:256] = jnp.zeros((64, 128), BF16)
        turned[top + 64 : top + 128, 128:256] = whole[tap * 192 : tap * 192 + 64, :]
    planes = out_ref.shape[0]
    cells = planes // 2
    rows = last_ref.shape[0]
    groups = rows // 16
    last[...] = (
        (last_ref[...] + upper_ref[:rows, :].astype(F32)) * slope_ref[(cells - 2) * rows :, :]
    ).astype(BF16)
    for cell in range(cells + 1):
        at = cell * rows
        if cell < cells - 1:
            source = low_ref.at[at : at + rows]
        else:
            source = last if cell == cells - 1 else upper_ref.at[rows : 2 * rows]
        pairs[at : at + rows, 0:128] = source[...]
        pairs[at : at + rows - 16, 128:256] = source[16:rows, :]
        pairs[at + rows - 16 : at + rows, 128:256] = jnp.zeros((16, 128), BF16)
    product[...] = lax.dot_general(
        pairs[...], turned[...], (((1,), (1,)), ((), ())), preferred_element_type=F32
    ).reshape(product.shape)

    def part(cell, a, e, parity):
        left = (a * 3 + e) * 128
        return product[cell * groups : (cell + 1) * groups, parity, :, left : left + 128]

    def after(block):
        flat = block.reshape(groups * 8, 128)
        return from_after(flat).reshape(groups, 8, 128)

    for plane in range(planes):
        taps = [(o, a) for o in range(cells + 1) for a in range(3) if 2 * o - 1 + a == plane]
        wide[:, pl.ds(0, 8, stride=4), :] = sum(part(o, a, 1, 0) for o, a in taps)
        wide[:, pl.ds(1, 8, stride=4), :] = sum(
            part(o, a, 2, 0) + part(o, a, 0, 1) for o, a in taps
        )
        wide[:, pl.ds(2, 8, stride=4), :] = sum(part(o, a, 1, 1) for o, a in taps)
        wide[:, pl.ds(3, 8, stride=4), :] = sum(part(o, a, 2, 1) for o, a in taps) + after(
            sum(part(o, a, 0, 0) for o, a in taps)
        )
        for group in range(groups):
            lanes = slice(group * 128, (group + 1) * 128)
            out_ref[plane, :, lanes] = wide[group].astype(BF16)


def back_input(low, last, slope, upper, shards, offsets, shape):
    planes, side, width = shape
    shard = shards[0].shape[0]
    rows = low.shape[0] + upper.shape[0]
    return call(
        back_input_kernel,
        sds(shape, BF16),
        [
            pltpu.VMEM((4 * shard, 128), BF16),
            pltpu.VMEM((9 * 128, 256), BF16),
            pltpu.VMEM((rows, 256), BF16),
            pltpu.VMEM((rows // 16, 2, 8, 9 * 128), F32),
            pltpu.VMEM((width // 128, side, 128), F32),
            pltpu.VMEM(last.shape, BF16),
        ],
        low, last, slope, upper, *shards,
        smem=(offsets,),
        micros=3.0,
    )


def unpack_kernel(scale_first, scale_second, order, *refs):
    *chunks, other, first_ref, second_ref, flat_first, flat_second = refs
    high = len(chunks)
    small = flat_first.shape[0] // (2 * high)
    big = flat_second.shape[0] // (2 * high)
    for low in range(2):
        for index in range(high):
            chunk = other.at[index] if low else chunks[index]
            place = order[low * high + index]
            flat_second[pl.ds(pl.multiple_of(place * big, 16), big), :] = chunk[:big, :]
            flat_first[pl.ds(pl.multiple_of(place * small, 16), small), :] = chunk[big:, :]
    rows, features = second_ref.shape
    for lane in range(features // 128):
        second_ref[:, lane * 128 : (lane + 1) * 128] = (
            flat_second[lane * rows : (lane + 1) * rows, :].astype(F32) * scale_second
        )
    first_ref[...] = flat_first[: first_ref.shape[0], :].astype(F32) * scale_first


def wide_sum(*pieces):
    return sum(piece.astype(F32) for piece in pieces)


def added(*pieces):
    return wide_sum(*pieces).astype(BF16)


def swap(value, axis, bits):
    size = lax.axis_size(axis)
    return lax.ppermute(value, axis, [(i, i ^ bits) for i in range(size)])


def shifted(value, axis, by):
    size = lax.axis_size(axis)
    pairs = [(i, i + by) for i in range(size) if 0 <= i + by < size]
    return lax.ppermute(value, axis, pairs)


def local(volume, weight_first, weight_second, cotangent):
    samples, planes, side, width = volume.shape
    data = lax.axis_index("dp")
    place = lax.axis_index("space")
    spaces = lax.axis_size("space")
    high = spaces // 2
    small, big = weight_first.shape[0], weight_second.shape[0]
    slots = jnp.arange(4, dtype=jnp.int32) ^ data
    offsets_first = slots * small
    offsets_second = slots * big
    alive = (place > 0).astype(F32).reshape(1)
    x_side = lax.shift_right_logical(data, 1)
    steps = jnp.arange(spaces, dtype=jnp.int32)
    order = place ^ (2 * (steps % high) + steps // high)
    lanes = weight_second.shape[1] // 128
    size_first = -(-small // (16 * spaces)) * 16
    size_second = -(-lanes * big // (16 * spaces)) * 16

    inputs = volume.reshape(planes, side, width)
    uppermost = last_planes(inputs, 3)
    weight_first, uppermost = lax.optimization_barrier((weight_first, uppermost))
    first_x = swap(weight_first, "dp", 2)
    first_core = swap(weight_first, "dp", 1)
    second_x = swap(weight_second, "dp", 2)
    second_core = swap(weight_second, "dp", 1)
    halo = shifted(uppermost, "space", 1)
    first_far = swap(first_x, "dp", 1)
    shards_first = (weight_first, first_core, first_x, first_far)

    sorted_volume = sorted_planes(inputs)
    slope, hidden, middle, partial, padded = forward_upper(
        sorted_volume, shards_first, offsets_first
    )
    middle_x, middle_core = swap(middle, "dp", 2), swap(middle, "dp", 1)
    second_x, hidden = lax.optimization_barrier((second_x, hidden))
    second_far = swap(second_x, "dp", 1)
    shards_second = (weight_second, second_core, second_x, second_far)
    slope_low, windows, sorted_halo, edge, edge_there = forward_lower(
        halo, hidden, partial, padded, alive, x_side.reshape(1)
    )
    cot = cotangent.reshape(cotangent.shape[1:])
    activations, delta_second = forward_second(windows, cot, shards_second, offsets_second)
    edge_x, edge_core = swap(edge_there, "dp", 2), swap(edge, "dp", 1)
    delta_x, delta_core = swap(delta_second, "dp", 2), swap(delta_second, "dp", 1)
    low, last, down, *first = back_second(
        delta_second, shards_second, (slope_low, slope), sorted_volume, sorted_halo,
        offsets_second, slots, order, spaces, size_first,
    )
    first, down, delta_x, edge_x, delta_core, edge_core, middle_x, middle_core = (
        lax.optimization_barrier(
            (first, down, delta_x, edge_x, delta_core, edge_core, middle_x, middle_core)
        )
    )
    second = second_rows(
        (edge, edge_core, edge_x, swap(edge_x, "dp", 1)),
        (middle, middle_core, middle_x, swap(middle_x, "dp", 1)),
        (delta_second, delta_core, delta_x, swap(delta_x, "dp", 1)),
        data, order, spaces, size_second,
    )
    upper = shifted(down, "space", -1)

    def pieces(value):
        return value.reshape(2, high, -1, 128)

    far, near = pieces(swap(first[3], "dp", 1)), pieces(swap(first[1], "dp", 1))
    own, there = pieces(first[0]), pieces(first[2])
    got_x = swap(added(there, far), "dp", 2)
    second = pieces(second)
    got_y = swap(
        jnp.concatenate([second[1], added(own[1], near[1], got_x[1])], axis=1), "space", 1
    )
    held = jnp.concatenate(
        [
            added(second[0], got_y[:, :size_second]),
            added(own[0], near[0], got_x[0], got_y[:, size_second:]),
        ],
        axis=1,
    )
    mine = added(held[0], *(swap(held[k], "space", 2 * k) for k in range(1, high)))
    chunks = [mine] + [swap(mine, "space", 2 * k) for k in range(1, high)]
    chunks.append(swap(jnp.stack(chunks), "space", 1))

    gradient = back_input(low, last, slope, upper, shards_first, offsets_first, inputs.shape)

    cells_first = samples * lax.axis_size("dp") * (planes // 2) * spaces * (side // 2) ** 2
    cells_second = cells_first // 8
    first_gradient, second_gradient = call(
        functools.partial(unpack_kernel, float(cells_first) ** -0.5, float(cells_second) ** -0.5),
        (sds(weight_first.shape, F32), sds(weight_second.shape, F32)),
        [
            pltpu.VMEM((spaces * size_first, 128), BF16),
            pltpu.VMEM((spaces * size_second, 128), BF16),
        ],
        *chunks,
        smem=(order,),
    )
    return (
        activations.reshape(cotangent.shape),
        gradient.reshape(volume.shape),
        first_gradient,
        second_gradient,
    )


def solution(mesh):
    return jax.shard_map(
        local,
        mesh=mesh,
        in_specs=(
            P("dp", "space", None, None),
            P("dp", None),
            P("dp", None),
            P("dp", "space", None, None),
        ),
        out_specs=(
            P("dp", "space", None, None),
            P("dp", "space", None, None),
            P("dp", None),
            P("dp", None),
        ),
        check_vma=False,
    )
```

```python
import functools

import jax
import jax.numpy as jnp
from jax import lax
from jax.experimental import pallas as pl
from jax.experimental.pallas import tpu as pltpu
from jax.sharding import PartitionSpec as P

LEAK_SLOPE = 0.2
F32 = jnp.float32
BF16 = jnp.bfloat16
VMEM_LIMIT = 24 * 1024 * 1024


def activate(values):
    small = jnp.exp(-jnp.abs(values))
    return LEAK_SLOPE * values + (1.0 - LEAK_SLOPE) * (
        jnp.maximum(values, 0.0) + jnp.log(1.0 + small)
    )


def activate_slope(values):
    small = jnp.exp(-jnp.abs(values))
    inverse = 1.0 / (1.0 + small)
    return LEAK_SLOPE + (1.0 - LEAK_SLOPE) * jnp.where(
        values >= 0.0, inverse, small * inverse
    )


def block_row(rows, width):
    return lax.broadcasted_iota(jnp.int32, (rows, width), 0) % 8


def from_before(block):
    moved = pltpu.roll(block, 1, 0)
    return jnp.where(block_row(*block.shape) == 0, 0.0, moved)


def from_after(block):
    moved = pltpu.roll(block, block.shape[0] - 1, 0)
    return jnp.where(block_row(*block.shape) == 7, 0.0, moved)


def call(kernel, out_shape, scratch, *operands, smem=(), micros=1.0):
    nbytes = sum(a.size * a.dtype.itemsize for a in (*operands, *jax.tree.leaves(out_shape)))
    specs = [pl.BlockSpec(memory_space=pltpu.SMEM)] * len(smem)
    specs += [pl.BlockSpec(memory_space=pltpu.VMEM)] * len(operands)
    return pl.pallas_call(
        kernel,
        out_shape=out_shape,
        in_specs=specs,
        out_specs=jax.tree.map(lambda _: pl.BlockSpec(memory_space=pltpu.VMEM), out_shape),
        scratch_shapes=scratch,
        compiler_params=pltpu.CompilerParams(vmem_limit_bytes=VMEM_LIMIT),
        cost_estimate=pl.CostEstimate(
            flops=int(micros * 1.15e9), bytes_accessed=nbytes, transcendentals=0
        ),
    )(*smem, *operands)


def sds(shape, dtype):
    return jax.ShapeDtypeStruct(shape, dtype)


def sort_kernel(planes, in_ref, out_ref, wide):
    pairs = wide.shape[0]
    for plane in range(planes):
        for pair in range(pairs):
            wide[pair] = in_ref[plane, :, pair * 128 : (pair + 1) * 128].astype(F32)
        classes = [
            wide[:, pl.ds(r, 8, stride=4), :].reshape(pairs * 8, 128) for r in range(4)
        ]
        before = from_before(classes[3])
        for tap, (even, odd) in enumerate(
            ((before, classes[1]), (classes[0], classes[2]), (classes[1], classes[3]))
        ):
            both = jnp.concatenate(
                [even.reshape(pairs, 1, 8, 128), odd.reshape(pairs, 1, 8, 128)], axis=1
            )
            out_ref[plane, tap] = both.reshape(pairs * 16, 128).astype(BF16)


def last_planes_kernel(volume_ref, out_ref, sem):
    count = out_ref.shape[0]
    copy = pltpu.make_async_copy(
        volume_ref.at[pl.ds(volume_ref.shape[0] - count, count)], out_ref, sem
    )
    copy.start()
    copy.wait()


def last_planes(volume, count):
    shape = (count, *volume.shape[1:])
    return pl.pallas_call(
        last_planes_kernel,
        out_shape=pltpu.VMEM(shape, BF16),
        in_specs=[pl.BlockSpec(memory_space=pltpu.HBM)],
        out_specs=pl.BlockSpec(memory_space=pltpu.VMEM),
        scratch_shapes=[pltpu.SemaphoreType.DMA],
        cost_estimate=pl.CostEstimate(
            flops=0, bytes_accessed=4 * shape[0] * shape[1] * shape[2], transcendentals=0
        ),
    )(volume)


def sorted_planes(volume):
    planes, rows, width = volume.shape
    pairs = width // 128
    return call(
        functools.partial(sort_kernel, planes),
        sds((planes, 3, pairs * 16, 128), BF16),
        [pltpu.VMEM((pairs, rows, 128), F32)],
        volume,
    )


def put_rows(dst, pieces, offsets):
    rows = pieces[0].shape[0]
    for index, piece in enumerate(pieces):
        dst[pl.ds(pl.multiple_of(offsets[index], 16), rows), :] = piece[...]


def put_tap(columns, at, left, source):
    rows = source.shape[0]
    columns[at : at + 16, left : left + 128] = jnp.zeros((16, 128), BF16)
    columns[at + 16 : at + rows, left : left + 128] = source[0 : rows - 16, :]
    columns[at : at + rows, left + 128 : left + 256] = source[...]


def gather_taps(columns, sorted_ref, halo_ref, first, count):
    rows = sorted_ref.shape[2]
    for cell in range(count):
        for a in range(3):
            plane = 2 * (first + cell) - 1 + a
            for e in range(3):
                source = (
                    halo_ref.at[halo_ref.shape[0] + plane, e] if plane < 0 else sorted_ref.at[plane, e]
                )
                put_tap(columns, cell * rows, (a * 3 + e) * 256, source)


def pad_first(whole, padded):
    for tap in range(9):
        padded[tap * 256 : tap * 256 + 64, :] = jnp.zeros((64, 128), BF16)
        padded[tap * 256 + 64 : (tap + 1) * 256, :] = whole[tap * 192 : (tap + 1) * 192, :]


def take_windows(read, dst, out, a, half):
    for e in range(3):
        for f in range(3):
            block = read(0 if f == 1 else 1, 0 if e == 1 else 1)
            if e == 0:
                block = from_before(block)
            if f == 0:
                block = jnp.concatenate(
                    [jnp.zeros((8, 128), F32), block[: half * 8 - 8]], axis=0
                )
            left = ((a * 3 + e) * 3 + f) * 128
            dst[out * half * 8 : (out + 1) * half * 8, left : left + 128] = block.astype(BF16)


def forward_upper_kernel(
    offsets, sorted_ref, w0, w1, w2, w3,
    slope_ref, hidden_ref, middle_ref, partial_ref, padded_ref, columns, some, whole,
):
    cells = sorted_ref.shape[0] // 2
    put_rows(whole, (w0, w1, w2, w3), offsets)
    pad_first(whole, padded_ref)
    gather_taps(columns, sorted_ref, None, 1, cells - 1)
    linear = jnp.dot(columns[...], padded_ref[...], preferred_element_type=F32)
    hidden = activate(linear)
    hidden_ref[...] = hidden.reshape(hidden_ref.shape)
    count = middle_ref.shape[0] * middle_ref.shape[1]
    middle_ref[...] = hidden[:count].reshape(middle_ref.shape).astype(BF16)
    slope_ref[...] = activate_slope(linear)
    for a in range(1, 3):
        for e in range(3):
            put_tap(some, 0, ((a - 1) * 3 + e) * 256, sorted_ref.at[a - 1, e])
    partial_ref[...] = jnp.dot(some[...], padded_ref[3 * 256 :, :], preferred_element_type=F32)


def forward_upper(sorted_volume, shards, offsets):
    planes, _, rows, _ = sorted_volume.shape
    cells = planes // 2
    shard = shards[0].shape[0]
    some = (cells - 1) * rows
    return call(
        forward_upper_kernel,
        (
            sds((some, 128), F32),
            sds((cells - 1, rows // 32, 2, 2, 8, 128), F32),
            sds((cells - 2, rows, 128), BF16),
            sds((rows, 128), F32),
            sds((9 * 256, 128), BF16),
        ),
        [
            pltpu.VMEM((some, 9 * 256), BF16),
            pltpu.VMEM((rows, 6 * 256), BF16),
            pltpu.VMEM((4 * shard, 128), BF16),
        ],
        sorted_volume, *shards,
        smem=(offsets,),
        micros=2.5,
    )


def forward_lower_kernel(
    alive, side, halo_ref, hidden_ref, partial_ref, padded_ref,
    slope_ref, windows_ref, sorted_ref, here_ref, there_ref, wide, columns, some, lowest, planes,
):
    rows = partial_ref.shape[0]
    cells = hidden_ref.shape[0] + 1
    half = rows // 32
    sort_kernel(halo_ref.shape[0], halo_ref, sorted_ref, wide)
    for e in range(3):
        for a in range(3):
            put_tap(columns, 0, (a * 3 + e) * 256, sorted_ref.at[a, e])
        put_tap(some, 0, e * 256, sorted_ref.at[2, e])
    below = jnp.dot(columns[...], padded_ref[...], preferred_element_type=F32)
    here = partial_ref[...] + jnp.dot(
        some[...], padded_ref[: 3 * 256, :], preferred_element_type=F32
    )
    slope_ref[:rows, :] = activate_slope(below)
    slope_ref[rows:, :] = activate_slope(here)
    lowest[0] = (activate(below) * alive[0]).reshape(lowest.shape[1:])
    lowest[1] = activate(here).reshape(lowest.shape[1:])
    planes[0] = lowest[0].reshape(rows, 128).astype(BF16)
    planes[1] = lowest[1].reshape(rows, 128).astype(BF16)
    planes[2] = planes[1]
    planes[3] = hidden_ref[cells - 2].reshape(rows, 128).astype(BF16)
    here_ref[...] = planes[pl.ds(2 * side[0], 2)]
    there_ref[...] = planes[pl.ds(2 - 2 * side[0], 2)]
    for out in range(cells // 2):
        for a in range(3):
            plane = 2 * out - 1 + a
            source = lowest.at[plane + 1] if plane < 1 else hidden_ref.at[plane - 1]

            def read(column, row):
                return source[:, column, row].reshape(half * 8, 128)

            take_windows(read, windows_ref, out, a, half)


def forward_lower(halo, hidden, partial, padded, alive, side):
    rows = partial.shape[0]
    cells = hidden.shape[0] + 1
    return call(
        forward_lower_kernel,
        (
            sds((2 * rows, 128), F32),
            sds((cells * rows // 8, 27 * 128), BF16),
            sds((halo.shape[0], 3, rows, 128), BF16),
            sds((2, rows, 128), BF16),
            sds((2, rows, 128), BF16),
        ),
        [
            pltpu.VMEM((rows // 16, halo.shape[1], 128), F32),
            pltpu.VMEM((rows, 9 * 256), BF16),
            pltpu.VMEM((rows, 3 * 256), BF16),
            pltpu.VMEM((2, *hidden.shape[1:]), F32),
            pltpu.VMEM((4, rows, 128), BF16),
        ],
        halo, hidden, partial, padded,
        smem=(alive, side),
        micros=1.5,
    )


def put_pieces(flat, outs, slots, order):
    for index, out in enumerate(outs):
        count, size, _ = out.shape
        for place in range(count):
            row = pl.multiple_of(order[place] * size, 8)
            out[place] = flat[slots[index], pl.ds(row, size), :].astype(BF16)


def forward_second_kernel(
    offsets, windows_ref, cot_ref, w0, w1, w2, w3, act_ref, delta_ref, whole
):
    put_rows(whole, (w0, w1, w2, w3), offsets)
    linear = jnp.dot(windows_ref[...], whole[...], preferred_element_type=F32)
    outs, _, width = cot_ref.shape
    features = linear.shape[1]
    count = width // features
    acted = activate(linear)
    slope = activate_slope(linear)
    deltas = []
    for out in range(outs):
        base = out * count * 8
        act_ref[out] = jnp.concatenate(
            [acted[base + q * 8 : base + (q + 1) * 8] for q in range(count)], axis=1
        ).astype(BF16)
        cot = cot_ref[out].astype(F32)
        deltas.append(
            jnp.concatenate(
                [cot[:, q * features : (q + 1) * features] for q in range(count)], axis=0
            )
        )
    delta_ref[...] = (jnp.concatenate(deltas, axis=0) * slope).astype(BF16)


def forward_second(windows, cot, shards, offsets):
    rows, features = shards[0].shape
    return call(
        forward_second_kernel,
        (sds(cot.shape, BF16), sds((windows.shape[0], features), BF16)),
        [pltpu.VMEM((4 * rows, features), BF16)],
        windows, cot, *shards,
        smem=(offsets,),
        micros=1.5,
    )


def second_rows_kernel(
    data, table, order, e0, e1, e2, e3, m0, m1, m2, m3, d0, d1, d2, d3,
    out_ref, wide, windows, deltas, product, flat,
):
    edges, rows, _ = e0.shape
    cells = edges + m0.shape[0]
    half = rows // 32
    outs = cells // 2
    size = half * 8
    taps = windows.shape[1] // 128
    samples = ((e0, m0, d0), (e1, m1, d1), (e2, m2, d2), (e3, m3, d3))
    for sample, (edge, middle, delta) in enumerate(samples):
        at = sample * cells
        wide[at : at + edges] = edge[...].astype(F32).reshape(edges, half, 2, 2, 8, 128)
        wide[at + edges : at + cells] = (
            middle[...].astype(F32).reshape(cells - edges, half, 2, 2, 8, 128)
        )
        deltas[sample * outs * size : (sample + 1) * outs * size, :] = delta[...]
    for tap in range(taps):
        e, f = table[data[0], tap], table[data[0], taps + tap]
        row = jnp.where(e == 1, 0, 1)
        column = jnp.where(f == 1, 0, 1)
        for sample in range(4):
            for out in range(outs):
                plane = sample * cells + table[data[0], (2 + out) * taps + tap]
                block = wide[plane, :, column, row].reshape(size, 128)
                block = jnp.where(e == 0, from_before(block), block)
                later = jnp.concatenate([jnp.zeros((8, 128), F32), block[: size - 8]], axis=0)
                block = jnp.where(f == 0, later, block)
                at = (sample * outs + out) * size
                windows[at : at + size, tap * 128 : (tap + 1) * 128] = block.astype(BF16)
    product[...] = lax.dot_general(
        windows[...], deltas[...], (((0,), (0,)), ((), ())), preferred_element_type=F32
    )
    lanes = product.shape[1] // 128
    count, piece, _ = out_ref.shape
    shard = 27 * 128 // 4
    for lane in range(lanes):
        flat[lane * shard : (lane + 1) * shard, :] = product[
            pl.ds(pl.multiple_of(table[data[0], (2 + outs) * taps], 16), shard), lane * 128 : (lane + 1) * 128
        ]
    rest = flat.shape[0] - lanes * shard
    if rest:
        flat[lanes * shard :, :] = jnp.zeros((rest, 128), F32)
    for place in range(count):
        row = pl.multiple_of(order[place] * piece, 8)
        out_ref[place] = flat[pl.ds(row, piece), :].astype(BF16)


def second_rows(edges, middles, deltas, data, order, places, size):
    _, rows, _ = edges[0].shape
    cells = edges[0].shape[0] + middles[0].shape[0]
    cellrows, features = deltas[0].shape
    taps = 8
    table = []
    for shard in range(4):
        start = shard * 27 // 4
        at = [min(start + tap, 26) for tap in range(taps)]
        held = (-1, 0, *range(1, cells - 1)) if shard < 2 else (0, cells - 1, *range(1, cells - 1))
        table.append(
            [tap // 3 % 3 for tap in at]
            + [tap % 3 for tap in at]
            + [held.index(2 * out - 1 + tap // 9) for out in range(cells // 2) for tap in at]
            + [shard * (27 * 128 // 4) - start * 128]
        )
    return call(
        second_rows_kernel,
        sds((places, size, 128), BF16),
        [
            pltpu.VMEM((4 * cells, rows // 32, 2, 2, 8, 128), F32),
            pltpu.VMEM((4 * cellrows, taps * 128), BF16),
            pltpu.VMEM((4 * cellrows, features), BF16),
            pltpu.VMEM((taps * 128, features), F32),
            pltpu.VMEM((places * size, 128), F32),
        ],
        *edges, *middles, *deltas,
        smem=(data.reshape(1), jnp.array(table, jnp.int32), order),
        micros=2.0,
    )


def back_second_kernel(
    offsets, slots, order, delta_ref, w0, w1, w2, w3,
    slope_low_ref, slope_ref, sorted_ref, halo_ref,
    low_ref, last_ref, down_ref, g0, g1, g2, g3,
    whole, product, columns, deltas, flat,
):
    rows = sorted_ref.shape[2]
    cells = sorted_ref.shape[0] // 2
    half = rows // 32
    size = half * 8
    put_rows(whole, (w0, w1, w2, w3), offsets)
    product[...] = lax.dot_general(
        delta_ref[...], whole[...], (((1,), (1,)), ((), ())), preferred_element_type=F32
    )
    gather_taps(columns, sorted_ref, halo_ref, -1, cells + 1)

    def term(out, a, e, f):
        left = ((a * 3 + e) * 3 + f) * 128
        block = product[out * size : (out + 1) * size, left : left + 128]
        if f == 0:
            block = jnp.concatenate([block[8:], jnp.zeros((8, 128), F32)], axis=0)
        if e == 0:
            block = from_after(block)
        return block.reshape(half, 8, 128)

    for plane in range(-1, cells):
        taps = [
            (out, a) for out in range(cells // 2) for a in range(3) if 2 * out - 1 + a == plane
        ]
        sums = [
            sum(
                term(out, a, e, f)
                for out, a in taps
                for e in ((0, 2) if row else (1,))
                for f in ((0, 2) if column else (1,))
            ).reshape(half, 1, 8, 128)
            for column in range(2)
            for row in range(2)
        ]
        spread = jnp.concatenate(sums, axis=1).reshape(rows, 128)
        if plane < 1:
            slope = slope_low_ref[(plane + 1) * rows : (plane + 2) * rows, :]
        else:
            slope = slope_ref[(plane - 1) * rows : plane * rows, :]
        delta = (spread * slope).astype(BF16)
        deltas[(plane + 1) * rows : (plane + 2) * rows, :] = delta
        if plane < 0:
            down_ref[:rows, :] = spread.astype(BF16)
        if plane == 0:
            down_ref[rows:, :] = delta
        if plane == cells - 1:
            last_ref[...] = spread
        elif plane >= 0:
            low_ref[plane * rows : (plane + 1) * rows, :] = delta
    flipped = jnp.transpose(deltas[...].astype(F32)).astype(BF16)
    tally = jnp.dot(flipped, columns[...], preferred_element_type=F32)
    shard_rows = 9 * 192 // 4
    for tap in range(9):
        turned = jnp.transpose(tally[:, tap * 256 : (tap + 1) * 256])[64:]
        at = tap * 192
        while at < (tap + 1) * 192:
            shard = at // shard_rows
            to = min((tap + 1) * 192, (shard + 1) * shard_rows)
            flat[shard, at - shard * shard_rows : to - shard * shard_rows, :] = turned[
                at - tap * 192 : to - tap * 192
            ]
            at = to
    rest = flat.shape[1] - shard_rows
    if rest:
        flat[:, shard_rows:, :] = jnp.zeros((4, rest, 128), F32)
    put_pieces(flat, (g0, g1, g2, g3), slots, order)


def back_second(delta, shards, slopes, sorted_volume, halo, offsets, slots, order, places, size):
    rows, features = shards[0].shape
    planes, _, width, _ = sorted_volume.shape
    cells = planes // 2
    piece = sds((places, size, 128), BF16)
    return call(
        back_second_kernel,
        (
            sds(((cells - 1) * width, 128), BF16),
            sds((width, 128), F32),
            sds((2 * width, 128), BF16),
            piece, piece, piece, piece,
        ),
        [
            pltpu.VMEM((4 * rows, features), BF16),
            pltpu.VMEM((delta.shape[0], 4 * rows), F32),
            pltpu.VMEM(((cells + 1) * width, 9 * 256), BF16),
            pltpu.VMEM(((cells + 1) * width, 128), BF16),
            pltpu.VMEM((4, places * size, 128), F32),
        ],
        delta, *shards, *slopes, sorted_volume, halo,
        smem=(offsets, slots, order),
        micros=3.5,
    )


def back_input_kernel(
    offsets, low_ref, last_ref, slope_ref, upper_ref, w0, w1, w2, w3,
    out_ref, whole, turned, pairs, product, wide, last,
):
    put_rows(whole, (w0, w1, w2, w3), offsets)
    for tap in range(9):
        top = tap * 128
        turned[top : top + 128, 0:128] = whole[tap * 192 + 64 : (tap + 1) * 192, :]
        turned[top : top + 64, 128:256] = jnp.zeros((64, 128), BF16)
        turned[top + 64 : top + 128, 128:256] = whole[tap * 192 : tap * 192 + 64, :]
    planes = out_ref.shape[0]
    cells = planes // 2
    rows = last_ref.shape[0]
    groups = rows // 16
    last[...] = (
        (last_ref[...] + upper_ref[:rows, :].astype(F32)) * slope_ref[(cells - 2) * rows :, :]
    ).astype(BF16)
    for cell in range(cells + 1):
        at = cell * rows
        if cell < cells - 1:
            source = low_ref.at[at : at + rows]
        else:
            source = last if cell == cells - 1 else upper_ref.at[rows : 2 * rows]
        pairs[at : at + rows, 0:128] = source[...]
        pairs[at : at + rows - 16, 128:256] = source[16:rows, :]
        pairs[at + rows - 16 : at + rows, 128:256] = jnp.zeros((16, 128), BF16)
    product[...] = lax.dot_general(
        pairs[...], turned[...], (((1,), (1,)), ((), ())), preferred_element_type=F32
    ).reshape(product.shape)

    def part(cell, a, e, parity):
        left = (a * 3 + e) * 128
        return product[cell * groups : (cell + 1) * groups, parity, :, left : left + 128]

    def after(block):
        flat = block.reshape(groups * 8, 128)
        return from_after(flat).reshape(groups, 8, 128)

    for plane in range(planes):
        taps = [(o, a) for o in range(cells + 1) for a in range(3) if 2 * o - 1 + a == plane]
        wide[:, pl.ds(0, 8, stride=4), :] = sum(part(o, a, 1, 0) for o, a in taps)
        wide[:, pl.ds(1, 8, stride=4), :] = sum(
            part(o, a, 2, 0) + part(o, a, 0, 1) for o, a in taps
        )
        wide[:, pl.ds(2, 8, stride=4), :] = sum(part(o, a, 1, 1) for o, a in taps)
        wide[:, pl.ds(3, 8, stride=4), :] = sum(part(o, a, 2, 1) for o, a in taps) + after(
            sum(part(o, a, 0, 0) for o, a in taps)
        )
        for group in range(groups):
            lanes = slice(group * 128, (group + 1) * 128)
            out_ref[plane, :, lanes] = wide[group].astype(BF16)


def back_input(low, last, slope, upper, shards, offsets, shape):
    planes, side, width = shape
    shard = shards[0].shape[0]
    rows = low.shape[0] + upper.shape[0]
    return call(
        back_input_kernel,
        sds(shape, BF16),
        [
            pltpu.VMEM((4 * shard, 128), BF16),
            pltpu.VMEM((9 * 128, 256), BF16),
            pltpu.VMEM((rows, 256), BF16),
            pltpu.VMEM((rows // 16, 2, 8, 9 * 128), F32),
            pltpu.VMEM((width // 128, side, 128), F32),
            pltpu.VMEM(last.shape, BF16),
        ],
        low, last, slope, upper, *shards,
        smem=(offsets,),
        micros=3.0,
    )


def unpack_kernel(scale_first, scale_second, order, *refs):
    *chunks, other, first_ref, second_ref, flat_first, flat_second = refs
    high = len(chunks)
    small = flat_first.shape[0] // (2 * high)
    big = flat_second.shape[0] // (2 * high)
    for low in range(2):
        for index in range(high):
            chunk = (other[index] if low else chunks[index][...]).astype(F32)
            place = order[low * high + index]
            flat_second[pl.ds(pl.multiple_of(place * big, 8), big), :] = chunk[:big, :]
            flat_first[pl.ds(pl.multiple_of(place * small, 8), small), :] = chunk[big:, :]
    rows, features = second_ref.shape
    for lane in range(features // 128):
        second_ref[:, lane * 128 : (lane + 1) * 128] = (
            flat_second[lane * rows : (lane + 1) * rows, :] * scale_second
        )
    first_ref[...] = flat_first[: first_ref.shape[0], :] * scale_first


def wide_sum(*pieces):
    return sum(piece.astype(F32) for piece in pieces)


def added(*pieces):
    return wide_sum(*pieces).astype(BF16)


def swap(value, axis, bits):
    size = lax.axis_size(axis)
    return lax.ppermute(value, axis, [(i, i ^ bits) for i in range(size)])


def shifted(value, axis, by):
    size = lax.axis_size(axis)
    pairs = [(i, i + by) for i in range(size) if 0 <= i + by < size]
    return lax.ppermute(value, axis, pairs)


def local(volume, weight_first, weight_second, cotangent):
    samples, planes, side, width = volume.shape
    data = lax.axis_index("dp")
    place = lax.axis_index("space")
    spaces = lax.axis_size("space")
    high = spaces // 2
    small, big = weight_first.shape[0], weight_second.shape[0]
    slots = jnp.arange(4, dtype=jnp.int32) ^ data
    offsets_first = slots * small
    offsets_second = slots * big
    alive = (place > 0).astype(F32).reshape(1)
    x_side = lax.shift_right_logical(data, 1)
    steps = jnp.arange(spaces, dtype=jnp.int32)
    order = place ^ (2 * (steps % high) + steps // high)
    lanes = weight_second.shape[1] // 128
    size_first = -(-small // (8 * spaces)) * 8
    size_second = -(-lanes * big // (8 * spaces)) * 8

    inputs = volume.reshape(planes, side, width)
    uppermost = last_planes(inputs, 3)
    first_x = swap(weight_first, "dp", 2)
    first_core = swap(weight_first, "dp", 1)
    second_x = swap(weight_second, "dp", 2)
    second_core = swap(weight_second, "dp", 1)
    halo = shifted(uppermost, "space", 1)
    first_far = swap(first_x, "dp", 1)
    shards_first = (weight_first, first_core, first_x, first_far)

    sorted_volume = sorted_planes(inputs)
    slope, hidden, middle, partial, padded = forward_upper(
        sorted_volume, shards_first, offsets_first
    )
    middle_x, middle_core = swap(middle, "dp", 2), swap(middle, "dp", 1)
    second_x, hidden = lax.optimization_barrier((second_x, hidden))
    second_far = swap(second_x, "dp", 1)
    shards_second = (weight_second, second_core, second_x, second_far)
    slope_low, windows, sorted_halo, edge, edge_there = forward_lower(
        halo, hidden, partial, padded, alive, x_side.reshape(1)
    )
    windows, middle_x, middle_core = lax.optimization_barrier((windows, middle_x, middle_core))
    middle_far = swap(middle_x, "dp", 1)
    cot = cotangent.reshape(cotangent.shape[1:])
    activations, delta_second = forward_second(windows, cot, shards_second, offsets_second)
    edge_x, edge_core = swap(edge_there, "dp", 2), swap(edge, "dp", 1)
    delta_x, delta_core = swap(delta_second, "dp", 2), swap(delta_second, "dp", 1)
    low, last, down, *first = back_second(
        delta_second, shards_second, (slope_low, slope), sorted_volume, sorted_halo,
        offsets_second, slots, order, spaces, size_first,
    )
    first, down, delta_x, edge_x, delta_core, edge_core, middle_far = lax.optimization_barrier(
        (first, down, delta_x, edge_x, delta_core, edge_core, middle_far)
    )
    second = second_rows(
        (edge, edge_core, edge_x, swap(edge_x, "dp", 1)),
        (middle, middle_core, middle_x, middle_far),
        (delta_second, delta_core, delta_x, swap(delta_x, "dp", 1)),
        data, order, spaces, size_second,
    )
    upper = shifted(down, "space", -1)

    def pieces(value):
        return value.reshape(2, high, -1, 128)

    far, near = pieces(swap(first[3], "dp", 1)), pieces(swap(first[1], "dp", 1))
    own, there = pieces(first[0]), pieces(first[2])
    both = [
        (d * spaces + s, (d ^ 2) * spaces + (s ^ 1)) for d in range(4) for s in range(spaces)
    ]
    second = pieces(second)
    got_y = swap(jnp.concatenate([second[1], added(own[1], near[1])], axis=1), "space", 1)
    got_x = swap(added(there[0], far[0]), "dp", 2)
    got_xy = lax.ppermute(added(there[1], far[1]), ("dp", "space"), both)
    held = jnp.concatenate(
        [
            added(second[0], got_y[:, :size_second]),
            added(own[0], near[0], got_x, got_xy, got_y[:, size_second:]),
        ],
        axis=1,
    )
    mine = added(held[0], *(swap(held[k], "space", 2 * k) for k in range(1, high)))
    chunks = [mine] + [swap(mine, "space", 2 * k) for k in range(1, high)]
    chunks.append(swap(jnp.stack(chunks), "space", 1))

    gradient = back_input(low, last, slope, upper, shards_first, offsets_first, inputs.shape)

    cells_first = samples * lax.axis_size("dp") * (planes // 2) * spaces * (side // 2) ** 2
    cells_second = cells_first // 8
    first_gradient, second_gradient = call(
        functools.partial(unpack_kernel, float(cells_first) ** -0.5, float(cells_second) ** -0.5),
        (sds(weight_first.shape, F32), sds(weight_second.shape, F32)),
        [
            pltpu.VMEM((spaces * size_first, 128), F32),
            pltpu.VMEM((spaces * size_second, 128), F32),
        ],
        *chunks,
        smem=(order,),
    )
    return (
        activations.reshape(cotangent.shape),
        gradient.reshape(volume.shape),
        first_gradient,
        second_gradient,
    )


def solution(mesh):
    return jax.shard_map(
        local,
        mesh=mesh,
        in_specs=(
            P("dp", "space", None, None),
            P("dp", None),
            P("dp", None),
            P("dp", "space", None, None),
        ),
        out_specs=(
            P("dp", "space", None, None),
            P("dp", "space", None, None),
            P("dp", None),
            P("dp", None),
        ),
        check_vma=False,
    )
```

```python
import functools

import jax
import jax.numpy as jnp
from jax import lax
from jax.experimental import pallas as pl
from jax.experimental.pallas import tpu as pltpu
from jax.sharding import PartitionSpec as P

LEAK_SLOPE = 0.2
F32 = jnp.float32
BF16 = jnp.bfloat16
VMEM_LIMIT = 24 * 1024 * 1024


def activate(values):
    small = jnp.exp(-jnp.abs(values))
    return LEAK_SLOPE * values + (1.0 - LEAK_SLOPE) * (
        jnp.maximum(values, 0.0) + jnp.log(1.0 + small)
    )


def activate_slope(values):
    small = jnp.exp(-jnp.abs(values))
    inverse = 1.0 / (1.0 + small)
    return LEAK_SLOPE + (1.0 - LEAK_SLOPE) * jnp.where(
        values >= 0.0, inverse, small * inverse
    )


def block_row(rows, width):
    return lax.broadcasted_iota(jnp.int32, (rows, width), 0) % 8


def from_before(block):
    moved = pltpu.roll(block, 1, 0)
    return jnp.where(block_row(*block.shape) == 0, 0.0, moved)


def from_after(block):
    moved = pltpu.roll(block, block.shape[0] - 1, 0)
    return jnp.where(block_row(*block.shape) == 7, 0.0, moved)


def call(kernel, out_shape, scratch, *operands, smem=(), micros=1.0):
    nbytes = sum(a.size * a.dtype.itemsize for a in operands)
    specs = [pl.BlockSpec(memory_space=pltpu.SMEM)] * len(smem)
    specs += [pl.BlockSpec(memory_space=pltpu.VMEM)] * len(operands)
    return pl.pallas_call(
        kernel,
        out_shape=out_shape,
        in_specs=specs,
        out_specs=jax.tree.map(lambda _: pl.BlockSpec(memory_space=pltpu.VMEM), out_shape),
        scratch_shapes=scratch,
        compiler_params=pltpu.CompilerParams(vmem_limit_bytes=VMEM_LIMIT),
        cost_estimate=pl.CostEstimate(
            flops=int(micros * 1.15e9), bytes_accessed=nbytes, transcendentals=0
        ),
    )(*smem, *operands)


def sds(shape, dtype):
    return jax.ShapeDtypeStruct(shape, dtype)


def near(shape, dtype):
    return pltpu.VMEM(shape, dtype)


def sort_kernel(planes, in_ref, out_ref, wide):
    pairs = wide.shape[0]
    for plane in range(planes):
        for pair in range(pairs):
            wide[pair] = in_ref[plane, :, pair * 128 : (pair + 1) * 128].astype(F32)
        classes = [
            wide[:, pl.ds(r, 8, stride=4), :].reshape(pairs * 8, 128) for r in range(4)
        ]
        before = from_before(classes[3])
        for tap, (even, odd) in enumerate(
            ((before, classes[1]), (classes[0], classes[2]), (classes[1], classes[3]))
        ):
            both = jnp.concatenate(
                [even.reshape(pairs, 1, 8, 128), odd.reshape(pairs, 1, 8, 128)], axis=1
            )
            out_ref[plane, tap] = both.reshape(pairs * 16, 128).astype(BF16)


def last_planes_kernel(volume_ref, out_ref, sem):
    count = out_ref.shape[0]
    copy = pltpu.make_async_copy(
        volume_ref.at[pl.ds(volume_ref.shape[0] - count, count)], out_ref, sem
    )
    copy.start()
    copy.wait()


def last_planes(volume, count):
    shape = (count, *volume.shape[1:])
    return pl.pallas_call(
        last_planes_kernel,
        out_shape=pltpu.VMEM(shape, BF16),
        in_specs=[pl.BlockSpec(memory_space=pltpu.HBM)],
        out_specs=pl.BlockSpec(memory_space=pltpu.VMEM),
        scratch_shapes=[pltpu.SemaphoreType.DMA],
        cost_estimate=pl.CostEstimate(
            flops=0, bytes_accessed=4 * shape[0] * shape[1] * shape[2], transcendentals=0
        ),
    )(volume)


def sorted_planes(volume):
    planes, rows, width = volume.shape
    pairs = width // 128
    return call(
        functools.partial(sort_kernel, planes),
        near((planes, 3, pairs * 16, 128), BF16),
        [pltpu.VMEM((pairs, rows, 128), F32)],
        volume,
    )


def put_rows(dst, pieces, offsets):
    rows = pieces[0].shape[0]
    for index, piece in enumerate(pieces):
        dst[pl.ds(pl.multiple_of(offsets[index], 16), rows), :] = piece[...]


def put_tap(columns, at, left, source):
    rows = source.shape[0]
    columns[at : at + 16, left : left + 128] = jnp.zeros((16, 128), BF16)
    columns[at + 16 : at + rows, left : left + 128] = source[0 : rows - 16, :]
    columns[at : at + rows, left + 128 : left + 256] = source[...]


def gather_taps(columns, sorted_ref, halo_ref, first, count):
    rows = sorted_ref.shape[2]
    for cell in range(count):
        for a in range(3):
            plane = 2 * (first + cell) - 1 + a
            for e in range(3):
                source = (
                    halo_ref.at[halo_ref.shape[0] + plane, e] if plane < 0 else sorted_ref.at[plane, e]
                )
                put_tap(columns, cell * rows, (a * 3 + e) * 256, source)


def pad_first(whole, padded):
    for tap in range(9):
        padded[tap * 256 : tap * 256 + 64, :] = jnp.zeros((64, 128), BF16)
        padded[tap * 256 + 64 : (tap + 1) * 256, :] = whole[tap * 192 : (tap + 1) * 192, :]


def take_windows(read, dst, out, a, half):
    for e in range(3):
        for f in range(3):
            block = read(0 if f == 1 else 1, 0 if e == 1 else 1)
            if e == 0:
                block = from_before(block)
            if f == 0:
                block = jnp.concatenate(
                    [jnp.zeros((8, 128), F32), block[: half * 8 - 8]], axis=0
                )
            left = ((a * 3 + e) * 3 + f) * 128
            dst[out * half * 8 : (out + 1) * half * 8, left : left + 128] = block.astype(BF16)


def forward_upper_kernel(
    offsets, sorted_ref, w0, w1, w2, w3,
    slope_ref, hidden_ref, middle_ref, partial_ref, padded_ref, columns, some, whole,
):
    cells = sorted_ref.shape[0] // 2
    put_rows(whole, (w0, w1, w2, w3), offsets)
    pad_first(whole, padded_ref)
    gather_taps(columns, sorted_ref, None, 1, cells - 1)
    linear = jnp.dot(columns[...], padded_ref[...], preferred_element_type=F32)
    hidden = activate(linear)
    hidden_ref[...] = hidden.reshape(hidden_ref.shape)
    count = middle_ref.shape[0] * middle_ref.shape[1]
    middle_ref[...] = hidden[:count].reshape(middle_ref.shape).astype(BF16)
    slope_ref[...] = activate_slope(linear)
    for a in range(1, 3):
        for e in range(3):
            put_tap(some, 0, ((a - 1) * 3 + e) * 256, sorted_ref.at[a - 1, e])
    partial_ref[...] = jnp.dot(some[...], padded_ref[3 * 256 :, :], preferred_element_type=F32)


def forward_upper(sorted_volume, shards, offsets):
    planes, _, rows, _ = sorted_volume.shape
    cells = planes // 2
    shard = shards[0].shape[0]
    some = (cells - 1) * rows
    return call(
        forward_upper_kernel,
        (
            near((some, 128), F32),
            near((cells - 1, rows // 32, 2, 2, 8, 128), F32),
            sds((cells - 2, rows, 128), BF16),
            near((rows, 128), F32),
            near((9 * 256, 128), BF16),
        ),
        [
            pltpu.VMEM((some, 9 * 256), BF16),
            pltpu.VMEM((rows, 6 * 256), BF16),
            pltpu.VMEM((4 * shard, 128), BF16),
        ],
        sorted_volume, *shards,
        smem=(offsets,),
        micros=2.5,
    )


def forward_lower_kernel(
    alive, side, halo_ref, hidden_ref, partial_ref, padded_ref,
    slope_ref, windows_ref, sorted_ref, here_ref, there_ref, wide, columns, some, lowest, planes,
):
    rows = partial_ref.shape[0]
    cells = hidden_ref.shape[0] + 1
    half = rows // 32
    sort_kernel(halo_ref.shape[0], halo_ref, sorted_ref, wide)
    for e in range(3):
        for a in range(3):
            put_tap(columns, 0, (a * 3 + e) * 256, sorted_ref.at[a, e])
        put_tap(some, 0, e * 256, sorted_ref.at[2, e])
    below = jnp.dot(columns[...], padded_ref[...], preferred_element_type=F32)
    here = partial_ref[...] + jnp.dot(
        some[...], padded_ref[: 3 * 256, :], preferred_element_type=F32
    )
    slope_ref[:rows, :] = activate_slope(below)
    slope_ref[rows:, :] = activate_slope(here)
    lowest[0] = (activate(below) * alive[0]).reshape(lowest.shape[1:])
    lowest[1] = activate(here).reshape(lowest.shape[1:])
    planes[0] = lowest[0].reshape(rows, 128).astype(BF16)
    planes[1] = lowest[1].reshape(rows, 128).astype(BF16)
    planes[2] = planes[1]
    planes[3] = hidden_ref[cells - 2].reshape(rows, 128).astype(BF16)
    here_ref[...] = planes[pl.ds(2 * side[0], 2)]
    there_ref[...] = planes[pl.ds(2 - 2 * side[0], 2)]
    for out in range(cells // 2):
        for a in range(3):
            plane = 2 * out - 1 + a
            source = lowest.at[plane + 1] if plane < 1 else hidden_ref.at[plane - 1]

            def read(column, row):
                return source[:, column, row].reshape(half * 8, 128)

            take_windows(read, windows_ref, out, a, half)


def forward_lower(halo, hidden, partial, padded, alive, side):
    rows = partial.shape[0]
    cells = hidden.shape[0] + 1
    return call(
        forward_lower_kernel,
        (
            near((2 * rows, 128), F32),
            near((cells * rows // 8, 27 * 128), BF16),
            near((halo.shape[0], 3, rows, 128), BF16),
            sds((2, rows, 128), BF16),
            sds((2, rows, 128), BF16),
        ),
        [
            pltpu.VMEM((rows // 16, halo.shape[1], 128), F32),
            pltpu.VMEM((rows, 9 * 256), BF16),
            pltpu.VMEM((rows, 3 * 256), BF16),
            pltpu.VMEM((2, *hidden.shape[1:]), F32),
            pltpu.VMEM((4, rows, 128), BF16),
        ],
        halo, hidden, partial, padded,
        smem=(alive, side),
        micros=1.5,
    )


def put_pieces(flat, outs, slots, order):
    for index, out in enumerate(outs):
        count, size, _ = out.shape
        for place in range(count):
            row = pl.multiple_of(order[place] * size, 8)
            out[place] = flat[slots[index], pl.ds(row, size), :].astype(BF16)


def forward_second_kernel(
    offsets, windows_ref, cot_ref, w0, w1, w2, w3, act_ref, delta_ref, whole
):
    put_rows(whole, (w0, w1, w2, w3), offsets)
    linear = jnp.dot(windows_ref[...], whole[...], preferred_element_type=F32)
    outs, _, width = cot_ref.shape
    features = linear.shape[1]
    count = width // features
    acted = activate(linear)
    slope = activate_slope(linear)
    deltas = []
    for out in range(outs):
        base = out * count * 8
        act_ref[out] = jnp.concatenate(
            [acted[base + q * 8 : base + (q + 1) * 8] for q in range(count)], axis=1
        ).astype(BF16)
        cot = cot_ref[out].astype(F32)
        deltas.append(
            jnp.concatenate(
                [cot[:, q * features : (q + 1) * features] for q in range(count)], axis=0
            )
        )
    delta_ref[...] = (jnp.concatenate(deltas, axis=0) * slope).astype(BF16)


def forward_second(windows, cot, shards, offsets):
    rows, features = shards[0].shape
    return call(
        forward_second_kernel,
        (sds(cot.shape, BF16), sds((windows.shape[0], features), BF16)),
        [pltpu.VMEM((4 * rows, features), BF16)],
        windows, cot, *shards,
        smem=(offsets,),
        micros=1.5,
    )


def second_rows_kernel(
    data, table, order, e0, e1, e2, e3, m0, m1, m2, m3, d0, d1, d2, d3,
    out_ref, wide, windows, deltas, product, flat,
):
    edges, rows, _ = e0.shape
    cells = edges + m0.shape[0]
    half = rows // 32
    outs = cells // 2
    size = half * 8
    taps = windows.shape[1] // 128
    samples = ((e0, m0, d0), (e1, m1, d1), (e2, m2, d2), (e3, m3, d3))
    for sample, (edge, middle, delta) in enumerate(samples):
        at = sample * cells
        wide[at : at + edges] = edge[...].astype(F32).reshape(edges, half, 2, 2, 8, 128)
        wide[at + edges : at + cells] = (
            middle[...].astype(F32).reshape(cells - edges, half, 2, 2, 8, 128)
        )
        deltas[sample * outs * size : (sample + 1) * outs * size, :] = delta[...]
    for tap in range(taps):
        e, f = table[data[0], tap], table[data[0], taps + tap]
        row = jnp.where(e == 1, 0, 1)
        column = jnp.where(f == 1, 0, 1)
        for sample in range(4):
            for out in range(outs):
                plane = sample * cells + table[data[0], (2 + out) * taps + tap]
                block = wide[plane, :, column, row].reshape(size, 128)
                block = jnp.where(e == 0, from_before(block), block)
                later = jnp.concatenate([jnp.zeros((8, 128), F32), block[: size - 8]], axis=0)
                block = jnp.where(f == 0, later, block)
                at = (sample * outs + out) * size
                windows[at : at + size, tap * 128 : (tap + 1) * 128] = block.astype(BF16)
    product[...] = lax.dot_general(
        windows[...], deltas[...], (((0,), (0,)), ((), ())), preferred_element_type=F32
    )
    lanes = product.shape[1] // 128
    count, piece, _ = out_ref.shape
    shard = 27 * 128 // 4
    for lane in range(lanes):
        flat[lane * shard : (lane + 1) * shard, :] = product[
            pl.ds(pl.multiple_of(table[data[0], (2 + outs) * taps], 16), shard), lane * 128 : (lane + 1) * 128
        ]
    rest = flat.shape[0] - lanes * shard
    if rest:
        flat[lanes * shard :, :] = jnp.zeros((rest, 128), F32)
    for place in range(count):
        row = pl.multiple_of(order[place] * piece, 8)
        out_ref[place] = flat[pl.ds(row, piece), :].astype(BF16)


def second_rows(edges, middles, deltas, data, order, places, size):
    _, rows, _ = edges[0].shape
    cells = edges[0].shape[0] + middles[0].shape[0]
    cellrows, features = deltas[0].shape
    taps = 8
    table = []
    for shard in range(4):
        start = shard * 27 // 4
        at = [min(start + tap, 26) for tap in range(taps)]
        held = (-1, 0, *range(1, cells - 1)) if shard < 2 else (0, cells - 1, *range(1, cells - 1))
        table.append(
            [tap // 3 % 3 for tap in at]
            + [tap % 3 for tap in at]
            + [held.index(2 * out - 1 + tap // 9) for out in range(cells // 2) for tap in at]
            + [shard * (27 * 128 // 4) - start * 128]
        )
    return call(
        second_rows_kernel,
        sds((places, size, 128), BF16),
        [
            pltpu.VMEM((4 * cells, rows // 32, 2, 2, 8, 128), F32),
            pltpu.VMEM((4 * cellrows, taps * 128), BF16),
            pltpu.VMEM((4 * cellrows, features), BF16),
            pltpu.VMEM((taps * 128, features), F32),
            pltpu.VMEM((places * size, 128), F32),
        ],
        *edges, *middles, *deltas,
        smem=(data.reshape(1), jnp.array(table, jnp.int32), order),
        micros=2.0,
    )


def back_second_kernel(
    offsets, slots, order, delta_ref, w0, w1, w2, w3,
    slope_low_ref, slope_ref, sorted_ref, halo_ref,
    low_ref, last_ref, down_ref, g0, g1, g2, g3,
    whole, product, columns, deltas, flat,
):
    rows = sorted_ref.shape[2]
    cells = sorted_ref.shape[0] // 2
    half = rows // 32
    size = half * 8
    put_rows(whole, (w0, w1, w2, w3), offsets)
    product[...] = lax.dot_general(
        delta_ref[...], whole[...], (((1,), (1,)), ((), ())), preferred_element_type=F32
    )
    gather_taps(columns, sorted_ref, halo_ref, -1, cells + 1)

    def term(out, a, e, f):
        left = ((a * 3 + e) * 3 + f) * 128
        block = product[out * size : (out + 1) * size, left : left + 128]
        if f == 0:
            block = jnp.concatenate([block[8:], jnp.zeros((8, 128), F32)], axis=0)
        if e == 0:
            block = from_after(block)
        return block.reshape(half, 8, 128)

    for plane in range(-1, cells):
        taps = [
            (out, a) for out in range(cells // 2) for a in range(3) if 2 * out - 1 + a == plane
        ]
        sums = [
            sum(
                term(out, a, e, f)
                for out, a in taps
                for e in ((0, 2) if row else (1,))
                for f in ((0, 2) if column else (1,))
            ).reshape(half, 1, 8, 128)
            for column in range(2)
            for row in range(2)
        ]
        spread = jnp.concatenate(sums, axis=1).reshape(rows, 128)
        if plane < 1:
            slope = slope_low_ref[(plane + 1) * rows : (plane + 2) * rows, :]
        else:
            slope = slope_ref[(plane - 1) * rows : plane * rows, :]
        delta = (spread * slope).astype(BF16)
        deltas[(plane + 1) * rows : (plane + 2) * rows, :] = delta
        if plane < 0:
            down_ref[:rows, :] = spread.astype(BF16)
        if plane == 0:
            down_ref[rows:, :] = delta
        if plane == cells - 1:
            last_ref[...] = spread
        elif plane >= 0:
            low_ref[plane * rows : (plane + 1) * rows, :] = delta
    flipped = jnp.transpose(deltas[...].astype(F32)).astype(BF16)
    tally = jnp.dot(flipped, columns[...], preferred_element_type=F32)
    shard_rows = 9 * 192 // 4
    for tap in range(9):
        turned = jnp.transpose(tally[:, tap * 256 : (tap + 1) * 256])[64:]
        at = tap * 192
        while at < (tap + 1) * 192:
            shard = at // shard_rows
            to = min((tap + 1) * 192, (shard + 1) * shard_rows)
            flat[shard, at - shard * shard_rows : to - shard * shard_rows, :] = turned[
                at - tap * 192 : to - tap * 192
            ]
            at = to
    rest = flat.shape[1] - shard_rows
    if rest:
        flat[:, shard_rows:, :] = jnp.zeros((4, rest, 128), F32)
    put_pieces(flat, (g0, g1, g2, g3), slots, order)


def back_second(delta, shards, slopes, sorted_volume, halo, offsets, slots, order, places, size):
    rows, features = shards[0].shape
    planes, _, width, _ = sorted_volume.shape
    cells = planes // 2
    piece = sds((places, size, 128), BF16)
    return call(
        back_second_kernel,
        (
            near(((cells - 1) * width, 128), BF16),
            near((width, 128), F32),
            sds((2 * width, 128), BF16),
            piece, piece, piece, piece,
        ),
        [
            pltpu.VMEM((4 * rows, features), BF16),
            pltpu.VMEM((delta.shape[0], 4 * rows), F32),
            pltpu.VMEM(((cells + 1) * width, 9 * 256), BF16),
            pltpu.VMEM(((cells + 1) * width, 128), BF16),
            pltpu.VMEM((4, places * size, 128), F32),
        ],
        delta, *shards, *slopes, sorted_volume, halo,
        smem=(offsets, slots, order),
        micros=3.5,
    )


def back_input_kernel(
    offsets, low_ref, last_ref, slope_ref, upper_ref, w0, w1, w2, w3,
    out_ref, whole, turned, pairs, product, wide, last,
):
    put_rows(whole, (w0, w1, w2, w3), offsets)
    for tap in range(9):
        top = tap * 128
        turned[top : top + 128, 0:128] = whole[tap * 192 + 64 : (tap + 1) * 192, :]
        turned[top : top + 64, 128:256] = jnp.zeros((64, 128), BF16)
        turned[top + 64 : top + 128, 128:256] = whole[tap * 192 : tap * 192 + 64, :]
    planes = out_ref.shape[0]
    cells = planes // 2
    rows = last_ref.shape[0]
    groups = rows // 16
    last[...] = (
        (last_ref[...] + upper_ref[:rows, :].astype(F32)) * slope_ref[(cells - 2) * rows :, :]
    ).astype(BF16)
    for cell in range(cells + 1):
        at = cell * rows
        if cell < cells - 1:
            source = low_ref.at[at : at + rows]
        else:
            source = last if cell == cells - 1 else upper_ref.at[rows : 2 * rows]
        pairs[at : at + rows, 0:128] = source[...]
        pairs[at : at + rows - 16, 128:256] = source[16:rows, :]
        pairs[at + rows - 16 : at + rows, 128:256] = jnp.zeros((16, 128), BF16)
    product[...] = lax.dot_general(
        pairs[...], turned[...], (((1,), (1,)), ((), ())), preferred_element_type=F32
    ).reshape(product.shape)

    def part(cell, a, e, parity):
        left = (a * 3 + e) * 128
        return product[cell * groups : (cell + 1) * groups, parity, :, left : left + 128]

    def after(block):
        flat = block.reshape(groups * 8, 128)
        return from_after(flat).reshape(groups, 8, 128)

    for plane in range(planes):
        taps = [(o, a) for o in range(cells + 1) for a in range(3) if 2 * o - 1 + a == plane]
        wide[:, pl.ds(0, 8, stride=4), :] = sum(part(o, a, 1, 0) for o, a in taps)
        wide[:, pl.ds(1, 8, stride=4), :] = sum(
            part(o, a, 2, 0) + part(o, a, 0, 1) for o, a in taps
        )
        wide[:, pl.ds(2, 8, stride=4), :] = sum(part(o, a, 1, 1) for o, a in taps)
        wide[:, pl.ds(3, 8, stride=4), :] = sum(part(o, a, 2, 1) for o, a in taps) + after(
            sum(part(o, a, 0, 0) for o, a in taps)
        )
        for group in range(groups):
            lanes = slice(group * 128, (group + 1) * 128)
            out_ref[plane, :, lanes] = wide[group].astype(BF16)


def back_input(low, last, slope, upper, shards, offsets, shape):
    planes, side, width = shape
    shard = shards[0].shape[0]
    rows = low.shape[0] + upper.shape[0]
    return call(
        back_input_kernel,
        sds(shape, BF16),
        [
            pltpu.VMEM((4 * shard, 128), BF16),
            pltpu.VMEM((9 * 128, 256), BF16),
            pltpu.VMEM((rows, 256), BF16),
            pltpu.VMEM((rows // 16, 2, 8, 9 * 128), F32),
            pltpu.VMEM((width // 128, side, 128), F32),
            pltpu.VMEM(last.shape, BF16),
        ],
        low, last, slope, upper, *shards,
        smem=(offsets,),
        micros=3.0,
    )


def unpack_kernel(scale_first, scale_second, order, *refs):
    *chunks, other, first_ref, second_ref, flat_first, flat_second = refs
    high = len(chunks)
    small = flat_first.shape[0] // (2 * high)
    big = flat_second.shape[0] // (2 * high)
    for low in range(2):
        for index in range(high):
            chunk = (other[index] if low else chunks[index][...]).astype(F32)
            place = order[low * high + index]
            flat_second[pl.ds(pl.multiple_of(place * big, 8), big), :] = chunk[:big, :]
            flat_first[pl.ds(pl.multiple_of(place * small, 8), small), :] = chunk[big:, :]
    rows, features = second_ref.shape
    for lane in range(features // 128):
        second_ref[:, lane * 128 : (lane + 1) * 128] = (
            flat_second[lane * rows : (lane + 1) * rows, :] * scale_second
        )
    first_ref[...] = flat_first[: first_ref.shape[0], :] * scale_first


def wide_sum(*pieces):
    return sum(piece.astype(F32) for piece in pieces)


def added(*pieces):
    return wide_sum(*pieces).astype(BF16)


def swap(value, axis, bits):
    size = lax.axis_size(axis)
    return lax.ppermute(value, axis, [(i, i ^ bits) for i in range(size)])


def shifted(value, axis, by):
    size = lax.axis_size(axis)
    pairs = [(i, i + by) for i in range(size) if 0 <= i + by < size]
    return lax.ppermute(value, axis, pairs)


def local(volume, weight_first, weight_second, cotangent):
    samples, planes, side, width = volume.shape
    data = lax.axis_index("dp")
    place = lax.axis_index("space")
    spaces = lax.axis_size("space")
    high = spaces // 2
    small, big = weight_first.shape[0], weight_second.shape[0]
    slots = jnp.arange(4, dtype=jnp.int32) ^ data
    offsets_first = slots * small
    offsets_second = slots * big
    alive = (place > 0).astype(F32).reshape(1)
    x_side = lax.shift_right_logical(data, 1)
    steps = jnp.arange(spaces, dtype=jnp.int32)
    order = place ^ (2 * (steps % high) + steps // high)
    lanes = weight_second.shape[1] // 128
    size_first = -(-small // (8 * spaces)) * 8
    size_second = -(-lanes * big // (8 * spaces)) * 8

    inputs = volume.reshape(planes, side, width)
    uppermost = last_planes(inputs, 3)
    first_x = swap(weight_first, "dp", 2)
    first_core = swap(weight_first, "dp", 1)
    second_x = swap(weight_second, "dp", 2)
    second_core = swap(weight_second, "dp", 1)
    halo = shifted(uppermost, "space", 1)
    first_far = swap(first_x, "dp", 1)
    shards_first = (weight_first, first_core, first_x, first_far)

    sorted_volume = sorted_planes(inputs)
    slope, hidden, middle, partial, padded = forward_upper(
        sorted_volume, shards_first, offsets_first
    )
    middle_x, middle_core = swap(middle, "dp", 2), swap(middle, "dp", 1)
    second_x, hidden = lax.optimization_barrier((second_x, hidden))
    second_far = swap(second_x, "dp", 1)
    shards_second = (weight_second, second_core, second_x, second_far)
    slope_low, windows, sorted_halo, edge, edge_there = forward_lower(
        halo, hidden, partial, padded, alive, x_side.reshape(1)
    )
    cot = cotangent.reshape(cotangent.shape[1:])
    activations, delta_second = forward_second(windows, cot, shards_second, offsets_second)
    edge_x, edge_core = swap(edge_there, "dp", 2), swap(edge, "dp", 1)
    delta_x, delta_core = swap(delta_second, "dp", 2), swap(delta_second, "dp", 1)
    low, last, down, *first = back_second(
        delta_second, shards_second, (slope_low, slope), sorted_volume, sorted_halo,
        offsets_second, slots, order, spaces, size_first,
    )
    first, down, delta_x, edge_x, delta_core, edge_core, middle_x, middle_core = (
        lax.optimization_barrier(
            (first, down, delta_x, edge_x, delta_core, edge_core, middle_x, middle_core)
        )
    )
    second = second_rows(
        (edge, edge_core, edge_x, swap(edge_x, "dp", 1)),
        (middle, middle_core, middle_x, swap(middle_x, "dp", 1)),
        (delta_second, delta_core, delta_x, swap(delta_x, "dp", 1)),
        data, order, spaces, size_second,
    )
    upper = shifted(down, "space", -1)

    def pieces(value):
        return value.reshape(2, high, -1, 128)

    far, beside = pieces(swap(first[3], "dp", 1)), pieces(swap(first[1], "dp", 1))
    own, there = pieces(first[0]), pieces(first[2])
    both = [
        (d * spaces + s, (d ^ 2) * spaces + (s ^ 1)) for d in range(4) for s in range(spaces)
    ]
    second = pieces(second)
    got_y = swap(jnp.concatenate([second[1], added(own[1], beside[1])], axis=1), "space", 1)
    got_x = swap(added(there[0], far[0]), "dp", 2)
    got_xy = lax.ppermute(added(there[1], far[1]), ("dp", "space"), both)
    held = jnp.concatenate(
        [
            added(second[0], got_y[:, :size_second]),
            added(own[0], beside[0], got_x, got_xy, got_y[:, size_second:]),
        ],
        axis=1,
    )
    mine = added(held[0], *(swap(held[k], "space", 2 * k) for k in range(1, high)))
    chunks = [mine] + [swap(mine, "space", 2 * k) for k in range(1, high)]
    chunks.append(swap(jnp.stack(chunks), "space", 1))

    gradient = back_input(low, last, slope, upper, shards_first, offsets_first, inputs.shape)

    cells_first = samples * lax.axis_size("dp") * (planes // 2) * spaces * (side // 2) ** 2
    cells_second = cells_first // 8
    first_gradient, second_gradient = call(
        functools.partial(unpack_kernel, float(cells_first) ** -0.5, float(cells_second) ** -0.5),
        (sds(weight_first.shape, F32), sds(weight_second.shape, F32)),
        [
            pltpu.VMEM((spaces * size_first, 128), F32),
            pltpu.VMEM((spaces * size_second, 128), F32),
        ],
        *chunks,
        smem=(order,),
    )
    return (
        activations.reshape(cotangent.shape),
        gradient.reshape(volume.shape),
        first_gradient,
        second_gradient,
    )


def solution(mesh):
    return jax.shard_map(
        local,
        mesh=mesh,
        in_specs=(
            P("dp", "space", None, None),
            P("dp", None),
            P("dp", None),
            P("dp", "space", None, None),
        ),
        out_specs=(
            P("dp", "space", None, None),
            P("dp", "space", None, None),
            P("dp", None),
            P("dp", None),
        ),
        check_vma=False,
    )
```

```python
import functools

import jax
import jax.numpy as jnp
from jax import lax
from jax.experimental import pallas as pl
from jax.experimental.pallas import tpu as pltpu
from jax.sharding import PartitionSpec as P

LEAK_SLOPE = 0.2
F32 = jnp.float32
BF16 = jnp.bfloat16
VMEM_LIMIT = 24 * 1024 * 1024


def activate(values):
    small = jnp.exp(-jnp.abs(values))
    return LEAK_SLOPE * values + (1.0 - LEAK_SLOPE) * (
        jnp.maximum(values, 0.0) + jnp.log(1.0 + small)
    )


def activate_slope(values):
    small = jnp.exp(-jnp.abs(values))
    inverse = 1.0 / (1.0 + small)
    return LEAK_SLOPE + (1.0 - LEAK_SLOPE) * jnp.where(
        values >= 0.0, inverse, small * inverse
    )


def block_row(rows, width):
    return lax.broadcasted_iota(jnp.int32, (rows, width), 0) % 8


def from_before(block):
    moved = pltpu.roll(block, 1, 0)
    return jnp.where(block_row(*block.shape) == 0, 0.0, moved)


def from_after(block):
    moved = pltpu.roll(block, block.shape[0] - 1, 0)
    return jnp.where(block_row(*block.shape) == 7, 0.0, moved)


def call(kernel, out_shape, scratch, *operands, smem=(), micros=1.0):
    nbytes = sum(a.size * a.dtype.itemsize for a in operands)
    specs = [pl.BlockSpec(memory_space=pltpu.SMEM)] * len(smem)
    specs += [pl.BlockSpec(memory_space=pltpu.VMEM)] * len(operands)
    return pl.pallas_call(
        kernel,
        out_shape=out_shape,
        in_specs=specs,
        out_specs=jax.tree.map(lambda _: pl.BlockSpec(memory_space=pltpu.VMEM), out_shape),
        scratch_shapes=scratch,
        compiler_params=pltpu.CompilerParams(vmem_limit_bytes=VMEM_LIMIT),
        cost_estimate=pl.CostEstimate(
            flops=int(micros * 1.15e9), bytes_accessed=nbytes, transcendentals=0
        ),
    )(*smem, *operands)


def sds(shape, dtype):
    return jax.ShapeDtypeStruct(shape, dtype)


def near(shape, dtype):
    return pltpu.VMEM(shape, dtype)


def sort_kernel(planes, in_ref, out_ref, wide):
    pairs = wide.shape[0]
    for plane in range(planes):
        for pair in range(pairs):
            wide[pair] = in_ref[plane, :, pair * 128 : (pair + 1) * 128].astype(F32)
        classes = [
            wide[:, pl.ds(r, 8, stride=4), :].reshape(pairs * 8, 128) for r in range(4)
        ]
        before = from_before(classes[3])
        for tap, (even, odd) in enumerate(
            ((before, classes[1]), (classes[0], classes[2]), (classes[1], classes[3]))
        ):
            both = jnp.concatenate(
                [even.reshape(pairs, 1, 8, 128), odd.reshape(pairs, 1, 8, 128)], axis=1
            )
            out_ref[plane, tap] = both.reshape(pairs * 16, 128).astype(BF16)


def last_planes_kernel(volume_ref, out_ref, sem):
    count = out_ref.shape[0]
    copy = pltpu.make_async_copy(
        volume_ref.at[pl.ds(volume_ref.shape[0] - count, count)], out_ref, sem
    )
    copy.start()
    copy.wait()


def last_planes(volume, count):
    shape = (count, *volume.shape[1:])
    return pl.pallas_call(
        last_planes_kernel,
        out_shape=pltpu.VMEM(shape, BF16),
        in_specs=[pl.BlockSpec(memory_space=pltpu.HBM)],
        out_specs=pl.BlockSpec(memory_space=pltpu.VMEM),
        scratch_shapes=[pltpu.SemaphoreType.DMA],
        cost_estimate=pl.CostEstimate(
            flops=0, bytes_accessed=4 * shape[0] * shape[1] * shape[2], transcendentals=0
        ),
    )(volume)


def sorted_planes(volume):
    planes, rows, width = volume.shape
    pairs = width // 128
    return call(
        functools.partial(sort_kernel, planes),
        near((planes, 3, pairs * 16, 128), BF16),
        [pltpu.VMEM((pairs, rows, 128), F32)],
        volume,
    )


def put_rows(dst, pieces, offsets):
    rows = pieces[0].shape[0]
    for index, piece in enumerate(pieces):
        dst[pl.ds(pl.multiple_of(offsets[index], 16), rows), :] = piece[...]


def put_tap(columns, at, left, source):
    rows = source.shape[0]
    columns[at : at + 16, left : left + 128] = jnp.zeros((16, 128), BF16)
    columns[at + 16 : at + rows, left : left + 128] = source[0 : rows - 16, :]
    columns[at : at + rows, left + 128 : left + 256] = source[...]


def gather_taps(columns, sorted_ref, halo_ref, first, count):
    rows = sorted_ref.shape[2]
    for cell in range(count):
        for a in range(3):
            plane = 2 * (first + cell) - 1 + a
            for e in range(3):
                source = (
                    halo_ref.at[halo_ref.shape[0] + plane, e] if plane < 0 else sorted_ref.at[plane, e]
                )
                put_tap(columns, cell * rows, (a * 3 + e) * 256, source)


def pad_first(whole, padded):
    for tap in range(9):
        padded[tap * 256 : tap * 256 + 64, :] = jnp.zeros((64, 128), BF16)
        padded[tap * 256 + 64 : (tap + 1) * 256, :] = whole[tap * 192 : (tap + 1) * 192, :]


def take_windows(read, dst, row, left, half):
    for e in range(3):
        for f in range(3):
            block = read(0 if f == 1 else 1, 0 if e == 1 else 1)
            if e == 0:
                block = from_before(block)
            if f == 0:
                block = jnp.concatenate(
                    [jnp.zeros((8, 128), F32), block[: half * 8 - 8]], axis=0
                )
            at = left + (e * 3 + f) * 128
            dst[row : row + half * 8, at : at + 128] = block.astype(BF16)


def forward_upper_kernel(
    offsets, sorted_ref, w0, w1, w2, w3,
    slope_ref, windows_ref, middle_ref, top_ref, partial_ref, padded_ref,
    columns, some, whole, upper,
):
    cells = sorted_ref.shape[0] // 2
    put_rows(whole, (w0, w1, w2, w3), offsets)
    pad_first(whole, padded_ref)
    gather_taps(columns, sorted_ref, None, 1, cells - 1)
    linear = jnp.dot(columns[...], padded_ref[...], preferred_element_type=F32)
    hidden = activate(linear)
    upper[...] = hidden.reshape(upper.shape)
    count = middle_ref.shape[0] * middle_ref.shape[1]
    middle_ref[...] = hidden[:count].reshape(middle_ref.shape).astype(BF16)
    top_ref[...] = hidden[count:].astype(BF16)
    slope_ref[...] = activate_slope(linear)
    half = upper.shape[1]
    for out in range(cells // 2):
        for a in range(3):
            plane = 2 * out - 1 + a
            if plane > 0:

                def read(column, row):
                    return upper[plane - 1, :, column, row].reshape(half * 8, 128)

                take_windows(read, windows_ref, out * half * 8, a * 9 * 128, half)
    for a in range(1, 3):
        for e in range(3):
            put_tap(some, 0, ((a - 1) * 3 + e) * 256, sorted_ref.at[a - 1, e])
    partial_ref[...] = jnp.dot(some[...], padded_ref[3 * 256 :, :], preferred_element_type=F32)


def forward_upper(sorted_volume, shards, offsets):
    planes, _, rows, _ = sorted_volume.shape
    cells = planes // 2
    shard = shards[0].shape[0]
    some = (cells - 1) * rows
    return call(
        forward_upper_kernel,
        (
            near((some, 128), F32),
            near((cells * rows // 8, 27 * 128), BF16),
            sds((cells - 2, rows, 128), BF16),
            near((rows, 128), BF16),
            near((rows, 128), F32),
            near((9 * 256, 128), BF16),
        ),
        [
            pltpu.VMEM((some, 9 * 256), BF16),
            pltpu.VMEM((rows, 6 * 256), BF16),
            pltpu.VMEM((4 * shard, 128), BF16),
            pltpu.VMEM((cells - 1, rows // 32, 2, 2, 8, 128), F32),
        ],
        sorted_volume, *shards,
        smem=(offsets,),
        micros=2.5,
    )


def forward_lower_kernel(
    alive, side, halo_ref, top_ref, partial_ref, padded_ref,
    slope_ref, windows_ref, sorted_ref, here_ref, there_ref, wide, columns, some, lowest, planes,
):
    rows = partial_ref.shape[0]
    half = rows // 32
    sort_kernel(halo_ref.shape[0], halo_ref, sorted_ref, wide)
    for e in range(3):
        for a in range(3):
            put_tap(columns, 0, (a * 3 + e) * 256, sorted_ref.at[a, e])
        put_tap(some, 0, e * 256, sorted_ref.at[2, e])
    below = jnp.dot(columns[...], padded_ref[...], preferred_element_type=F32)
    here = partial_ref[...] + jnp.dot(
        some[...], padded_ref[: 3 * 256, :], preferred_element_type=F32
    )
    slope_ref[:rows, :] = activate_slope(below)
    slope_ref[rows:, :] = activate_slope(here)
    lowest[0] = (activate(below) * alive[0]).reshape(lowest.shape[1:])
    lowest[1] = activate(here).reshape(lowest.shape[1:])
    planes[0] = lowest[0].reshape(rows, 128).astype(BF16)
    planes[1] = lowest[1].reshape(rows, 128).astype(BF16)
    planes[2] = planes[1]
    planes[3] = top_ref[...]
    here_ref[...] = planes[pl.ds(2 * side[0], 2)]
    there_ref[...] = planes[pl.ds(2 - 2 * side[0], 2)]
    for a in range(2):

        def read(column, row):
            return lowest[a, :, column, row].reshape(half * 8, 128)

        take_windows(read, windows_ref, 0, a * 9 * 128, half)


def forward_lower(halo, top, partial, padded, alive, side):
    rows = partial.shape[0]
    return call(
        forward_lower_kernel,
        (
            near((2 * rows, 128), F32),
            near((rows // 4, 2 * 9 * 128), BF16),
            near((halo.shape[0], 3, rows, 128), BF16),
            sds((2, rows, 128), BF16),
            sds((2, rows, 128), BF16),
        ),
        [
            pltpu.VMEM((rows // 16, halo.shape[1], 128), F32),
            pltpu.VMEM((rows, 9 * 256), BF16),
            pltpu.VMEM((rows, 3 * 256), BF16),
            pltpu.VMEM((2, rows // 32, 2, 2, 8, 128), F32),
            pltpu.VMEM((4, rows, 128), BF16),
        ],
        halo, top, partial, padded,
        smem=(alive, side),
        micros=1.5,
    )


def put_pieces(flat, outs, slots, order):
    for index, out in enumerate(outs):
        count, size, _ = out.shape
        for place in range(count):
            row = pl.multiple_of(order[place] * size, 8)
            out[place] = flat[slots[index], pl.ds(row, size), :].astype(BF16)


def forward_second_kernel(
    offsets, upper_ref, lower_ref, cot_ref, w0, w1, w2, w3, act_ref, delta_ref, whole, windows
):
    put_rows(whole, (w0, w1, w2, w3), offsets)
    low, width = lower_ref.shape
    windows[:low, :width] = lower_ref[...]
    windows[:low, width:] = upper_ref[:low, width:]
    windows[low:, :] = upper_ref[low:, :]
    linear = jnp.dot(windows[...], whole[...], preferred_element_type=F32)
    outs, _, width = cot_ref.shape
    features = linear.shape[1]
    count = width // features
    acted = activate(linear)
    slope = activate_slope(linear)
    deltas = []
    for out in range(outs):
        base = out * count * 8
        act_ref[out] = jnp.concatenate(
            [acted[base + q * 8 : base + (q + 1) * 8] for q in range(count)], axis=1
        ).astype(BF16)
        cot = cot_ref[out].astype(F32)
        deltas.append(
            jnp.concatenate(
                [cot[:, q * features : (q + 1) * features] for q in range(count)], axis=0
            )
        )
    delta_ref[...] = (jnp.concatenate(deltas, axis=0) * slope).astype(BF16)


def forward_second(upper, lower, cot, shards, offsets):
    rows, features = shards[0].shape
    return call(
        forward_second_kernel,
        (sds(cot.shape, BF16), sds((upper.shape[0], features), BF16)),
        [pltpu.VMEM((4 * rows, features), BF16), pltpu.VMEM(upper.shape, BF16)],
        upper, lower, cot, *shards,
        smem=(offsets,),
        micros=1.5,
    )


def second_rows_kernel(
    data, table, order, e0, e1, e2, e3, m0, m1, m2, m3, d0, d1, d2, d3,
    out_ref, wide, windows, deltas, product, flat,
):
    edges, rows, _ = e0.shape
    cells = edges + m0.shape[0]
    half = rows // 32
    outs = cells // 2
    size = half * 8
    taps = windows.shape[1] // 128
    samples = ((e0, m0, d0), (e1, m1, d1), (e2, m2, d2), (e3, m3, d3))
    for sample, (edge, middle, delta) in enumerate(samples):
        at = sample * cells
        wide[at : at + edges] = edge[...].astype(F32).reshape(edges, half, 2, 2, 8, 128)
        wide[at + edges : at + cells] = (
            middle[...].astype(F32).reshape(cells - edges, half, 2, 2, 8, 128)
        )
        deltas[sample * outs * size : (sample + 1) * outs * size, :] = delta[...]
    for tap in range(taps):
        e, f = table[data[0], tap], table[data[0], taps + tap]
        row = jnp.where(e == 1, 0, 1)
        column = jnp.where(f == 1, 0, 1)
        for sample in range(4):
            for out in range(outs):
                plane = sample * cells + table[data[0], (2 + out) * taps + tap]
                block = wide[plane, :, column, row].reshape(size, 128)
                block = jnp.where(e == 0, from_before(block), block)
                later = jnp.concatenate([jnp.zeros((8, 128), F32), block[: size - 8]], axis=0)
                block = jnp.where(f == 0, later, block)
                at = (sample * outs + out) * size
                windows[at : at + size, tap * 128 : (tap + 1) * 128] = block.astype(BF16)
    product[...] = lax.dot_general(
        windows[...], deltas[...], (((0,), (0,)), ((), ())), preferred_element_type=F32
    )
    lanes = product.shape[1] // 128
    count, piece, _ = out_ref.shape
    shard = 27 * 128 // 4
    for lane in range(lanes):
        flat[lane * shard : (lane + 1) * shard, :] = product[
            pl.ds(pl.multiple_of(table[data[0], (2 + outs) * taps], 16), shard), lane * 128 : (lane + 1) * 128
        ]
    rest = flat.shape[0] - lanes * shard
    if rest:
        flat[lanes * shard :, :] = jnp.zeros((rest, 128), F32)
    for place in range(count):
        row = pl.multiple_of(order[place] * piece, 8)
        out_ref[place] = flat[pl.ds(row, piece), :].astype(BF16)


def second_rows(edges, middles, deltas, data, order, places, size):
    _, rows, _ = edges[0].shape
    cells = edges[0].shape[0] + middles[0].shape[0]
    cellrows, features = deltas[0].shape
    taps = 8
    table = []
    for shard in range(4):
        start = shard * 27 // 4
        at = [min(start + tap, 26) for tap in range(taps)]
        held = (-1, 0, *range(1, cells - 1)) if shard < 2 else (0, cells - 1, *range(1, cells - 1))
        table.append(
            [tap // 3 % 3 for tap in at]
            + [tap % 3 for tap in at]
            + [held.index(2 * out - 1 + tap // 9) for out in range(cells // 2) for tap in at]
            + [shard * (27 * 128 // 4) - start * 128]
        )
    return call(
        second_rows_kernel,
        sds((places, size, 128), BF16),
        [
            pltpu.VMEM((4 * cells, rows // 32, 2, 2, 8, 128), F32),
            pltpu.VMEM((4 * cellrows, taps * 128), BF16),
            pltpu.VMEM((4 * cellrows, features), BF16),
            pltpu.VMEM((taps * 128, features), F32),
            pltpu.VMEM((places * size, 128), F32),
        ],
        *edges, *middles, *deltas,
        smem=(data.reshape(1), jnp.array(table, jnp.int32), order),
        micros=2.0,
    )


def back_second_kernel(
    offsets, slots, order, delta_ref, w0, w1, w2, w3,
    slope_low_ref, slope_ref, sorted_ref, halo_ref,
    low_ref, last_ref, down_ref, g0, g1, g2, g3,
    whole, product, columns, deltas, flat,
):
    rows = sorted_ref.shape[2]
    cells = sorted_ref.shape[0] // 2
    half = rows // 32
    size = half * 8
    put_rows(whole, (w0, w1, w2, w3), offsets)
    product[...] = lax.dot_general(
        delta_ref[...], whole[...], (((1,), (1,)), ((), ())), preferred_element_type=F32
    )
    gather_taps(columns, sorted_ref, halo_ref, -1, cells + 1)

    def term(out, a, e, f):
        left = ((a * 3 + e) * 3 + f) * 128
        block = product[out * size : (out + 1) * size, left : left + 128]
        if f == 0:
            block = jnp.concatenate([block[8:], jnp.zeros((8, 128), F32)], axis=0)
        if e == 0:
            block = from_after(block)
        return block.reshape(half, 8, 128)

    for plane in range(-1, cells):
        taps = [
            (out, a) for out in range(cells // 2) for a in range(3) if 2 * out - 1 + a == plane
        ]
        sums = [
            sum(
                term(out, a, e, f)
                for out, a in taps
                for e in ((0, 2) if row else (1,))
                for f in ((0, 2) if column else (1,))
            ).reshape(half, 1, 8, 128)
            for column in range(2)
            for row in range(2)
        ]
        spread = jnp.concatenate(sums, axis=1).reshape(rows, 128)
        if plane < 1:
            slope = slope_low_ref[(plane + 1) * rows : (plane + 2) * rows, :]
        else:
            slope = slope_ref[(plane - 1) * rows : plane * rows, :]
        delta = (spread * slope).astype(BF16)
        deltas[(plane + 1) * rows : (plane + 2) * rows, :] = delta
        if plane < 0:
            down_ref[:rows, :] = spread.astype(BF16)
        if plane == 0:
            down_ref[rows:, :] = delta
        if plane == cells - 1:
            last_ref[...] = spread
        elif plane >= 0:
            low_ref[plane * rows : (plane + 1) * rows, :] = delta
    flipped = jnp.transpose(deltas[...].astype(F32)).astype(BF16)
    tally = jnp.dot(flipped, columns[...], preferred_element_type=F32)
    shard_rows = 9 * 192 // 4
    for tap in range(9):
        turned = jnp.transpose(tally[:, tap * 256 : (tap + 1) * 256])[64:]
        at = tap * 192
        while at < (tap + 1) * 192:
            shard = at // shard_rows
            to = min((tap + 1) * 192, (shard + 1) * shard_rows)
            flat[shard, at - shard * shard_rows : to - shard * shard_rows, :] = turned[
                at - tap * 192 : to - tap * 192
            ]
            at = to
    rest = flat.shape[1] - shard_rows
    if rest:
        flat[:, shard_rows:, :] = jnp.zeros((4, rest, 128), F32)
    put_pieces(flat, (g0, g1, g2, g3), slots, order)


def back_second(delta, shards, slopes, sorted_volume, halo, offsets, slots, order, places, size):
    rows, features = shards[0].shape
    planes, _, width, _ = sorted_volume.shape
    cells = planes // 2
    piece = sds((places, size, 128), BF16)
    return call(
        back_second_kernel,
        (
            near(((cells - 1) * width, 128), BF16),
            near((width, 128), F32),
            sds((2 * width, 128), BF16),
            piece, piece, piece, piece,
        ),
        [
            pltpu.VMEM((4 * rows, features), BF16),
            pltpu.VMEM((delta.shape[0], 4 * rows), F32),
            pltpu.VMEM(((cells + 1) * width, 9 * 256), BF16),
            pltpu.VMEM(((cells + 1) * width, 128), BF16),
            pltpu.VMEM((4, places * size, 128), F32),
        ],
        delta, *shards, *slopes, sorted_volume, halo,
        smem=(offsets, slots, order),
        micros=3.5,
    )


def back_input_kernel(
    offsets, low_ref, last_ref, slope_ref, upper_ref, w0, w1, w2, w3,
    out_ref, whole, turned, pairs, product, wide, last,
):
    put_rows(whole, (w0, w1, w2, w3), offsets)
    for tap in range(9):
        top = tap * 128
        turned[top : top + 128, 0:128] = whole[tap * 192 + 64 : (tap + 1) * 192, :]
        turned[top : top + 64, 128:256] = jnp.zeros((64, 128), BF16)
        turned[top + 64 : top + 128, 128:256] = whole[tap * 192 : tap * 192 + 64, :]
    planes = out_ref.shape[0]
    cells = planes // 2
    rows = last_ref.shape[0]
    groups = rows // 16
    last[...] = (
        (last_ref[...] + upper_ref[:rows, :].astype(F32)) * slope_ref[(cells - 2) * rows :, :]
    ).astype(BF16)
    for cell in range(cells + 1):
        at = cell * rows
        if cell < cells - 1:
            source = low_ref.at[at : at + rows]
        else:
            source = last if cell == cells - 1 else upper_ref.at[rows : 2 * rows]
        pairs[at : at + rows, 0:128] = source[...]
        pairs[at : at + rows - 16, 128:256] = source[16:rows, :]
        pairs[at + rows - 16 : at + rows, 128:256] = jnp.zeros((16, 128), BF16)
    product[...] = lax.dot_general(
        pairs[...], turned[...], (((1,), (1,)), ((), ())), preferred_element_type=F32
    ).reshape(product.shape)

    def part(cell, a, e, parity):
        left = (a * 3 + e) * 128
        return product[cell * groups : (cell + 1) * groups, parity, :, left : left + 128]

    def after(block):
        flat = block.reshape(groups * 8, 128)
        return from_after(flat).reshape(groups, 8, 128)

    for plane in range(planes):
        taps = [(o, a) for o in range(cells + 1) for a in range(3) if 2 * o - 1 + a == plane]
        wide[:, pl.ds(0, 8, stride=4), :] = sum(part(o, a, 1, 0) for o, a in taps)
        wide[:, pl.ds(1, 8, stride=4), :] = sum(
            part(o, a, 2, 0) + part(o, a, 0, 1) for o, a in taps
        )
        wide[:, pl.ds(2, 8, stride=4), :] = sum(part(o, a, 1, 1) for o, a in taps)
        wide[:, pl.ds(3, 8, stride=4), :] = sum(part(o, a, 2, 1) for o, a in taps) + after(
            sum(part(o, a, 0, 0) for o, a in taps)
        )
        for group in range(groups):
            lanes = slice(group * 128, (group + 1) * 128)
            out_ref[plane, :, lanes] = wide[group].astype(BF16)


def back_input(low, last, slope, upper, shards, offsets, shape):
    planes, side, width = shape
    shard = shards[0].shape[0]
    rows = low.shape[0] + upper.shape[0]
    return call(
        back_input_kernel,
        sds(shape, BF16),
        [
            pltpu.VMEM((4 * shard, 128), BF16),
            pltpu.VMEM((9 * 128, 256), BF16),
            pltpu.VMEM((rows, 256), BF16),
            pltpu.VMEM((rows // 16, 2, 8, 9 * 128), F32),
            pltpu.VMEM((width // 128, side, 128), F32),
            pltpu.VMEM(last.shape, BF16),
        ],
        low, last, slope, upper, *shards,
        smem=(offsets,),
        micros=3.0,
    )


def unpack_kernel(scale_first, scale_second, order, *refs):
    *chunks, other, first_ref, second_ref, flat_first, flat_second = refs
    high = len(chunks)
    small = flat_first.shape[0] // (2 * high)
    big = flat_second.shape[0] // (2 * high)
    for low in range(2):
        for index in range(high):
            chunk = (other[index] if low else chunks[index][...]).astype(F32)
            place = order[low * high + index]
            flat_second[pl.ds(pl.multiple_of(place * big, 8), big), :] = chunk[:big, :]
            flat_first[pl.ds(pl.multiple_of(place * small, 8), small), :] = chunk[big:, :]
    rows, features = second_ref.shape
    for lane in range(features // 128):
        second_ref[:, lane * 128 : (lane + 1) * 128] = (
            flat_second[lane * rows : (lane + 1) * rows, :] * scale_second
        )
    first_ref[...] = flat_first[: first_ref.shape[0], :] * scale_first


def wide_sum(*pieces):
    return sum(piece.astype(F32) for piece in pieces)


def added(*pieces):
    return wide_sum(*pieces).astype(BF16)


def swap(value, axis, bits):
    size = lax.axis_size(axis)
    return lax.ppermute(value, axis, [(i, i ^ bits) for i in range(size)])


def shifted(value, axis, by):
    size = lax.axis_size(axis)
    pairs = [(i, i + by) for i in range(size) if 0 <= i + by < size]
    return lax.ppermute(value, axis, pairs)


def local(volume, weight_first, weight_second, cotangent):
    samples, planes, side, width = volume.shape
    data = lax.axis_index("dp")
    place = lax.axis_index("space")
    spaces = lax.axis_size("space")
    high = spaces // 2
    small, big = weight_first.shape[0], weight_second.shape[0]
    slots = jnp.arange(4, dtype=jnp.int32) ^ data
    offsets_first = slots * small
    offsets_second = slots * big
    alive = (place > 0).astype(F32).reshape(1)
    x_side = lax.shift_right_logical(data, 1)
    steps = jnp.arange(spaces, dtype=jnp.int32)
    order = place ^ (2 * (steps % high) + steps // high)
    lanes = weight_second.shape[1] // 128
    size_first = -(-small // (8 * spaces)) * 8
    size_second = -(-lanes * big // (8 * spaces)) * 8

    inputs = volume.reshape(planes, side, width)
    uppermost = last_planes(inputs, 3)
    first_x = swap(weight_first, "dp", 2)
    first_core = swap(weight_first, "dp", 1)
    second_x = swap(weight_second, "dp", 2)
    second_core = swap(weight_second, "dp", 1)
    halo = shifted(uppermost, "space", 1)
    first_far = swap(first_x, "dp", 1)
    shards_first = (weight_first, first_core, first_x, first_far)

    sorted_volume = sorted_planes(inputs)
    slope, windows, middle, top, partial, padded = forward_upper(
        sorted_volume, shards_first, offsets_first
    )
    middle_x, middle_core = swap(middle, "dp", 2), swap(middle, "dp", 1)
    second_x, partial = lax.optimization_barrier((second_x, partial))
    second_far = swap(second_x, "dp", 1)
    shards_second = (weight_second, second_core, second_x, second_far)
    slope_low, windows_low, sorted_halo, edge, edge_there = forward_lower(
        halo, top, partial, padded, alive, x_side.reshape(1)
    )
    cot = cotangent.reshape(cotangent.shape[1:])
    activations, delta_second = forward_second(
        windows, windows_low, cot, shards_second, offsets_second
    )
    delta_second, middle_x = lax.optimization_barrier((delta_second, middle_x))
    edge_x, edge_core = swap(edge_there, "dp", 2), swap(edge, "dp", 1)
    delta_x, delta_core = swap(delta_second, "dp", 2), swap(delta_second, "dp", 1)
    low, last, down, *first = back_second(
        delta_second, shards_second, (slope_low, slope), sorted_volume, sorted_halo,
        offsets_second, slots, order, spaces, size_first,
    )
    middle_far = swap(middle_x, "dp", 1)
    first, down, delta_x, edge_x, delta_core, edge_core, middle_far = lax.optimization_barrier(
        (first, down, delta_x, edge_x, delta_core, edge_core, middle_far)
    )
    second = second_rows(
        (edge, edge_core, edge_x, swap(edge_x, "dp", 1)),
        (middle, middle_core, middle_x, middle_far),
        (delta_second, delta_core, delta_x, swap(delta_x, "dp", 1)),
        data, order, spaces, size_second,
    )
    upper = shifted(down, "space", -1)

    def pieces(value):
        return value.reshape(2, high, -1, 128)

    far, beside = pieces(swap(first[3], "dp", 1)), pieces(swap(first[1], "dp", 1))
    own, there = pieces(first[0]), pieces(first[2])
    both = [
        (d * spaces + s, (d ^ 2) * spaces + (s ^ 1)) for d in range(4) for s in range(spaces)
    ]
    second = pieces(second)
    sent_y = jnp.concatenate([second[1], added(own[1], beside[1])], axis=1)
    got_y = swap(sent_y[1:], "space", 1)
    got_x = swap(added(there[0], far[0]), "dp", 2)
    sent_own, got_x = lax.optimization_barrier((sent_y[:1], got_x))
    got_y_own = swap(sent_own, "space", 1)
    got_xy = lax.ppermute(added(there[1], far[1]), ("dp", "space"), both)

    def held(places, got):
        return jnp.concatenate(
            [
                wide_sum(second[0][places], got[:, :size_second]),
                wide_sum(
                    own[0][places], beside[0][places], got_x[places], got_xy[places],
                    got[:, size_second:],
                ),
            ],
            axis=1,
        )

    sent = held(slice(1, high), got_y).astype(BF16)
    mine = added(
        held(slice(0, 1), got_y_own)[0],
        *(swap(sent[k - 1], "space", 2 * k) for k in range(1, high)),
    )
    chunks = [mine] + [swap(mine, "space", 2 * k) for k in range(1, high)]
    chunks.append(swap(jnp.stack(chunks), "space", 1))

    gradient = back_input(low, last, slope, upper, shards_first, offsets_first, inputs.shape)

    cells_first = samples * lax.axis_size("dp") * (planes // 2) * spaces * (side // 2) ** 2
    cells_second = cells_first // 8
    first_gradient, second_gradient = call(
        functools.partial(unpack_kernel, float(cells_first) ** -0.5, float(cells_second) ** -0.5),
        (sds(weight_first.shape, F32), sds(weight_second.shape, F32)),
        [
            pltpu.VMEM((spaces * size_first, 128), F32),
            pltpu.VMEM((spaces * size_second, 128), F32),
        ],
        *chunks,
        smem=(order,),
    )
    return (
        activations.reshape(cotangent.shape),
        gradient.reshape(volume.shape),
        first_gradient,
        second_gradient,
    )


def solution(mesh):
    return jax.shard_map(
        local,
        mesh=mesh,
        in_specs=(
            P("dp", "space", None, None),
            P("dp", None),
            P("dp", None),
            P("dp", "space", None, None),
        ),
        out_specs=(
            P("dp", "space", None, None),
            P("dp", "space", None, None),
            P("dp", None),
            P("dp", None),
        ),
        check_vma=False,
    )
```

```python
import functools

import jax
import jax.numpy as jnp
from jax import lax
from jax.experimental import pallas as pl
from jax.experimental.pallas import tpu as pltpu
from jax.sharding import PartitionSpec as P

LEAK_SLOPE = 0.2
F32 = jnp.float32
BF16 = jnp.bfloat16
VMEM_LIMIT = 24 * 1024 * 1024


def activate(values):
    small = jnp.exp(-jnp.abs(values))
    return LEAK_SLOPE * values + (1.0 - LEAK_SLOPE) * (
        jnp.maximum(values, 0.0) + jnp.log(1.0 + small)
    )


def activate_slope(values):
    small = jnp.exp(-jnp.abs(values))
    inverse = 1.0 / (1.0 + small)
    return LEAK_SLOPE + (1.0 - LEAK_SLOPE) * jnp.where(
        values >= 0.0, inverse, small * inverse
    )


def block_row(rows, width):
    return lax.broadcasted_iota(jnp.int32, (rows, width), 0) % 8


def from_before(block):
    moved = pltpu.roll(block, 1, 0)
    return jnp.where(block_row(*block.shape) == 0, 0.0, moved)


def from_after(block):
    moved = pltpu.roll(block, block.shape[0] - 1, 0)
    return jnp.where(block_row(*block.shape) == 7, 0.0, moved)


def call(kernel, out_shape, scratch, *operands, smem=(), micros=1.0):
    nbytes = sum(a.size * a.dtype.itemsize for a in operands)
    specs = [pl.BlockSpec(memory_space=pltpu.SMEM)] * len(smem)
    specs += [pl.BlockSpec(memory_space=pltpu.VMEM)] * len(operands)
    return pl.pallas_call(
        kernel,
        out_shape=out_shape,
        in_specs=specs,
        out_specs=jax.tree.map(lambda _: pl.BlockSpec(memory_space=pltpu.VMEM), out_shape),
        scratch_shapes=scratch,
        compiler_params=pltpu.CompilerParams(vmem_limit_bytes=VMEM_LIMIT),
        cost_estimate=pl.CostEstimate(
            flops=int(micros * 1.15e9), bytes_accessed=nbytes, transcendentals=0
        ),
    )(*smem, *operands)


def sds(shape, dtype):
    return jax.ShapeDtypeStruct(shape, dtype)


def near(shape, dtype):
    return pltpu.VMEM(shape, dtype)


def sort_kernel(planes, in_ref, out_ref, wide):
    pairs = wide.shape[0]
    for plane in range(planes):
        for pair in range(pairs):
            wide[pair] = in_ref[plane, :, pair * 128 : (pair + 1) * 128].astype(F32)
        classes = [
            wide[:, pl.ds(r, 8, stride=4), :].reshape(pairs * 8, 128) for r in range(4)
        ]
        before = from_before(classes[3])
        for tap, (even, odd) in enumerate(
            ((before, classes[1]), (classes[0], classes[2]), (classes[1], classes[3]))
        ):
            both = jnp.concatenate(
                [even.reshape(pairs, 1, 8, 128), odd.reshape(pairs, 1, 8, 128)], axis=1
            )
            out_ref[plane, tap] = both.reshape(pairs * 16, 128).astype(BF16)


def last_planes_kernel(volume_ref, out_ref, sem):
    count = out_ref.shape[0]
    copy = pltpu.make_async_copy(
        volume_ref.at[pl.ds(volume_ref.shape[0] - count, count)], out_ref, sem
    )
    copy.start()
    copy.wait()


def last_planes(volume, count):
    shape = (count, *volume.shape[1:])
    return pl.pallas_call(
        last_planes_kernel,
        out_shape=pltpu.VMEM(shape, BF16),
        in_specs=[pl.BlockSpec(memory_space=pltpu.HBM)],
        out_specs=pl.BlockSpec(memory_space=pltpu.VMEM),
        scratch_shapes=[pltpu.SemaphoreType.DMA],
        cost_estimate=pl.CostEstimate(
            flops=0, bytes_accessed=4 * shape[0] * shape[1] * shape[2], transcendentals=0
        ),
    )(volume)


def sorted_planes(volume):
    planes, rows, width = volume.shape
    pairs = width // 128
    return call(
        functools.partial(sort_kernel, planes),
        near((planes, 3, pairs * 16, 128), BF16),
        [pltpu.VMEM((pairs, rows, 128), F32)],
        volume,
    )


def put_rows(dst, pieces, offsets):
    rows = pieces[0].shape[0]
    for index, piece in enumerate(pieces):
        dst[pl.ds(pl.multiple_of(offsets[index], 16), rows), :] = piece[...]


def put_tap(columns, at, left, source):
    rows = source.shape[0]
    columns[at : at + 16, left : left + 128] = jnp.zeros((16, 128), BF16)
    columns[at + 16 : at + rows, left : left + 128] = source[0 : rows - 16, :]
    columns[at : at + rows, left + 128 : left + 256] = source[...]


def gather_taps(columns, sorted_ref, halo_ref, first, count):
    rows = sorted_ref.shape[2]
    for cell in range(count):
        for a in range(3):
            plane = 2 * (first + cell) - 1 + a
            for e in range(3):
                source = (
                    halo_ref.at[halo_ref.shape[0] + plane, e] if plane < 0 else sorted_ref.at[plane, e]
                )
                put_tap(columns, cell * rows, (a * 3 + e) * 256, source)


def pad_first(whole, padded):
    for tap in range(9):
        padded[tap * 256 : tap * 256 + 64, :] = jnp.zeros((64, 128), BF16)
        padded[tap * 256 + 64 : (tap + 1) * 256, :] = whole[tap * 192 : (tap + 1) * 192, :]


def take_windows(read, dst, row, left, half):
    for e in range(3):
        for f in range(3):
            block = read(0 if f == 1 else 1, 0 if e == 1 else 1)
            if e == 0:
                block = from_before(block)
            if f == 0:
                block = jnp.concatenate(
                    [jnp.zeros((8, 128), F32), block[: half * 8 - 8]], axis=0
                )
            at = left + (e * 3 + f) * 128
            dst[row : row + half * 8, at : at + 128] = block.astype(BF16)


def forward_upper_kernel(
    offsets, sorted_ref, w0, w1, w2, w3,
    slope_ref, windows_ref, middle_ref, top_ref, partial_ref, padded_ref,
    columns, some, whole, upper,
):
    cells = sorted_ref.shape[0] // 2
    put_rows(whole, (w0, w1, w2, w3), offsets)
    pad_first(whole, padded_ref)
    gather_taps(columns, sorted_ref, None, 1, cells - 1)
    linear = jnp.dot(columns[...], padded_ref[...], preferred_element_type=F32)
    hidden = activate(linear)
    upper[...] = hidden.reshape(upper.shape)
    count = middle_ref.shape[0] * middle_ref.shape[1]
    middle_ref[...] = hidden[:count].reshape(middle_ref.shape).astype(BF16)
    top_ref[...] = hidden[count:].astype(BF16)
    slope_ref[...] = activate_slope(linear)
    half = upper.shape[1]
    for out in range(cells // 2):
        for a in range(3):
            plane = 2 * out - 1 + a
            if plane > 0:

                def read(column, row):
                    return upper[plane - 1, :, column, row].reshape(half * 8, 128)

                take_windows(read, windows_ref, out * half * 8, a * 9 * 128, half)
    for a in range(1, 3):
        for e in range(3):
            put_tap(some, 0, ((a - 1) * 3 + e) * 256, sorted_ref.at[a - 1, e])
    partial_ref[...] = jnp.dot(some[...], padded_ref[3 * 256 :, :], preferred_element_type=F32)


def forward_upper(sorted_volume, shards, offsets):
    planes, _, rows, _ = sorted_volume.shape
    cells = planes // 2
    shard = shards[0].shape[0]
    some = (cells - 1) * rows
    return call(
        forward_upper_kernel,
        (
            near((some, 128), F32),
            near((cells * rows // 8, 27 * 128), BF16),
            sds((cells - 2, rows, 128), BF16),
            near((rows, 128), BF16),
            near((rows, 128), F32),
            near((9 * 256, 128), BF16),
        ),
        [
            pltpu.VMEM((some, 9 * 256), BF16),
            pltpu.VMEM((rows, 6 * 256), BF16),
            pltpu.VMEM((4 * shard, 128), BF16),
            pltpu.VMEM((cells - 1, rows // 32, 2, 2, 8, 128), F32),
        ],
        sorted_volume, *shards,
        smem=(offsets,),
        micros=2.5,
    )


def forward_lower_kernel(
    alive, side, halo_ref, top_ref, partial_ref, padded_ref,
    slope_ref, windows_ref, sorted_ref, here_ref, there_ref, wide, columns, some, lowest, planes,
):
    rows = partial_ref.shape[0]
    half = rows // 32
    sort_kernel(halo_ref.shape[0], halo_ref, sorted_ref, wide)
    for e in range(3):
        for a in range(3):
            put_tap(columns, 0, (a * 3 + e) * 256, sorted_ref.at[a, e])
        put_tap(some, 0, e * 256, sorted_ref.at[2, e])
    below = jnp.dot(columns[...], padded_ref[...], preferred_element_type=F32)
    here = partial_ref[...] + jnp.dot(
        some[...], padded_ref[: 3 * 256, :], preferred_element_type=F32
    )
    slope_ref[:rows, :] = activate_slope(below)
    slope_ref[rows:, :] = activate_slope(here)
    lowest[0] = (activate(below) * alive[0]).reshape(lowest.shape[1:])
    lowest[1] = activate(here).reshape(lowest.shape[1:])
    planes[0] = lowest[0].reshape(rows, 128).astype(BF16)
    planes[1] = lowest[1].reshape(rows, 128).astype(BF16)
    planes[2] = planes[1]
    planes[3] = top_ref[...]
    here_ref[...] = planes[pl.ds(2 * side[0], 2)]
    there_ref[...] = planes[pl.ds(2 - 2 * side[0], 2)]
    for a in range(2):

        def read(column, row):
            return lowest[a, :, column, row].reshape(half * 8, 128)

        take_windows(read, windows_ref, 0, a * 9 * 128, half)


def forward_lower(halo, top, partial, padded, alive, side):
    rows = partial.shape[0]
    return call(
        forward_lower_kernel,
        (
            near((2 * rows, 128), F32),
            near((rows // 4, 2 * 9 * 128), BF16),
            near((halo.shape[0], 3, rows, 128), BF16),
            sds((2, rows, 128), BF16),
            sds((2, rows, 128), BF16),
        ),
        [
            pltpu.VMEM((rows // 16, halo.shape[1], 128), F32),
            pltpu.VMEM((rows, 9 * 256), BF16),
            pltpu.VMEM((rows, 3 * 256), BF16),
            pltpu.VMEM((2, rows // 32, 2, 2, 8, 128), F32),
            pltpu.VMEM((4, rows, 128), BF16),
        ],
        halo, top, partial, padded,
        smem=(alive, side),
        micros=1.5,
    )


def put_pieces(flat, outs, slots, order):
    for index, out in enumerate(outs):
        count, size, _ = out.shape
        for place in range(count):
            row = pl.multiple_of(order[place] * size, 8)
            out[place] = flat[slots[index], pl.ds(row, size), :].astype(BF16)


def forward_second_kernel(
    offsets, upper_ref, lower_ref, cot_ref, w0, w1, w2, w3, act_ref, delta_ref, whole, windows
):
    put_rows(whole, (w0, w1, w2, w3), offsets)
    low, width = lower_ref.shape
    windows[:low, :width] = lower_ref[...]
    windows[:low, width:] = upper_ref[:low, width:]
    windows[low:, :] = upper_ref[low:, :]
    linear = jnp.dot(windows[...], whole[...], preferred_element_type=F32)
    outs, _, width = cot_ref.shape
    features = linear.shape[1]
    count = width // features
    acted = activate(linear)
    slope = activate_slope(linear)
    deltas = []
    for out in range(outs):
        base = out * count * 8
        act_ref[out] = jnp.concatenate(
            [acted[base + q * 8 : base + (q + 1) * 8] for q in range(count)], axis=1
        ).astype(BF16)
        cot = cot_ref[out].astype(F32)
        deltas.append(
            jnp.concatenate(
                [cot[:, q * features : (q + 1) * features] for q in range(count)], axis=0
            )
        )
    delta_ref[...] = (jnp.concatenate(deltas, axis=0) * slope).astype(BF16)


def forward_second(upper, lower, cot, shards, offsets):
    rows, features = shards[0].shape
    return call(
        forward_second_kernel,
        (sds(cot.shape, BF16), sds((upper.shape[0], features), BF16)),
        [pltpu.VMEM((4 * rows, features), BF16), pltpu.VMEM(upper.shape, BF16)],
        upper, lower, cot, *shards,
        smem=(offsets,),
        micros=1.5,
    )


def second_rows_kernel(
    data, table, order, e0, e1, e2, e3, m0, m1, m2, m3, d0, d1, d2, d3,
    out_ref, wide, windows, deltas, product, flat,
):
    edges, rows, _ = e0.shape
    cells = edges + m0.shape[0]
    half = rows // 32
    outs = cells // 2
    size = half * 8
    taps = windows.shape[1] // 128
    samples = ((e0, m0, d0), (e1, m1, d1), (e2, m2, d2), (e3, m3, d3))
    for sample, (edge, middle, delta) in enumerate(samples):
        at = sample * cells
        wide[at : at + edges] = edge[...].astype(F32).reshape(edges, half, 2, 2, 8, 128)
        wide[at + edges : at + cells] = (
            middle[...].astype(F32).reshape(cells - edges, half, 2, 2, 8, 128)
        )
        deltas[sample * outs * size : (sample + 1) * outs * size, :] = delta[...]
    for tap in range(taps):
        e, f = table[data[0], tap], table[data[0], taps + tap]
        row = jnp.where(e == 1, 0, 1)
        column = jnp.where(f == 1, 0, 1)
        for sample in range(4):
            for out in range(outs):
                plane = sample * cells + table[data[0], (2 + out) * taps + tap]
                block = wide[plane, :, column, row].reshape(size, 128)
                block = jnp.where(e == 0, from_before(block), block)
                later = jnp.concatenate([jnp.zeros((8, 128), F32), block[: size - 8]], axis=0)
                block = jnp.where(f == 0, later, block)
                at = (sample * outs + out) * size
                windows[at : at + size, tap * 128 : (tap + 1) * 128] = block.astype(BF16)
    product[...] = lax.dot_general(
        windows[...], deltas[...], (((0,), (0,)), ((), ())), preferred_element_type=F32
    )
    lanes = product.shape[1] // 128
    count, piece, _ = out_ref.shape
    shard = 27 * 128 // 4
    for lane in range(lanes):
        flat[lane * shard : (lane + 1) * shard, :] = product[
            pl.ds(pl.multiple_of(table[data[0], (2 + outs) * taps], 16), shard), lane * 128 : (lane + 1) * 128
        ]
    rest = flat.shape[0] - lanes * shard
    if rest:
        flat[lanes * shard :, :] = jnp.zeros((rest, 128), F32)
    for place in range(count):
        row = pl.multiple_of(order[place] * piece, 8)
        out_ref[place] = flat[pl.ds(row, piece), :].astype(BF16)


def second_rows(edges, middles, deltas, data, order, places, size):
    _, rows, _ = edges[0].shape
    cells = edges[0].shape[0] + middles[0].shape[0]
    cellrows, features = deltas[0].shape
    taps = 8
    table = []
    for shard in range(4):
        start = shard * 27 // 4
        at = [min(start + tap, 26) for tap in range(taps)]
        held = (-1, 0, *range(1, cells - 1)) if shard < 2 else (0, cells - 1, *range(1, cells - 1))
        table.append(
            [tap // 3 % 3 for tap in at]
            + [tap % 3 for tap in at]
            + [held.index(2 * out - 1 + tap // 9) for out in range(cells // 2) for tap in at]
            + [shard * (27 * 128 // 4) - start * 128]
        )
    return call(
        second_rows_kernel,
        sds((places, size, 128), BF16),
        [
            pltpu.VMEM((4 * cells, rows // 32, 2, 2, 8, 128), F32),
            pltpu.VMEM((4 * cellrows, taps * 128), BF16),
            pltpu.VMEM((4 * cellrows, features), BF16),
            pltpu.VMEM((taps * 128, features), F32),
            pltpu.VMEM((places * size, 128), F32),
        ],
        *edges, *middles, *deltas,
        smem=(data.reshape(1), jnp.array(table, jnp.int32), order),
        micros=2.0,
    )


def back_second_kernel(
    offsets, slots, order, delta_ref, w0, w1, w2, w3,
    slope_low_ref, slope_ref, sorted_ref, halo_ref,
    low_ref, last_ref, down_ref, g0, g1, g2, g3,
    whole, product, columns, deltas, flat,
):
    rows = sorted_ref.shape[2]
    cells = sorted_ref.shape[0] // 2
    half = rows // 32
    size = half * 8
    put_rows(whole, (w0, w1, w2, w3), offsets)
    product[...] = lax.dot_general(
        delta_ref[...], whole[...], (((1,), (1,)), ((), ())), preferred_element_type=F32
    )
    gather_taps(columns, sorted_ref, halo_ref, -1, cells + 1)

    def term(out, a, e, f):
        left = ((a * 3 + e) * 3 + f) * 128
        block = product[out * size : (out + 1) * size, left : left + 128]
        if f == 0:
            block = jnp.concatenate([block[8:], jnp.zeros((8, 128), F32)], axis=0)
        if e == 0:
            block = from_after(block)
        return block.reshape(half, 8, 128)

    for plane in range(-1, cells):
        taps = [
            (out, a) for out in range(cells // 2) for a in range(3) if 2 * out - 1 + a == plane
        ]
        sums = [
            sum(
                term(out, a, e, f)
                for out, a in taps
                for e in ((0, 2) if row else (1,))
                for f in ((0, 2) if column else (1,))
            ).reshape(half, 1, 8, 128)
            for column in range(2)
            for row in range(2)
        ]
        spread = jnp.concatenate(sums, axis=1).reshape(rows, 128)
        if plane < 1:
            slope = slope_low_ref[(plane + 1) * rows : (plane + 2) * rows, :]
        else:
            slope = slope_ref[(plane - 1) * rows : plane * rows, :]
        delta = (spread * slope).astype(BF16)
        deltas[(plane + 1) * rows : (plane + 2) * rows, :] = delta
        if plane < 0:
            down_ref[:rows, :] = spread.astype(BF16)
        if plane == 0:
            down_ref[rows:, :] = delta
        if plane == cells - 1:
            last_ref[...] = spread
        elif plane >= 0:
            low_ref[plane * rows : (plane + 1) * rows, :] = delta
    flipped = jnp.transpose(deltas[...].astype(F32)).astype(BF16)
    tally = jnp.dot(flipped, columns[...], preferred_element_type=F32)
    shard_rows = 9 * 192 // 4
    for tap in range(9):
        turned = jnp.transpose(tally[:, tap * 256 : (tap + 1) * 256])[64:]
        at = tap * 192
        while at < (tap + 1) * 192:
            shard = at // shard_rows
            to = min((tap + 1) * 192, (shard + 1) * shard_rows)
            flat[shard, at - shard * shard_rows : to - shard * shard_rows, :] = turned[
                at - tap * 192 : to - tap * 192
            ]
            at = to
    rest = flat.shape[1] - shard_rows
    if rest:
        flat[:, shard_rows:, :] = jnp.zeros((4, rest, 128), F32)
    put_pieces(flat, (g0, g1, g2, g3), slots, order)


def back_second(delta, shards, slopes, sorted_volume, halo, offsets, slots, order, places, size):
    rows, features = shards[0].shape
    planes, _, width, _ = sorted_volume.shape
    cells = planes // 2
    piece = sds((places, size, 128), BF16)
    return call(
        back_second_kernel,
        (
            near(((cells - 1) * width, 128), BF16),
            near((width, 128), F32),
            sds((2 * width, 128), BF16),
            piece, piece, piece, piece,
        ),
        [
            pltpu.VMEM((4 * rows, features), BF16),
            pltpu.VMEM((delta.shape[0], 4 * rows), F32),
            pltpu.VMEM(((cells + 1) * width, 9 * 256), BF16),
            pltpu.VMEM(((cells + 1) * width, 128), BF16),
            pltpu.VMEM((4, places * size, 128), F32),
        ],
        delta, *shards, *slopes, sorted_volume, halo,
        smem=(offsets, slots, order),
        micros=3.5,
    )


def back_input_kernel(
    offsets, low_ref, last_ref, slope_ref, upper_ref, w0, w1, w2, w3,
    out_ref, whole, turned, pairs, product, wide, last,
):
    put_rows(whole, (w0, w1, w2, w3), offsets)
    for tap in range(9):
        top = tap * 128
        turned[top : top + 128, 0:128] = whole[tap * 192 + 64 : (tap + 1) * 192, :]
        turned[top : top + 64, 128:256] = jnp.zeros((64, 128), BF16)
        turned[top + 64 : top + 128, 128:256] = whole[tap * 192 : tap * 192 + 64, :]
    planes = out_ref.shape[0]
    cells = planes // 2
    rows = last_ref.shape[0]
    groups = rows // 16
    last[...] = (
        (last_ref[...] + upper_ref[:rows, :].astype(F32)) * slope_ref[(cells - 2) * rows :, :]
    ).astype(BF16)
    for cell in range(cells + 1):
        at = cell * rows
        if cell < cells - 1:
            source = low_ref.at[at : at + rows]
        else:
            source = last if cell == cells - 1 else upper_ref.at[rows : 2 * rows]
        pairs[at : at + rows, 0:128] = source[...]
        pairs[at : at + rows - 16, 128:256] = source[16:rows, :]
        pairs[at + rows - 16 : at + rows, 128:256] = jnp.zeros((16, 128), BF16)
    product[...] = lax.dot_general(
        pairs[...], turned[...], (((1,), (1,)), ((), ())), preferred_element_type=F32
    ).reshape(product.shape)

    def part(cell, a, e, parity):
        left = (a * 3 + e) * 128
        return product[cell * groups : (cell + 1) * groups, parity, :, left : left + 128]

    def after(block):
        flat = block.reshape(groups * 8, 128)
        return from_after(flat).reshape(groups, 8, 128)

    for plane in range(planes):
        taps = [(o, a) for o in range(cells + 1) for a in range(3) if 2 * o - 1 + a == plane]
        wide[:, pl.ds(0, 8, stride=4), :] = sum(part(o, a, 1, 0) for o, a in taps)
        wide[:, pl.ds(1, 8, stride=4), :] = sum(
            part(o, a, 2, 0) + part(o, a, 0, 1) for o, a in taps
        )
        wide[:, pl.ds(2, 8, stride=4), :] = sum(part(o, a, 1, 1) for o, a in taps)
        wide[:, pl.ds(3, 8, stride=4), :] = sum(part(o, a, 2, 1) for o, a in taps) + after(
            sum(part(o, a, 0, 0) for o, a in taps)
        )
        for group in range(groups):
            lanes = slice(group * 128, (group + 1) * 128)
            out_ref[plane, :, lanes] = wide[group].astype(BF16)


def back_input(low, last, slope, upper, shards, offsets, shape):
    planes, side, width = shape
    shard = shards[0].shape[0]
    rows = low.shape[0] + upper.shape[0]
    return call(
        back_input_kernel,
        sds(shape, BF16),
        [
            pltpu.VMEM((4 * shard, 128), BF16),
            pltpu.VMEM((9 * 128, 256), BF16),
            pltpu.VMEM((rows, 256), BF16),
            pltpu.VMEM((rows // 16, 2, 8, 9 * 128), F32),
            pltpu.VMEM((width // 128, side, 128), F32),
            pltpu.VMEM(last.shape, BF16),
        ],
        low, last, slope, upper, *shards,
        smem=(offsets,),
        micros=3.0,
    )


def unpack_kernel(scale_first, scale_second, order, *refs):
    *chunks, other, first_ref, second_ref, flat_first, flat_second = refs
    high = len(chunks)
    small = flat_first.shape[0] // (2 * high)
    big = flat_second.shape[0] // (2 * high)
    for low in range(2):
        for index in range(high):
            chunk = (other[index] if low else chunks[index][...]).astype(F32)
            place = order[low * high + index]
            flat_second[pl.ds(pl.multiple_of(place * big, 8), big), :] = chunk[:big, :]
            flat_first[pl.ds(pl.multiple_of(place * small, 8), small), :] = chunk[big:, :]
    rows, features = second_ref.shape
    for lane in range(features // 128):
        second_ref[:, lane * 128 : (lane + 1) * 128] = (
            flat_second[lane * rows : (lane + 1) * rows, :] * scale_second
        )
    first_ref[...] = flat_first[: first_ref.shape[0], :] * scale_first


def wide_sum(*pieces):
    return sum(piece.astype(F32) for piece in pieces)


def added(*pieces):
    return wide_sum(*pieces).astype(BF16)


def swap(value, axis, bits):
    size = lax.axis_size(axis)
    return lax.ppermute(value, axis, [(i, i ^ bits) for i in range(size)])


def shifted(value, axis, by):
    size = lax.axis_size(axis)
    pairs = [(i, i + by) for i in range(size) if 0 <= i + by < size]
    return lax.ppermute(value, axis, pairs)


def local(volume, weight_first, weight_second, cotangent):
    samples, planes, side, width = volume.shape
    data = lax.axis_index("dp")
    place = lax.axis_index("space")
    spaces = lax.axis_size("space")
    high = spaces // 2
    small, big = weight_first.shape[0], weight_second.shape[0]
    slots = jnp.arange(4, dtype=jnp.int32) ^ data
    offsets_first = slots * small
    offsets_second = slots * big
    alive = (place > 0).astype(F32).reshape(1)
    x_side = lax.shift_right_logical(data, 1)
    steps = jnp.arange(spaces, dtype=jnp.int32)
    order = place ^ (2 * (steps % high) + steps // high)
    lanes = weight_second.shape[1] // 128
    size_first = -(-small // (8 * spaces)) * 8
    size_second = -(-lanes * big // (8 * spaces)) * 8

    inputs = volume.reshape(planes, side, width)
    uppermost = last_planes(inputs, 3)
    first_x = swap(weight_first, "dp", 2)
    first_core = swap(weight_first, "dp", 1)
    second_x = swap(weight_second, "dp", 2)
    second_core = swap(weight_second, "dp", 1)
    halo = shifted(uppermost, "space", 1)
    first_far = swap(first_x, "dp", 1)
    shards_first = (weight_first, first_core, first_x, first_far)

    sorted_volume = sorted_planes(inputs)
    slope, windows, middle, top, partial, padded = forward_upper(
        sorted_volume, shards_first, offsets_first
    )
    middle_x, middle_core = swap(middle, "dp", 2), swap(middle, "dp", 1)
    second_x, partial = lax.optimization_barrier((second_x, partial))
    second_far = swap(second_x, "dp", 1)
    shards_second = (weight_second, second_core, second_x, second_far)
    slope_low, windows_low, sorted_halo, edge, edge_there = forward_lower(
        halo, top, partial, padded, alive, x_side.reshape(1)
    )
    cot = cotangent.reshape(cotangent.shape[1:])
    activations, delta_second = forward_second(
        windows, windows_low, cot, shards_second, offsets_second
    )
    delta_second, middle_x = lax.optimization_barrier((delta_second, middle_x))
    edge_x, edge_core = swap(edge_there, "dp", 2), swap(edge, "dp", 1)
    delta_x, delta_core = swap(delta_second, "dp", 2), swap(delta_second, "dp", 1)
    low, last, down, *first = back_second(
        delta_second, shards_second, (slope_low, slope), sorted_volume, sorted_halo,
        offsets_second, slots, order, spaces, size_first,
    )
    middle_far = swap(middle_x, "dp", 1)
    first, down, delta_x, edge_x, delta_core, edge_core, middle_far = lax.optimization_barrier(
        (first, down, delta_x, edge_x, delta_core, edge_core, middle_far)
    )
    second = second_rows(
        (edge, edge_core, edge_x, swap(edge_x, "dp", 1)),
        (middle, middle_core, middle_x, middle_far),
        (delta_second, delta_core, delta_x, swap(delta_x, "dp", 1)),
        data, order, spaces, size_second,
    )
    upper = shifted(down, "space", -1)

    def pieces(value):
        return value.reshape(2, high, -1, 128)

    far, beside = pieces(swap(first[3], "dp", 1)), pieces(swap(first[1], "dp", 1))
    own, there = pieces(first[0]), pieces(first[2])
    both = [
        (d * spaces + s, (d ^ 2) * spaces + (s ^ 1)) for d in range(4) for s in range(spaces)
    ]
    second = pieces(second)
    sent_y = jnp.concatenate([second[1], added(own[1], beside[1])], axis=1)
    got_y = swap(sent_y[1:], "space", 1)
    got_x = swap(added(there[0], far[0]), "dp", 2)
    got_y_own = swap(sent_y[:1], "space", 1)
    got_xy = lax.ppermute(added(there[1], far[1]), ("dp", "space"), both)

    def held(places, got):
        return jnp.concatenate(
            [
                wide_sum(second[0][places], got[:, :size_second]),
                wide_sum(
                    own[0][places], beside[0][places], got_x[places], got_xy[places],
                    got[:, size_second:],
                ),
            ],
            axis=1,
        )

    sent = held(slice(1, high), got_y).astype(BF16)
    *received, got_y_own = lax.optimization_barrier(
        (*(swap(sent[k - 1], "space", 2 * k) for k in range(1, high)), got_y_own)
    )
    mine = added(held(slice(0, 1), got_y_own)[0], *received)
    chunks = [mine] + [swap(mine, "space", 2 * k) for k in range(1, high)]
    chunks.append(swap(jnp.stack(chunks), "space", 1))

    gradient = back_input(low, last, slope, upper, shards_first, offsets_first, inputs.shape)

    cells_first = samples * lax.axis_size("dp") * (planes // 2) * spaces * (side // 2) ** 2
    cells_second = cells_first // 8
    first_gradient, second_gradient = call(
        functools.partial(unpack_kernel, float(cells_first) ** -0.5, float(cells_second) ** -0.5),
        (sds(weight_first.shape, F32), sds(weight_second.shape, F32)),
        [
            pltpu.VMEM((spaces * size_first, 128), F32),
            pltpu.VMEM((spaces * size_second, 128), F32),
        ],
        *chunks,
        smem=(order,),
    )
    return (
        activations.reshape(cotangent.shape),
        gradient.reshape(volume.shape),
        first_gradient,
        second_gradient,
    )


def solution(mesh):
    return jax.shard_map(
        local,
        mesh=mesh,
        in_specs=(
            P("dp", "space", None, None),
            P("dp", None),
            P("dp", None),
            P("dp", "space", None, None),
        ),
        out_specs=(
            P("dp", "space", None, None),
            P("dp", "space", None, None),
            P("dp", None),
            P("dp", None),
        ),
        check_vma=False,
    )
```

```python
import functools

import jax
import jax.numpy as jnp
from jax import lax
from jax.experimental import pallas as pl
from jax.experimental.pallas import tpu as pltpu
from jax.sharding import PartitionSpec as P

LEAK_SLOPE = 0.2
F32 = jnp.float32
BF16 = jnp.bfloat16
VMEM_LIMIT = 24 * 1024 * 1024


def activate(values):
    small = jnp.exp(-jnp.abs(values))
    return LEAK_SLOPE * values + (1.0 - LEAK_SLOPE) * (
        jnp.maximum(values, 0.0) + jnp.log(1.0 + small)
    )


def activate_slope(values):
    small = jnp.exp(-jnp.abs(values))
    inverse = 1.0 / (1.0 + small)
    return LEAK_SLOPE + (1.0 - LEAK_SLOPE) * jnp.where(
        values >= 0.0, inverse, small * inverse
    )


def block_row(rows, width):
    return lax.broadcasted_iota(jnp.int32, (rows, width), 0) % 8


def from_before(block):
    moved = pltpu.roll(block, 1, 0)
    return jnp.where(block_row(*block.shape) == 0, 0.0, moved)


def from_after(block):
    moved = pltpu.roll(block, block.shape[0] - 1, 0)
    return jnp.where(block_row(*block.shape) == 7, 0.0, moved)


def call(kernel, out_shape, scratch, *operands, smem=(), micros=1.0):
    nbytes = sum(a.size * a.dtype.itemsize for a in operands)
    specs = [pl.BlockSpec(memory_space=pltpu.SMEM)] * len(smem)
    specs += [pl.BlockSpec(memory_space=pltpu.VMEM)] * len(operands)
    return pl.pallas_call(
        kernel,
        out_shape=out_shape,
        in_specs=specs,
        out_specs=jax.tree.map(lambda _: pl.BlockSpec(memory_space=pltpu.VMEM), out_shape),
        scratch_shapes=scratch,
        compiler_params=pltpu.CompilerParams(vmem_limit_bytes=VMEM_LIMIT),
        cost_estimate=pl.CostEstimate(
            flops=int(micros * 1.15e9), bytes_accessed=nbytes, transcendentals=0
        ),
    )(*smem, *operands)


def sds(shape, dtype):
    return jax.ShapeDtypeStruct(shape, dtype)


def near(shape, dtype):
    return pltpu.VMEM(shape, dtype)


def sort_kernel(planes, in_ref, out_ref, wide):
    pairs = wide.shape[0]
    for plane in range(planes):
        for pair in range(pairs):
            wide[pair] = in_ref[plane, :, pair * 128 : (pair + 1) * 128].astype(F32)
        classes = [
            wide[:, pl.ds(r, 8, stride=4), :].reshape(pairs * 8, 128) for r in range(4)
        ]
        before = from_before(classes[3])
        for tap, (even, odd) in enumerate(
            ((before, classes[1]), (classes[0], classes[2]), (classes[1], classes[3]))
        ):
            both = jnp.concatenate(
                [even.reshape(pairs, 1, 8, 128), odd.reshape(pairs, 1, 8, 128)], axis=1
            )
            out_ref[plane, tap] = both.reshape(pairs * 16, 128).astype(BF16)


def last_planes_kernel(volume_ref, out_ref, sem):
    count = out_ref.shape[0]
    copy = pltpu.make_async_copy(
        volume_ref.at[pl.ds(volume_ref.shape[0] - count, count)], out_ref, sem
    )
    copy.start()
    copy.wait()


def last_planes(volume, count):
    shape = (count, *volume.shape[1:])
    return pl.pallas_call(
        last_planes_kernel,
        out_shape=pltpu.VMEM(shape, BF16),
        in_specs=[pl.BlockSpec(memory_space=pltpu.HBM)],
        out_specs=pl.BlockSpec(memory_space=pltpu.VMEM),
        scratch_shapes=[pltpu.SemaphoreType.DMA],
        cost_estimate=pl.CostEstimate(
            flops=0, bytes_accessed=4 * shape[0] * shape[1] * shape[2], transcendentals=0
        ),
    )(volume)


def sorted_planes(volume):
    planes, rows, width = volume.shape
    pairs = width // 128
    return call(
        functools.partial(sort_kernel, planes),
        near((planes, 3, pairs * 16, 128), BF16),
        [pltpu.VMEM((pairs, rows, 128), F32)],
        volume,
    )


def put_rows(dst, pieces, offsets):
    rows = pieces[0].shape[0]
    for index, piece in enumerate(pieces):
        dst[pl.ds(pl.multiple_of(offsets[index], 16), rows), :] = piece[...]


def put_tap(columns, at, left, source):
    rows = source.shape[0]
    columns[at : at + 16, left : left + 128] = jnp.zeros((16, 128), BF16)
    columns[at + 16 : at + rows, left : left + 128] = source[0 : rows - 16, :]
    columns[at : at + rows, left + 128 : left + 256] = source[...]


def gather_taps(columns, sorted_ref, halo_ref, first, count):
    rows = sorted_ref.shape[2]
    for cell in range(count):
        for a in range(3):
            plane = 2 * (first + cell) - 1 + a
            for e in range(3):
                source = (
                    halo_ref.at[halo_ref.shape[0] + plane, e] if plane < 0 else sorted_ref.at[plane, e]
                )
                put_tap(columns, cell * rows, (a * 3 + e) * 256, source)


def pad_first(whole, padded):
    for tap in range(9):
        padded[tap * 256 : tap * 256 + 64, :] = jnp.zeros((64, 128), BF16)
        padded[tap * 256 + 64 : (tap + 1) * 256, :] = whole[tap * 192 : (tap + 1) * 192, :]


def take_windows(read, dst, row, left, half):
    for e in range(3):
        for f in range(3):
            block = read(0 if f == 1 else 1, 0 if e == 1 else 1)
            if e == 0:
                block = from_before(block)
            if f == 0:
                block = jnp.concatenate(
                    [jnp.zeros((8, 128), F32), block[: half * 8 - 8]], axis=0
                )
            at = left + (e * 3 + f) * 128
            dst[row : row + half * 8, at : at + 128] = block.astype(BF16)


def forward_upper_kernel(
    offsets, sorted_ref, w0, w1, w2, w3,
    slope_ref, windows_ref, middle_ref, top_ref, partial_ref, padded_ref,
    columns, some, whole, upper,
):
    cells = sorted_ref.shape[0] // 2
    put_rows(whole, (w0, w1, w2, w3), offsets)
    pad_first(whole, padded_ref)
    gather_taps(columns, sorted_ref, None, 1, cells - 1)
    linear = jnp.dot(columns[...], padded_ref[...], preferred_element_type=F32)
    hidden = activate(linear)
    upper[...] = hidden.reshape(upper.shape)
    count = middle_ref.shape[0] * middle_ref.shape[1]
    middle_ref[...] = hidden[:count].reshape(middle_ref.shape).astype(BF16)
    top_ref[...] = hidden[count:].astype(BF16)
    slope_ref[...] = activate_slope(linear)
    half = upper.shape[1]
    for out in range(cells // 2):
        for a in range(3):
            plane = 2 * out - 1 + a
            if plane > 0:

                def read(column, row):
                    return upper[plane - 1, :, column, row].reshape(half * 8, 128)

                take_windows(read, windows_ref, out * half * 8, a * 9 * 128, half)
    for a in range(1, 3):
        for e in range(3):
            put_tap(some, 0, ((a - 1) * 3 + e) * 256, sorted_ref.at[a - 1, e])
    partial_ref[...] = jnp.dot(some[...], padded_ref[3 * 256 :, :], preferred_element_type=F32)


def forward_upper(sorted_volume, shards, offsets):
    planes, _, rows, _ = sorted_volume.shape
    cells = planes // 2
    shard = shards[0].shape[0]
    some = (cells - 1) * rows
    return call(
        forward_upper_kernel,
        (
            near((some, 128), F32),
            near((cells * rows // 8, 27 * 128), BF16),
            sds((cells - 2, rows, 128), BF16),
            near((rows, 128), BF16),
            near((rows, 128), F32),
            near((9 * 256, 128), BF16),
        ),
        [
            pltpu.VMEM((some, 9 * 256), BF16),
            pltpu.VMEM((rows, 6 * 256), BF16),
            pltpu.VMEM((4 * shard, 128), BF16),
            pltpu.VMEM((cells - 1, rows // 32, 2, 2, 8, 128), F32),
        ],
        sorted_volume, *shards,
        smem=(offsets,),
        micros=2.5,
    )


def forward_lower_kernel(
    alive, side, halo_ref, top_ref, partial_ref, padded_ref,
    slope_ref, windows_ref, sorted_ref, here_ref, there_ref, wide, columns, some, lowest, planes,
):
    rows = partial_ref.shape[0]
    half = rows // 32
    sort_kernel(halo_ref.shape[0], halo_ref, sorted_ref, wide)
    for e in range(3):
        for a in range(3):
            put_tap(columns, 0, (a * 3 + e) * 256, sorted_ref.at[a, e])
        put_tap(some, 0, e * 256, sorted_ref.at[2, e])
    below = jnp.dot(columns[...], padded_ref[...], preferred_element_type=F32)
    here = partial_ref[...] + jnp.dot(
        some[...], padded_ref[: 3 * 256, :], preferred_element_type=F32
    )
    slope_ref[:rows, :] = activate_slope(below)
    slope_ref[rows:, :] = activate_slope(here)
    lowest[0] = (activate(below) * alive[0]).reshape(lowest.shape[1:])
    lowest[1] = activate(here).reshape(lowest.shape[1:])
    planes[0] = lowest[0].reshape(rows, 128).astype(BF16)
    planes[1] = lowest[1].reshape(rows, 128).astype(BF16)
    planes[2] = planes[1]
    planes[3] = top_ref[...]
    here_ref[...] = planes[pl.ds(2 * side[0], 2)]
    there_ref[...] = planes[pl.ds(2 - 2 * side[0], 2)]
    for a in range(2):

        def read(column, row):
            return lowest[a, :, column, row].reshape(half * 8, 128)

        take_windows(read, windows_ref, 0, a * 9 * 128, half)


def forward_lower(halo, top, partial, padded, alive, side):
    rows = partial.shape[0]
    return call(
        forward_lower_kernel,
        (
            near((2 * rows, 128), F32),
            near((rows // 4, 2 * 9 * 128), BF16),
            near((halo.shape[0], 3, rows, 128), BF16),
            sds((2, rows, 128), BF16),
            sds((2, rows, 128), BF16),
        ),
        [
            pltpu.VMEM((rows // 16, halo.shape[1], 128), F32),
            pltpu.VMEM((rows, 9 * 256), BF16),
            pltpu.VMEM((rows, 3 * 256), BF16),
            pltpu.VMEM((2, rows // 32, 2, 2, 8, 128), F32),
            pltpu.VMEM((4, rows, 128), BF16),
        ],
        halo, top, partial, padded,
        smem=(alive, side),
        micros=1.5,
    )


def put_pieces(flat, outs, slots, order):
    for index, out in enumerate(outs):
        count, size, _ = out.shape
        for place in range(count):
            row = pl.multiple_of(order[place] * size, 8)
            out[place] = flat[slots[index], pl.ds(row, size), :].astype(BF16)


def forward_second_kernel(
    offsets, upper_ref, lower_ref, cot_ref, w0, w1, w2, w3, act_ref, delta_ref, whole, windows
):
    put_rows(whole, (w0, w1, w2, w3), offsets)
    low, width = lower_ref.shape
    windows[:low, :width] = lower_ref[...]
    windows[:low, width:] = upper_ref[:low, width:]
    windows[low:, :] = upper_ref[low:, :]
    linear = jnp.dot(windows[...], whole[...], preferred_element_type=F32)
    outs, _, width = cot_ref.shape
    features = linear.shape[1]
    count = width // features
    acted = activate(linear)
    slope = activate_slope(linear)
    deltas = []
    for out in range(outs):
        base = out * count * 8
        act_ref[out] = jnp.concatenate(
            [acted[base + q * 8 : base + (q + 1) * 8] for q in range(count)], axis=1
        ).astype(BF16)
        cot = cot_ref[out].astype(F32)
        deltas.append(
            jnp.concatenate(
                [cot[:, q * features : (q + 1) * features] for q in range(count)], axis=0
            )
        )
    delta_ref[...] = (jnp.concatenate(deltas, axis=0) * slope).astype(BF16)


def forward_second(upper, lower, cot, shards, offsets):
    rows, features = shards[0].shape
    return call(
        forward_second_kernel,
        (sds(cot.shape, BF16), sds((upper.shape[0], features), BF16)),
        [pltpu.VMEM((4 * rows, features), BF16), pltpu.VMEM(upper.shape, BF16)],
        upper, lower, cot, *shards,
        smem=(offsets,),
        micros=1.5,
    )


def second_rows_kernel(
    data, table, order, e0, e1, e2, e3, m0, m1, m2, m3, d0, d1, d2, d3,
    out_ref, wide, windows, deltas, product, flat,
):
    edges, rows, _ = e0.shape
    cells = edges + m0.shape[0]
    half = rows // 32
    outs = cells // 2
    size = half * 8
    taps = windows.shape[1] // 128
    samples = ((e0, m0, d0), (e1, m1, d1), (e2, m2, d2), (e3, m3, d3))
    for sample, (edge, middle, delta) in enumerate(samples):
        at = sample * cells
        wide[at : at + edges] = edge[...].astype(F32).reshape(edges, half, 2, 2, 8, 128)
        wide[at + edges : at + cells] = (
            middle[...].astype(F32).reshape(cells - edges, half, 2, 2, 8, 128)
        )
        deltas[sample * outs * size : (sample + 1) * outs * size, :] = delta[...]
    for tap in range(taps):
        e, f = table[data[0], tap], table[data[0], taps + tap]
        row = jnp.where(e == 1, 0, 1)
        column = jnp.where(f == 1, 0, 1)
        for sample in range(4):
            for out in range(outs):
                plane = sample * cells + table[data[0], (2 + out) * taps + tap]
                block = wide[plane, :, column, row].reshape(size, 128)
                block = jnp.where(e == 0, from_before(block), block)
                later = jnp.concatenate([jnp.zeros((8, 128), F32), block[: size - 8]], axis=0)
                block = jnp.where(f == 0, later, block)
                at = (sample * outs + out) * size
                windows[at : at + size, tap * 128 : (tap + 1) * 128] = block.astype(BF16)
    product[...] = lax.dot_general(
        windows[...], deltas[...], (((0,), (0,)), ((), ())), preferred_element_type=F32
    )
    lanes = product.shape[1] // 128
    count, piece, _ = out_ref.shape
    shard = 27 * 128 // 4
    for lane in range(lanes):
        flat[lane * shard : (lane + 1) * shard, :] = product[
            pl.ds(pl.multiple_of(table[data[0], (2 + outs) * taps], 16), shard), lane * 128 : (lane + 1) * 128
        ]
    rest = flat.shape[0] - lanes * shard
    if rest:
        flat[lanes * shard :, :] = jnp.zeros((rest, 128), F32)
    for place in range(count):
        row = pl.multiple_of(order[place] * piece, 8)
        out_ref[place] = flat[pl.ds(row, piece), :].astype(BF16)


def second_rows(edges, middles, deltas, data, order, places, size):
    _, rows, _ = edges[0].shape
    cells = edges[0].shape[0] + middles[0].shape[0]
    cellrows, features = deltas[0].shape
    taps = 8
    table = []
    for shard in range(4):
        start = shard * 27 // 4
        at = [min(start + tap, 26) for tap in range(taps)]
        held = (-1, 0, *range(1, cells - 1)) if shard < 2 else (0, cells - 1, *range(1, cells - 1))
        table.append(
            [tap // 3 % 3 for tap in at]
            + [tap % 3 for tap in at]
            + [held.index(2 * out - 1 + tap // 9) for out in range(cells // 2) for tap in at]
            + [shard * (27 * 128 // 4) - start * 128]
        )
    return call(
        second_rows_kernel,
        sds((places, size, 128), BF16),
        [
            pltpu.VMEM((4 * cells, rows // 32, 2, 2, 8, 128), F32),
            pltpu.VMEM((4 * cellrows, taps * 128), BF16),
            pltpu.VMEM((4 * cellrows, features), BF16),
            pltpu.VMEM((taps * 128, features), F32),
            pltpu.VMEM((places * size, 128), F32),
        ],
        *edges, *middles, *deltas,
        smem=(data.reshape(1), jnp.array(table, jnp.int32), order),
        micros=2.0,
    )


def back_second_kernel(
    offsets, slots, order, delta_ref, w0, w1, w2, w3,
    slope_low_ref, slope_ref, sorted_ref, halo_ref,
    low_ref, last_ref, down_ref, g0, g1, g2, g3,
    whole, product, columns, deltas, flat,
):
    rows = sorted_ref.shape[2]
    cells = sorted_ref.shape[0] // 2
    half = rows // 32
    size = half * 8
    put_rows(whole, (w0, w1, w2, w3), offsets)
    product[...] = lax.dot_general(
        delta_ref[...], whole[...], (((1,), (1,)), ((), ())), preferred_element_type=F32
    )
    gather_taps(columns, sorted_ref, halo_ref, -1, cells + 1)

    def term(out, a, e, f):
        left = ((a * 3 + e) * 3 + f) * 128
        block = product[out * size : (out + 1) * size, left : left + 128]
        if f == 0:
            block = jnp.concatenate([block[8:], jnp.zeros((8, 128), F32)], axis=0)
        if e == 0:
            block = from_after(block)
        return block.reshape(half, 8, 128)

    for plane in range(-1, cells):
        taps = [
            (out, a) for out in range(cells // 2) for a in range(3) if 2 * out - 1 + a == plane
        ]
        sums = [
            sum(
                term(out, a, e, f)
                for out, a in taps
                for e in ((0, 2) if row else (1,))
                for f in ((0, 2) if column else (1,))
            ).reshape(half, 1, 8, 128)
            for column in range(2)
            for row in range(2)
        ]
        spread = jnp.concatenate(sums, axis=1).reshape(rows, 128)
        if plane < 1:
            slope = slope_low_ref[(plane + 1) * rows : (plane + 2) * rows, :]
        else:
            slope = slope_ref[(plane - 1) * rows : plane * rows, :]
        delta = (spread * slope).astype(BF16)
        deltas[(plane + 1) * rows : (plane + 2) * rows, :] = delta
        if plane < 0:
            down_ref[:rows, :] = spread.astype(BF16)
        if plane == 0:
            down_ref[rows:, :] = delta
        if plane == cells - 1:
            last_ref[...] = spread
        elif plane >= 0:
            low_ref[plane * rows : (plane + 1) * rows, :] = delta
    flipped = jnp.transpose(deltas[...].astype(F32)).astype(BF16)
    tally = jnp.dot(flipped, columns[...], preferred_element_type=F32)
    shard_rows = 9 * 192 // 4
    for tap in range(9):
        turned = jnp.transpose(tally[:, tap * 256 : (tap + 1) * 256])[64:]
        at = tap * 192
        while at < (tap + 1) * 192:
            shard = at // shard_rows
            to = min((tap + 1) * 192, (shard + 1) * shard_rows)
            flat[shard, at - shard * shard_rows : to - shard * shard_rows, :] = turned[
                at - tap * 192 : to - tap * 192
            ]
            at = to
    rest = flat.shape[1] - shard_rows
    if rest:
        flat[:, shard_rows:, :] = jnp.zeros((4, rest, 128), F32)
    put_pieces(flat, (g0, g1, g2, g3), slots, order)


def back_second(delta, shards, slopes, sorted_volume, halo, offsets, slots, order, places, size):
    rows, features = shards[0].shape
    planes, _, width, _ = sorted_volume.shape
    cells = planes // 2
    piece = sds((places, size, 128), BF16)
    return call(
        back_second_kernel,
        (
            near(((cells - 1) * width, 128), BF16),
            near((width, 128), F32),
            sds((2 * width, 128), BF16),
            piece, piece, piece, piece,
        ),
        [
            pltpu.VMEM((4 * rows, features), BF16),
            pltpu.VMEM((delta.shape[0], 4 * rows), F32),
            pltpu.VMEM(((cells + 1) * width, 9 * 256), BF16),
            pltpu.VMEM(((cells + 1) * width, 128), BF16),
            pltpu.VMEM((4, places * size, 128), F32),
        ],
        delta, *shards, *slopes, sorted_volume, halo,
        smem=(offsets, slots, order),
        micros=3.5,
    )


def back_input_kernel(
    offsets, low_ref, last_ref, slope_ref, upper_ref, w0, w1, w2, w3,
    out_ref, whole, turned, pairs, product, wide, last,
):
    put_rows(whole, (w0, w1, w2, w3), offsets)
    for tap in range(9):
        top = tap * 128
        turned[top : top + 128, 0:128] = whole[tap * 192 + 64 : (tap + 1) * 192, :]
        turned[top : top + 64, 128:256] = jnp.zeros((64, 128), BF16)
        turned[top + 64 : top + 128, 128:256] = whole[tap * 192 : tap * 192 + 64, :]
    planes = out_ref.shape[0]
    cells = planes // 2
    rows = last_ref.shape[0]
    groups = rows // 16
    last[...] = (
        (last_ref[...] + upper_ref[:rows, :].astype(F32)) * slope_ref[(cells - 2) * rows :, :]
    ).astype(BF16)
    for cell in range(cells + 1):
        at = cell * rows
        if cell < cells - 1:
            source = low_ref.at[at : at + rows]
        else:
            source = last if cell == cells - 1 else upper_ref.at[rows : 2 * rows]
        pairs[at : at + rows, 0:128] = source[...]
        pairs[at : at + rows - 16, 128:256] = source[16:rows, :]
        pairs[at + rows - 16 : at + rows, 128:256] = jnp.zeros((16, 128), BF16)
    product[...] = lax.dot_general(
        pairs[...], turned[...], (((1,), (1,)), ((), ())), preferred_element_type=F32
    ).reshape(product.shape)

    def part(cell, a, e, parity):
        left = (a * 3 + e) * 128
        return product[cell * groups : (cell + 1) * groups, parity, :, left : left + 128]

    def after(block):
        flat = block.reshape(groups * 8, 128)
        return from_after(flat).reshape(groups, 8, 128)

    for plane in range(planes):
        taps = [(o, a) for o in range(cells + 1) for a in range(3) if 2 * o - 1 + a == plane]
        wide[:, pl.ds(0, 8, stride=4), :] = sum(part(o, a, 1, 0) for o, a in taps)
        wide[:, pl.ds(1, 8, stride=4), :] = sum(
            part(o, a, 2, 0) + part(o, a, 0, 1) for o, a in taps
        )
        wide[:, pl.ds(2, 8, stride=4), :] = sum(part(o, a, 1, 1) for o, a in taps)
        wide[:, pl.ds(3, 8, stride=4), :] = sum(part(o, a, 2, 1) for o, a in taps) + after(
            sum(part(o, a, 0, 0) for o, a in taps)
        )
        for group in range(groups):
            lanes = slice(group * 128, (group + 1) * 128)
            out_ref[plane, :, lanes] = wide[group].astype(BF16)


def back_input(low, last, slope, upper, shards, offsets, shape):
    planes, side, width = shape
    shard = shards[0].shape[0]
    rows = low.shape[0] + upper.shape[0]
    return call(
        back_input_kernel,
        sds(shape, BF16),
        [
            pltpu.VMEM((4 * shard, 128), BF16),
            pltpu.VMEM((9 * 128, 256), BF16),
            pltpu.VMEM((rows, 256), BF16),
            pltpu.VMEM((rows // 16, 2, 8, 9 * 128), F32),
            pltpu.VMEM((width // 128, side, 128), F32),
            pltpu.VMEM(last.shape, BF16),
        ],
        low, last, slope, upper, *shards,
        smem=(offsets,),
        micros=3.0,
    )


def unpack_kernel(scale_first, scale_second, order, *refs):
    *chunks, first_ref, second_ref, flat_first, flat_second = refs
    high = order.shape[0] // 2
    small = flat_first.shape[0] // (2 * high)
    big = flat_second.shape[0] // (2 * high)
    for low in range(2):
        for index in range(high):
            if low and index:
                chunk = chunks[high + 1][index - 1].astype(F32)
            else:
                chunk = chunks[index + low * high][...].astype(F32)
            place = order[low * high + index]
            flat_second[pl.ds(pl.multiple_of(place * big, 8), big), :] = chunk[:big, :]
            flat_first[pl.ds(pl.multiple_of(place * small, 8), small), :] = chunk[big:, :]
    rows, features = second_ref.shape
    for lane in range(features // 128):
        second_ref[:, lane * 128 : (lane + 1) * 128] = (
            flat_second[lane * rows : (lane + 1) * rows, :] * scale_second
        )
    first_ref[...] = flat_first[: first_ref.shape[0], :] * scale_first


def wide_sum(*pieces):
    return sum(piece.astype(F32) for piece in pieces)


def added(*pieces):
    return wide_sum(*pieces).astype(BF16)


def swap(value, axis, bits):
    size = lax.axis_size(axis)
    return lax.ppermute(value, axis, [(i, i ^ bits) for i in range(size)])


def shifted(value, axis, by):
    size = lax.axis_size(axis)
    pairs = [(i, i + by) for i in range(size) if 0 <= i + by < size]
    return lax.ppermute(value, axis, pairs)


def local(volume, weight_first, weight_second, cotangent):
    samples, planes, side, width = volume.shape
    data = lax.axis_index("dp")
    place = lax.axis_index("space")
    spaces = lax.axis_size("space")
    high = spaces // 2
    small, big = weight_first.shape[0], weight_second.shape[0]
    slots = jnp.arange(4, dtype=jnp.int32) ^ data
    offsets_first = slots * small
    offsets_second = slots * big
    alive = (place > 0).astype(F32).reshape(1)
    x_side = lax.shift_right_logical(data, 1)
    steps = jnp.arange(spaces, dtype=jnp.int32)
    order = place ^ (2 * (steps % high) + steps // high)
    lanes = weight_second.shape[1] // 128
    size_first = -(-small // (8 * spaces)) * 8
    size_second = -(-lanes * big // (8 * spaces)) * 8

    inputs = volume.reshape(planes, side, width)
    uppermost = last_planes(inputs, 3)
    first_x = swap(weight_first, "dp", 2)
    first_core = swap(weight_first, "dp", 1)
    second_x = swap(weight_second, "dp", 2)
    second_core = swap(weight_second, "dp", 1)
    halo = shifted(uppermost, "space", 1)
    first_far = swap(first_x, "dp", 1)
    shards_first = (weight_first, first_core, first_x, first_far)

    sorted_volume = sorted_planes(inputs)
    slope, windows, middle, top, partial, padded = forward_upper(
        sorted_volume, shards_first, offsets_first
    )
    middle_x, middle_core = swap(middle, "dp", 2), swap(middle, "dp", 1)
    second_x, partial = lax.optimization_barrier((second_x, partial))
    second_far = swap(second_x, "dp", 1)
    shards_second = (weight_second, second_core, second_x, second_far)
    slope_low, windows_low, sorted_halo, edge, edge_there = forward_lower(
        halo, top, partial, padded, alive, x_side.reshape(1)
    )
    cot = cotangent.reshape(cotangent.shape[1:])
    activations, delta_second = forward_second(
        windows, windows_low, cot, shards_second, offsets_second
    )
    delta_second, middle_x = lax.optimization_barrier((delta_second, middle_x))
    edge_x, edge_core = swap(edge_there, "dp", 2), swap(edge, "dp", 1)
    delta_x, delta_core = swap(delta_second, "dp", 2), swap(delta_second, "dp", 1)
    low, last, down, *first = back_second(
        delta_second, shards_second, (slope_low, slope), sorted_volume, sorted_halo,
        offsets_second, slots, order, spaces, size_first,
    )
    middle_far = swap(middle_x, "dp", 1)
    first, down, delta_x, edge_x, delta_core, edge_core, middle_far = lax.optimization_barrier(
        (first, down, delta_x, edge_x, delta_core, edge_core, middle_far)
    )
    second = second_rows(
        (edge, edge_core, edge_x, swap(edge_x, "dp", 1)),
        (middle, middle_core, middle_x, middle_far),
        (delta_second, delta_core, delta_x, swap(delta_x, "dp", 1)),
        data, order, spaces, size_second,
    )
    second, down = lax.optimization_barrier((second, down))
    upper = shifted(down, "space", -1)

    def pieces(value):
        return value.reshape(2, high, -1, 128)

    far, beside = pieces(swap(first[3], "dp", 1)), pieces(swap(first[1], "dp", 1))
    own, there = pieces(first[0]), pieces(first[2])
    both = [
        (d * spaces + s, (d ^ 2) * spaces + (s ^ 1)) for d in range(4) for s in range(spaces)
    ]
    second = pieces(second)
    sent_y = jnp.concatenate([second[1], added(own[1], beside[1])], axis=1)
    got_y = swap(sent_y[1:], "space", 1)
    got_x = swap(added(there[0], far[0]), "dp", 2)
    got_y_own = swap(sent_y[:1], "space", 1)
    got_xy = lax.ppermute(added(there[1], far[1]), ("dp", "space"), both)

    def held(places, got):
        return jnp.concatenate(
            [
                wide_sum(second[0][places], got[:, :size_second]),
                wide_sum(
                    own[0][places], beside[0][places], got_x[places], got_xy[places],
                    got[:, size_second:],
                ),
            ],
            axis=1,
        )

    sent = held(slice(1, high), got_y).astype(BF16)
    *received, got_y_own, upper = lax.optimization_barrier(
        (*(swap(sent[k - 1], "space", 2 * k) for k in range(1, high)), got_y_own, upper)
    )
    mine = added(held(slice(0, 1), got_y_own)[0], *received)
    others = [swap(mine, "space", 2 * k) for k in range(1, high)]
    mine_y = swap(mine, "space", 1)
    chunks = [mine, *others, mine_y]
    if others:
        chunks.append(swap(jnp.stack(others), "space", 1))
    upper, mine_y = lax.optimization_barrier((upper, mine_y))
    chunks[high] = mine_y

    gradient = back_input(low, last, slope, upper, shards_first, offsets_first, inputs.shape)

    cells_first = samples * lax.axis_size("dp") * (planes // 2) * spaces * (side // 2) ** 2
    cells_second = cells_first // 8
    first_gradient, second_gradient = call(
        functools.partial(unpack_kernel, float(cells_first) ** -0.5, float(cells_second) ** -0.5),
        (sds(weight_first.shape, F32), sds(weight_second.shape, F32)),
        [
            pltpu.VMEM((spaces * size_first, 128), F32),
            pltpu.VMEM((spaces * size_second, 128), F32),
        ],
        *chunks,
        smem=(order,),
    )
    return (
        activations.reshape(cotangent.shape),
        gradient.reshape(volume.shape),
        first_gradient,
        second_gradient,
    )


def solution(mesh):
    return jax.shard_map(
        local,
        mesh=mesh,
        in_specs=(
            P("dp", "space", None, None),
            P("dp", None),
            P("dp", None),
            P("dp", "space", None, None),
        ),
        out_specs=(
            P("dp", "space", None, None),
            P("dp", "space", None, None),
            P("dp", None),
            P("dp", None),
        ),
        check_vma=False,
    )
```

```python
import functools

import jax
import jax.numpy as jnp
from jax import lax
from jax.experimental import pallas as pl
from jax.experimental.pallas import tpu as pltpu
from jax.sharding import PartitionSpec as P

LEAK_SLOPE = 0.2
F32 = jnp.float32
BF16 = jnp.bfloat16
VMEM_LIMIT = 24 * 1024 * 1024


def activate(values):
    small = jnp.exp(-jnp.abs(values))
    return LEAK_SLOPE * values + (1.0 - LEAK_SLOPE) * (
        jnp.maximum(values, 0.0) + jnp.log(1.0 + small)
    )


def activate_slope(values):
    small = jnp.exp(-jnp.abs(values))
    inverse = 1.0 / (1.0 + small)
    return LEAK_SLOPE + (1.0 - LEAK_SLOPE) * jnp.where(
        values >= 0.0, inverse, small * inverse
    )


def block_row(rows, width):
    return lax.broadcasted_iota(jnp.int32, (rows, width), 0) % 8


def from_before(block):
    moved = pltpu.roll(block, 1, 0)
    return jnp.where(block_row(*block.shape) == 0, 0.0, moved)


def from_after(block):
    moved = pltpu.roll(block, block.shape[0] - 1, 0)
    return jnp.where(block_row(*block.shape) == 7, 0.0, moved)


def call(kernel, out_shape, scratch, *operands, smem=(), micros=1.0):
    nbytes = sum(a.size * a.dtype.itemsize for a in operands)
    specs = [pl.BlockSpec(memory_space=pltpu.SMEM)] * len(smem)
    specs += [pl.BlockSpec(memory_space=pltpu.VMEM)] * len(operands)
    return pl.pallas_call(
        kernel,
        out_shape=out_shape,
        in_specs=specs,
        out_specs=jax.tree.map(lambda _: pl.BlockSpec(memory_space=pltpu.VMEM), out_shape),
        scratch_shapes=scratch,
        compiler_params=pltpu.CompilerParams(vmem_limit_bytes=VMEM_LIMIT),
        cost_estimate=pl.CostEstimate(
            flops=int(micros * 1.15e9), bytes_accessed=nbytes, transcendentals=0
        ),
    )(*smem, *operands)


def sds(shape, dtype):
    return jax.ShapeDtypeStruct(shape, dtype)


def near(shape, dtype):
    return pltpu.VMEM(shape, dtype)


def sort_kernel(planes, in_ref, out_ref, wide):
    pairs = wide.shape[0]
    for plane in range(planes):
        for pair in range(pairs):
            wide[pair] = in_ref[plane, :, pair * 128 : (pair + 1) * 128].astype(F32)
        classes = [
            wide[:, pl.ds(r, 8, stride=4), :].reshape(pairs * 8, 128) for r in range(4)
        ]
        before = from_before(classes[3])
        for tap, (even, odd) in enumerate(
            ((before, classes[1]), (classes[0], classes[2]), (classes[1], classes[3]))
        ):
            both = jnp.concatenate(
                [even.reshape(pairs, 1, 8, 128), odd.reshape(pairs, 1, 8, 128)], axis=1
            )
            out_ref[plane, tap] = both.reshape(pairs * 16, 128).astype(BF16)


def last_planes_kernel(volume_ref, out_ref, sem):
    count = out_ref.shape[0]
    copy = pltpu.make_async_copy(
        volume_ref.at[pl.ds(volume_ref.shape[0] - count, count)], out_ref, sem
    )
    copy.start()
    copy.wait()


def last_planes(volume, count):
    shape = (count, *volume.shape[1:])
    return pl.pallas_call(
        last_planes_kernel,
        out_shape=pltpu.VMEM(shape, BF16),
        in_specs=[pl.BlockSpec(memory_space=pltpu.HBM)],
        out_specs=pl.BlockSpec(memory_space=pltpu.VMEM),
        scratch_shapes=[pltpu.SemaphoreType.DMA],
        cost_estimate=pl.CostEstimate(
            flops=0, bytes_accessed=4 * shape[0] * shape[1] * shape[2], transcendentals=0
        ),
    )(volume)


def sorted_planes(volume):
    planes, rows, width = volume.shape
    pairs = width // 128
    return call(
        functools.partial(sort_kernel, planes),
        near((planes, 3, pairs * 16, 128), BF16),
        [pltpu.VMEM((pairs, rows, 128), F32)],
        volume,
    )


def put_rows(dst, pieces, offsets):
    rows = pieces[0].shape[0]
    for index, piece in enumerate(pieces):
        dst[pl.ds(pl.multiple_of(offsets[index], 16), rows), :] = piece[...]


def put_tap(columns, at, left, source):
    rows = source.shape[0]
    columns[at : at + 16, left : left + 128] = jnp.zeros((16, 128), BF16)
    columns[at + 16 : at + rows, left : left + 128] = source[0 : rows - 16, :]
    columns[at : at + rows, left + 128 : left + 256] = source[...]


def gather_taps(columns, sorted_ref, halo_ref, first, count):
    rows = sorted_ref.shape[2]
    for cell in range(count):
        for a in range(3):
            plane = 2 * (first + cell) - 1 + a
            for e in range(3):
                source = (
                    halo_ref.at[halo_ref.shape[0] + plane, e] if plane < 0 else sorted_ref.at[plane, e]
                )
                put_tap(columns, cell * rows, (a * 3 + e) * 256, source)


def pad_first(whole, padded):
    for tap in range(9):
        padded[tap * 256 : tap * 256 + 64, :] = jnp.zeros((64, 128), BF16)
        padded[tap * 256 + 64 : (tap + 1) * 256, :] = whole[tap * 192 : (tap + 1) * 192, :]


def take_windows(read, dst, row, left, half):
    for e in range(3):
        for f in range(3):
            block = read(0 if f == 1 else 1, 0 if e == 1 else 1)
            if e == 0:
                block = from_before(block)
            if f == 0:
                block = jnp.concatenate(
                    [jnp.zeros((8, 128), F32), block[: half * 8 - 8]], axis=0
                )
            at = left + (e * 3 + f) * 128
            dst[row : row + half * 8, at : at + 128] = block.astype(BF16)


def forward_upper_kernel(
    offsets, sorted_ref, w0, w1, w2, w3,
    slope_ref, windows_ref, middle_ref, top_ref, partial_ref, padded_ref,
    columns, some, whole, upper,
):
    cells = sorted_ref.shape[0] // 2
    put_rows(whole, (w0, w1, w2, w3), offsets)
    pad_first(whole, padded_ref)
    gather_taps(columns, sorted_ref, None, 1, cells - 1)
    linear = jnp.dot(columns[...], padded_ref[...], preferred_element_type=F32)
    hidden = activate(linear)
    upper[...] = hidden.reshape(upper.shape)
    count = middle_ref.shape[0] * middle_ref.shape[1]
    middle_ref[...] = hidden[:count].reshape(middle_ref.shape).astype(BF16)
    top_ref[...] = hidden[count:].astype(BF16)
    slope_ref[...] = activate_slope(linear)
    half = upper.shape[1]
    for out in range(cells // 2):
        for a in range(3):
            plane = 2 * out - 1 + a
            if plane > 0:

                def read(column, row):
                    return upper[plane - 1, :, column, row].reshape(half * 8, 128)

                take_windows(read, windows_ref, out * half * 8, a * 9 * 128, half)
    for a in range(1, 3):
        for e in range(3):
            put_tap(some, 0, ((a - 1) * 3 + e) * 256, sorted_ref.at[a - 1, e])
    partial_ref[...] = jnp.dot(some[...], padded_ref[3 * 256 :, :], preferred_element_type=F32)


def forward_upper(sorted_volume, shards, offsets):
    planes, _, rows, _ = sorted_volume.shape
    cells = planes // 2
    shard = shards[0].shape[0]
    some = (cells - 1) * rows
    return call(
        forward_upper_kernel,
        (
            near((some, 128), F32),
            near((cells * rows // 8, 27 * 128), BF16),
            sds((cells - 2, rows, 128), BF16),
            near((rows, 128), BF16),
            near((rows, 128), F32),
            near((9 * 256, 128), BF16),
        ),
        [
            pltpu.VMEM((some, 9 * 256), BF16),
            pltpu.VMEM((rows, 6 * 256), BF16),
            pltpu.VMEM((4 * shard, 128), BF16),
            pltpu.VMEM((cells - 1, rows // 32, 2, 2, 8, 128), F32),
        ],
        sorted_volume, *shards,
        smem=(offsets,),
        micros=2.5,
    )


def forward_lower_kernel(
    alive, side, halo_ref, top_ref, partial_ref, padded_ref,
    slope_ref, windows_ref, sorted_ref, here_ref, there_ref, wide, columns, some, lowest, planes,
):
    rows = partial_ref.shape[0]
    half = rows // 32
    sort_kernel(halo_ref.shape[0], halo_ref, sorted_ref, wide)
    for e in range(3):
        for a in range(3):
            put_tap(columns, 0, (a * 3 + e) * 256, sorted_ref.at[a, e])
        put_tap(some, 0, e * 256, sorted_ref.at[2, e])
    below = jnp.dot(columns[...], padded_ref[...], preferred_element_type=F32)
    here = partial_ref[...] + jnp.dot(
        some[...], padded_ref[: 3 * 256, :], preferred_element_type=F32
    )
    slope_ref[:rows, :] = activate_slope(below)
    slope_ref[rows:, :] = activate_slope(here)
    lowest[0] = (activate(below) * alive[0]).reshape(lowest.shape[1:])
    lowest[1] = activate(here).reshape(lowest.shape[1:])
    planes[0] = lowest[0].reshape(rows, 128).astype(BF16)
    planes[1] = lowest[1].reshape(rows, 128).astype(BF16)
    planes[2] = planes[1]
    planes[3] = top_ref[...]
    here_ref[...] = planes[pl.ds(2 * side[0], 2)]
    there_ref[...] = planes[pl.ds(2 - 2 * side[0], 2)]
    for a in range(2):

        def read(column, row):
            return lowest[a, :, column, row].reshape(half * 8, 128)

        take_windows(read, windows_ref, 0, a * 9 * 128, half)


def forward_lower(halo, top, partial, padded, alive, side):
    rows = partial.shape[0]
    return call(
        forward_lower_kernel,
        (
            near((2 * rows, 128), F32),
            near((rows // 4, 2 * 9 * 128), BF16),
            near((halo.shape[0], 3, rows, 128), BF16),
            sds((2, rows, 128), BF16),
            sds((2, rows, 128), BF16),
        ),
        [
            pltpu.VMEM((rows // 16, halo.shape[1], 128), F32),
            pltpu.VMEM((rows, 9 * 256), BF16),
            pltpu.VMEM((rows, 3 * 256), BF16),
            pltpu.VMEM((2, rows // 32, 2, 2, 8, 128), F32),
            pltpu.VMEM((4, rows, 128), BF16),
        ],
        halo, top, partial, padded,
        smem=(alive, side),
        micros=1.5,
    )


def put_pieces(flat, outs, slots, order):
    for index, out in enumerate(outs):
        count, size, _ = out.shape
        for place in range(count):
            row = pl.multiple_of(order[place] * size, 8)
            out[place] = flat[slots[index], pl.ds(row, size), :].astype(BF16)


def forward_second_kernel(
    offsets, upper_ref, lower_ref, cot_ref, w0, w1, w2, w3, act_ref, delta_ref, whole, windows
):
    put_rows(whole, (w0, w1, w2, w3), offsets)
    low, width = lower_ref.shape
    windows[:low, :width] = lower_ref[...]
    windows[:low, width:] = upper_ref[:low, width:]
    windows[low:, :] = upper_ref[low:, :]
    linear = jnp.dot(windows[...], whole[...], preferred_element_type=F32)
    outs, _, width = cot_ref.shape
    features = linear.shape[1]
    count = width // features
    acted = activate(linear)
    slope = activate_slope(linear)
    deltas = []
    for out in range(outs):
        base = out * count * 8
        act_ref[out] = jnp.concatenate(
            [acted[base + q * 8 : base + (q + 1) * 8] for q in range(count)], axis=1
        ).astype(BF16)
        cot = cot_ref[out].astype(F32)
        deltas.append(
            jnp.concatenate(
                [cot[:, q * features : (q + 1) * features] for q in range(count)], axis=0
            )
        )
    delta_ref[...] = (jnp.concatenate(deltas, axis=0) * slope).astype(BF16)


def forward_second(upper, lower, cot, shards, offsets):
    rows, features = shards[0].shape
    return call(
        forward_second_kernel,
        (sds(cot.shape, BF16), sds((upper.shape[0], features), BF16)),
        [pltpu.VMEM((4 * rows, features), BF16), pltpu.VMEM(upper.shape, BF16)],
        upper, lower, cot, *shards,
        smem=(offsets,),
        micros=1.5,
    )


def second_rows_kernel(
    data, table, order, e0, e1, e2, e3, m0, m1, m2, m3, d0, d1, d2, d3,
    out_ref, wide, windows, deltas, product, flat,
):
    edges, rows, _ = e0.shape
    cells = edges + m0.shape[0]
    half = rows // 32
    outs = cells // 2
    size = half * 8
    taps = windows.shape[1] // 128
    samples = ((e0, m0, d0), (e1, m1, d1), (e2, m2, d2), (e3, m3, d3))
    for sample, (edge, middle, delta) in enumerate(samples):
        at = sample * cells
        wide[at : at + edges] = edge[...].astype(F32).reshape(edges, half, 2, 2, 8, 128)
        wide[at + edges : at + cells] = (
            middle[...].astype(F32).reshape(cells - edges, half, 2, 2, 8, 128)
        )
        deltas[sample * outs * size : (sample + 1) * outs * size, :] = delta[...]
    for tap in range(taps):
        e, f = table[data[0], tap], table[data[0], taps + tap]
        row = jnp.where(e == 1, 0, 1)
        column = jnp.where(f == 1, 0, 1)
        for sample in range(4):
            for out in range(outs):
                plane = sample * cells + table[data[0], (2 + out) * taps + tap]
                block = wide[plane, :, column, row].reshape(size, 128)
                block = jnp.where(e == 0, from_before(block), block)
                later = jnp.concatenate([jnp.zeros((8, 128), F32), block[: size - 8]], axis=0)
                block = jnp.where(f == 0, later, block)
                at = (sample * outs + out) * size
                windows[at : at + size, tap * 128 : (tap + 1) * 128] = block.astype(BF16)
    product[...] = lax.dot_general(
        windows[...], deltas[...], (((0,), (0,)), ((), ())), preferred_element_type=F32
    )
    lanes = product.shape[1] // 128
    count, piece, _ = out_ref.shape
    shard = 27 * 128 // 4
    for lane in range(lanes):
        flat[lane * shard : (lane + 1) * shard, :] = product[
            pl.ds(pl.multiple_of(table[data[0], (2 + outs) * taps], 16), shard), lane * 128 : (lane + 1) * 128
        ]
    rest = flat.shape[0] - lanes * shard
    if rest:
        flat[lanes * shard :, :] = jnp.zeros((rest, 128), F32)
    for place in range(count):
        row = pl.multiple_of(order[place] * piece, 8)
        out_ref[place] = flat[pl.ds(row, piece), :].astype(BF16)


def second_rows(edges, middles, deltas, data, order, places, size):
    _, rows, _ = edges[0].shape
    cells = edges[0].shape[0] + middles[0].shape[0]
    cellrows, features = deltas[0].shape
    taps = 8
    table = []
    for shard in range(4):
        start = shard * 27 // 4
        at = [min(start + tap, 26) for tap in range(taps)]
        held = (-1, 0, *range(1, cells - 1)) if shard < 2 else (0, cells - 1, *range(1, cells - 1))
        table.append(
            [tap // 3 % 3 for tap in at]
            + [tap % 3 for tap in at]
            + [held.index(2 * out - 1 + tap // 9) for out in range(cells // 2) for tap in at]
            + [shard * (27 * 128 // 4) - start * 128]
        )
    return call(
        second_rows_kernel,
        sds((places, size, 128), BF16),
        [
            pltpu.VMEM((4 * cells, rows // 32, 2, 2, 8, 128), F32),
            pltpu.VMEM((4 * cellrows, taps * 128), BF16),
            pltpu.VMEM((4 * cellrows, features), BF16),
            pltpu.VMEM((taps * 128, features), F32),
            pltpu.VMEM((places * size, 128), F32),
        ],
        *edges, *middles, *deltas,
        smem=(data.reshape(1), jnp.array(table, jnp.int32), order),
        micros=2.0,
    )


def back_second_kernel(
    offsets, slots, order, delta_ref, w0, w1, w2, w3,
    slope_low_ref, slope_ref, sorted_ref, halo_ref,
    low_ref, last_ref, down_ref, g0, g1, g2, g3,
    whole, product, columns, deltas, flat,
):
    rows = sorted_ref.shape[2]
    cells = sorted_ref.shape[0] // 2
    half = rows // 32
    size = half * 8
    put_rows(whole, (w0, w1, w2, w3), offsets)
    product[...] = lax.dot_general(
        delta_ref[...], whole[...], (((1,), (1,)), ((), ())), preferred_element_type=F32
    )
    gather_taps(columns, sorted_ref, halo_ref, -1, cells + 1)

    def term(out, a, e, f):
        left = ((a * 3 + e) * 3 + f) * 128
        block = product[out * size : (out + 1) * size, left : left + 128]
        if f == 0:
            block = jnp.concatenate([block[8:], jnp.zeros((8, 128), F32)], axis=0)
        if e == 0:
            block = from_after(block)
        return block.reshape(half, 8, 128)

    for plane in range(-1, cells):
        taps = [
            (out, a) for out in range(cells // 2) for a in range(3) if 2 * out - 1 + a == plane
        ]
        sums = [
            sum(
                term(out, a, e, f)
                for out, a in taps
                for e in ((0, 2) if row else (1,))
                for f in ((0, 2) if column else (1,))
            ).reshape(half, 1, 8, 128)
            for column in range(2)
            for row in range(2)
        ]
        spread = jnp.concatenate(sums, axis=1).reshape(rows, 128)
        if plane < 1:
            slope = slope_low_ref[(plane + 1) * rows : (plane + 2) * rows, :]
        else:
            slope = slope_ref[(plane - 1) * rows : plane * rows, :]
        delta = (spread * slope).astype(BF16)
        deltas[(plane + 1) * rows : (plane + 2) * rows, :] = delta
        if plane < 0:
            down_ref[:rows, :] = spread.astype(BF16)
        if plane == 0:
            down_ref[rows:, :] = delta
        if plane == cells - 1:
            last_ref[...] = spread
        elif plane >= 0:
            low_ref[plane * rows : (plane + 1) * rows, :] = delta
    flipped = jnp.transpose(deltas[...].astype(F32)).astype(BF16)
    tally = jnp.dot(flipped, columns[...], preferred_element_type=F32)
    shard_rows = 9 * 192 // 4
    for tap in range(9):
        turned = jnp.transpose(tally[:, tap * 256 : (tap + 1) * 256])[64:]
        at = tap * 192
        while at < (tap + 1) * 192:
            shard = at // shard_rows
            to = min((tap + 1) * 192, (shard + 1) * shard_rows)
            flat[shard, at - shard * shard_rows : to - shard * shard_rows, :] = turned[
                at - tap * 192 : to - tap * 192
            ]
            at = to
    rest = flat.shape[1] - shard_rows
    if rest:
        flat[:, shard_rows:, :] = jnp.zeros((4, rest, 128), F32)
    put_pieces(flat, (g0, g1, g2, g3), slots, order)


def back_second(delta, shards, slopes, sorted_volume, halo, offsets, slots, order, places, size):
    rows, features = shards[0].shape
    planes, _, width, _ = sorted_volume.shape
    cells = planes // 2
    piece = sds((places, size, 128), BF16)
    return call(
        back_second_kernel,
        (
            near(((cells - 1) * width, 128), BF16),
            near((width, 128), F32),
            sds((2 * width, 128), BF16),
            piece, piece, piece, piece,
        ),
        [
            pltpu.VMEM((4 * rows, features), BF16),
            pltpu.VMEM((delta.shape[0], 4 * rows), F32),
            pltpu.VMEM(((cells + 1) * width, 9 * 256), BF16),
            pltpu.VMEM(((cells + 1) * width, 128), BF16),
            pltpu.VMEM((4, places * size, 128), F32),
        ],
        delta, *shards, *slopes, sorted_volume, halo,
        smem=(offsets, slots, order),
        micros=3.5,
    )


def back_input_kernel(
    offsets, low_ref, last_ref, slope_ref, upper_ref, w0, w1, w2, w3,
    out_ref, whole, turned, pairs, product, wide, last,
):
    put_rows(whole, (w0, w1, w2, w3), offsets)
    for tap in range(9):
        top = tap * 128
        turned[top : top + 128, 0:128] = whole[tap * 192 + 64 : (tap + 1) * 192, :]
        turned[top : top + 64, 128:256] = jnp.zeros((64, 128), BF16)
        turned[top + 64 : top + 128, 128:256] = whole[tap * 192 : tap * 192 + 64, :]
    planes = out_ref.shape[0]
    cells = planes // 2
    rows = last_ref.shape[0]
    groups = rows // 16
    last[...] = (
        (last_ref[...] + upper_ref[:rows, :].astype(F32)) * slope_ref[(cells - 2) * rows :, :]
    ).astype(BF16)
    for cell in range(cells + 1):
        at = cell * rows
        if cell < cells - 1:
            source = low_ref.at[at : at + rows]
        else:
            source = last if cell == cells - 1 else upper_ref.at[rows : 2 * rows]
        pairs[at : at + rows, 0:128] = source[...]
        pairs[at : at + rows - 16, 128:256] = source[16:rows, :]
        pairs[at + rows - 16 : at + rows, 128:256] = jnp.zeros((16, 128), BF16)
    product[...] = lax.dot_general(
        pairs[...], turned[...], (((1,), (1,)), ((), ())), preferred_element_type=F32
    ).reshape(product.shape)

    def part(cell, a, e, parity):
        left = (a * 3 + e) * 128
        return product[cell * groups : (cell + 1) * groups, parity, :, left : left + 128]

    def after(block):
        flat = block.reshape(groups * 8, 128)
        return from_after(flat).reshape(groups, 8, 128)

    for plane in range(planes):
        taps = [(o, a) for o in range(cells + 1) for a in range(3) if 2 * o - 1 + a == plane]
        wide[:, pl.ds(0, 8, stride=4), :] = sum(part(o, a, 1, 0) for o, a in taps)
        wide[:, pl.ds(1, 8, stride=4), :] = sum(
            part(o, a, 2, 0) + part(o, a, 0, 1) for o, a in taps
        )
        wide[:, pl.ds(2, 8, stride=4), :] = sum(part(o, a, 1, 1) for o, a in taps)
        wide[:, pl.ds(3, 8, stride=4), :] = sum(part(o, a, 2, 1) for o, a in taps) + after(
            sum(part(o, a, 0, 0) for o, a in taps)
        )
        for group in range(groups):
            lanes = slice(group * 128, (group + 1) * 128)
            out_ref[plane, :, lanes] = wide[group].astype(BF16)


def back_input(low, last, slope, upper, shards, offsets, shape):
    planes, side, width = shape
    shard = shards[0].shape[0]
    rows = low.shape[0] + upper.shape[0]
    return call(
        back_input_kernel,
        sds(shape, BF16),
        [
            pltpu.VMEM((4 * shard, 128), BF16),
            pltpu.VMEM((9 * 128, 256), BF16),
            pltpu.VMEM((rows, 256), BF16),
            pltpu.VMEM((rows // 16, 2, 8, 9 * 128), F32),
            pltpu.VMEM((width // 128, side, 128), F32),
            pltpu.VMEM(last.shape, BF16),
        ],
        low, last, slope, upper, *shards,
        smem=(offsets,),
        micros=3.0,
    )


def unpack_kernel(scale_first, scale_second, order, *refs):
    *chunks, first_ref, second_ref, flat_first, flat_second = refs
    high = order.shape[0] // 2
    small = flat_first.shape[0] // (2 * high)
    big = flat_second.shape[0] // (2 * high)
    for low in range(2):
        for index in range(high):
            if low and index and index == high - 1:
                chunk = chunks[-1][0].astype(F32)
            elif low and index:
                chunk = chunks[high + 1][index - 1].astype(F32)
            else:
                chunk = chunks[index + low * high][...].astype(F32)
            place = order[low * high + index]
            flat_second[pl.ds(pl.multiple_of(place * big, 8), big), :] = chunk[:big, :]
            flat_first[pl.ds(pl.multiple_of(place * small, 8), small), :] = chunk[big:, :]
    rows, features = second_ref.shape
    for lane in range(features // 128):
        second_ref[:, lane * 128 : (lane + 1) * 128] = (
            flat_second[lane * rows : (lane + 1) * rows, :] * scale_second
        )
    first_ref[...] = flat_first[: first_ref.shape[0], :] * scale_first


def wide_sum(*pieces):
    return sum(piece.astype(F32) for piece in pieces)


def added(*pieces):
    return wide_sum(*pieces).astype(BF16)


def swap(value, axis, bits):
    size = lax.axis_size(axis)
    return lax.ppermute(value, axis, [(i, i ^ bits) for i in range(size)])


def shifted(value, axis, by):
    size = lax.axis_size(axis)
    pairs = [(i, i + by) for i in range(size) if 0 <= i + by < size]
    return lax.ppermute(value, axis, pairs)


def local(volume, weight_first, weight_second, cotangent):
    samples, planes, side, width = volume.shape
    data = lax.axis_index("dp")
    place = lax.axis_index("space")
    spaces = lax.axis_size("space")
    high = spaces // 2
    small, big = weight_first.shape[0], weight_second.shape[0]
    slots = jnp.arange(4, dtype=jnp.int32) ^ data
    offsets_first = slots * small
    offsets_second = slots * big
    alive = (place > 0).astype(F32).reshape(1)
    x_side = lax.shift_right_logical(data, 1)
    steps = jnp.arange(spaces, dtype=jnp.int32)
    order = place ^ (2 * (steps % high) + steps // high)
    lanes = weight_second.shape[1] // 128
    size_first = -(-small // (8 * spaces)) * 8
    size_second = -(-lanes * big // (8 * spaces)) * 8

    inputs = volume.reshape(planes, side, width)
    uppermost = last_planes(inputs, 3)
    first_x = swap(weight_first, "dp", 2)
    first_core = swap(weight_first, "dp", 1)
    second_x = swap(weight_second, "dp", 2)
    second_core = swap(weight_second, "dp", 1)
    halo = shifted(uppermost, "space", 1)
    first_far = swap(first_x, "dp", 1)
    shards_first = (weight_first, first_core, first_x, first_far)

    sorted_volume = sorted_planes(inputs)
    slope, windows, middle, top, partial, padded = forward_upper(
        sorted_volume, shards_first, offsets_first
    )
    middle_x, middle_core = swap(middle, "dp", 2), swap(middle, "dp", 1)
    second_x, partial = lax.optimization_barrier((second_x, partial))
    second_far = swap(second_x, "dp", 1)
    shards_second = (weight_second, second_core, second_x, second_far)
    slope_low, windows_low, sorted_halo, edge, edge_there = forward_lower(
        halo, top, partial, padded, alive, x_side.reshape(1)
    )
    cot = cotangent.reshape(cotangent.shape[1:])
    activations, delta_second = forward_second(
        windows, windows_low, cot, shards_second, offsets_second
    )
    delta_second, middle_x = lax.optimization_barrier((delta_second, middle_x))
    edge_x, edge_core = swap(edge_there, "dp", 2), swap(edge, "dp", 1)
    delta_x, delta_core = swap(delta_second, "dp", 2), swap(delta_second, "dp", 1)
    low, last, down, *first = back_second(
        delta_second, shards_second, (slope_low, slope), sorted_volume, sorted_halo,
        offsets_second, slots, order, spaces, size_first,
    )
    middle_far = swap(middle_x, "dp", 1)
    first, down, delta_x, edge_x, delta_core, edge_core, middle_far = lax.optimization_barrier(
        (first, down, delta_x, edge_x, delta_core, edge_core, middle_far)
    )
    second = second_rows(
        (edge, edge_core, edge_x, swap(edge_x, "dp", 1)),
        (middle, middle_core, middle_x, middle_far),
        (delta_second, delta_core, delta_x, swap(delta_x, "dp", 1)),
        data, order, spaces, size_second,
    )
    second, down = lax.optimization_barrier((second, down))
    upper = shifted(down, "space", -1)

    def pieces(value):
        return value.reshape(2, high, -1, 128)

    far, beside = pieces(swap(first[3], "dp", 1)), pieces(swap(first[1], "dp", 1))
    own, there = pieces(first[0]), pieces(first[2])
    both = [
        (d * spaces + s, (d ^ 2) * spaces + (s ^ 1)) for d in range(4) for s in range(spaces)
    ]
    second = pieces(second)
    sent_y = jnp.concatenate([second[1], added(own[1], beside[1])], axis=1)
    got_y = swap(sent_y[1:], "space", 1)
    got_x = swap(added(there[0], far[0]), "dp", 2)
    got_y_own = swap(sent_y[:1], "space", 1)
    got_xy = lax.ppermute(added(there[1], far[1]), ("dp", "space"), both)

    def held(places, got):
        return jnp.concatenate(
            [
                wide_sum(second[0][places], got[:, :size_second]),
                wide_sum(
                    own[0][places], beside[0][places], got_x[places], got_xy[places],
                    got[:, size_second:],
                ),
            ],
            axis=1,
        )

    sent = held(slice(1, high), got_y).astype(BF16)
    *received, got_y_own, upper = lax.optimization_barrier(
        (*(swap(sent[k - 1], "space", 2 * k) for k in range(1, high)), got_y_own, upper)
    )
    mine = added(held(slice(0, 1), got_y_own)[0], *received)
    others = [swap(mine, "space", 2 * k) for k in range(1, high)]
    mine_y = swap(mine, "space", 1)
    late = [swap(jnp.stack(others[-1:]), "space", 1)] if others else []
    early = [swap(jnp.stack(others[:-1]), "space", 1)] if len(others) > 1 else []
    upper, mine_y = lax.optimization_barrier((upper, mine_y))
    chunks = [mine, *others, mine_y, *early, *late]

    gradient = back_input(low, last, slope, upper, shards_first, offsets_first, inputs.shape)

    cells_first = samples * lax.axis_size("dp") * (planes // 2) * spaces * (side // 2) ** 2
    cells_second = cells_first // 8
    first_gradient, second_gradient = call(
        functools.partial(unpack_kernel, float(cells_first) ** -0.5, float(cells_second) ** -0.5),
        (sds(weight_first.shape, F32), sds(weight_second.shape, F32)),
        [
            pltpu.VMEM((spaces * size_first, 128), F32),
            pltpu.VMEM((spaces * size_second, 128), F32),
        ],
        *chunks,
        smem=(order,),
    )
    return (
        activations.reshape(cotangent.shape),
        gradient.reshape(volume.shape),
        first_gradient,
        second_gradient,
    )


def solution(mesh):
    return jax.shard_map(
        local,
        mesh=mesh,
        in_specs=(
            P("dp", "space", None, None),
            P("dp", None),
            P("dp", None),
            P("dp", "space", None, None),
        ),
        out_specs=(
            P("dp", "space", None, None),
            P("dp", "space", None, None),
            P("dp", None),
            P("dp", None),
        ),
        check_vma=False,
    )
```

```python
import functools

import jax
import jax.numpy as jnp
from jax import lax
from jax.experimental import pallas as pl
from jax.experimental.pallas import tpu as pltpu
from jax.sharding import PartitionSpec as P

LEAK_SLOPE = 0.2
F32 = jnp.float32
BF16 = jnp.bfloat16
VMEM_LIMIT = 24 * 1024 * 1024


def activate(values):
    small = jnp.exp(-jnp.abs(values))
    return LEAK_SLOPE * values + (1.0 - LEAK_SLOPE) * (
        jnp.maximum(values, 0.0) + jnp.log(1.0 + small)
    )


def activate_slope(values):
    small = jnp.exp(-jnp.abs(values))
    inverse = 1.0 / (1.0 + small)
    return LEAK_SLOPE + (1.0 - LEAK_SLOPE) * jnp.where(
        values >= 0.0, inverse, small * inverse
    )


def block_row(rows, width):
    return lax.broadcasted_iota(jnp.int32, (rows, width), 0) % 8


def from_before(block):
    moved = pltpu.roll(block, 1, 0)
    return jnp.where(block_row(*block.shape) == 0, 0.0, moved)


def from_after(block):
    moved = pltpu.roll(block, block.shape[0] - 1, 0)
    return jnp.where(block_row(*block.shape) == 7, 0.0, moved)


def call(kernel, out_shape, scratch, *operands, smem=(), micros=1.0, out_space=pltpu.VMEM):
    nbytes = sum(a.size * a.dtype.itemsize for a in operands)
    specs = [pl.BlockSpec(memory_space=pltpu.SMEM)] * len(smem)
    specs += [pl.BlockSpec(memory_space=pltpu.VMEM)] * len(operands)
    return pl.pallas_call(
        kernel,
        out_shape=out_shape,
        in_specs=specs,
        out_specs=jax.tree.map(lambda _: pl.BlockSpec(memory_space=out_space), out_shape),
        scratch_shapes=scratch,
        compiler_params=pltpu.CompilerParams(vmem_limit_bytes=VMEM_LIMIT),
        cost_estimate=pl.CostEstimate(
            flops=int(micros * 1.15e9), bytes_accessed=nbytes, transcendentals=0
        ),
    )(*smem, *operands)


def sds(shape, dtype):
    return jax.ShapeDtypeStruct(shape, dtype)


def near(shape, dtype):
    return pltpu.VMEM(shape, dtype)


def sort_kernel(planes, in_ref, out_ref, wide):
    pairs = wide.shape[0]
    for plane in range(planes):
        for pair in range(pairs):
            wide[pair] = in_ref[plane, :, pair * 128 : (pair + 1) * 128].astype(F32)
        classes = [
            wide[:, pl.ds(r, 8, stride=4), :].reshape(pairs * 8, 128) for r in range(4)
        ]
        before = from_before(classes[3])
        for tap, (even, odd) in enumerate(
            ((before, classes[1]), (classes[0], classes[2]), (classes[1], classes[3]))
        ):
            both = jnp.concatenate(
                [even.reshape(pairs, 1, 8, 128), odd.reshape(pairs, 1, 8, 128)], axis=1
            )
            out_ref[plane, tap] = both.reshape(pairs * 16, 128).astype(BF16)


def last_planes_kernel(volume_ref, out_ref, sem):
    count = out_ref.shape[0]
    copy = pltpu.make_async_copy(
        volume_ref.at[pl.ds(volume_ref.shape[0] - count, count)], out_ref, sem
    )
    copy.start()
    copy.wait()


def last_planes(volume, count):
    shape = (count, *volume.shape[1:])
    return pl.pallas_call(
        last_planes_kernel,
        out_shape=pltpu.VMEM(shape, BF16),
        in_specs=[pl.BlockSpec(memory_space=pltpu.HBM)],
        out_specs=pl.BlockSpec(memory_space=pltpu.VMEM),
        scratch_shapes=[pltpu.SemaphoreType.DMA],
        cost_estimate=pl.CostEstimate(
            flops=0, bytes_accessed=4 * shape[0] * shape[1] * shape[2], transcendentals=0
        ),
    )(volume)


def sorted_planes(volume):
    planes, rows, width = volume.shape
    pairs = width // 128
    return call(
        functools.partial(sort_kernel, planes),
        near((planes, 3, pairs * 16, 128), BF16),
        [pltpu.VMEM((pairs, rows, 128), F32)],
        volume,
    )


def put_rows(dst, pieces, offsets):
    rows = pieces[0].shape[0]
    for index, piece in enumerate(pieces):
        dst[pl.ds(pl.multiple_of(offsets[index], 16), rows), :] = piece[...]


def put_tap(columns, at, left, source):
    rows = source.shape[0]
    columns[at : at + 16, left : left + 128] = jnp.zeros((16, 128), BF16)
    columns[at + 16 : at + rows, left : left + 128] = source[0 : rows - 16, :]
    columns[at : at + rows, left + 128 : left + 256] = source[...]


def gather_taps(columns, sorted_ref, halo_ref, first, count):
    rows = sorted_ref.shape[2]
    for cell in range(count):
        for a in range(3):
            plane = 2 * (first + cell) - 1 + a
            for e in range(3):
                source = (
                    halo_ref.at[halo_ref.shape[0] + plane, e] if plane < 0 else sorted_ref.at[plane, e]
                )
                put_tap(columns, cell * rows, (a * 3 + e) * 256, source)


def pad_first(whole, padded):
    for tap in range(9):
        padded[tap * 256 : tap * 256 + 64, :] = jnp.zeros((64, 128), BF16)
        padded[tap * 256 + 64 : (tap + 1) * 256, :] = whole[tap * 192 : (tap + 1) * 192, :]


def take_windows(read, dst, row, left, half):
    for e in range(3):
        for f in range(3):
            block = read(0 if f == 1 else 1, 0 if e == 1 else 1)
            if e == 0:
                block = from_before(block)
            if f == 0:
                block = jnp.concatenate(
                    [jnp.zeros((8, 128), F32), block[: half * 8 - 8]], axis=0
                )
            at = left + (e * 3 + f) * 128
            dst[row : row + half * 8, at : at + 128] = block.astype(BF16)


def forward_upper_kernel(
    offsets, sorted_ref, w0, w1, w2, w3,
    slope_ref, windows_ref, middle_ref, top_ref, partial_ref, padded_ref,
    columns, some, whole, upper,
):
    cells = sorted_ref.shape[0] // 2
    put_rows(whole, (w0, w1, w2, w3), offsets)
    pad_first(whole, padded_ref)
    gather_taps(columns, sorted_ref, None, 1, cells - 1)
    linear = jnp.dot(columns[...], padded_ref[...], preferred_element_type=F32)
    hidden = activate(linear)
    upper[...] = hidden.reshape(upper.shape)
    count = middle_ref.shape[0] * middle_ref.shape[1]
    middle_ref[...] = hidden[:count].reshape(middle_ref.shape).astype(BF16)
    top_ref[...] = hidden[count:].astype(BF16)
    slope_ref[...] = activate_slope(linear)
    half = upper.shape[1]
    for out in range(cells // 2):
        for a in range(3):
            plane = 2 * out - 1 + a
            if plane > 0:

                def read(column, row):
                    return upper[plane - 1, :, column, row].reshape(half * 8, 128)

                take_windows(read, windows_ref, out * half * 8, a * 9 * 128, half)
    for a in range(1, 3):
        for e in range(3):
            put_tap(some, 0, ((a - 1) * 3 + e) * 256, sorted_ref.at[a - 1, e])
    partial_ref[...] = jnp.dot(some[...], padded_ref[3 * 256 :, :], preferred_element_type=F32)


def forward_upper(sorted_volume, shards, offsets):
    planes, _, rows, _ = sorted_volume.shape
    cells = planes // 2
    shard = shards[0].shape[0]
    some = (cells - 1) * rows
    return call(
        forward_upper_kernel,
        (
            near((some, 128), F32),
            near((cells * rows // 8, 27 * 128), BF16),
            sds((cells - 2, rows, 128), BF16),
            near((rows, 128), BF16),
            near((rows, 128), F32),
            near((9 * 256, 128), BF16),
        ),
        [
            pltpu.VMEM((some, 9 * 256), BF16),
            pltpu.VMEM((rows, 6 * 256), BF16),
            pltpu.VMEM((4 * shard, 128), BF16),
            pltpu.VMEM((cells - 1, rows // 32, 2, 2, 8, 128), F32),
        ],
        sorted_volume, *shards,
        smem=(offsets,),
        micros=2.5,
    )


def forward_lower_kernel(
    alive, side, halo_ref, top_ref, partial_ref, padded_ref,
    slope_ref, windows_ref, sorted_ref, here_ref, there_ref, wide, columns, some, lowest, planes,
):
    rows = partial_ref.shape[0]
    half = rows // 32
    sort_kernel(halo_ref.shape[0], halo_ref, sorted_ref, wide)
    for e in range(3):
        for a in range(3):
            put_tap(columns, 0, (a * 3 + e) * 256, sorted_ref.at[a, e])
        put_tap(some, 0, e * 256, sorted_ref.at[2, e])
    below = jnp.dot(columns[...], padded_ref[...], preferred_element_type=F32)
    here = partial_ref[...] + jnp.dot(
        some[...], padded_ref[: 3 * 256, :], preferred_element_type=F32
    )
    slope_ref[:rows, :] = activate_slope(below)
    slope_ref[rows:, :] = activate_slope(here)
    lowest[0] = (activate(below) * alive[0]).reshape(lowest.shape[1:])
    lowest[1] = activate(here).reshape(lowest.shape[1:])
    planes[0] = lowest[0].reshape(rows, 128).astype(BF16)
    planes[1] = lowest[1].reshape(rows, 128).astype(BF16)
    planes[2] = planes[1]
    planes[3] = top_ref[...]
    here_ref[...] = planes[pl.ds(2 * side[0], 2)]
    there_ref[...] = planes[pl.ds(2 - 2 * side[0], 2)]
    for a in range(2):

        def read(column, row):
            return lowest[a, :, column, row].reshape(half * 8, 128)

        take_windows(read, windows_ref, 0, a * 9 * 128, half)


def forward_lower(halo, top, partial, padded, alive, side):
    rows = partial.shape[0]
    return call(
        forward_lower_kernel,
        (
            near((2 * rows, 128), F32),
            near((rows // 4, 2 * 9 * 128), BF16),
            near((halo.shape[0], 3, rows, 128), BF16),
            sds((2, rows, 128), BF16),
            sds((2, rows, 128), BF16),
        ),
        [
            pltpu.VMEM((rows // 16, halo.shape[1], 128), F32),
            pltpu.VMEM((rows, 9 * 256), BF16),
            pltpu.VMEM((rows, 3 * 256), BF16),
            pltpu.VMEM((2, rows // 32, 2, 2, 8, 128), F32),
            pltpu.VMEM((4, rows, 128), BF16),
        ],
        halo, top, partial, padded,
        smem=(alive, side),
        micros=1.5,
    )


def put_pieces(flat, outs, slots, order):
    for index, out in enumerate(outs):
        count, size, _ = out.shape
        for place in range(count):
            row = pl.multiple_of(order[place] * size, 8)
            out[place] = flat[slots[index], pl.ds(row, size), :].astype(BF16)


def forward_second_kernel(
    offsets, upper_ref, lower_ref, cot_ref, w0, w1, w2, w3, act_ref, delta_ref, whole, windows
):
    put_rows(whole, (w0, w1, w2, w3), offsets)
    low, width = lower_ref.shape
    windows[:low, :width] = lower_ref[...]
    windows[:low, width:] = upper_ref[:low, width:]
    windows[low:, :] = upper_ref[low:, :]
    linear = jnp.dot(windows[...], whole[...], preferred_element_type=F32)
    outs, _, width = cot_ref.shape
    features = linear.shape[1]
    count = width // features
    acted = activate(linear)
    slope = activate_slope(linear)
    deltas = []
    for out in range(outs):
        base = out * count * 8
        act_ref[out] = jnp.concatenate(
            [acted[base + q * 8 : base + (q + 1) * 8] for q in range(count)], axis=1
        ).astype(BF16)
        cot = cot_ref[out].astype(F32)
        deltas.append(
            jnp.concatenate(
                [cot[:, q * features : (q + 1) * features] for q in range(count)], axis=0
            )
        )
    delta_ref[...] = (jnp.concatenate(deltas, axis=0) * slope).astype(BF16)


def forward_second(upper, lower, cot, shards, offsets):
    rows, features = shards[0].shape
    return call(
        forward_second_kernel,
        (sds(cot.shape, BF16), sds((upper.shape[0], features), BF16)),
        [pltpu.VMEM((4 * rows, features), BF16), pltpu.VMEM(upper.shape, BF16)],
        upper, lower, cot, *shards,
        smem=(offsets,),
        micros=1.5,
    )


def second_rows_kernel(
    data, table, order, e0, e1, e2, e3, m0, m1, m2, m3, d0, d1, d2, d3,
    out_ref, wide, windows, deltas, product, flat,
):
    edges, rows, _ = e0.shape
    cells = edges + m0.shape[0]
    half = rows // 32
    outs = cells // 2
    size = half * 8
    taps = windows.shape[1] // 128
    samples = ((e0, m0, d0), (e1, m1, d1), (e2, m2, d2), (e3, m3, d3))
    for sample, (edge, middle, delta) in enumerate(samples):
        at = sample * cells
        wide[at : at + edges] = edge[...].astype(F32).reshape(edges, half, 2, 2, 8, 128)
        wide[at + edges : at + cells] = (
            middle[...].astype(F32).reshape(cells - edges, half, 2, 2, 8, 128)
        )
        deltas[sample * outs * size : (sample + 1) * outs * size, :] = delta[...]
    for tap in range(taps):
        e, f = table[data[0], tap], table[data[0], taps + tap]
        row = jnp.where(e == 1, 0, 1)
        column = jnp.where(f == 1, 0, 1)
        for sample in range(4):
            for out in range(outs):
                plane = sample * cells + table[data[0], (2 + out) * taps + tap]
                block = wide[plane, :, column, row].reshape(size, 128)
                block = jnp.where(e == 0, from_before(block), block)
                later = jnp.concatenate([jnp.zeros((8, 128), F32), block[: size - 8]], axis=0)
                block = jnp.where(f == 0, later, block)
                at = (sample * outs + out) * size
                windows[at : at + size, tap * 128 : (tap + 1) * 128] = block.astype(BF16)
    product[...] = lax.dot_general(
        windows[...], deltas[...], (((0,), (0,)), ((), ())), preferred_element_type=F32
    )
    lanes = product.shape[1] // 128
    count, piece, _ = out_ref.shape
    shard = 27 * 128 // 4
    for lane in range(lanes):
        flat[lane * shard : (lane + 1) * shard, :] = product[
            pl.ds(pl.multiple_of(table[data[0], (2 + outs) * taps], 16), shard), lane * 128 : (lane + 1) * 128
        ]
    rest = flat.shape[0] - lanes * shard
    if rest:
        flat[lanes * shard :, :] = jnp.zeros((rest, 128), F32)
    for place in range(count):
        row = pl.multiple_of(order[place] * piece, 8)
        out_ref[place] = flat[pl.ds(row, piece), :].astype(BF16)


def second_rows(edges, middles, deltas, data, order, places, size):
    _, rows, _ = edges[0].shape
    cells = edges[0].shape[0] + middles[0].shape[0]
    cellrows, features = deltas[0].shape
    taps = 8
    table = []
    for shard in range(4):
        start = shard * 27 // 4
        at = [min(start + tap, 26) for tap in range(taps)]
        held = (-1, 0, *range(1, cells - 1)) if shard < 2 else (0, cells - 1, *range(1, cells - 1))
        table.append(
            [tap // 3 % 3 for tap in at]
            + [tap % 3 for tap in at]
            + [held.index(2 * out - 1 + tap // 9) for out in range(cells // 2) for tap in at]
            + [shard * (27 * 128 // 4) - start * 128]
        )
    return call(
        second_rows_kernel,
        sds((places, size, 128), BF16),
        [
            pltpu.VMEM((4 * cells, rows // 32, 2, 2, 8, 128), F32),
            pltpu.VMEM((4 * cellrows, taps * 128), BF16),
            pltpu.VMEM((4 * cellrows, features), BF16),
            pltpu.VMEM((taps * 128, features), F32),
            pltpu.VMEM((places * size, 128), F32),
        ],
        *edges, *middles, *deltas,
        smem=(data.reshape(1), jnp.array(table, jnp.int32), order),
        micros=2.0,
    )


def back_second_kernel(
    offsets, slots, order, delta_ref, w0, w1, w2, w3,
    slope_low_ref, slope_ref, sorted_ref, halo_ref,
    low_ref, last_ref, down_ref, g0, g1, g2, g3,
    whole, product, columns, deltas, flat,
):
    rows = sorted_ref.shape[2]
    cells = sorted_ref.shape[0] // 2
    half = rows // 32
    size = half * 8
    put_rows(whole, (w0, w1, w2, w3), offsets)
    product[...] = lax.dot_general(
        delta_ref[...], whole[...], (((1,), (1,)), ((), ())), preferred_element_type=F32
    )
    gather_taps(columns, sorted_ref, halo_ref, -1, cells + 1)

    def term(out, a, e, f):
        left = ((a * 3 + e) * 3 + f) * 128
        block = product[out * size : (out + 1) * size, left : left + 128]
        if f == 0:
            block = jnp.concatenate([block[8:], jnp.zeros((8, 128), F32)], axis=0)
        if e == 0:
            block = from_after(block)
        return block.reshape(half, 8, 128)

    for plane in range(-1, cells):
        taps = [
            (out, a) for out in range(cells // 2) for a in range(3) if 2 * out - 1 + a == plane
        ]
        sums = [
            sum(
                term(out, a, e, f)
                for out, a in taps
                for e in ((0, 2) if row else (1,))
                for f in ((0, 2) if column else (1,))
            ).reshape(half, 1, 8, 128)
            for column in range(2)
            for row in range(2)
        ]
        spread = jnp.concatenate(sums, axis=1).reshape(rows, 128)
        if plane < 1:
            slope = slope_low_ref[(plane + 1) * rows : (plane + 2) * rows, :]
        else:
            slope = slope_ref[(plane - 1) * rows : plane * rows, :]
        delta = (spread * slope).astype(BF16)
        deltas[(plane + 1) * rows : (plane + 2) * rows, :] = delta
        if plane < 0:
            down_ref[:rows, :] = spread.astype(BF16)
        if plane == 0:
            down_ref[rows:, :] = delta
        if plane == cells - 1:
            last_ref[...] = spread
        elif plane >= 0:
            low_ref[plane * rows : (plane + 1) * rows, :] = delta
    flipped = jnp.transpose(deltas[...].astype(F32)).astype(BF16)
    tally = jnp.dot(flipped, columns[...], preferred_element_type=F32)
    shard_rows = 9 * 192 // 4
    for tap in range(9):
        turned = jnp.transpose(tally[:, tap * 256 : (tap + 1) * 256])[64:]
        at = tap * 192
        while at < (tap + 1) * 192:
            shard = at // shard_rows
            to = min((tap + 1) * 192, (shard + 1) * shard_rows)
            flat[shard, at - shard * shard_rows : to - shard * shard_rows, :] = turned[
                at - tap * 192 : to - tap * 192
            ]
            at = to
    rest = flat.shape[1] - shard_rows
    if rest:
        flat[:, shard_rows:, :] = jnp.zeros((4, rest, 128), F32)
    put_pieces(flat, (g0, g1, g2, g3), slots, order)


def back_second(delta, shards, slopes, sorted_volume, halo, offsets, slots, order, places, size):
    rows, features = shards[0].shape
    planes, _, width, _ = sorted_volume.shape
    cells = planes // 2
    piece = sds((places, size, 128), BF16)
    return call(
        back_second_kernel,
        (
            near(((cells - 1) * width, 128), BF16),
            near((width, 128), F32),
            sds((2 * width, 128), BF16),
            piece, piece, piece, piece,
        ),
        [
            pltpu.VMEM((4 * rows, features), BF16),
            pltpu.VMEM((delta.shape[0], 4 * rows), F32),
            pltpu.VMEM(((cells + 1) * width, 9 * 256), BF16),
            pltpu.VMEM(((cells + 1) * width, 128), BF16),
            pltpu.VMEM((4, places * size, 128), F32),
        ],
        delta, *shards, *slopes, sorted_volume, halo,
        smem=(offsets, slots, order),
        micros=3.5,
    )


def back_input_kernel(
    offsets, low_ref, last_ref, slope_ref, upper_ref, w0, w1, w2, w3,
    out_ref, whole, turned, pairs, product, wide, last,
):
    put_rows(whole, (w0, w1, w2, w3), offsets)
    for tap in range(9):
        top = tap * 128
        turned[top : top + 128, 0:128] = whole[tap * 192 + 64 : (tap + 1) * 192, :]
        turned[top : top + 64, 128:256] = jnp.zeros((64, 128), BF16)
        turned[top + 64 : top + 128, 128:256] = whole[tap * 192 : tap * 192 + 64, :]
    planes = out_ref.shape[0]
    cells = planes // 2
    rows = last_ref.shape[0]
    groups = rows // 16
    last[...] = (
        (last_ref[...] + upper_ref[:rows, :].astype(F32)) * slope_ref[(cells - 2) * rows :, :]
    ).astype(BF16)
    for cell in range(cells + 1):
        at = cell * rows
        if cell < cells - 1:
            source = low_ref.at[at : at + rows]
        else:
            source = last if cell == cells - 1 else upper_ref.at[rows : 2 * rows]
        pairs[at : at + rows, 0:128] = source[...]
        pairs[at : at + rows - 16, 128:256] = source[16:rows, :]
        pairs[at + rows - 16 : at + rows, 128:256] = jnp.zeros((16, 128), BF16)
    product[...] = lax.dot_general(
        pairs[...], turned[...], (((1,), (1,)), ((), ())), preferred_element_type=F32
    ).reshape(product.shape)

    def part(cell, a, e, parity):
        left = (a * 3 + e) * 128
        return product[cell * groups : (cell + 1) * groups, parity, :, left : left + 128]

    def after(block):
        flat = block.reshape(groups * 8, 128)
        return from_after(flat).reshape(groups, 8, 128)

    for plane in range(planes):
        taps = [(o, a) for o in range(cells + 1) for a in range(3) if 2 * o - 1 + a == plane]
        wide[:, pl.ds(0, 8, stride=4), :] = sum(part(o, a, 1, 0) for o, a in taps)
        wide[:, pl.ds(1, 8, stride=4), :] = sum(
            part(o, a, 2, 0) + part(o, a, 0, 1) for o, a in taps
        )
        wide[:, pl.ds(2, 8, stride=4), :] = sum(part(o, a, 1, 1) for o, a in taps)
        wide[:, pl.ds(3, 8, stride=4), :] = sum(part(o, a, 2, 1) for o, a in taps) + after(
            sum(part(o, a, 0, 0) for o, a in taps)
        )
        for group in range(groups):
            lanes = slice(group * 128, (group + 1) * 128)
            out_ref[plane, :, lanes] = wide[group].astype(BF16)


def back_input(low, last, slope, upper, shards, offsets, shape):
    planes, side, width = shape
    shard = shards[0].shape[0]
    rows = low.shape[0] + upper.shape[0]
    return call(
        back_input_kernel,
        sds(shape, BF16),
        [
            pltpu.VMEM((4 * shard, 128), BF16),
            pltpu.VMEM((9 * 128, 256), BF16),
            pltpu.VMEM((rows, 256), BF16),
            pltpu.VMEM((rows // 16, 2, 8, 9 * 128), F32),
            pltpu.VMEM((width // 128, side, 128), F32),
            pltpu.VMEM(last.shape, BF16),
        ],
        low, last, slope, upper, *shards,
        smem=(offsets,),
        micros=3.0,
    )


def unpack_kernel(scale_first, scale_second, order, *refs):
    *chunks, first_ref, second_ref, flat_first, flat_second, sems = refs
    high = order.shape[0] // 2
    small = flat_first.shape[0] // (2 * high)
    big = flat_second.shape[0] // (2 * high)
    for low in range(2):
        for index in range(high):
            if low and index and index == high - 1:
                chunk = chunks[-1][0].astype(F32)
            elif low and index:
                chunk = chunks[high + 1][index - 1].astype(F32)
            else:
                chunk = chunks[index + low * high][...].astype(F32)
            place = order[low * high + index]
            flat_second[pl.ds(pl.multiple_of(place * big, 8), big), :] = chunk[:big, :] * scale_second
            flat_first[pl.ds(pl.multiple_of(place * small, 8), small), :] = chunk[big:, :] * scale_first
    rows, features = second_ref.shape
    copies = [
        pltpu.make_async_copy(
            flat_second.at[lane * rows : (lane + 1) * rows],
            second_ref.at[:, lane * 128 : (lane + 1) * 128],
            sems.at[lane],
        )
        for lane in range(features // 128)
    ]
    copies.append(
        pltpu.make_async_copy(
            flat_first.at[: first_ref.shape[0]], first_ref, sems.at[features // 128]
        )
    )
    for copy in copies:
        copy.start()
    for copy in copies:
        copy.wait()


def wide_sum(*pieces):
    return sum(piece.astype(F32) for piece in pieces)


def added(*pieces):
    return wide_sum(*pieces).astype(BF16)


def swap(value, axis, bits):
    size = lax.axis_size(axis)
    return lax.ppermute(value, axis, [(i, i ^ bits) for i in range(size)])


def shifted(value, axis, by):
    size = lax.axis_size(axis)
    pairs = [(i, i + by) for i in range(size) if 0 <= i + by < size]
    return lax.ppermute(value, axis, pairs)


def local(volume, weight_first, weight_second, cotangent):
    samples, planes, side, width = volume.shape
    data = lax.axis_index("dp")
    place = lax.axis_index("space")
    spaces = lax.axis_size("space")
    high = spaces // 2
    small, big = weight_first.shape[0], weight_second.shape[0]
    slots = jnp.arange(4, dtype=jnp.int32) ^ data
    offsets_first = slots * small
    offsets_second = slots * big
    alive = (place > 0).astype(F32).reshape(1)
    x_side = lax.shift_right_logical(data, 1)
    steps = jnp.arange(spaces, dtype=jnp.int32)
    order = place ^ (2 * (steps % high) + steps // high)
    lanes = weight_second.shape[1] // 128
    size_first = -(-small // (8 * spaces)) * 8
    size_second = -(-lanes * big // (8 * spaces)) * 8

    inputs = volume.reshape(planes, side, width)
    uppermost = last_planes(inputs, 3)
    first_x = swap(weight_first, "dp", 2)
    first_core = swap(weight_first, "dp", 1)
    second_x = swap(weight_second, "dp", 2)
    second_core = swap(weight_second, "dp", 1)
    halo = shifted(uppermost, "space", 1)
    first_far = swap(first_x, "dp", 1)
    shards_first = (weight_first, first_core, first_x, first_far)

    sorted_volume = sorted_planes(inputs)
    slope, windows, middle, top, partial, padded = forward_upper(
        sorted_volume, shards_first, offsets_first
    )
    middle_x, middle_core = swap(middle, "dp", 2), swap(middle, "dp", 1)
    second_x, partial = lax.optimization_barrier((second_x, partial))
    second_far = swap(second_x, "dp", 1)
    shards_second = (weight_second, second_core, second_x, second_far)
    slope_low, windows_low, sorted_halo, edge, edge_there = forward_lower(
        halo, top, partial, padded, alive, x_side.reshape(1)
    )
    cot = cotangent.reshape(cotangent.shape[1:])
    activations, delta_second = forward_second(
        windows, windows_low, cot, shards_second, offsets_second
    )
    delta_second, middle_x = lax.optimization_barrier((delta_second, middle_x))
    edge_x, edge_core = swap(edge_there, "dp", 2), swap(edge, "dp", 1)
    delta_x, delta_core = swap(delta_second, "dp", 2), swap(delta_second, "dp", 1)
    low, last, down, *first = back_second(
        delta_second, shards_second, (slope_low, slope), sorted_volume, sorted_halo,
        offsets_second, slots, order, spaces, size_first,
    )
    middle_far = swap(middle_x, "dp", 1)
    first, down, delta_x, edge_x, delta_core, edge_core, middle_far = lax.optimization_barrier(
        (first, down, delta_x, edge_x, delta_core, edge_core, middle_far)
    )
    second = second_rows(
        (edge, edge_core, edge_x, swap(edge_x, "dp", 1)),
        (middle, middle_core, middle_x, middle_far),
        (delta_second, delta_core, delta_x, swap(delta_x, "dp", 1)),
        data, order, spaces, size_second,
    )
    second, down = lax.optimization_barrier((second, down))
    upper = shifted(down, "space", -1)

    def pieces(value):
        return value.reshape(2, high, -1, 128)

    far, beside = pieces(swap(first[3], "dp", 1)), pieces(swap(first[1], "dp", 1))
    own, there = pieces(first[0]), pieces(first[2])
    both = [
        (d * spaces + s, (d ^ 2) * spaces + (s ^ 1)) for d in range(4) for s in range(spaces)
    ]
    second = pieces(second)
    sent_y = jnp.concatenate([second[1], added(own[1], beside[1])], axis=1)
    got_y = swap(sent_y[1:], "space", 1)
    got_x = swap(added(there[0], far[0]), "dp", 2)
    got_y_own = swap(sent_y[:1], "space", 1)
    got_xy = lax.ppermute(added(there[1], far[1]), ("dp", "space"), both)

    def held(places, got):
        return jnp.concatenate(
            [
                wide_sum(second[0][places], got[:, :size_second]),
                wide_sum(
                    own[0][places], beside[0][places], got_x[places], got_xy[places],
                    got[:, size_second:],
                ),
            ],
            axis=1,
        )

    sent = held(slice(1, high), got_y).astype(BF16)
    *received, got_y_own, upper = lax.optimization_barrier(
        (*(swap(sent[k - 1], "space", 2 * k) for k in range(1, high)), got_y_own, upper)
    )
    mine = added(held(slice(0, 1), got_y_own)[0], *received)
    others = [swap(mine, "space", 2 * k) for k in range(1, high)]
    mine_y = swap(mine, "space", 1)
    late = [swap(jnp.stack(others[-1:]), "space", 1)] if others else []
    early = [swap(jnp.stack(others[:-1]), "space", 1)] if len(others) > 1 else []
    upper, mine_y = lax.optimization_barrier((upper, mine_y))
    chunks = [mine, *others, mine_y, *early, *late]

    gradient = back_input(low, last, slope, upper, shards_first, offsets_first, inputs.shape)

    cells_first = samples * lax.axis_size("dp") * (planes // 2) * spaces * (side // 2) ** 2
    cells_second = cells_first // 8
    first_gradient, second_gradient = call(
        functools.partial(unpack_kernel, float(cells_first) ** -0.5, float(cells_second) ** -0.5),
        (sds(weight_first.shape, F32), sds(weight_second.shape, F32)),
        [
            pltpu.VMEM((spaces * size_first, 128), F32),
            pltpu.VMEM((spaces * size_second, 128), F32),
            pltpu.SemaphoreType.DMA((lanes + 1,)),
        ],
        *chunks,
        smem=(order,),
        out_space=pltpu.HBM,
    )
    return (
        activations.reshape(cotangent.shape),
        gradient.reshape(volume.shape),
        first_gradient,
        second_gradient,
    )


def solution(mesh):
    return jax.shard_map(
        local,
        mesh=mesh,
        in_specs=(
            P("dp", "space", None, None),
            P("dp", None),
            P("dp", None),
            P("dp", "space", None, None),
        ),
        out_specs=(
            P("dp", "space", None, None),
            P("dp", "space", None, None),
            P("dp", None),
            P("dp", None),
        ),
        check_vma=False,
    )
```
